128 devices in a mesh: rep: 4 (over x_lo, core), fsdp: 32 (over z, x_hi, y).
Axes of the slice: x: 4 (x_hi: 2, x_lo: 2; x = x_hi * 2 + x_lo), y: 4, z: 4, core: 2. Of those that a mesh axis runs over, the one named last changes fastest.
Arguments:
- patches: bfloat16 [4, 1, 2, 32, 196, 768], P('rep', None, None, 'fsdp'), may hold values from -6 to 6
- labels: int32 [4, 1, 2, 32], P('rep', None, None, 'fsdp'), may hold values from 0 to 999
- counts: int32 [4, 1, 2], P('rep'), may hold values from 17 to 32
- weights: float32 [8593408], P('fsdp')
- first_moments: float32 [4, 8593408], P('rep', 'fsdp')
- second_moments: float32 [4, 8593408], P('rep', 'fsdp')
- outer_momentum: float32 [8593408], P('fsdp')
Outputs:
- averaged_diff: float32 [8593408], P('fsdp')
- momentum_out: float32 [8593408], P('fsdp')
- new_weights: float32 [8593408], P('fsdp')
- first_out: float32 [4, 8593408], P('rep', 'fsdp')
- second_out: float32 [4, 8593408], P('rep', 'fsdp')
- loss_sums: float32 [4, 1], P('rep')
The draws below stay inside these ranges and needn't reach their ends.
All inputs are finite; a program needn't handle non-finite values.
Results may differ from the reference program's by a relative error of at most 0.013.
Values may be sent and summed in bfloat16 or wider, within the bound.
A program may use at most 320 MiB of HBM per device.

```python
import math
from functools import partial
import jax
import jax.numpy as jnp
from jax import lax

D = 768
HEADS = 12
HEAD_DIM = 64
FF = 3072
CLS = 1000
PIX = 768
P_SIZE = 196
LAYERS = 1
INNER = 1
MB = 2
STEP = 10
IMGS = 32
REPS = 4
NIMG = 48
NPARAM = 8593408
N_REP = 4


def segment_table():
    grad = 1.8 * D ** (-0.5) * (NIMG * P_SIZE) ** (-0.5)
    rows = [(PIX * D, 0.0, PIX ** (-0.5), grad), (P_SIZE * D, 0.0, 0.5, 1.4 * grad * P_SIZE ** (-0.5)), (D, 1.0, 0.1, 2.0 * grad), (D, 0.0, 0.2, 2.0 * grad), (D * CLS, 0.0, 2.0 * D ** (-0.5), 0.2 / NIMG)]
    for layer in range(LAYERS):
        rows += [(D, 1.0, 0.1, grad), (D, 0.0, 0.2, grad), (D, 1.0, 0.1, grad), (D, 0.0, 0.2, grad), (3 * D * D, 0.0, D ** (-0.5), grad), (D * D, 0.0, 4.0 * D ** (-0.5), grad), (D * FF, 0.0, D ** (-0.5), grad), (FF * D, 0.0, FF ** (-0.5), grad)]
    used = sum((row[0] for row in rows))
    rows.append((NPARAM - used, 0.0, 0.02, grad))
    return rows


def spread_out(column):
    return jnp.concatenate([jnp.full((row[0],), row[column], jnp.float32) for row in segment_table()])


def signed_noise(key, shape, width):
    return width * jax.random.truncated_normal(key, -3.0, 3.0, shape, jnp.float32)


def draw_weights(key, part):
    key = jax.random.fold_in(key, 1)
    return spread_out(1) + spread_out(2) * signed_noise(key, (NPARAM,), 1.0)


def draw_first_moments(key, part):
    key = jax.random.fold_in(key, 2)
    return 0.11 * spread_out(3)[None, :] * signed_noise(key, (REPS, NPARAM), 1.0)


def draw_second_moments(key, part):
    key = jax.random.fold_in(key, 3)
    factor = jnp.exp(jax.random.uniform(key, (REPS, NPARAM), jnp.float32, 0.0, math.log(4.0)))
    scale = spread_out(3)
    return 0.0526 * factor * (scale * scale)[None, :]


def draw_outer_momentum(key, part):
    key = jax.random.fold_in(key, 4)
    return 0.3 * spread_out(2) * signed_noise(key, (NPARAM,), 1.0)


def with_ends(array, own_key, low, top_value):
    longest = array.shape.index(max(array.shape))
    spots = []
    for shift in (0, 1):
        where = [jax.random.randint(jax.random.fold_in(own_key, axis), (), 0, length) for axis, length in enumerate(array.shape)]
        where[longest] = (where[longest] + shift) % array.shape[longest]
        spots.append(tuple(where))
    return array.at[spots[0]].set(low).at[spots[1]].set(top_value)


def block_levels(own_key, dims, cuts, smallest, top_value):
    def one(dim, parts):
        steps = jax.random.uniform(jax.random.fold_in(jax.random.fold_in(own_key, 6), dim), (parts,), jnp.float32, smallest / len(cuts), top_value / len(cuts))
        return jnp.repeat(jnp.exp(steps), dims[dim] // parts).reshape((-1,) + (1,) * (len(dims) - dim - 1))

    loudness = one(*cuts[0])
    for cut in cuts[1:]:
        loudness = loudness * one(*cut)
    return loudness


def noise(key, extent, scale, reach, cuts=(), kind=jnp.bfloat16):
    drawn = jax.random.normal(key, extent, jnp.float32) * scale
    if len(cuts) > 0:
        drawn = block_levels(key, extent, cuts, -0.22, 0.18) * drawn
    return jnp.clip(drawn, min=-reach, max=reach).astype(kind)


def setup_inputs(seed: int = 0) -> dict:
    splits = jax.random.split(jax.random.key(seed), 8)
    return {
        "patches": noise(splits[0], (REPS, INNER, MB, IMGS, P_SIZE, PIX), 1.0, 6.0, ((0, 4), (3, 32))),
        "labels": with_ends(jax.random.randint(splits[1], (REPS, INNER, MB, IMGS), 0, CLS), jax.random.fold_in(splits[1], 1), 0, CLS - 1).astype(jnp.int32),
        "counts": with_ends(jax.random.randint(splits[2], (REPS, INNER, MB), IMGS // 2 + 1, IMGS + 1), jax.random.fold_in(splits[2], 1), IMGS // 2 + 1, IMGS).astype(jnp.int32),
        "weights": draw_weights(jax.random.fold_in(splits[7], 71), 0),
        "first_moments": draw_first_moments(jax.random.fold_in(splits[7], 71), 0),
        "second_moments": draw_second_moments(jax.random.fold_in(splits[7], 71), 0),
        "outer_momentum": draw_outer_momentum(jax.random.fold_in(splits[7], 71), 0),
    }


@jax.custom_vjp
def low(v):
    return lax.optimization_barrier(v.astype(jnp.bfloat16)).astype(jnp.float32)

@jax.custom_vjp
def low_back(v):
    return v

def low_keep(v):
    return (low(v), None)

def low_pass(kept, grad):
    return (grad,)

def back_keep(v):
    return (v, None)

def back_low(kept, grad):
    return (low(grad),)
low.defvjp(low_keep, low_pass)
low_back.defvjp(back_keep, back_low)
NORM_EPS = 1e-06
SMOOTHING = 0.1
BETA_ONE = 0.9
BETA_TWO = 0.95
ADAM_EPS = 1e-08
DECAY = 0.05
INNER_RATE = 0.01
OUTER_RATE = 0.7
OUTER_MU = 0.9
HIGH = lax.Precision.HIGHEST

def layout():
    shapes = [(PIX, D), (P_SIZE, D), (2, D), (D, CLS)]
    for layer in range(LAYERS):
        shapes += [(4, D), (D, 3 * D), (D, D), (D, FF), (FF, D)]
    return shapes

def unflatten(flat):
    pieces = []
    start = 0
    for shape in layout():
        count = shape[0] * shape[1]
        pieces.append(flat[start:start + count].reshape(shape))
        start += count
    return pieces

def normalize(x, gain, shift):
    mean = lax.optimization_barrier(jnp.mean(x, -1, keepdims=True))
    centred = x - mean
    var = lax.optimization_barrier(jnp.mean(centred * centred, -1, keepdims=True))
    return centred * lax.rsqrt(var + NORM_EPS) * gain + shift

def matmul(left, right):
    return jnp.dot(left, right, precision=HIGH)

def image_loss(pieces, patch, label):
    embed, pos, final, head = pieces[:4]
    h = low_back(matmul(patch, embed)) + pos
    for layer in range(LAYERS):
        norms, qkv, out, fc_in, fc_out = pieces[4 + 5 * layer:9 + 5 * layer]
        a = low(normalize(h, norms[0], norms[1]))
        mix = low(low_back(matmul(a, qkv)))
        query = mix[:, :D].reshape(P_SIZE, HEADS, HEAD_DIM)
        key_rows = mix[:, D:2 * D].reshape(P_SIZE, HEADS, HEAD_DIM)
        value = mix[:, 2 * D:].reshape(P_SIZE, HEADS, HEAD_DIM)
        scores = low_back(jnp.einsum('qhe,khe->hqk', query, key_rows, precision=HIGH) * HEAD_DIM ** (-0.5))
        prob = jax.nn.softmax(scores, -1)
        mixed = jnp.einsum('hqk,khe->qhe', low(prob), value, precision=HIGH).reshape(P_SIZE, D)
        mixed = low(low_back(mixed))
        h = h + low_back(matmul(mixed, out))
        a_two = low(normalize(h, norms[2], norms[3]))
        pre = low_back(matmul(a_two, fc_in))
        hidden = low(jax.nn.gelu(pre, approximate=False))
        h = h + low_back(matmul(hidden, fc_out))
    pooled = low(lax.optimization_barrier(jnp.mean(normalize(h, final[0], final[1]), 0)))
    logits = low_back(jnp.dot(pooled, head, precision=HIGH))
    logp = jax.nn.log_softmax(logits)
    target = (1.0 - SMOOTHING) * (jnp.arange(CLS) == label).astype(jnp.float32) + SMOOTHING / CLS
    return -jnp.sum(target * logp)

def batch_objective(flat, patches, labels, scales):
    pieces = unflatten(low(flat))
    block = 8 if IMGS % 8 == 0 else 1
    shaped = (patches.reshape((IMGS // block, block) + patches.shape[1:]), labels.reshape(IMGS // block, block), scales.reshape(IMGS // block, block))

    def one_block(pieces_in, patch_block, label_block):
        return jax.vmap(image_loss, in_axes=(None, 0, 0))(pieces_in, patch_block, label_block)

    def step(carry, item):
        patch_block, label_block, scale_block = item
        values = jax.checkpoint(one_block)(pieces, patch_block, label_block)
        return (carry + jnp.sum(scale_block * values), values)
    total, values = lax.scan(step, jnp.zeros((), jnp.float32), shaped)
    return (total, values.reshape(IMGS))

def adam_step(master, first, second, grad, number):
    first = BETA_ONE * first + (1.0 - BETA_ONE) * grad
    second = BETA_TWO * second + (1.0 - BETA_TWO) * grad * grad
    fix_one = 1.0 - BETA_ONE ** number
    fix_two = 1.0 - BETA_TWO ** number
    update = first / fix_one / (jnp.sqrt(second / fix_two) + ADAM_EPS)
    master = master - INNER_RATE * (update + DECAY * master)
    return (master, first, second)

def reference(patches, labels, counts, weights, first_moments, second_moments, outer_momentum):

    def run_group(item):
        group_patches, group_labels, group_counts, first, second = item
        master = weights
        sums = []
        for step in range(INNER):
            total = jnp.sum(group_counts[step]).astype(jnp.float32)
            grad = jnp.zeros_like(master)
            loss_sum = jnp.zeros((), jnp.float32)
            for micro in range(MB):
                valid = (jnp.arange(IMGS) < group_counts[step, micro]).astype(jnp.float32)
                objective = partial(batch_objective, patches=group_patches[step, micro].astype(jnp.float32), labels=group_labels[step, micro], scales=valid / total)
                unused, pull, values = jax.vjp(objective, master, has_aux=True)
                grad = grad + pull(jnp.ones((), jnp.float32))[0]
                loss_sum = loss_sum + jnp.sum(values * valid)
            sums.append(loss_sum)
            master, first, second = adam_step(master, first, second, grad, STEP + step)
        return (master, first, second, jnp.stack(sums))
    masters, firsts, seconds, losses = lax.map(run_group, (patches, labels, counts, first_moments, second_moments))
    averaged = lax.optimization_barrier(jnp.sum(weights[None, :] - masters, 0)) / N_REP
    momentum = OUTER_MU * outer_momentum + averaged
    new_weights = weights - OUTER_RATE * (averaged + OUTER_MU * momentum)
    return (averaged, momentum, new_weights, firsts, seconds, losses)
```

```python
from functools import partial

import jax
import jax.numpy as jnp
from jax import lax
from jax.experimental import pallas as pl
from jax.experimental.pallas import tpu as pltpu
from jax.sharding import PartitionSpec as P

SHARD = 2098
SLOT = 132
HALF = 66
QUART = 33
NSLOT = 32
SECTIONS = []
_t = 0
for _base, _c, _g, _rpg in ((0, 6, 61, 96), (5796, 8, 48, 125), (11796, 6, 1, 96), (11820, 18, 48, 288), (25644, 6, 48, 96), (30252, 24, 48, 384), (48684, 6, 192, 96)):
    SECTIONS.append((_base, _c, _g, _rpg, _t))
    _t += _c * _g
NTILE = _t
HI = 352
LO = 224
MARGIN = 512
FROWS = 3072
HEAD_ROWS = 16
MESH = pl.DeviceIdType.MESH


def coords():
    rep = lax.axis_index("rep")
    fs = lax.axis_index("fsdp")
    return lax.div(rep, 2), lax.rem(rep, 2), lax.div(fs, 8), lax.rem(lax.div(fs, 4), 2), lax.rem(fs, 4)


def device(xl, xh, core, z, y):
    return {"rep": xl * 2 + core, "fsdp": z * 8 + xh * 4 + y}


def gather_kernel(w_ref, patch_ref, meta_ref, t_out, patch_out, meta_out, flat, headrows, mainb, lob, hib, rmain, rlo, rhi, slot, local_sem, x_send, x_recv, g_send, g_recv):
    xl, b, z, a, y = coords()
    fs = z * 8 + a * 4 + y
    swap = a != b
    xo = lax.rem(xl + a + b, 2)
    up = lax.rem(fs + 1, NSLOT)
    down = lax.rem(fs + NSLOT - 1, NSLOT)

    def halo_to(s):
        return device(xo, b, lax.rem(lax.div(s, 4), 2), lax.div(s, 8), lax.rem(s, 4))

    def halo_from(s):
        sa = lax.rem(lax.div(s, 4), 2)
        return device(lax.rem(xl + sa + a, 2), sa, a, lax.div(s, 8), lax.rem(s, 4))

    partner = device(xo, b, a, z, y)
    mirror = device(xl, b, a, z, y)
    sibling = device(xl, a, 1 - b, z, y)

    def at_y(k):
        return device(xl, a, b, z, lax.rem(y + k, 4))

    def at_z(k):
        return device(xl, a, b, lax.rem(z + k, 4), y)

    load = pltpu.make_async_copy(w_ref, flat.at[pl.ds(MARGIN, SHARD)], local_sem.at[0])
    load.start()

    barrier = pltpu.get_barrier_semaphore()

    def greet(target):
        pl.semaphore_signal(barrier, inc=1, device_id=target, device_id_type=MESH)

    v = z * 8 + b * 4 + y
    for target in (halo_from(lax.rem(v + 1, NSLOT)), halo_from(lax.rem(v + NSLOT - 1, NSLOT)), at_y(1), at_y(3), at_z(1), at_z(3), sibling):
        greet(target)

    @pl.when(swap)
    def _():
        greet(partner)
        greet(mirror)

    def remote(src, dst, send, recv, k, target):
        return pltpu.make_async_remote_copy(src_ref=src, dst_ref=dst, send_sem=send.at[k], recv_sem=recv.at[k], device_id=target, device_id_type=MESH)

    pl.semaphore_wait(barrier, jnp.where(swap, 9, 7))

    load.wait()
    main = remote(mainb, rmain, x_send, x_recv, 0, partner)

    @pl.when(swap)
    def _():
        mainb[pl.ds(0, SHARD), :] = flat[pl.ds(MARGIN, SHARD), :].astype(jnp.bfloat16)
        main.start()

    hib[...] = flat[pl.ds(MARGIN + SHARD - HI, HI), :].astype(jnp.bfloat16)
    to_up = remote(hib, rlo, x_send, x_recv, 1, halo_to(up))
    to_up.start()
    lob[...] = flat[pl.ds(MARGIN, LO), :].astype(jnp.bfloat16)
    to_down = remote(lob, rhi, x_send, x_recv, 2, halo_to(down))
    to_down.start()

    patch_swap = remote(patch_ref, patch_out, x_send, x_recv, 3, mirror)
    meta_swap = remote(meta_ref, meta_out, x_send, x_recv, 4, mirror)
    patch_keep = pltpu.make_async_copy(patch_ref, patch_out, local_sem.at[1])
    meta_keep = pltpu.make_async_copy(meta_ref, meta_out, local_sem.at[2])

    @pl.when(swap)
    def _():
        patch_swap.start()
        meta_swap.start()
        main.wait_recv()
        flat[pl.ds(MARGIN, SHARD), :] = rmain[pl.ds(0, SHARD), :].astype(jnp.float32)

    @pl.when(jnp.logical_not(swap))
    def _():
        patch_keep.start()
        meta_keep.start()

    to_up.wait_recv()
    flat[pl.ds(MARGIN - HI, HI), :] = rlo[...].astype(jnp.float32)
    to_down.wait_recv()
    flat[pl.ds(MARGIN + SHARD, LO), :] = rhi[...].astype(jnp.float32)

    first = SLOT * v
    origin = SHARD * v - MARGIN
    for index, (base, c, groups, per, start) in enumerate(SECTIONS):
        lo = jnp.maximum(first, start)
        hi = jnp.minimum(first + SLOT, start + c * groups)
        if index == 1:
            lane = lax.broadcasted_iota(jnp.int32, (8, 128), 1)
            g0 = lax.div(jnp.maximum(lo, start) - start, 8)
            g1 = lax.div(jnp.maximum(hi, start) - start + 7, 8)

            def head_group(g, carry):
                row = base + per * g - origin
                for i in range(16):
                    q, s = divmod(1000 * i, 128)
                    one = flat[pl.ds(row + q, 8), :]
                    if s:
                        two = flat[pl.ds(row + q + 1, 8), :]
                        one = jnp.where(lane < 128 - s, pltpu.roll(one, 128 - s, 1), pltpu.roll(two, 128 - s, 1))
                    headrows[pl.ds(i * 8, 8), :] = one
                for j in range(8):
                    t = start + g * 8 + j - first

                    @pl.when(jnp.logical_and(t >= 0, t < SLOT))
                    def _():
                        slot[t] = headrows[pl.ds(j, 16, stride=8), :].astype(jnp.bfloat16)
                return carry

            lax.fori_loop(g0, g1, head_group, 0)
        else:

            def tile(t, carry):
                g = lax.div(t - start, c)
                j = lax.rem(t - start, c)
                row = base + 16 * c * g + j - origin
                slot[t - first] = flat[pl.ds(row, 16, stride=c), :].astype(jnp.bfloat16)
                return carry

            lax.fori_loop(lo, hi, tile, 0)
    pads = jnp.maximum(NTILE - first, 0)

    def blank(t, carry):
        slot[t] = jnp.zeros((16, 128), jnp.bfloat16)
        return carry

    lax.fori_loop(jnp.minimum(pads, SLOT), SLOT, blank, 0)

    def place(axis, k):
        return z * 8 + b * 4 + lax.rem(y + k, 4) if axis == 0 else (lax.rem(z + k, 4)) * 8 + b * 4 + y

    def place2(axis, k, j):
        if axis == 0:
            return (lax.rem(z + j, 4)) * 8 + b * 4 + lax.rem(y + k, 4)
        return (lax.rem(z + k, 4)) * 8 + b * 4 + lax.rem(y + j, 4)

    move = (at_y, at_z)
    keep = pltpu.make_async_copy(slot, t_out.at[v], local_sem.at[3])
    keep.start()
    sends = []
    GS = g_send
    GR = g_recv

    def gsend(k, src, dst, target):
        copy = remote(src, dst, GS, GR, k, target)
        copy.start()
        sends.append(copy)
        return copy

    def arrived(k, dst):
        remote(dst, dst, GS, GR, k, sibling).wait_recv()

    def part(slot_id, lo, n):
        return t_out.at[slot_id, pl.ds(lo, n)]

    def p1(h, k):
        return h * 20 + k

    def p2(h, m, k):
        return h * 20 + 4 + m * 4 + k

    def dd(h, j):
        return 40 + h * 16 + j

    own = lambda lo, n: slot.at[pl.ds(lo, n)]
    for h in range(2):
        A, B = h, 1 - h
        gsend(p1(h, 0), own(HALF * h, HALF), part(v, HALF * h, HALF), move[A](1))
        gsend(p1(h, 1), own(HALF * h, HALF), part(v, HALF * h, HALF), move[A](3))
    for h in range(2):
        A, B = h, 1 - h
        gsend(p2(h, 0, 0), own(HALF * h, HALF), part(v, HALF * h, HALF), move[B](1))
        gsend(p2(h, 0, 1), own(HALF * h, HALF), part(v, HALF * h, HALF), move[B](3))
        gsend(dd(h, 0), own(HALF * h, HALF), part(v, HALF * h, HALF), sibling)
    order = (0, 3, 1, 2)

    def spread(h, m):
        A, B = h, 1 - h
        s = place2(A, order[m], 0)
        gsend(p2(h, m, 0), part(s, HALF * h, HALF), part(s, HALF * h, HALF), move[B](1))
        gsend(p2(h, m, 1), part(s, HALF * h, HALF), part(s, HALF * h, HALF), move[B](3))
        gsend(dd(h, m), part(s, HALF * h, HALF), part(s, HALF * h, HALF), sibling)

    for h in range(2):
        A, B = h, 1 - h
        s = place2(A, 3, 0)
        arrived(p1(h, 0), part(s, HALF * h, HALF))
        gsend(p1(h, 2), part(s, HALF * h, QUART), part(s, HALF * h, QUART), move[A](1))
        s = place2(A, 1, 0)
        arrived(p1(h, 1), part(s, HALF * h, HALF))
        gsend(p1(h, 3), part(s, HALF * h + QUART, QUART), part(s, HALF * h + QUART, QUART), move[A](3))
        spread(h, 1)
        spread(h, 2)
    for h in range(2):
        A, B = h, 1 - h
        s = place2(A, 2, 0)
        arrived(p1(h, 2), part(s, HALF * h, QUART))
        arrived(p1(h, 3), part(s, HALF * h + QUART, QUART))
        spread(h, 3)
    for m in range(4):
        for h in range(2):
            A, B = h, 1 - h
            s = place2(A, order[m], 3)
            arrived(p2(h, m, 0), part(s, HALF * h, HALF))
            gsend(p2(h, m, 2), part(s, HALF * h, QUART), part(s, HALF * h, QUART), move[B](1))
            gsend(dd(h, 4 + m * 3), part(s, HALF * h, HALF), part(s, HALF * h, HALF), sibling)
            s = place2(A, order[m], 1)
            arrived(p2(h, m, 1), part(s, HALF * h, HALF))
            gsend(p2(h, m, 3), part(s, HALF * h + QUART, QUART), part(s, HALF * h + QUART, QUART), move[B](3))
            gsend(dd(h, 5 + m * 3), part(s, HALF * h, HALF), part(s, HALF * h, HALF), sibling)
    for m in range(4):
        for h in range(2):
            A, B = h, 1 - h
            s = place2(A, order[m], 2)
            arrived(p2(h, m, 2), part(s, HALF * h, QUART))
            arrived(p2(h, m, 3), part(s, HALF * h + QUART, QUART))
            gsend(dd(h, 6 + m * 3), part(s, HALF * h, HALF), part(s, HALF * h, HALF), sibling)
    for j in range(16):
        for h in range(2):
            arrived(dd(h, j), part(0, HALF * h, HALF))
    for copy in sends:
        copy.wait_send()
    keep.wait()
    to_up.wait_send()
    to_down.wait_send()

    @pl.when(swap)
    def _():
        main.wait_send()
        patch_swap.wait()
        meta_swap.wait()

    @pl.when(jnp.logical_not(swap))
    def _():
        patch_keep.wait()
        meta_keep.wait()


def gather(weights, patches, meta):
    hbm = pl.BlockSpec(memory_space=pl.ANY)
    return pl.pallas_call(
        gather_kernel,
        out_shape=(
            jax.ShapeDtypeStruct((NSLOT, SLOT, 16, 128), jnp.bfloat16),
            jax.ShapeDtypeStruct(patches.shape, patches.dtype),
            jax.ShapeDtypeStruct(meta.shape, meta.dtype),
        ),
        in_specs=[hbm] * 3,
        out_specs=(hbm,) * 3,
        scratch_shapes=[
            pltpu.VMEM((FROWS, 128), jnp.float32),
            pltpu.VMEM((128, 128), jnp.float32),
            pltpu.VMEM((2112, 128), jnp.bfloat16),
            pltpu.VMEM((LO, 128), jnp.bfloat16),
            pltpu.VMEM((HI, 128), jnp.bfloat16),
            pltpu.VMEM((2112, 128), jnp.bfloat16),
            pltpu.VMEM((HI, 128), jnp.bfloat16),
            pltpu.VMEM((LO, 128), jnp.bfloat16),
            pltpu.VMEM((SLOT, 16, 128), jnp.bfloat16),
            pltpu.SemaphoreType.DMA((4,)),
            pltpu.SemaphoreType.DMA((5,)),
            pltpu.SemaphoreType.DMA((5,)),
            pltpu.SemaphoreType.DMA((72,)),
            pltpu.SemaphoreType.DMA((72,)),
        ],
        compiler_params=pltpu.CompilerParams(collective_id=0, has_side_effects=True, vmem_limit_bytes=32 * 1024 * 1024),
        name="gather_weights",
    )(weights, patches, meta)


D = 768
HEADS = 12
HEAD_DIM = 64
FF = 3072
CLS = 1000
P_SIZE = 196
ROWS = 208
TOK = 2 * ROWS
NORM_EPS = 1e-06
SMOOTHING = 0.1
NTILES = 4224
T_E, T_HEAD, T_NORM, T_QKV, T_OUT, T_IN, T_FO = 0, 366, 750, 756, 1620, 1908, 3060
T_POS = 288
BLK = 256
STEP_ROWS = 32
F32 = jnp.float32
BF16 = jnp.bfloat16
ROOT_HALF = 0.7071067811865476
INV_ROOT_TWO_PI = 0.3989422804014327


def dot(x, w):
    return lax.dot_general(x, w, (((1,), (0,)), ((), ())), preferred_element_type=F32)


def dot_t(x, w):
    return lax.dot_general(x, w, (((1,), (1,)), ((), ())), preferred_element_type=F32)


def t_dot(x, w):
    return lax.dot_general(x, w, (((0,), (0,)), ((), ())), preferred_element_type=F32)


def stats(x):
    mean = jnp.sum(x, -1, keepdims=True) * (1.0 / D)
    centred = x - mean
    var = jnp.sum(centred * centred, -1, keepdims=True) * (1.0 / D)
    rstd = lax.rsqrt(var + NORM_EPS)
    return centred * rstd, rstd


def norm_back(d_hat, hat, rstd):
    m1 = jnp.sum(d_hat, -1, keepdims=True) * (1.0 / D)
    m2 = jnp.sum(d_hat * hat, -1, keepdims=True) * (1.0 / D)
    return rstd * (d_hat - m1 - hat * m2)


def compute_kernel(t_hbm, patch_ref, meta_ref, g_hbm, loss_ref, T, G, x, xt, h, a, at, mix, prob, o, h1, a2, hid, slope, h2, dh, dyb, du, dmix, sem, gsem):
    bounds = [(0, T_HEAD), (T_QKV, T_OUT), (T_NORM, T_QKV), (T_OUT, T_IN), (T_IN, T_FO), (T_FO, 4212), (T_HEAD, T_NORM)]
    loads = []
    for i, (lo, hi) in enumerate(bounds):
        copy = pltpu.make_async_copy(t_hbm.at[pl.ds(lo, hi - lo)], T.at[pl.ds(lo, hi - lo)], sem.at[i])
        copy.start()
        loads.append(copy)

    def section(ref, start, c, groups):
        return ref.at[pl.ds(start, groups * c)].reshape(groups, c, 16, 128)

    def cols(start, c, groups, j):
        part = section(T, start, c, groups)
        return jnp.concatenate([part[:, 2 * j + k].reshape(groups * 16, 128) for k in range(2)], axis=1)

    def put_cols(start, c, groups, j, value):
        low = value.astype(BF16)
        part = section(G, start, c, groups)
        for k in range(2):
            part[:, 2 * j + k] = low[:, k * 128 : (k + 1) * 128].reshape(groups, 16, 128)

    def row_of(start, k):
        return jnp.concatenate([T[start + j][k : k + 1, :] for j in range(6)], axis=1).astype(F32)

    def lanes(j):
        return pl.ds(pl.multiple_of(j * BLK, BLK), BLK)

    def rows(i):
        return pl.ds(pl.multiple_of(i * STEP_ROWS, STEP_ROWS), STEP_ROWS)

    steps = TOK // STEP_ROWS
    for i in range(2):
        x[pl.ds(i * ROWS, 192), :] = patch_ref[i, pl.ds(0, 192), :]
        x[pl.ds(i * ROWS + 192, 16), :] = jnp.concatenate([patch_ref[i, pl.ds(192, 4), :], jnp.zeros((12, D), BF16)], axis=0)

    real = lax.broadcasted_iota(jnp.int32, (ROWS, 128), 0) < P_SIZE
    loads[0].wait()
    for j in range(3):
        acc = dot(x[...], cols(T_E, 6, 48, j))
        p = cols(T_POS, 6, 13, j).astype(F32)
        p = jnp.where(lax.broadcasted_iota(jnp.int32, (ROWS, BLK), 0) < P_SIZE, p, 0.0)
        for i in range(2):
            h[pl.ds(i * ROWS, ROWS), pl.ds(j * BLK, BLK)] = acc[i * ROWS : (i + 1) * ROWS] + p

    loads[2].wait()
    gain1, shift1, gain2, shift2 = (row_of(T_NORM, k) for k in range(4))

    def norm_one(i, carry):
        hat, unused = stats(h[rows(i), :])
        a[rows(i), :] = (hat * gain1 + shift1).astype(BF16)
        return carry

    lax.fori_loop(0, steps, norm_one, 0)
    loads[1].wait()

    def mix_block(j, carry):
        mix[:, lanes(j)] = dot(a[...], cols(T_QKV, 18, 48, j)).astype(BF16)
        return carry

    lax.fori_loop(0, 9, mix_block, 0)

    first_half = lax.broadcasted_iota(jnp.int32, (ROWS, 128), 1) < HEAD_DIM
    key_ok = lax.broadcasted_iota(jnp.int32, (ROWS, ROWS), 1) < P_SIZE
    zero = jnp.zeros((ROWS, 128), BF16)

    def qkv_of(n):
        i = lax.div(n, 6)
        p = lax.rem(n, 6)
        r = pl.ds(pl.multiple_of(i * ROWS, ROWS), ROWS)
        ls = [pl.ds(pl.multiple_of(p * 128 + D * k, 128), 128) for k in range(3)]
        return r, ls

    def attend(n, carry):
        r, ls = qkv_of(n)
        q, k, v = (mix[r, l] for l in ls)
        q = q * jnp.asarray(0.125, BF16)
        outs = []
        for e in range(2):
            mask = first_half if e == 0 else jnp.logical_not(first_half)
            s = dot_t(jnp.where(mask, q, zero), k)
            s = jnp.where(key_ok, s, -jnp.inf)
            top = jnp.max(s, -1, keepdims=True)
            ex = jnp.exp(s - top)
            pr = (ex / jnp.sum(ex, -1, keepdims=True)).astype(BF16)
            prob[n * 2 + e] = pr
            outs.append(dot(pr, v))
        o[r, ls[0]] = jnp.where(first_half, outs[0], outs[1]).astype(BF16)
        return carry

    lax.fori_loop(0, 12, attend, 0)
    loads[3].wait()
    for j in range(3):
        h1[:, pl.ds(j * BLK, BLK)] = h[:, pl.ds(j * BLK, BLK)] + dot(o[...], cols(T_OUT, 6, 48, j))

    def norm_two(i, carry):
        hat, unused = stats(h1[rows(i), :])
        a2[rows(i), :] = (hat * gain2 + shift2).astype(BF16)
        return carry

    lax.fori_loop(0, steps, norm_two, 0)
    loads[4].wait()

    def up_block(j, carry):
        u = dot(a2[...], cols(T_IN, 24, 48, j))
        phi = 0.5 * (1.0 + lax.erf(u * ROOT_HALF))
        pdf = jnp.exp(-0.5 * u * u) * INV_ROOT_TWO_PI
        hid[:, lanes(j)] = (u * phi).astype(BF16)
        slope[:, lanes(j)] = (phi + u * pdf).astype(BF16)
        return carry

    lax.fori_loop(0, 12, up_block, 0)
    loads[5].wait()
    for j in range(3):
        h2[:, pl.ds(j * BLK, BLK)] = h1[:, pl.ds(j * BLK, BLK)] + dot(hid[...], cols(T_FO, 6, 192, j))

    gain_end, shift_end = (row_of(T_POS + 72, 4 + k) for k in range(2))
    means = []
    for i in range(2):

        def pool_step(n, carry):
            hat, unused = stats(h2[pl.ds(pl.multiple_of(i * ROWS + n * 16, 16), 16), :])
            ok = lax.broadcasted_iota(jnp.int32, (16, D), 0) + n * 16 < P_SIZE
            hat = jnp.where(ok, hat, 0.0)
            return carry + hat[:8] + hat[8:]

        total = lax.fori_loop(0, 13, pool_step, jnp.zeros((8, D), F32))
        means.append(jnp.sum(total, 0, keepdims=True) * (1.0 / P_SIZE))
    mean_hat = jnp.concatenate(means + [jnp.zeros((14, D), F32)], axis=0)
    two = lax.broadcasted_iota(jnp.int32, (16, D), 0) < 2
    pooled = jnp.where(two, mean_hat * gain_end + shift_end, 0.0).astype(BF16)
    loads[6].wait()
    logits = jnp.concatenate([dot(pooled, cols(T_HEAD, 8, 48, j)) for j in range(4)], axis=1)
    lane = lax.broadcasted_iota(jnp.int32, (16, 1024), 1)
    lane_f = lane.astype(F32)
    inside = lane < CLS
    logits = jnp.where(inside, logits, -1e30)
    top = jnp.max(logits, -1, keepdims=True)
    total = jnp.sum(jnp.where(inside, jnp.exp(logits - top), 0.0), -1, keepdims=True)
    logp = logits - top - jnp.log(total)
    meta = meta_ref[...]
    pad14 = jnp.zeros((14, 1), F32)
    label = jnp.concatenate([meta[0:2, 0:1], pad14], axis=0)
    scale = jnp.concatenate([meta[2:4, 0:1], pad14], axis=0)
    valid = jnp.concatenate([meta[4:6, 0:1], pad14], axis=0)
    target = jnp.where(lane_f == label, 1.0 - SMOOTHING, 0.0) + SMOOTHING / CLS
    values = -jnp.sum(jnp.where(inside, target * logp, 0.0), -1, keepdims=True)
    loss_ref[...] = jnp.broadcast_to(jnp.sum(values * valid, 0, keepdims=True), (8, 128))
    d_logits = jnp.where(inside, scale * (jnp.exp(logp) - target), 0.0).astype(BF16)
    d_pooled = jnp.zeros((16, D), F32)
    for j in range(4):
        w = cols(T_HEAD, 8, 48, j)
        d_pooled = d_pooled + dot_t(d_logits[:, j * BLK : (j + 1) * BLK], w)
        put_cols(T_HEAD, 8, 48, j, t_dot(pooled, d_logits[:, j * BLK : (j + 1) * BLK]))
    d_gain_end = jnp.sum(d_pooled * mean_hat, 0, keepdims=True)
    d_shift_end = jnp.sum(d_pooled, 0, keepdims=True)
    for i in range(2):
        d_hat = d_pooled[i : i + 1, :] * (1.0 / P_SIZE) * gain_end

        def end_step(n, carry):
            r = pl.ds(pl.multiple_of(i * ROWS + n * 16, 16), 16)
            hat, rstd = stats(h2[r, :])
            ok = lax.broadcasted_iota(jnp.int32, (16, D), 0) + n * 16 < P_SIZE
            d = jnp.where(ok, norm_back(jnp.broadcast_to(d_hat, (16, D)), hat, rstd), 0.0)
            dh[r, :] = d
            dyb[r, :] = d.astype(BF16)
            return carry

        lax.fori_loop(0, 13, end_step, 0)

    at[...] = a2[...].T
    da = h2
    da[...] = jnp.zeros((TOK, D), F32)

    def mlp_block(j, carry):
        dy = dyb[...]
        d_w = t_dot(hid[:, lanes(j)], dy).astype(BF16)
        part = section(G, T_FO + j * 96, 6, 16)
        for k in range(6):
            part[:, k] = d_w[:, k * 128 : (k + 1) * 128].reshape(16, 16, 128)
        part = section(T, T_FO + j * 96, 6, 16)
        w = jnp.concatenate([part[:, k].reshape(BLK, 128) for k in range(6)], axis=1)
        d_u = (dot_t(dy, w) * slope[:, lanes(j)].astype(F32)).astype(BF16)
        put_cols(T_IN, 24, 48, j, dot(at[...], d_u))
        da[...] += dot_t(d_u, cols(T_IN, 24, 48, j))
        return carry

    lax.fori_loop(0, 12, mlp_block, 0)

    def back_two(i, carry):
        dg, ds = carry
        hat, rstd = stats(h1[rows(i), :])
        d = da[rows(i), :]
        new = dh[rows(i), :] + norm_back(d * gain2, hat, rstd)
        dh[rows(i), :] = new
        dyb[rows(i), :] = new.astype(BF16)
        return dg + jnp.sum((d * hat).reshape(4, 8, D), 0), ds + jnp.sum(d.reshape(4, 8, D), 0)

    none = jnp.zeros((8, D), F32)
    d_gain2, d_shift2 = lax.fori_loop(0, steps, back_two, (none, none))

    at[...] = o[...].T
    da[...] = jnp.zeros((TOK, D), F32)
    for j in range(3):
        dz = dyb[:, pl.ds(j * BLK, BLK)]
        put_cols(T_OUT, 6, 48, j, dot(at[...], dz))
        da[...] += dot_t(dz, cols(T_OUT, 6, 48, j))
    o[...] = da[...].astype(BF16)

    def attend_back(n, carry):
        r, ls = qkv_of(n)
        q, k, v = (mix[r, l] for l in ls)
        q = q * jnp.asarray(0.125, BF16)
        k8 = k * jnp.asarray(0.125, BF16)
        do = o[r, ls[0]]
        dq, dk, dv = [], [], []
        for e in range(2):
            mask = first_half if e == 0 else jnp.logical_not(first_half)
            pr = prob[n * 2 + e]
            dv.append(t_dot(pr, do))
            dp = dot_t(jnp.where(mask, do, zero), v)
            prf = pr.astype(F32)
            row = jnp.sum(prf * dp, -1, keepdims=True)
            ds = (prf * (dp - row)).astype(BF16)
            dq.append(dot(ds, k8))
            dk.append(t_dot(ds, q))
        for l, pair in zip(ls, (dq, dk, dv)):
            dmix[r, l] = jnp.where(first_half, pair[0], pair[1]).astype(BF16)
        return carry

    lax.fori_loop(0, 12, attend_back, 0)

    at[...] = a[...].T
    da[...] = jnp.zeros((TOK, D), F32)

    def qkv_block(j, carry):
        d = dmix[:, lanes(j)]
        put_cols(T_QKV, 18, 48, j, dot(at[...], d))
        da[...] += dot_t(d, cols(T_QKV, 18, 48, j))
        return carry

    lax.fori_loop(0, 9, qkv_block, 0)

    def back_one(i, carry):
        dg, ds = carry
        hat, rstd = stats(h[rows(i), :])
        d = da[rows(i), :]
        new = dh[rows(i), :] + norm_back(d * gain1, hat, rstd)
        dh[rows(i), :] = new
        dyb[rows(i), :] = new.astype(BF16)
        return dg + jnp.sum((d * hat).reshape(4, 8, D), 0), ds + jnp.sum(d.reshape(4, 8, D), 0)

    d_gain1, d_shift1 = lax.fori_loop(0, steps, back_one, (none, none))
    d_norms = jnp.concatenate([jnp.sum(d, 0, keepdims=True) for d in (d_gain1, d_shift1, d_gain2, d_shift2)] + [jnp.zeros((12, D), F32)], axis=0).astype(BF16)
    for j in range(6):
        G[T_NORM + j] = d_norms[:, j * 128 : (j + 1) * 128]
    at[...] = x[...].T
    row_id = lax.broadcasted_iota(jnp.int32, (ROWS, BLK), 0)
    for j in range(3):
        put_cols(T_E, 6, 48, j, dot(at[...], dyb[:, pl.ds(j * BLK, BLK)]))
        c = pl.ds(j * BLK, BLK)
        s = slice(j * BLK, (j + 1) * BLK)
        d_pos = dh[pl.ds(0, ROWS), c] + dh[pl.ds(ROWS, ROWS), c]
        d_pos = jnp.where(row_id < P_SIZE, d_pos, 0.0)
        d_pos = jnp.where(row_id == P_SIZE, jnp.broadcast_to(d_gain_end[:, s], (ROWS, BLK)), d_pos)
        d_pos = jnp.where(row_id == P_SIZE + 1, jnp.broadcast_to(d_shift_end[:, s], (ROWS, BLK)), d_pos)
        put_cols(T_POS, 6, 13, j, d_pos)
    G[pl.ds(4212, 12)] = jnp.zeros((12, 16, 128), BF16)
    out = pltpu.make_async_copy(G, g_hbm, gsem)
    out.start()
    out.wait()


def compute(tiles, patches, meta):
    hbm = pl.BlockSpec(memory_space=pl.ANY)
    vmem = pl.BlockSpec(memory_space=pltpu.VMEM)
    V = pltpu.VMEM
    return pl.pallas_call(
        compute_kernel,
        out_shape=(jax.ShapeDtypeStruct((NTILES, 16, 128), BF16), jax.ShapeDtypeStruct((8, 128), F32)),
        in_specs=[hbm, vmem, vmem],
        out_specs=(hbm, vmem),
        scratch_shapes=[
            V((NTILES, 16, 128), BF16),
            V((NTILES, 16, 128), BF16),
            V((TOK, D), BF16),
            V((8, 128), BF16),
            V((TOK, D), F32),
            V((TOK, D), BF16),
            V((D, TOK), BF16),
            V((TOK, 3 * D), BF16),
            V((24, ROWS, ROWS), BF16),
            V((TOK, D), BF16),
            V((TOK, D), F32),
            V((TOK, D), BF16),
            V((TOK, FF), BF16),
            V((TOK, FF), BF16),
            V((TOK, D), F32),
            V((TOK, D), F32),
            V((TOK, D), BF16),
            V((8, 128), BF16),
            V((TOK, 3 * D), BF16),
            pltpu.SemaphoreType.DMA((8,)),
            pltpu.SemaphoreType.DMA,
        ],
        compiler_params=pltpu.CompilerParams(vmem_limit_bytes=62 * 1024 * 1024),
        name="grads",
    )(tiles, patches, meta)


EDGE = 24
FRONT = 768
BACK_ROWS = FRONT + SHARD + 640 + 6
PADDED = 2112
STEP = 10
BETA_ONE = 0.9
BETA_TWO = 0.95
ADAM_EPS = 1e-08
DECAY = 0.05
INNER_RATE = 0.01
OUTER_RATE = 0.7
OUTER_MU = 0.9
F32 = jnp.float32
BF16 = jnp.bfloat16
ORDER = (2, 1, 3, 0)


def reduce_kernel(
    g_ref, w_ref, first_ref, second_ref, mom_ref,
    avg_out, mom_out, new_out, first_out, second_out,
    L, R, RA, RB, window, flat, headrows, w, first, second, mom, upd, low, low2, pair, pair2, total, total2,
    load_sem, d_send, d_recv, a_send, a_recv, b_send, b_recv, x_send, x_recv,
):
    xl, b, z, a, y = coords()
    fs = z * 8 + a * 4 + y
    v = z * 8 + b * 4 + y
    swap = a != b

    def owner(s):
        return device(xl, lax.rem(lax.div(s, 4), 2), a, lax.div(s, 8), lax.rem(s, 4))

    def server(s):
        return device(xl, b, lax.rem(lax.div(s, 4), 2), lax.div(s, 8), lax.rem(s, 4))

    def around(s):
        return lax.rem(s + NSLOT, NSLOT)

    mirror = device(xl, b, a, z, y)
    sibling = device(xl, a, 1 - b, z, y)
    across = device(1 - xl, a, b, z, y)

    def at_z(k):
        return device(xl, a, b, lax.rem(z + k, 4), y)

    def at_y(k):
        return device(xl, a, b, z, lax.rem(y + k, 4))

    barrier = pltpu.get_barrier_semaphore()
    for target in (sibling, across, at_y(1), at_y(3), at_z(1), at_z(3), server(around(fs + 1)), server(around(fs - 1))):
        pl.semaphore_signal(barrier, inc=1, device_id=target, device_id_type=MESH)

    @pl.when(swap)
    def _():
        pl.semaphore_signal(barrier, inc=1, device_id=mirror, device_id_type=MESH)

    own = []
    for kz in range(4):
        for ky in range(4):
            s = lax.rem(z + ORDER[kz], 4) * 8 + b * 4 + lax.rem(y + ORDER[ky], 4)
            own.append(pltpu.make_async_copy(g_ref.at[s], L.at[kz, ky], load_sem.at[kz * 4 + ky]))
    extra = [pltpu.make_async_copy(src, dst, load_sem.at[16 + i]) for i, (src, dst) in enumerate(((w_ref, w), (first_ref, first), (second_ref, second), (mom_ref, mom)))]

    pl.semaphore_wait(barrier, jnp.where(swap, 9, 8))

    def remote(src, dst, send, recv, k, target):
        return pltpu.make_async_remote_copy(src_ref=src, dst_ref=dst, send_sem=send.at[k], recv_sem=recv.at[k], device_id=target, device_id_type=MESH)

    sends = []

    def go(*args):
        copy = remote(*args)
        copy.start()
        sends.append(copy)
        return copy

    sequence = [(0, 0), (0, 1), (1, 0), (0, 2), (0, 3), (2, 0), (3, 0), (1, 2), (1, 3), (2, 1), (3, 1), (1, 1), (2, 2), (2, 3), (3, 2), (3, 3)]
    for kz, ky in sequence:
        s = lax.rem(z + ORDER[kz], 4) * 8 + (1 - b) * 4 + lax.rem(y + ORDER[ky], 4)
        go(g_ref.at[s], R.at[kz, ky], d_send, d_recv, kz * 4 + ky, sibling)
        own[kz * 4 + ky].start()
    for copy in extra:
        copy.start()

    def add_into(dst, src, n):
        def one(i, carry):
            for k in range(3):
                t = i * 3 + k
                dst[t] = dst[t] + src[t]
            return carry

        lax.fori_loop(0, n // 3, one, 0)

    def arrive(dst, recv, k):
        remote(dst, dst, d_send, recv, k, sibling).wait_recv()

    done = set()

    def need(*slots):
        for kz, ky in slots:
            if (kz, ky) not in done:
                done.add((kz, ky))
                own[kz * 4 + ky].wait()
                arrive(R.at[kz, ky], d_recv, kz * 4 + ky)
                add_into(L.at[kz, ky], R.at[kz, ky], SLOT)

    move = (at_z, at_y)

    def block(h, ka, p):
        t = pl.ds(HALF * h, HALF)
        return L.at[ka, pl.ds(2 * p, 2), t] if h == 0 else L.at[pl.ds(2 * p, 2), ka, t]

    def cells(h, ka, p):
        return [(ka, 2 * p + i) if h == 0 else (2 * p + i, ka) for i in range(2)]

    def send_a(h, k, ka, p, step):
        need(*cells(h, ka, p))
        go(block(h, ka, p), RA.at[h, k], a_send, a_recv, h * 6 + k, move[h](step))

    def take_a(h, k, ka, p):
        need(*cells(h, ka, p))
        arrive(RA.at[h, k], a_recv, h * 6 + k)
        for i in range(2):
            add_into(block(h, ka, p).at[i], RA.at[h, k, i], HALF)

    for k, ka, p, step in ((0, 0, 0, 1), (1, 0, 1, 3), (2, 1, 1, 1), (3, 2, 0, 3)):
        for h in range(2):
            send_a(h, k, ka, p, step)
    for k, ka, p, step in ((0, 1, 0, 1), (1, 2, 1, 3)):
        for h in range(2):
            take_a(h, k, ka, p)
            send_a(h, k + 4, ka, p, step)

    def sum_three(h, p):
        ks = (3, 4) if p == 0 else (2, 5)
        need(*cells(h, 3, p))
        for k in ks:
            arrive(RA.at[h, k], a_recv, h * 6 + k)
        for i in range(2):
            dst, one, two = block(h, 3, p).at[i], RA.at[h, ks[0], i], RA.at[h, ks[1], i]

            def body(n, carry):
                for k in range(3):
                    t = n * 3 + k
                    dst[t] = (dst[t].astype(F32) + one[t].astype(F32) + two[t].astype(F32)).astype(BF16)
                return carry

            lax.fori_loop(0, HALF // 3, body, 0)

    def cell(h, kb, q):
        t = pl.ds(HALF * h + QUART * q, QUART)
        return L.at[3, kb, t] if h == 0 else L.at[kb, 3, t]

    def send_b(h, k, kb, q, step):
        go(cell(h, kb, q), RB.at[h, k], b_send, b_recv, h * 6 + k, move[1 - h](step))

    def take_b(h, k, kb, q):
        arrive(RB.at[h, k], b_recv, h * 6 + k)
        add_into(cell(h, kb, q), RB.at[h, k], QUART)

    for h in range(2):
        sum_three(h, 0)
        send_b(h, 0, 0, 0, 1)
        send_b(h, 1, 0, 1, 3)
        send_b(h, 2, 1, 1, 1)
    for h in range(2):
        sum_three(h, 1)
        send_b(h, 3, 2, 0, 3)
    for h in range(2):
        take_b(h, 0, 1, 0)
        send_b(h, 4, 1, 0, 1)
        take_b(h, 1, 2, 1)
        send_b(h, 5, 2, 1, 3)
    for h in range(2):
        for q, ks in ((0, (3, 4)), (1, (2, 5))):
            for k in ks:
                arrive(RB.at[h, k], b_recv, h * 6 + k)
            dst, one, two = cell(h, 3, q), RB.at[h, ks[0]], RB.at[h, ks[1]]

            def body(n, carry):
                for k in range(3):
                    t = n * 3 + k
                    dst[t] = (dst[t].astype(F32) + one[t].astype(F32) + two[t].astype(F32)).astype(BF16)
                return carry

            lax.fori_loop(0, QUART // 3, body, 0)

    mine = L.at[3, 3]
    main = remote(mine, window.at[pl.ds(EDGE, SLOT)], x_send, x_recv, 0, mirror)
    main_keep = pltpu.make_async_copy(mine, window.at[pl.ds(EDGE, SLOT)], load_sem.at[20])

    @pl.when(swap)
    def _():
        main.start()

    @pl.when(jnp.logical_not(swap))
    def _():
        main_keep.start()

    go(mine.at[pl.ds(0, EDGE)], window.at[pl.ds(EDGE + SLOT, EDGE)], x_send, x_recv, 1, owner(around(v - 1)))
    go(mine.at[pl.ds(SLOT - EDGE, EDGE)], window.at[pl.ds(0, EDGE)], x_send, x_recv, 2, owner(around(v + 1)))

    def clear(i, carry):
        flat[pl.ds(pl.multiple_of(i * 32, 32), 32), :] = jnp.zeros((32, 128), F32)
        return carry

    lax.fori_loop(0, BACK_ROWS // 32, clear, 0)
    for copy in extra:
        copy.wait()
    arrive(window.at[pl.ds(EDGE + SLOT, EDGE)], x_recv, 1)
    arrive(window.at[pl.ds(0, EDGE)], x_recv, 2)

    @pl.when(swap)
    def _():
        main.wait()

    @pl.when(jnp.logical_not(swap))
    def _():
        main_keep.wait()

    low_tile = SLOT * fs - EDGE
    high_tile = SLOT * fs + SLOT + EDGE
    origin = SHARD * fs - FRONT
    for index, (base, c, groups, per, start) in enumerate(SECTIONS):
        if index == 1:
            lane = lax.broadcasted_iota(jnp.int32, (8, 128), 1)
            g0 = lax.div(jnp.maximum(SHARD * fs - base, 0), per)
            g1 = lax.div(jnp.maximum(SHARD * (fs + 1) - base, 0) + per - 1, per)

            def head_group(g, carry):
                t = start + g * 8 - low_tile
                for j in range(8):
                    headrows[pl.ds(j, 16, stride=8), :] = window[t + j].astype(F32)
                row = base + per * g - origin
                for i in range(16):
                    q, s = divmod(1000 * i, 128)
                    value = headrows[pl.ds(i * 8, 8), :]
                    if s:
                        value = pltpu.roll(value, s, 1)
                        flat[pl.ds(row + q, 8), :] += jnp.where(lane >= s, value, 0.0)
                        flat[pl.ds(row + q + 1, 8), :] += jnp.where(lane < s, value, 0.0)
                    else:
                        flat[pl.ds(row + q, 8), :] += value
                return carry

            lax.fori_loop(jnp.minimum(g0, groups), jnp.minimum(g1, groups), head_group, 0)
        else:

            def tile(t, carry):
                g = lax.div(t - start, c)
                j = lax.rem(t - start, c)
                flat[pl.ds(base + 16 * c * g + j - origin, 16, stride=c), :] = window[t - low_tile].astype(F32)
                return carry

            lax.fori_loop(jnp.maximum(low_tile, start), jnp.minimum(high_tile, start + c * groups), tile, 0)

    fix_one = 1.0 / (1.0 - BETA_ONE**STEP)
    fix_two = 1.0 / (1.0 - BETA_TWO**STEP)

    def in_rows(fn, lo, hi, step=32):
        def body(i, carry):
            fn(pl.multiple_of(i * step, step), step)
            return carry

        n = (hi - lo) // step
        lax.fori_loop(lo // step, lo // step + n, body, 0)
        if lo + n * step < hi:
            fn(lo + n * step, hi - lo - n * step)

    def adam(r, n):
        grad = flat[pl.ds(FRONT + r, n), :]
        m = BETA_ONE * first[pl.ds(r, n), :] + (1.0 - BETA_ONE) * grad
        s = BETA_TWO * second[pl.ds(r, n), :] + (1.0 - BETA_TWO) * grad * grad
        first[pl.ds(r, n), :] = m
        second[pl.ds(r, n), :] = s
        u = (m * fix_one) / (jnp.sqrt(s * fix_two) + ADAM_EPS)
        upd[pl.ds(r, n), :] = u

    in_rows(adam, 0, SHARD)
    upd[pl.ds(SHARD, PADDED - SHARD), :] = jnp.zeros((PADDED - SHARD, 128), F32)
    outs = [pltpu.make_async_copy(src, dst, load_sem.at[16 + i]) for i, (src, dst) in enumerate(((first, first_out), (second, second_out)))]
    for copy in outs:
        copy.start()

    def lower(r, n):
        low[pl.ds(r, n), :] = upd[pl.ds(r, n), :].astype(BF16)

    in_rows(lower, 0, PADDED)
    go(low, low2, x_send, x_recv, 3, sibling)
    arrive(low2, x_recv, 3)
    half = PADDED // 2

    def pairs(r, n):
        at = pl.ds(pl.multiple_of(b * half + r, 16), n)
        pair[pl.ds(r, n), :] = low[at, :] + low2[at, :]

    in_rows(pairs, 0, half)
    go(pair, pair2, x_send, x_recv, 4, across)
    arrive(pair2, x_recv, 4)

    def fours(r, n):
        total[pl.ds(r, n), :] = pair[pl.ds(r, n), :].astype(F32) + pair2[pl.ds(r, n), :].astype(F32)

    in_rows(fours, 0, half)
    go(total, total2, x_send, x_recv, 5, sibling)

    def outer(source, shift):
        def rows_of(r, n):
            at = pl.ds(shift + r, n)
            t = source[pl.ds(r, n), :]
            old = w[at, :]
            averaged = INNER_RATE * (t * 0.25 + DECAY * old)
            momentum = OUTER_MU * mom[at, :] + averaged
            upd[at, :] = averaged
            mom[at, :] = momentum
            w[at, :] = old - OUTER_RATE * (averaged + OUTER_MU * momentum)

        return rows_of

    def both(here, there):
        in_rows(outer(here, 0), 0, half)
        in_rows(outer(there, half), 0, SHARD - half)

    arrive(total2, x_recv, 5)

    @pl.when(b == 0)
    def _():
        both(total, total2)

    @pl.when(b == 1)
    def _():
        both(total2, total)

    final = [(upd.at[pl.ds(0, SHARD)], avg_out), (mom, mom_out), (w, new_out)]
    final = [pltpu.make_async_copy(src, dst, load_sem.at[18 + i]) for i, (src, dst) in enumerate(final)]
    for copy in final:
        copy.start()
    for copy in sends:
        copy.wait_send()
    for copy in outs + final:
        copy.wait()


def reduce_update(grads, weights, first, second, momentum):
    hbm = pl.BlockSpec(memory_space=pl.ANY)
    V = pltpu.VMEM
    flat = jax.ShapeDtypeStruct((SHARD, 128), F32)
    dma = pltpu.SemaphoreType.DMA
    return pl.pallas_call(
        reduce_kernel,
        out_shape=(flat,) * 5,
        in_specs=[hbm] * 5,
        out_specs=(hbm,) * 5,
        scratch_shapes=[
            V((4, 4, SLOT, 16, 128), BF16),
            V((4, 4, SLOT, 16, 128), BF16),
            V((2, 6, 2, HALF, 16, 128), BF16),
            V((2, 6, QUART, 16, 128), BF16),
            V((EDGE + SLOT + EDGE, 16, 128), BF16),
            V((BACK_ROWS, 128), F32),
            V((128, 128), F32),
            V((SHARD, 128), F32),
            V((SHARD, 128), F32),
            V((SHARD, 128), F32),
            V((SHARD, 128), F32),
            V((PADDED, 128), F32),
            V((PADDED, 128), BF16),
            V((PADDED, 128), BF16),
            V((PADDED // 2, 128), BF16),
            V((PADDED // 2, 128), BF16),
            V((PADDED // 2, 128), F32),
            V((PADDED // 2, 128), F32),
            dma((21,)),
            dma((16,)),
            dma((16,)),
            dma((12,)),
            dma((12,)),
            dma((12,)),
            dma((12,)),
            dma((6,)),
            dma((6,)),
        ],
        compiler_params=pltpu.CompilerParams(collective_id=1, has_side_effects=True, vmem_limit_bytes=52 * 1024 * 1024),
        name="reduce_update",
    )(grads, weights, first, second, momentum)


def body(patches, labels, counts, weights, first_moments, second_moments, outer_momentum):
    rep = lax.axis_index("rep")
    rank = lax.axis_index("fsdp")
    total_count = jnp.sum(counts[0, 0]).astype(jnp.float32)
    valid = (rank < counts[0, 0]).astype(jnp.float32)
    fields = jnp.concatenate([labels[0, 0, :, 0].astype(jnp.float32), valid / total_count, valid, jnp.zeros((2,), jnp.float32)])
    meta = jnp.broadcast_to(fields[:, None], (8, 128))
    flat = weights.reshape(SHARD, 128)
    tiles, images, meta = gather(flat, patches.reshape(2, P_SIZE, D), meta)
    grads, loss = compute(tiles.reshape(NTILES, 16, 128), images, meta)
    group = 2 * lax.div(rep, 2) + lax.rem(lax.div(rank, 4), 2)
    losses = lax.psum(jnp.where(jnp.arange(4) == group, loss[0, 0], 0.0), ("rep", "fsdp"))
    averaged, momentum, new_weights, first, second = reduce_update(
        grads.reshape(NSLOT, SLOT, 16, 128),
        flat,
        first_moments.reshape(SHARD, 128),
        second_moments.reshape(SHARD, 128),
        outer_momentum.reshape(SHARD, 128),
    )
    return (
        averaged.reshape(-1),
        momentum.reshape(-1),
        new_weights.reshape(-1),
        first.reshape(1, -1),
        second.reshape(1, -1),
        lax.dynamic_slice(losses, (rep,), (1,)).reshape(1, 1),
    )


def solution(mesh):
    placed = (
        P("rep", None, None, "fsdp", None, None),
        P("rep", None, None, "fsdp"),
        P("rep", None, None),
        P("fsdp"),
        P("rep", "fsdp"),
        P("rep", "fsdp"),
        P("fsdp"),
    )
    return jax.shard_map(
        body,
        mesh=mesh,
        in_specs=placed,
        out_specs=(
            P("fsdp"),
            P("fsdp"),
            P("fsdp"),
            P("rep", "fsdp"),
            P("rep", "fsdp"),
            P("rep", None),
        ),
        check_vma=False,
    )
```

```python
from functools import partial

import jax
import jax.numpy as jnp
from jax import lax
from jax.experimental import pallas as pl
from jax.experimental.pallas import tpu as pltpu
from jax.sharding import PartitionSpec as P

SHARD = 2098
SLOT = 132
HALF = 66
QUART = 33
NSLOT = 32
SECTIONS = []
_t = 0
for _base, _c, _g, _rpg in ((0, 6, 61, 96), (5796, 8, 48, 125), (11796, 6, 1, 96), (11820, 18, 48, 288), (25644, 6, 48, 96), (30252, 24, 48, 384), (48684, 6, 192, 96)):
    SECTIONS.append((_base, _c, _g, _rpg, _t))
    _t += _c * _g
NTILE = _t
HI = 352
LO = 224
MARGIN = 512
FROWS = 3072
HEAD_ROWS = 16
MESH = pl.DeviceIdType.MESH


def coords():
    rep = lax.axis_index("rep")
    fs = lax.axis_index("fsdp")
    return lax.div(rep, 2), lax.rem(rep, 2), lax.div(fs, 8), lax.rem(lax.div(fs, 4), 2), lax.rem(fs, 4)


def device(xl, xh, core, z, y):
    return {"rep": xl * 2 + core, "fsdp": z * 8 + xh * 4 + y}


def gather_kernel(w_ref, patch_ref, meta_ref, t_out, patch_out, meta_out, flat, headrows, mainb, lob, hib, rmain, rlo, rhi, slot, local_sem, x_send, x_recv, g_send, g_recv):
    xl, b, z, a, y = coords()
    fs = z * 8 + a * 4 + y
    swap = a != b
    xo = lax.rem(xl + a + b, 2)
    up = lax.rem(fs + 1, NSLOT)
    down = lax.rem(fs + NSLOT - 1, NSLOT)

    def halo_to(s):
        return device(xo, b, lax.rem(lax.div(s, 4), 2), lax.div(s, 8), lax.rem(s, 4))

    def halo_from(s):
        sa = lax.rem(lax.div(s, 4), 2)
        return device(lax.rem(xl + sa + a, 2), sa, a, lax.div(s, 8), lax.rem(s, 4))

    partner = device(xo, b, a, z, y)
    mirror = device(xl, b, a, z, y)
    sibling = device(xl, a, 1 - b, z, y)

    def at_y(k):
        return device(xl, a, b, z, lax.rem(y + k, 4))

    def at_z(k):
        return device(xl, a, b, lax.rem(z + k, 4), y)

    load = pltpu.make_async_copy(w_ref, flat.at[pl.ds(MARGIN, SHARD)], local_sem.at[0])
    load.start()

    barrier = pltpu.get_barrier_semaphore()

    def greet(target):
        pl.semaphore_signal(barrier, inc=1, device_id=target, device_id_type=MESH)

    v = z * 8 + b * 4 + y
    for target in (halo_from(lax.rem(v + 1, NSLOT)), halo_from(lax.rem(v + NSLOT - 1, NSLOT)), at_y(1), at_y(3), at_z(1), at_z(3), sibling):
        greet(target)

    @pl.when(swap)
    def _():
        greet(partner)
        greet(mirror)

    def remote(src, dst, send, recv, k, target):
        return pltpu.make_async_remote_copy(src_ref=src, dst_ref=dst, send_sem=send.at[k], recv_sem=recv.at[k], device_id=target, device_id_type=MESH)

    pl.semaphore_wait(barrier, jnp.where(swap, 9, 7))

    load.wait()
    main = remote(mainb, rmain, x_send, x_recv, 0, partner)

    @pl.when(swap)
    def _():
        mainb[pl.ds(0, SHARD), :] = flat[pl.ds(MARGIN, SHARD), :].astype(jnp.bfloat16)
        main.start()

    hib[...] = flat[pl.ds(MARGIN + SHARD - HI, HI), :].astype(jnp.bfloat16)
    to_up = remote(hib, rlo, x_send, x_recv, 1, halo_to(up))
    to_up.start()
    lob[...] = flat[pl.ds(MARGIN, LO), :].astype(jnp.bfloat16)
    to_down = remote(lob, rhi, x_send, x_recv, 2, halo_to(down))
    to_down.start()

    patch_swap = remote(patch_ref, patch_out, x_send, x_recv, 3, mirror)
    meta_swap = remote(meta_ref, meta_out, x_send, x_recv, 4, mirror)
    patch_keep = pltpu.make_async_copy(patch_ref, patch_out, local_sem.at[1])
    meta_keep = pltpu.make_async_copy(meta_ref, meta_out, local_sem.at[2])

    @pl.when(swap)
    def _():
        patch_swap.start()
        meta_swap.start()
        main.wait_recv()
        flat[pl.ds(MARGIN, SHARD), :] = rmain[pl.ds(0, SHARD), :].astype(jnp.float32)

    @pl.when(jnp.logical_not(swap))
    def _():
        patch_keep.start()
        meta_keep.start()

    to_up.wait_recv()
    flat[pl.ds(MARGIN - HI, HI), :] = rlo[...].astype(jnp.float32)
    to_down.wait_recv()
    flat[pl.ds(MARGIN + SHARD, LO), :] = rhi[...].astype(jnp.float32)

    first = SLOT * v
    origin = SHARD * v - MARGIN
    for index, (base, c, groups, per, start) in enumerate(SECTIONS):
        lo = jnp.maximum(first, start)
        hi = jnp.minimum(first + SLOT, start + c * groups)
        if index == 1:
            lane = lax.broadcasted_iota(jnp.int32, (8, 128), 1)
            g0 = lax.div(jnp.maximum(lo, start) - start, 8)
            g1 = lax.div(jnp.maximum(hi, start) - start + 7, 8)

            def head_group(g, carry):
                row = base + per * g - origin
                for i in range(16):
                    q, s = divmod(1000 * i, 128)
                    one = flat[pl.ds(row + q, 8), :]
                    if s:
                        two = flat[pl.ds(row + q + 1, 8), :]
                        one = jnp.where(lane < 128 - s, pltpu.roll(one, 128 - s, 1), pltpu.roll(two, 128 - s, 1))
                    headrows[pl.ds(i * 8, 8), :] = one
                for j in range(8):
                    t = start + g * 8 + j - first

                    @pl.when(jnp.logical_and(t >= 0, t < SLOT))
                    def _():
                        slot[t] = headrows[pl.ds(j, 16, stride=8), :].astype(jnp.bfloat16)
                return carry

            lax.fori_loop(g0, g1, head_group, 0)
        else:

            def tile(t, carry):
                g = lax.div(t - start, c)
                j = lax.rem(t - start, c)
                row = base + 16 * c * g + j - origin
                slot[t - first] = flat[pl.ds(row, 16, stride=c), :].astype(jnp.bfloat16)
                return carry

            lax.fori_loop(lo, hi, tile, 0)
    pads = jnp.maximum(NTILE - first, 0)

    def blank(t, carry):
        slot[t] = jnp.zeros((16, 128), jnp.bfloat16)
        return carry

    lax.fori_loop(jnp.minimum(pads, SLOT), SLOT, blank, 0)

    def place(axis, k):
        return z * 8 + b * 4 + lax.rem(y + k, 4) if axis == 0 else (lax.rem(z + k, 4)) * 8 + b * 4 + y

    def place2(axis, k, j):
        if axis == 0:
            return (lax.rem(z + j, 4)) * 8 + b * 4 + lax.rem(y + k, 4)
        return (lax.rem(z + k, 4)) * 8 + b * 4 + lax.rem(y + j, 4)

    move = (at_y, at_z)
    keep = pltpu.make_async_copy(slot, t_out.at[pl.ds(v * SLOT, SLOT)], local_sem.at[3])
    keep.start()
    sends = []
    GS = g_send
    GR = g_recv

    def gsend(k, src, dst, target):
        copy = remote(src, dst, GS, GR, k, target)
        copy.start()
        sends.append(copy)
        return copy

    def arrived(k, dst):
        remote(dst, dst, GS, GR, k, sibling).wait_recv()

    def part(slot_id, lo, n):
        return t_out.at[pl.ds(slot_id * SLOT + lo, n)]

    def p1(h, k):
        return h * 20 + k

    def p2(h, m, k):
        return h * 20 + 4 + m * 4 + k

    def dd(h, j):
        return 40 + h * 16 + j

    own = lambda lo, n: slot.at[pl.ds(lo, n)]
    for h in range(2):
        A, B = h, 1 - h
        gsend(p1(h, 0), own(HALF * h, HALF), part(v, HALF * h, HALF), move[A](1))
        gsend(p1(h, 1), own(HALF * h, HALF), part(v, HALF * h, HALF), move[A](3))
    for h in range(2):
        A, B = h, 1 - h
        gsend(p2(h, 0, 0), own(HALF * h, HALF), part(v, HALF * h, HALF), move[B](1))
        gsend(p2(h, 0, 1), own(HALF * h, HALF), part(v, HALF * h, HALF), move[B](3))
        gsend(dd(h, 0), own(HALF * h, HALF), part(v, HALF * h, HALF), sibling)
    order = (0, 3, 1, 2)

    def spread(h, m):
        A, B = h, 1 - h
        s = place2(A, order[m], 0)
        gsend(p2(h, m, 0), part(s, HALF * h, HALF), part(s, HALF * h, HALF), move[B](1))
        gsend(p2(h, m, 1), part(s, HALF * h, HALF), part(s, HALF * h, HALF), move[B](3))
        gsend(dd(h, m), part(s, HALF * h, HALF), part(s, HALF * h, HALF), sibling)

    for h in range(2):
        A, B = h, 1 - h
        s = place2(A, 3, 0)
        arrived(p1(h, 0), part(s, HALF * h, HALF))
        gsend(p1(h, 2), part(s, HALF * h, QUART), part(s, HALF * h, QUART), move[A](1))
        s = place2(A, 1, 0)
        arrived(p1(h, 1), part(s, HALF * h, HALF))
        gsend(p1(h, 3), part(s, HALF * h + QUART, QUART), part(s, HALF * h + QUART, QUART), move[A](3))
        spread(h, 1)
        spread(h, 2)
    for h in range(2):
        A, B = h, 1 - h
        s = place2(A, 2, 0)
        arrived(p1(h, 2), part(s, HALF * h, QUART))
        arrived(p1(h, 3), part(s, HALF * h + QUART, QUART))
        spread(h, 3)
    for m in range(4):
        for h in range(2):
            A, B = h, 1 - h
            s = place2(A, order[m], 3)
            arrived(p2(h, m, 0), part(s, HALF * h, HALF))
            gsend(p2(h, m, 2), part(s, HALF * h, QUART), part(s, HALF * h, QUART), move[B](1))
            gsend(dd(h, 4 + m * 3), part(s, HALF * h, HALF), part(s, HALF * h, HALF), sibling)
            s = place2(A, order[m], 1)
            arrived(p2(h, m, 1), part(s, HALF * h, HALF))
            gsend(p2(h, m, 3), part(s, HALF * h + QUART, QUART), part(s, HALF * h + QUART, QUART), move[B](3))
            gsend(dd(h, 5 + m * 3), part(s, HALF * h, HALF), part(s, HALF * h, HALF), sibling)
    for m in range(4):
        for h in range(2):
            A, B = h, 1 - h
            s = place2(A, order[m], 2)
            arrived(p2(h, m, 2), part(s, HALF * h, QUART))
            arrived(p2(h, m, 3), part(s, HALF * h + QUART, QUART))
            gsend(dd(h, 6 + m * 3), part(s, HALF * h, HALF), part(s, HALF * h, HALF), sibling)
    for j in range(16):
        for h in range(2):
            arrived(dd(h, j), part(0, HALF * h, HALF))
    for copy in sends:
        copy.wait_send()
    keep.wait()
    to_up.wait_send()
    to_down.wait_send()

    @pl.when(swap)
    def _():
        main.wait_send()
        patch_swap.wait()
        meta_swap.wait()

    @pl.when(jnp.logical_not(swap))
    def _():
        patch_keep.wait()
        meta_keep.wait()


D = 768
HEADS = 12
HEAD_DIM = 64
FF = 3072
CLS = 1000
P_SIZE = 196
ROWS = 208
TOK = 2 * ROWS
NORM_EPS = 1e-06
SMOOTHING = 0.1
NTILES = 4224
T_E, T_HEAD, T_NORM, T_QKV, T_OUT, T_IN, T_FO = 0, 366, 750, 756, 1620, 1908, 3060
T_POS = 288
BLK = 256
STEP_ROWS = 32
F32 = jnp.float32
BF16 = jnp.bfloat16
ROOT_HALF = 0.7071067811865476
INV_ROOT_TWO_PI = 0.3989422804014327


def dot(x, w):
    return lax.dot_general(x, w, (((1,), (0,)), ((), ())), preferred_element_type=F32)


def dot_t(x, w):
    return lax.dot_general(x, w, (((1,), (1,)), ((), ())), preferred_element_type=F32)


def t_dot(x, w):
    return lax.dot_general(x, w, (((0,), (0,)), ((), ())), preferred_element_type=F32)


def stats(x):
    mean = jnp.sum(x, -1, keepdims=True) * (1.0 / D)
    centred = x - mean
    var = jnp.sum(centred * centred, -1, keepdims=True) * (1.0 / D)
    rstd = lax.rsqrt(var + NORM_EPS)
    return centred * rstd, rstd


def norm_back(d_hat, hat, rstd):
    m1 = jnp.sum(d_hat, -1, keepdims=True) * (1.0 / D)
    m2 = jnp.sum(d_hat * hat, -1, keepdims=True) * (1.0 / D)
    return rstd * (d_hat - m1 - hat * m2)


def compute_kernel(patch_ref, meta_ref, loss_ref, T, x, h, a, at, mix, prob, o, h1, a2, hid, slope, h2, dh, dyb, dmix):
    G = T

    def section(ref, start, c, groups):
        return ref.at[pl.ds(start, groups * c)].reshape(groups, c, 16, 128)

    def cols(start, c, groups, j):
        part = section(T, start, c, groups)
        return jnp.concatenate([part[:, 2 * j + k].reshape(groups * 16, 128) for k in range(2)], axis=1)

    def put_cols(start, c, groups, j, value):
        low = value.astype(BF16)
        part = section(G, start, c, groups)
        for k in range(2):
            part[:, 2 * j + k] = low[:, k * 128 : (k + 1) * 128].reshape(groups, 16, 128)

    def row_of(start, k):
        return jnp.concatenate([T[start + j][k : k + 1, :] for j in range(6)], axis=1).astype(F32)

    def lanes(j):
        return pl.ds(pl.multiple_of(j * BLK, BLK), BLK)

    def rows(i):
        return pl.ds(pl.multiple_of(i * STEP_ROWS, STEP_ROWS), STEP_ROWS)

    steps = TOK // STEP_ROWS
    for i in range(2):
        x[pl.ds(i * ROWS, 192), :] = patch_ref[i, pl.ds(0, 192), :]
        x[pl.ds(i * ROWS + 192, 16), :] = jnp.concatenate([patch_ref[i, pl.ds(192, 4), :], jnp.zeros((12, D), BF16)], axis=0)

    real = lax.broadcasted_iota(jnp.int32, (ROWS, 128), 0) < P_SIZE
    for j in range(3):
        acc = dot(x[...], cols(T_E, 6, 48, j))
        p = cols(T_POS, 6, 13, j).astype(F32)
        p = jnp.where(lax.broadcasted_iota(jnp.int32, (ROWS, BLK), 0) < P_SIZE, p, 0.0)
        for i in range(2):
            h[pl.ds(i * ROWS, ROWS), pl.ds(j * BLK, BLK)] = acc[i * ROWS : (i + 1) * ROWS] + p

    gain1, shift1, gain2, shift2 = (row_of(T_NORM, k) for k in range(4))

    def norm_one(i, carry):
        hat, unused = stats(h[rows(i), :])
        a[rows(i), :] = (hat * gain1 + shift1).astype(BF16)
        return carry

    lax.fori_loop(0, steps, norm_one, 0)

    def mix_block(j, carry):
        mix[:, lanes(j)] = dot(a[...], cols(T_QKV, 18, 48, j)).astype(BF16)
        return carry

    lax.fori_loop(0, 9, mix_block, 0)

    first_half = lax.broadcasted_iota(jnp.int32, (ROWS, 128), 1) < HEAD_DIM
    key_ok = lax.broadcasted_iota(jnp.int32, (ROWS, ROWS), 1) < P_SIZE
    zero = jnp.zeros((ROWS, 128), BF16)

    def qkv_of(n):
        i = lax.div(n, 6)
        p = lax.rem(n, 6)
        r = pl.ds(pl.multiple_of(i * ROWS, ROWS), ROWS)
        ls = [pl.ds(pl.multiple_of(p * 128 + D * k, 128), 128) for k in range(3)]
        return r, ls

    def attend(n, carry):
        r, ls = qkv_of(n)
        q, k, v = (mix[r, l] for l in ls)
        q = q * jnp.asarray(0.125, BF16)
        outs = []
        for e in range(2):
            mask = first_half if e == 0 else jnp.logical_not(first_half)
            s = dot_t(jnp.where(mask, q, zero), k)
            s = jnp.where(key_ok, s, -jnp.inf)
            top = jnp.max(s, -1, keepdims=True)
            ex = jnp.exp(s - top)
            pr = (ex / jnp.sum(ex, -1, keepdims=True)).astype(BF16)
            prob[n * 2 + e] = pr
            outs.append(dot(pr, v))
        o[r, ls[0]] = jnp.where(first_half, outs[0], outs[1]).astype(BF16)
        return carry

    lax.fori_loop(0, 12, attend, 0)
    for j in range(3):
        h1[:, pl.ds(j * BLK, BLK)] = h[:, pl.ds(j * BLK, BLK)] + dot(o[...], cols(T_OUT, 6, 48, j))

    def norm_two(i, carry):
        hat, unused = stats(h1[rows(i), :])
        a2[rows(i), :] = (hat * gain2 + shift2).astype(BF16)
        return carry

    lax.fori_loop(0, steps, norm_two, 0)

    def up_block(j, carry):
        u = dot(a2[...], cols(T_IN, 24, 48, j))
        phi = 0.5 * (1.0 + lax.erf(u * ROOT_HALF))
        pdf = jnp.exp(-0.5 * u * u) * INV_ROOT_TWO_PI
        hid[:, lanes(j)] = (u * phi).astype(BF16)
        slope[:, lanes(j)] = (phi + u * pdf).astype(BF16)
        return carry

    lax.fori_loop(0, 12, up_block, 0)
    for j in range(3):
        h2[:, pl.ds(j * BLK, BLK)] = h1[:, pl.ds(j * BLK, BLK)] + dot(hid[...], cols(T_FO, 6, 192, j))

    gain_end, shift_end = (row_of(T_POS + 72, 4 + k) for k in range(2))
    means = []
    for i in range(2):

        def pool_step(n, carry):
            hat, unused = stats(h2[pl.ds(pl.multiple_of(i * ROWS + n * 16, 16), 16), :])
            ok = lax.broadcasted_iota(jnp.int32, (16, D), 0) + n * 16 < P_SIZE
            hat = jnp.where(ok, hat, 0.0)
            return carry + hat[:8] + hat[8:]

        total = lax.fori_loop(0, 13, pool_step, jnp.zeros((8, D), F32))
        means.append(jnp.sum(total, 0, keepdims=True) * (1.0 / P_SIZE))
    mean_hat = jnp.concatenate(means + [jnp.zeros((14, D), F32)], axis=0)
    two = lax.broadcasted_iota(jnp.int32, (16, D), 0) < 2
    pooled = jnp.where(two, mean_hat * gain_end + shift_end, 0.0).astype(BF16)
    logits = jnp.concatenate([dot(pooled, cols(T_HEAD, 8, 48, j)) for j in range(4)], axis=1)
    lane = lax.broadcasted_iota(jnp.int32, (16, 1024), 1)
    lane_f = lane.astype(F32)
    inside = lane < CLS
    logits = jnp.where(inside, logits, -1e30)
    top = jnp.max(logits, -1, keepdims=True)
    total = jnp.sum(jnp.where(inside, jnp.exp(logits - top), 0.0), -1, keepdims=True)
    logp = logits - top - jnp.log(total)
    meta = meta_ref[...]
    pad14 = jnp.zeros((14, 1), F32)
    label = jnp.concatenate([meta[0:2, 0:1], pad14], axis=0)
    scale = jnp.concatenate([meta[2:4, 0:1], pad14], axis=0)
    valid = jnp.concatenate([meta[4:6, 0:1], pad14], axis=0)
    target = jnp.where(lane_f == label, 1.0 - SMOOTHING, 0.0) + SMOOTHING / CLS
    values = -jnp.sum(jnp.where(inside, target * logp, 0.0), -1, keepdims=True)
    loss_ref[...] = jnp.broadcast_to(jnp.sum(values * valid, 0, keepdims=True), (8, 128))
    d_logits = jnp.where(inside, scale * (jnp.exp(logp) - target), 0.0).astype(BF16)
    d_pooled = jnp.zeros((16, D), F32)
    for j in range(4):
        w = cols(T_HEAD, 8, 48, j)
        d_pooled = d_pooled + dot_t(d_logits[:, j * BLK : (j + 1) * BLK], w)
        put_cols(T_HEAD, 8, 48, j, t_dot(pooled, d_logits[:, j * BLK : (j + 1) * BLK]))
    d_gain_end = jnp.sum(d_pooled * mean_hat, 0, keepdims=True)
    d_shift_end = jnp.sum(d_pooled, 0, keepdims=True)
    for i in range(2):
        d_hat = d_pooled[i : i + 1, :] * (1.0 / P_SIZE) * gain_end

        def end_step(n, carry):
            r = pl.ds(pl.multiple_of(i * ROWS + n * 16, 16), 16)
            hat, rstd = stats(h2[r, :])
            ok = lax.broadcasted_iota(jnp.int32, (16, D), 0) + n * 16 < P_SIZE
            d = jnp.where(ok, norm_back(jnp.broadcast_to(d_hat, (16, D)), hat, rstd), 0.0)
            dh[r, :] = d
            dyb[r, :] = d.astype(BF16)
            return carry

        lax.fori_loop(0, 13, end_step, 0)

    at[...] = a2[...].T
    da = h2
    da[...] = jnp.zeros((TOK, D), F32)

    def mlp_block(j, carry):
        dy = dyb[...]
        d_w = t_dot(hid[:, lanes(j)], dy).astype(BF16)
        part = section(T, T_FO + j * 96, 6, 16)
        w = jnp.concatenate([part[:, k].reshape(BLK, 128) for k in range(6)], axis=1)
        for k in range(6):
            part[:, k] = d_w[:, k * 128 : (k + 1) * 128].reshape(16, 16, 128)
        d_u = (dot_t(dy, w) * slope[:, lanes(j)].astype(F32)).astype(BF16)
        da[...] += dot_t(d_u, cols(T_IN, 24, 48, j))
        put_cols(T_IN, 24, 48, j, dot(at[...], d_u))
        return carry

    lax.fori_loop(0, 12, mlp_block, 0)

    def back_two(i, carry):
        dg, ds = carry
        hat, rstd = stats(h1[rows(i), :])
        d = da[rows(i), :]
        new = dh[rows(i), :] + norm_back(d * gain2, hat, rstd)
        dh[rows(i), :] = new
        dyb[rows(i), :] = new.astype(BF16)
        return dg + jnp.sum((d * hat).reshape(4, 8, D), 0), ds + jnp.sum(d.reshape(4, 8, D), 0)

    none = jnp.zeros((8, D), F32)
    d_gain2, d_shift2 = lax.fori_loop(0, steps, back_two, (none, none))

    at[...] = o[...].T
    da[...] = jnp.zeros((TOK, D), F32)
    for j in range(3):
        dz = dyb[:, pl.ds(j * BLK, BLK)]
        da[...] += dot_t(dz, cols(T_OUT, 6, 48, j))
        put_cols(T_OUT, 6, 48, j, dot(at[...], dz))
    o[...] = da[...].astype(BF16)

    def attend_back(n, carry):
        r, ls = qkv_of(n)
        q, k, v = (mix[r, l] for l in ls)
        q = q * jnp.asarray(0.125, BF16)
        k8 = k * jnp.asarray(0.125, BF16)
        do = o[r, ls[0]]
        dq, dk, dv = [], [], []
        for e in range(2):
            mask = first_half if e == 0 else jnp.logical_not(first_half)
            pr = prob[n * 2 + e]
            dv.append(t_dot(pr, do))
            dp = dot_t(jnp.where(mask, do, zero), v)
            prf = pr.astype(F32)
            row = jnp.sum(prf * dp, -1, keepdims=True)
            ds = (prf * (dp - row)).astype(BF16)
            dq.append(dot(ds, k8))
            dk.append(t_dot(ds, q))
        for l, pair in zip(ls, (dq, dk, dv)):
            dmix[r, l] = jnp.where(first_half, pair[0], pair[1]).astype(BF16)
        return carry

    lax.fori_loop(0, 12, attend_back, 0)

    at[...] = a[...].T
    da[...] = jnp.zeros((TOK, D), F32)

    def qkv_block(j, carry):
        d = dmix[:, lanes(j)]
        da[...] += dot_t(d, cols(T_QKV, 18, 48, j))
        put_cols(T_QKV, 18, 48, j, dot(at[...], d))
        return carry

    lax.fori_loop(0, 9, qkv_block, 0)

    def back_one(i, carry):
        dg, ds = carry
        hat, rstd = stats(h[rows(i), :])
        d = da[rows(i), :]
        new = dh[rows(i), :] + norm_back(d * gain1, hat, rstd)
        dh[rows(i), :] = new
        dyb[rows(i), :] = new.astype(BF16)
        return dg + jnp.sum((d * hat).reshape(4, 8, D), 0), ds + jnp.sum(d.reshape(4, 8, D), 0)

    d_gain1, d_shift1 = lax.fori_loop(0, steps, back_one, (none, none))
    d_norms = jnp.concatenate([jnp.sum(d, 0, keepdims=True) for d in (d_gain1, d_shift1, d_gain2, d_shift2)] + [jnp.zeros((12, D), F32)], axis=0).astype(BF16)
    for j in range(6):
        G[T_NORM + j] = d_norms[:, j * 128 : (j + 1) * 128]
    at[...] = x[...].T
    row_id = lax.broadcasted_iota(jnp.int32, (ROWS, BLK), 0)
    for j in range(3):
        put_cols(T_E, 6, 48, j, dot(at[...], dyb[:, pl.ds(j * BLK, BLK)]))
        c = pl.ds(j * BLK, BLK)
        s = slice(j * BLK, (j + 1) * BLK)
        d_pos = dh[pl.ds(0, ROWS), c] + dh[pl.ds(ROWS, ROWS), c]
        d_pos = jnp.where(row_id < P_SIZE, d_pos, 0.0)
        d_pos = jnp.where(row_id == P_SIZE, jnp.broadcast_to(d_gain_end[:, s], (ROWS, BLK)), d_pos)
        d_pos = jnp.where(row_id == P_SIZE + 1, jnp.broadcast_to(d_shift_end[:, s], (ROWS, BLK)), d_pos)
        put_cols(T_POS, 6, 13, j, d_pos)
    G[pl.ds(4212, 12)] = jnp.zeros((12, 16, 128), BF16)


def front_kernel(w_ref, patch_ref, meta_ref, g_hbm, loss_ref, patch_in, meta_in, *rest):
    gather_part, compute_part, gsem = rest[:14], rest[14:-1], rest[-1]
    T = compute_part[0]
    gather_kernel(w_ref, patch_ref, meta_ref, T, patch_in, meta_in, *gather_part)
    compute_kernel(patch_in, meta_in, loss_ref, *compute_part)
    out = pltpu.make_async_copy(T, g_hbm, gsem)
    out.start()
    out.wait()


def front(weights, patches, meta):
    hbm = pl.BlockSpec(memory_space=pl.ANY)
    vmem = pl.BlockSpec(memory_space=pltpu.VMEM)
    V = pltpu.VMEM
    dma = pltpu.SemaphoreType.DMA
    return pl.pallas_call(
        front_kernel,
        out_shape=(jax.ShapeDtypeStruct((NTILES, 16, 128), BF16), jax.ShapeDtypeStruct((8, 128), F32)),
        in_specs=[hbm] * 3,
        out_specs=(hbm, vmem),
        scratch_shapes=[
            V(patches.shape, BF16),
            V((8, 128), F32),
            V((FROWS, 128), F32),
            V((128, 128), F32),
            V((2112, 128), BF16),
            V((LO, 128), BF16),
            V((HI, 128), BF16),
            V((2112, 128), BF16),
            V((HI, 128), BF16),
            V((LO, 128), BF16),
            V((SLOT, 16, 128), BF16),
            dma((4,)),
            dma((5,)),
            dma((5,)),
            dma((72,)),
            dma((72,)),
            V((NTILES, 16, 128), BF16),
            V((TOK, D), BF16),
            V((TOK, D), F32),
            V((TOK, D), BF16),
            V((D, TOK), BF16),
            V((TOK, 3 * D), BF16),
            V((24, ROWS, ROWS), BF16),
            V((TOK, D), BF16),
            V((TOK, D), F32),
            V((TOK, D), BF16),
            V((TOK, FF), BF16),
            V((TOK, FF), BF16),
            V((TOK, D), F32),
            V((TOK, D), F32),
            V((TOK, D), BF16),
            V((TOK, 3 * D), BF16),
            dma,
        ],
        compiler_params=pltpu.CompilerParams(collective_id=0, has_side_effects=True, vmem_limit_bytes=60 * 1024 * 1024),
        name="front",
    )(weights, patches, meta)


EDGE = 24
FRONT = 768
BACK_ROWS = FRONT + SHARD + 640 + 6
PADDED = 2112
STEP = 10
BETA_ONE = 0.9
BETA_TWO = 0.95
ADAM_EPS = 1e-08
DECAY = 0.05
INNER_RATE = 0.01
OUTER_RATE = 0.7
OUTER_MU = 0.9
F32 = jnp.float32
BF16 = jnp.bfloat16
ORDER = (2, 1, 3, 0)


def reduce_kernel(
    g_ref, loss_ref, w_ref, first_ref, second_ref, mom_ref,
    avg_out, mom_out, new_out, first_out, second_out, loss_out,
    L, R, RA, RB, window, flat, headrows, w, first, second, mom, upd, low, low2, pair, pair2, total, total2,
    load_sem, d_send, d_recv, a_send, a_recv, b_send, b_recv, x_send, x_recv, LS, l_send, l_recv,
):
    xl, b, z, a, y = coords()
    fs = z * 8 + a * 4 + y
    v = z * 8 + b * 4 + y
    swap = a != b

    def owner(s):
        return device(xl, lax.rem(lax.div(s, 4), 2), a, lax.div(s, 8), lax.rem(s, 4))

    def server(s):
        return device(xl, b, lax.rem(lax.div(s, 4), 2), lax.div(s, 8), lax.rem(s, 4))

    def around(s):
        return lax.rem(s + NSLOT, NSLOT)

    mirror = device(xl, b, a, z, y)
    sibling = device(xl, a, 1 - b, z, y)
    across = device(1 - xl, a, b, z, y)

    def at_z(k):
        return device(xl, a, b, lax.rem(z + k, 4), y)

    def at_y(k):
        return device(xl, a, b, z, lax.rem(y + k, 4))

    barrier = pltpu.get_barrier_semaphore()
    for target in (sibling, across, at_y(1), at_y(3), at_z(1), at_z(3), server(around(fs + 1)), server(around(fs - 1))):
        pl.semaphore_signal(barrier, inc=1, device_id=target, device_id_type=MESH)

    @pl.when(swap)
    def _():
        pl.semaphore_signal(barrier, inc=1, device_id=mirror, device_id_type=MESH)

    own = []
    for kz in range(4):
        for ky in range(4):
            s = lax.rem(z + ORDER[kz], 4) * 8 + b * 4 + lax.rem(y + ORDER[ky], 4)
            own.append(pltpu.make_async_copy(g_ref.at[s], L.at[kz, ky], load_sem.at[kz * 4 + ky]))
    extra = [pltpu.make_async_copy(src, dst, load_sem.at[16 + i]) for i, (src, dst) in enumerate(((w_ref, w), (first_ref, first), (second_ref, second), (mom_ref, mom)))]

    pl.semaphore_wait(barrier, jnp.where(swap, 9, 8))

    def remote(src, dst, send, recv, k, target):
        return pltpu.make_async_remote_copy(src_ref=src, dst_ref=dst, send_sem=send.at[k], recv_sem=recv.at[k], device_id=target, device_id_type=MESH)

    sends = []

    def go(*args):
        copy = remote(*args)
        copy.start()
        sends.append(copy)
        return copy

    sequence = [(0, 0), (0, 1), (1, 0), (0, 2), (0, 3), (2, 0), (3, 0), (1, 2), (1, 3), (2, 1), (3, 1), (1, 1), (2, 2), (2, 3), (3, 2), (3, 3)]
    for kz, ky in sequence:
        s = lax.rem(z + ORDER[kz], 4) * 8 + (1 - b) * 4 + lax.rem(y + ORDER[ky], 4)
        go(g_ref.at[s], R.at[kz, ky], d_send, d_recv, kz * 4 + ky, sibling)
        own[kz * 4 + ky].start()
    for copy in extra:
        copy.start()

    LS[0] = loss_ref[...]

    def loss_send(src, dst, target):
        go(LS.at[src], LS.at[dst], l_send, l_recv, dst - 1, target)

    loss_send(0, 1, sibling)

    def add_into(dst, src, n):
        def one(i, carry):
            for k in range(3):
                t = i * 3 + k
                dst[t] = dst[t] + src[t]
            return carry

        lax.fori_loop(0, n // 3, one, 0)

    def arrive(dst, recv, k):
        remote(dst, dst, d_send, recv, k, sibling).wait_recv()

    done = set()

    def need(*slots):
        for kz, ky in slots:
            if (kz, ky) not in done:
                done.add((kz, ky))
                own[kz * 4 + ky].wait()
                arrive(R.at[kz, ky], d_recv, kz * 4 + ky)
                add_into(L.at[kz, ky], R.at[kz, ky], SLOT)

    move = (at_z, at_y)

    def block(h, ka, p):
        t = pl.ds(HALF * h, HALF)
        return L.at[ka, pl.ds(2 * p, 2), t] if h == 0 else L.at[pl.ds(2 * p, 2), ka, t]

    def cells(h, ka, p):
        return [(ka, 2 * p + i) if h == 0 else (2 * p + i, ka) for i in range(2)]

    def send_a(h, k, ka, p, step):
        need(*cells(h, ka, p))
        go(block(h, ka, p), RA.at[h, k], a_send, a_recv, h * 6 + k, move[h](step))

    def take_a(h, k, ka, p):
        need(*cells(h, ka, p))
        arrive(RA.at[h, k], a_recv, h * 6 + k)
        for i in range(2):
            add_into(block(h, ka, p).at[i], RA.at[h, k, i], HALF)

    for k, ka, p, step in ((0, 0, 0, 1), (1, 0, 1, 3), (2, 1, 1, 1), (3, 2, 0, 3)):
        for h in range(2):
            send_a(h, k, ka, p, step)
    arrive(LS.at[1], l_recv, 0)
    LS[8] = loss_ref[...] + LS[1]
    loss_send(8, 2, at_y(1))
    loss_send(8, 3, at_y(3))
    for k, ka, p, step in ((0, 1, 0, 1), (1, 2, 1, 3)):
        for h in range(2):
            take_a(h, k, ka, p)
            send_a(h, k + 4, ka, p, step)

    def sum_three(h, p):
        ks = (3, 4) if p == 0 else (2, 5)
        need(*cells(h, 3, p))
        for k in ks:
            arrive(RA.at[h, k], a_recv, h * 6 + k)
        for i in range(2):
            dst, one, two = block(h, 3, p).at[i], RA.at[h, ks[0], i], RA.at[h, ks[1], i]

            def body(n, carry):
                for k in range(3):
                    t = n * 3 + k
                    dst[t] = (dst[t].astype(F32) + one[t].astype(F32) + two[t].astype(F32)).astype(BF16)
                return carry

            lax.fori_loop(0, HALF // 3, body, 0)

    def cell(h, kb, q):
        t = pl.ds(HALF * h + QUART * q, QUART)
        return L.at[3, kb, t] if h == 0 else L.at[kb, 3, t]

    def send_b(h, k, kb, q, step):
        go(cell(h, kb, q), RB.at[h, k], b_send, b_recv, h * 6 + k, move[1 - h](step))

    def take_b(h, k, kb, q):
        arrive(RB.at[h, k], b_recv, h * 6 + k)
        add_into(cell(h, kb, q), RB.at[h, k], QUART)

    arrive(LS.at[2], l_recv, 1)
    loss_send(2, 4, at_y(1))
    arrive(LS.at[3], l_recv, 2)
    for h in range(2):
        sum_three(h, 0)
        send_b(h, 0, 0, 0, 1)
        send_b(h, 1, 0, 1, 3)
        send_b(h, 2, 1, 1, 1)
    for h in range(2):
        sum_three(h, 1)
        send_b(h, 3, 2, 0, 3)
    arrive(LS.at[4], l_recv, 3)
    LS[9] = (LS[8] + LS[4]) + (LS[2] + LS[3])
    loss_send(9, 5, at_z(1))
    loss_send(9, 6, at_z(3))
    for h in range(2):
        take_b(h, 0, 1, 0)
        send_b(h, 4, 1, 0, 1)
        take_b(h, 1, 2, 1)
        send_b(h, 5, 2, 1, 3)
    for h in range(2):
        for q, ks in ((0, (3, 4)), (1, (2, 5))):
            for k in ks:
                arrive(RB.at[h, k], b_recv, h * 6 + k)
            dst, one, two = cell(h, 3, q), RB.at[h, ks[0]], RB.at[h, ks[1]]

            def body(n, carry):
                for k in range(3):
                    t = n * 3 + k
                    dst[t] = (dst[t].astype(F32) + one[t].astype(F32) + two[t].astype(F32)).astype(BF16)
                return carry

            lax.fori_loop(0, QUART // 3, body, 0)

    arrive(LS.at[5], l_recv, 4)
    loss_send(5, 7, at_z(1))
    arrive(LS.at[6], l_recv, 5)
    mine = L.at[3, 3]
    main = remote(mine, window.at[pl.ds(EDGE, SLOT)], x_send, x_recv, 0, mirror)
    main_keep = pltpu.make_async_copy(mine, window.at[pl.ds(EDGE, SLOT)], load_sem.at[20])

    @pl.when(swap)
    def _():
        main.start()

    @pl.when(jnp.logical_not(swap))
    def _():
        main_keep.start()

    go(mine.at[pl.ds(0, EDGE)], window.at[pl.ds(EDGE + SLOT, EDGE)], x_send, x_recv, 1, owner(around(v - 1)))
    go(mine.at[pl.ds(SLOT - EDGE, EDGE)], window.at[pl.ds(0, EDGE)], x_send, x_recv, 2, owner(around(v + 1)))

    def clear(i, carry):
        flat[pl.ds(pl.multiple_of(i * 32, 32), 32), :] = jnp.zeros((32, 128), F32)
        return carry

    lax.fori_loop(0, BACK_ROWS // 32, clear, 0)
    for copy in extra:
        copy.wait()
    arrive(window.at[pl.ds(EDGE + SLOT, EDGE)], x_recv, 1)
    arrive(window.at[pl.ds(0, EDGE)], x_recv, 2)

    @pl.when(swap)
    def _():
        main.wait()

    @pl.when(jnp.logical_not(swap))
    def _():
        main_keep.wait()

    low_tile = SLOT * fs - EDGE
    high_tile = SLOT * fs + SLOT + EDGE
    origin = SHARD * fs - FRONT
    for index, (base, c, groups, per, start) in enumerate(SECTIONS):
        if index == 1:
            lane = lax.broadcasted_iota(jnp.int32, (8, 128), 1)
            g0 = lax.div(jnp.maximum(SHARD * fs - base, 0), per)
            g1 = lax.div(jnp.maximum(SHARD * (fs + 1) - base, 0) + per - 1, per)

            def head_group(g, carry):
                t = start + g * 8 - low_tile
                for j in range(8):
                    headrows[pl.ds(j, 16, stride=8), :] = window[t + j].astype(F32)
                row = base + per * g - origin
                for i in range(16):
                    q, s = divmod(1000 * i, 128)
                    value = headrows[pl.ds(i * 8, 8), :]
                    if s:
                        value = pltpu.roll(value, s, 1)
                        flat[pl.ds(row + q, 8), :] += jnp.where(lane >= s, value, 0.0)
                        flat[pl.ds(row + q + 1, 8), :] += jnp.where(lane < s, value, 0.0)
                    else:
                        flat[pl.ds(row + q, 8), :] += value
                return carry

            lax.fori_loop(jnp.minimum(g0, groups), jnp.minimum(g1, groups), head_group, 0)
        else:

            def tile(t, carry):
                g = lax.div(t - start, c)
                j = lax.rem(t - start, c)
                flat[pl.ds(base + 16 * c * g + j - origin, 16, stride=c), :] = window[t - low_tile].astype(F32)
                return carry

            lax.fori_loop(jnp.maximum(low_tile, start), jnp.minimum(high_tile, start + c * groups), tile, 0)

    arrive(LS.at[7], l_recv, 6)
    LS[10] = (LS[9] + LS[7]) + (LS[5] + LS[6])
    loss_swap = remote(LS.at[10], LS.at[11], l_send, l_recv, 10, mirror)

    @pl.when(swap)
    def _():
        loss_swap.start()

    fix_one = 1.0 / (1.0 - BETA_ONE**STEP)
    fix_two = 1.0 / (1.0 - BETA_TWO**STEP)

    def in_rows(fn, lo, hi, step=32):
        def body(i, carry):
            fn(pl.multiple_of(i * step, step), step)
            return carry

        n = (hi - lo) // step
        lax.fori_loop(lo // step, lo // step + n, body, 0)
        if lo + n * step < hi:
            fn(lo + n * step, hi - lo - n * step)

    def adam(r, n):
        grad = flat[pl.ds(FRONT + r, n), :]
        m = BETA_ONE * first[pl.ds(r, n), :] + (1.0 - BETA_ONE) * grad
        s = BETA_TWO * second[pl.ds(r, n), :] + (1.0 - BETA_TWO) * grad * grad
        first[pl.ds(r, n), :] = m
        second[pl.ds(r, n), :] = s
        u = (m * fix_one) / (jnp.sqrt(s * fix_two) + ADAM_EPS)
        upd[pl.ds(r, n), :] = u

    in_rows(adam, 0, SHARD)
    upd[pl.ds(SHARD, PADDED - SHARD), :] = jnp.zeros((PADDED - SHARD, 128), F32)
    outs = [pltpu.make_async_copy(src, dst, load_sem.at[16 + i]) for i, (src, dst) in enumerate(((first, first_out), (second, second_out)))]
    for copy in outs:
        copy.start()

    def lower(r, n):
        low[pl.ds(r, n), :] = upd[pl.ds(r, n), :].astype(BF16)

    in_rows(lower, 0, PADDED)
    go(low, low2, x_send, x_recv, 3, sibling)
    arrive(low2, x_recv, 3)
    half = PADDED // 2

    def pairs(r, n):
        at = pl.ds(pl.multiple_of(b * half + r, 16), n)
        pair[pl.ds(r, n), :] = low[at, :] + low2[at, :]

    in_rows(pairs, 0, half)
    go(pair, pair2, x_send, x_recv, 4, across)
    arrive(pair2, x_recv, 4)

    def fours(r, n):
        total[pl.ds(r, n), :] = pair[pl.ds(r, n), :].astype(F32) + pair2[pl.ds(r, n), :].astype(F32)

    in_rows(fours, 0, half)
    go(total, total2, x_send, x_recv, 5, sibling)

    def outer(source, shift):
        def rows_of(r, n):
            at = pl.ds(shift + r, n)
            t = source[pl.ds(r, n), :]
            old = w[at, :]
            averaged = INNER_RATE * (t * 0.25 + DECAY * old)
            momentum = OUTER_MU * mom[at, :] + averaged
            upd[at, :] = averaged
            mom[at, :] = momentum
            w[at, :] = old - OUTER_RATE * (averaged + OUTER_MU * momentum)

        return rows_of

    def both(here, there):
        in_rows(outer(here, 0), 0, half)
        in_rows(outer(there, half), 0, SHARD - half)

    arrive(total2, x_recv, 5)

    @pl.when(b == 0)
    def _():
        both(total, total2)

    @pl.when(b == 1)
    def _():
        both(total2, total)

    final = [(upd.at[pl.ds(0, SHARD)], avg_out), (mom, mom_out), (w, new_out)]
    final = [pltpu.make_async_copy(src, dst, load_sem.at[18 + i]) for i, (src, dst) in enumerate(final)]
    for copy in final:
        copy.start()
    @pl.when(swap)
    def _():
        loss_swap.wait()
        loss_out[...] = LS[11]

    @pl.when(jnp.logical_not(swap))
    def _():
        loss_out[...] = LS[10]

    for copy in sends:
        copy.wait_send()
    for copy in outs + final:
        copy.wait()


def reduce_update(grads, loss, weights, first, second, momentum):
    hbm = pl.BlockSpec(memory_space=pl.ANY)
    V = pltpu.VMEM
    vmem = pl.BlockSpec(memory_space=pltpu.VMEM)
    flat = jax.ShapeDtypeStruct((SHARD, 128), F32)
    dma = pltpu.SemaphoreType.DMA
    return pl.pallas_call(
        reduce_kernel,
        out_shape=(flat,) * 5 + (jax.ShapeDtypeStruct((8, 128), F32),),
        in_specs=[hbm, vmem] + [hbm] * 4,
        out_specs=(hbm,) * 5 + (vmem,),
        scratch_shapes=[
            V((4, 4, SLOT, 16, 128), BF16),
            V((4, 4, SLOT, 16, 128), BF16),
            V((2, 6, 2, HALF, 16, 128), BF16),
            V((2, 6, QUART, 16, 128), BF16),
            V((EDGE + SLOT + EDGE, 16, 128), BF16),
            V((BACK_ROWS, 128), F32),
            V((128, 128), F32),
            V((SHARD, 128), F32),
            V((SHARD, 128), F32),
            V((SHARD, 128), F32),
            V((SHARD, 128), F32),
            V((PADDED, 128), F32),
            V((PADDED, 128), BF16),
            V((PADDED, 128), BF16),
            V((PADDED // 2, 128), BF16),
            V((PADDED // 2, 128), BF16),
            V((PADDED // 2, 128), F32),
            V((PADDED // 2, 128), F32),
            dma((21,)),
            dma((16,)),
            dma((16,)),
            dma((12,)),
            dma((12,)),
            dma((12,)),
            dma((12,)),
            dma((6,)),
            dma((6,)),
            V((12, 8, 128), F32),
            dma((11,)),
            dma((11,)),
        ],
        compiler_params=pltpu.CompilerParams(collective_id=1, has_side_effects=True, vmem_limit_bytes=52 * 1024 * 1024),
        name="reduce_update",
    )(grads, loss, weights, first, second, momentum)


def rows_kernel(one, two, out_one, out_two, sem):
    copies = [pltpu.make_async_copy(src.reshape(SHARD, 128), dst, sem.at[i]) for i, (src, dst) in enumerate(((one, out_one), (two, out_two)))]
    for copy in copies:
        copy.start()
    for copy in copies:
        copy.wait()


def as_rows(one, two):
    hbm = pl.BlockSpec(memory_space=pl.ANY)
    shape = jax.ShapeDtypeStruct((SHARD, 128), F32)
    return pl.pallas_call(
        rows_kernel,
        out_shape=(shape,) * 2,
        in_specs=[hbm] * 2,
        out_specs=(hbm,) * 2,
        scratch_shapes=[pltpu.SemaphoreType.DMA((2,))],
        name="as_rows",
    )(one, two)


def flat_kernel(*refs):
    count = len(refs) // 2
    sem = refs[-1]
    copies = []
    for i in range(count):
        src, dst = refs[i], refs[count + i]
        if len(dst.shape) == 2 and dst.shape[0] == 1:
            dst = dst.reshape(SHARD, 128)
        copies.append(pltpu.make_async_copy(src, dst, sem.at[i]))
    for copy in copies:
        copy.start()
    for copy in copies:
        copy.wait()


def finish(averaged, momentum, new_weights, first, second):
    hbm = pl.BlockSpec(memory_space=pl.ANY)
    shape = jax.ShapeDtypeStruct((SHARD, 128), F32)
    row = jax.ShapeDtypeStruct((1, SHARD * 128), F32)
    return pl.pallas_call(
        flat_kernel,
        out_shape=(shape,) * 3 + (row,) * 2,
        in_specs=[hbm] * 5,
        out_specs=(hbm,) * 5,
        scratch_shapes=[pltpu.SemaphoreType.DMA((5,))],
        name="finish",
    )(averaged, momentum, new_weights, first, second)


def body(patches, labels, counts, weights, first_moments, second_moments, outer_momentum):
    rank = lax.axis_index("fsdp")
    total_count = jnp.sum(counts[0, 0]).astype(jnp.float32)
    valid = (rank < counts[0, 0]).astype(jnp.float32)
    fields = jnp.concatenate([labels[0, 0, :, 0].astype(jnp.float32), valid / total_count, valid, jnp.zeros((2,), jnp.float32)])
    meta = jnp.broadcast_to(fields[:, None], (8, 128))
    flat = weights.reshape(SHARD, 128)
    first, second = as_rows(first_moments, second_moments)
    grads, loss = front(flat, patches.reshape(2, P_SIZE, D), meta)
    averaged, momentum, new_weights, first, second, losses = reduce_update(
        grads.reshape(NSLOT, SLOT, 16, 128),
        loss,
        flat,
        first,
        second,
        outer_momentum.reshape(SHARD, 128),
    )
    averaged, momentum, new_weights, first, second = finish(averaged, momentum, new_weights, first, second)
    return (
        averaged.reshape(-1),
        momentum.reshape(-1),
        new_weights.reshape(-1),
        first,
        second,
        losses[:1, :1],
    )


def solution(mesh):
    placed = (
        P("rep", None, None, "fsdp", None, None),
        P("rep", None, None, "fsdp"),
        P("rep", None, None),
        P("fsdp"),
        P("rep", "fsdp"),
        P("rep", "fsdp"),
        P("fsdp"),
    )
    return jax.shard_map(
        body,
        mesh=mesh,
        in_specs=placed,
        out_specs=(
            P("fsdp"),
            P("fsdp"),
            P("fsdp"),
            P("rep", "fsdp"),
            P("rep", "fsdp"),
            P("rep", None),
        ),
        check_vma=False,
    )
```

```python
from functools import partial

import jax
import jax.numpy as jnp
from jax import lax
from jax.experimental import pallas as pl
from jax.experimental.pallas import tpu as pltpu
from jax.sharding import PartitionSpec as P

SHARD = 2098
SLOT = 132
HALF = 66
QUART = 33
NSLOT = 32
ROUNDS = 22
UNIT = 6
STAGES = ((0, 4), (4, 10), (10, 16), (16, 22))
SECTIONS = []
_t = 0
for _base, _c, _g, _rpg in ((0, 6, 61, 96), (5796, 8, 48, 125), (11796, 6, 1, 96), (11820, 18, 48, 288), (25644, 6, 48, 96), (30252, 24, 48, 384), (48684, 6, 192, 96)):
    SECTIONS.append((_base, _c, _g, _rpg, _t))
    _t += _c * _g
NTILE = _t
HI = 352
LO = 224
MARGIN = 512
FROWS = 3072
HEAD_ROWS = 16
MESH = pl.DeviceIdType.MESH


def coords():
    rep = lax.axis_index("rep")
    fs = lax.axis_index("fsdp")
    return lax.div(rep, 2), lax.rem(rep, 2), lax.div(fs, 8), lax.rem(lax.div(fs, 4), 2), lax.rem(fs, 4)


def device(xl, xh, core, z, y):
    return {"rep": xl * 2 + core, "fsdp": z * 8 + xh * 4 + y}


def flat_device(xl, core, s):
    return device(xl, lax.rem(lax.div(s, 4), 2), core, lax.div(s, 8), lax.rem(s, 4))


class Links:

    def __init__(self, T, R, RA, RB, g_send, g_recv, r_send, r_recv):
        self.xl, self.b, self.z, self.a, self.y = coords()
        self.T5 = T.reshape(ROUNDS, 4, 2, 4, UNIT, 16, 128)
        self.R, self.RA, self.RB = R, RA, RB
        self.g_send, self.g_recv, self.r_send, self.r_recv = g_send, g_recv, r_send, r_recv
        self.pending = []
        self.sibling = device(self.xl, self.a, 1 - self.b, self.z, self.y)

    def at_y(self, k):
        return device(self.xl, self.a, self.b, self.z, lax.rem(self.y + k, 4))

    def at_z(self, k):
        return device(self.xl, self.a, self.b, lax.rem(self.z + k, 4), self.y)

    def go(self, src, dst, send, recv, target):
        copy = pltpu.make_async_remote_copy(src_ref=src, dst_ref=dst, send_sem=send, recv_sem=recv, device_id=target, device_id_type=MESH)
        copy.start()
        self.pending.append(copy)

    def landed(self, dst, send, recv):
        pltpu.make_async_remote_copy(src_ref=dst, dst_ref=dst, send_sem=send, recv_sem=recv, device_id=self.sibling, device_id_type=MESH).wait_recv()

    def sent(self):
        for copy in self.pending:
            copy.wait_send()
        self.pending = []

    def span(self, i, h):
        lo, hi = STAGES[i]
        n = (hi - lo) // 2
        return pl.ds(lo + h * n, n)

    def first_axis(self, h, k):
        return (self.at_y if h == 0 else self.at_z)(k)

    def second_axis(self, h, k):
        return (self.at_z if h == 0 else self.at_y)(k)

    def one(self, i, h, k, q=None):
        rd = self.span(i, h)
        t = pl.ds(0, UNIT) if q is None else pl.ds(3 * q, 3)
        if h == 0:
            return self.T5.at[rd, self.z, self.b, lax.rem(self.y + k, 4), t]
        return self.T5.at[rd, lax.rem(self.z + k, 4), self.b, self.y, t]

    def row(self, i, h, k, core=None, p=None):
        rd = self.span(i, h)
        core = self.b if core is None else core
        t = pl.ds(0, 4) if p is None else pl.ds(2 * p, 2)
        if h == 0:
            return self.T5.at[rd, lax.rem(self.z + k, 4), core, t]
        return self.T5.at[rd, t, core, lax.rem(self.y + k, 4)]

    def gsem(self, i, h, k):
        n = (i * 2 + h) * 12 + k
        return self.g_send.at[n], self.g_recv.at[n]

    def gather_go(self, i, h, k, view, target):
        self.go(view, view, *self.gsem(i, h, k), target)

    def gather_wait(self, i, h, k, view):
        self.landed(view, *self.gsem(i, h, k))

    def gather_step(self, i, step):
        for h in range(2):
            if step == 0:
                self.gather_go(i, h, 0, self.one(i, h, 0), self.first_axis(h, 1))
                self.gather_go(i, h, 1, self.one(i, h, 0), self.first_axis(h, 3))
            elif step == 1:
                self.gather_wait(i, h, 0, self.one(i, h, 3))
                self.gather_go(i, h, 2, self.one(i, h, 3, 0), self.first_axis(h, 1))
                self.gather_wait(i, h, 1, self.one(i, h, 1))
                self.gather_go(i, h, 3, self.one(i, h, 1, 1), self.first_axis(h, 3))
            elif step == 2:
                self.gather_wait(i, h, 2, self.one(i, h, 2, 0))
                self.gather_wait(i, h, 3, self.one(i, h, 2, 1))
                self.gather_go(i, h, 4, self.row(i, h, 0), self.second_axis(h, 1))
                self.gather_go(i, h, 5, self.row(i, h, 0), self.second_axis(h, 3))
                self.gather_go(i, h, 8, self.row(i, h, 0), self.sibling)
            elif step == 3:
                self.gather_wait(i, h, 4, self.row(i, h, 3))
                self.gather_go(i, h, 6, self.row(i, h, 3, p=0), self.second_axis(h, 1))
                self.gather_go(i, h, 9, self.row(i, h, 3), self.sibling)
                self.gather_wait(i, h, 5, self.row(i, h, 1))
                self.gather_go(i, h, 7, self.row(i, h, 1, p=1), self.second_axis(h, 3))
                self.gather_go(i, h, 10, self.row(i, h, 1), self.sibling)
            elif step == 4:
                self.gather_wait(i, h, 6, self.row(i, h, 2, p=0))
                self.gather_wait(i, h, 7, self.row(i, h, 2, p=1))
                self.gather_go(i, h, 11, self.row(i, h, 2), self.sibling)
            else:
                for k, offset in ((8, 0), (9, 3), (10, 1), (11, 2)):
                    self.gather_wait(i, h, k, self.row(i, h, offset, core=1 - self.b))

    def rsem(self, i, h, k):
        n = (i * 2 + h) * 13 + k
        return self.r_send.at[n], self.r_recv.at[n]

    def cell(self, i, h, k, q):
        rd = self.span(i, h)
        t = pl.ds(3 * q, 3)
        if h == 0:
            return self.T5.at[rd, self.z, self.b, lax.rem(self.y + k, 4), t]
        return self.T5.at[rd, lax.rem(self.z + k, 4), self.b, self.y, t]

    def add(self, dst, *sources, inner=()):
        n = dst.shape[0]

        def one(r, carry):
            for k in range(inner) if inner else (None,):
                at = (r,) if k is None else (r, k)
                if len(sources) == 1:
                    dst[at] = dst[at] + sources[0][at]
                else:
                    total = dst[at].astype(jnp.float32)
                    for source in sources:
                        total = total + source[at].astype(jnp.float32)
                    dst[at] = total.astype(jnp.bfloat16)
            return carry

        lax.fori_loop(0, n, one, 0)

    def reduce_step(self, i, h, step):
        rd = self.span(i, h)
        T5 = self.T5

        def send_a(k, ka, p, shift):
            self.go(self.row(i, h, ka, p=p), self.RA.at[k, rd], *self.rsem(i, h, 1 + k), self.second_axis(h, shift))

        def wait_a(k):
            self.landed(self.RA.at[k, rd], *self.rsem(i, h, 1 + k))

        def send_b(k, kb, q, shift):
            self.go(self.cell(i, h, kb, q), self.RB.at[k, rd], *self.rsem(i, h, 7 + k), self.first_axis(h, shift))

        def wait_b(k):
            self.landed(self.RB.at[k, rd], *self.rsem(i, h, 7 + k))

        if step == 0:
            self.go(T5.at[rd, :, 1 - self.b], self.R.at[rd], *self.rsem(i, h, 0), self.sibling)
        elif step == 1:
            self.landed(self.R.at[rd], *self.rsem(i, h, 0))
            mine, theirs = T5.at[rd, :, self.b], self.R.at[rd]
            n = mine.shape[0]

            def both(r, carry):
                q = lax.div(r, 4)
                w = lax.rem(r, 4)
                for k in range(4):
                    mine[q, w, k] = mine[q, w, k] + theirs[q, w, k]
                return carry

            lax.fori_loop(0, 4 * n, both, 0)
            send_a(0, 2, 0, 1)
            send_a(1, 2, 1, 3)
            send_a(2, 1, 1, 1)
            send_a(3, 3, 0, 3)
        elif step == 2:
            wait_a(0)
            self.add(self.row(i, h, 1, p=0), self.RA.at[0, rd], inner=2)
            send_a(4, 1, 0, 1)
            wait_a(1)
            self.add(self.row(i, h, 3, p=1), self.RA.at[1, rd], inner=2)
            send_a(5, 3, 1, 3)
        elif step == 3:
            for k in (2, 3, 4, 5):
                wait_a(k)
            self.add(self.row(i, h, 0, p=0), self.RA.at[3, rd], self.RA.at[4, rd], inner=2)
            self.add(self.row(i, h, 0, p=1), self.RA.at[2, rd], self.RA.at[5, rd], inner=2)
            send_b(0, 2, 0, 1)
            send_b(1, 2, 1, 3)
            send_b(2, 1, 1, 1)
            send_b(3, 3, 0, 3)
        elif step == 4:
            wait_b(0)
            self.add(self.cell(i, h, 1, 0), self.RB.at[0, rd])
            send_b(4, 1, 0, 1)
            wait_b(1)
            self.add(self.cell(i, h, 3, 1), self.RB.at[1, rd])
            send_b(5, 3, 1, 3)
        else:
            for k in (2, 3, 4, 5):
                wait_b(k)
            self.add(self.cell(i, h, 0, 0), self.RB.at[3, rd], self.RB.at[4, rd])
            self.add(self.cell(i, h, 0, 1), self.RB.at[2, rd], self.RB.at[5, rd])


def start_gather(links, w_ref, patch_ref, meta_ref, T, patch_in, meta_in, flat, headrows, lob, hib, rlo, rhi, slot, local_sem, x_send, x_recv, u_send, u_recv):
    xl, b, z, a, y = links.xl, links.b, links.z, links.a, links.y
    fs = z * 8 + a * 4 + y
    swap = a != b
    xo = lax.rem(xl + a + b, 2)
    holder = z * 8 + b * 4 + y
    up = flat_device(xl, b, lax.rem(fs + 1, NSLOT))
    down = flat_device(xl, b, lax.rem(fs + NSLOT - 1, NSLOT))
    mirror = device(xl, b, a, z, y)
    load = pltpu.make_async_copy(w_ref, flat.at[pl.ds(MARGIN, SHARD)], local_sem.at[0])
    load.start()
    barrier = pltpu.get_barrier_semaphore()

    def greet(target):
        pl.semaphore_signal(barrier, inc=1, device_id=target, device_id_type=MESH)

    for target in (up, down, links.at_y(1), links.at_y(3), links.at_z(1), links.at_z(3), links.sibling):
        greet(target)

    @pl.when(swap)
    def _():
        greet(mirror)

    own_index = lax.rem(fs * 11, NSLOT)
    keeps = jnp.logical_and(a == b, own_index < ROUNDS)

    def greet_source(j, carry):
        s = lax.div(32 * j + holder, ROUNDS)
        sa = lax.rem(lax.div(s, 4), 2)

        @pl.when(jnp.logical_not(jnp.logical_and(keeps, s == fs)))
        def _():
            greet(device(lax.rem(xl + sa + a, 2), sa, a, lax.div(s, 8), lax.rem(s, 4)))

        return carry

    lax.fori_loop(0, ROUNDS, greet_source, 0)
    pl.semaphore_wait(barrier, 7 + ROUNDS + jnp.where(swap, 1, 0) - jnp.where(keeps, 1, 0))
    load.wait()

    def remote(src, dst, k, target):
        return pltpu.make_async_remote_copy(src_ref=src, dst_ref=dst, send_sem=x_send.at[k], recv_sem=x_recv.at[k], device_id=target, device_id_type=MESH)

    hib[...] = flat[pl.ds(MARGIN + SHARD - HI, HI), :].astype(jnp.bfloat16)
    to_up = remote(hib, rlo, 0, up)
    to_up.start()
    lob[...] = flat[pl.ds(MARGIN, LO), :].astype(jnp.bfloat16)
    to_down = remote(lob, rhi, 1, down)
    to_down.start()
    patch_swap = remote(patch_ref, patch_in, 2, mirror)
    meta_swap = remote(meta_ref, meta_in, 3, mirror)
    patch_keep = pltpu.make_async_copy(patch_ref, patch_in, local_sem.at[1])
    meta_keep = pltpu.make_async_copy(meta_ref, meta_in, local_sem.at[2])
    to_up.wait_recv()
    flat[pl.ds(MARGIN - HI, HI), :] = rlo[...].astype(jnp.float32)
    to_down.wait_recv()
    flat[pl.ds(MARGIN + SHARD, LO), :] = rhi[...].astype(jnp.float32)

    first = SLOT * fs
    origin = SHARD * fs - MARGIN
    for index, (base, c, groups, per, start) in enumerate(SECTIONS):
        lo = jnp.maximum(first, start)
        hi = jnp.minimum(first + SLOT, start + c * groups)
        if index == 1:
            lane = lax.broadcasted_iota(jnp.int32, (8, 128), 1)
            g0 = lax.div(jnp.maximum(lo, start) - start, 8)
            g1 = lax.div(jnp.maximum(hi, start) - start + 7, 8)

            def head_group(g, carry):
                row = base + per * g - origin
                for i in range(16):
                    q, s = divmod(1000 * i, 128)
                    one = flat[pl.ds(row + q, 8), :]
                    if s:
                        two = flat[pl.ds(row + q + 1, 8), :]
                        one = jnp.where(lane < 128 - s, pltpu.roll(one, 128 - s, 1), pltpu.roll(two, 128 - s, 1))
                    headrows[pl.ds(i * 8, 8), :] = one
                for j in range(8):
                    t = start + g * 8 + j - first

                    @pl.when(jnp.logical_and(t >= 0, t < SLOT))
                    def _():
                        slot[t] = headrows[pl.ds(j, 16, stride=8), :].astype(jnp.bfloat16)
                return carry

            lax.fori_loop(g0, g1, head_group, 0)
        else:

            def tile(t, carry):
                g = lax.div(t - start, c)
                j = lax.rem(t - start, c)
                row = base + 16 * c * g + j - origin
                slot[t - first] = flat[pl.ds(row, 16, stride=c), :].astype(jnp.bfloat16)
                return carry

            lax.fori_loop(lo, hi, tile, 0)
    pads = jnp.maximum(NTILE - first, 0)

    def blank(t, carry):
        slot[t] = jnp.zeros((16, 128), jnp.bfloat16)
        return carry

    lax.fori_loop(jnp.minimum(pads, SLOT), SLOT, blank, 0)


    def unit_copy(i):
        k = ROUNDS * fs + i
        d = lax.rem(k, 32)
        src = slot.at[pl.ds(UNIT * i, UNIT)]
        dst = T.at[pl.ds(UNIT * k, UNIT)]
        target = device(xo, b, lax.rem(lax.div(d, 4), 2), lax.div(d, 8), lax.rem(d, 4))
        mine = jnp.logical_and(keeps, i == own_index)
        away = pltpu.make_async_remote_copy(src_ref=src, dst_ref=dst, send_sem=u_send.at[i], recv_sem=u_recv.at[lax.div(k, 32)], device_id=target, device_id_type=MESH)
        here = pltpu.make_async_copy(src, dst, local_sem.at[3])
        return mine, away, here

    def send_unit(i, carry):
        mine, away, here = unit_copy(i)

        @pl.when(mine)
        def _():
            here.start()

        @pl.when(jnp.logical_not(mine))
        def _():
            away.start()

        return carry

    lax.fori_loop(0, ROUNDS, send_unit, 0)

    @pl.when(swap)
    def _():
        patch_swap.start()
        meta_swap.start()

    @pl.when(jnp.logical_not(swap))
    def _():
        patch_keep.start()
        meta_keep.start()

    def units_here(i):
        def wait(j, carry):
            place = T.at[pl.ds(UNIT * (32 * j + holder), UNIT)]
            mine = jnp.logical_and(keeps, lax.div(32 * j + holder, ROUNDS) == fs)

            @pl.when(mine)
            def _():
                pltpu.make_async_copy(place, place, local_sem.at[3]).wait()

            @pl.when(jnp.logical_not(mine))
            def _():
                pltpu.make_async_remote_copy(src_ref=place, dst_ref=place, send_sem=u_send.at[0], recv_sem=u_recv.at[j], device_id=links.sibling, device_id_type=MESH).wait_recv()

            return carry

        lax.fori_loop(*STAGES[i], wait, 0)

    def finish_start():
        def wait(i, carry):
            mine, away, here = unit_copy(i)

            @pl.when(jnp.logical_not(mine))
            def _():
                away.wait_send()

            return carry

        lax.fori_loop(0, ROUNDS, wait, 0)
        to_up.wait_send()
        to_down.wait_send()

        @pl.when(swap)
        def _():
            patch_swap.wait()
            meta_swap.wait()

        @pl.when(jnp.logical_not(swap))
        def _():
            patch_keep.wait()
            meta_keep.wait()

    return units_here, finish_start


D = 768
HEADS = 12
HEAD_DIM = 64
FF = 3072
CLS = 1000
P_SIZE = 196
ROWS = 208
TOK = 2 * ROWS
NORM_EPS = 1e-06
SMOOTHING = 0.1
NTILES = 4224
T_E, T_HEAD, T_NORM, T_QKV, T_OUT, T_IN, T_FO = 0, 366, 750, 756, 1620, 1908, 3060
T_POS = 288
BLK = 256
STEP_ROWS = 32
F32 = jnp.float32
BF16 = jnp.bfloat16
ROOT_HALF = 0.7071067811865476
INV_ROOT_TWO_PI = 0.3989422804014327


def dot(x, w):
    return lax.dot_general(x, w, (((1,), (0,)), ((), ())), preferred_element_type=F32)


def dot_t(x, w):
    return lax.dot_general(x, w, (((1,), (1,)), ((), ())), preferred_element_type=F32)


def t_dot(x, w):
    return lax.dot_general(x, w, (((0,), (0,)), ((), ())), preferred_element_type=F32)


def stats(x):
    mean = jnp.sum(x, -1, keepdims=True) * (1.0 / D)
    centred = x - mean
    var = jnp.sum(centred * centred, -1, keepdims=True) * (1.0 / D)
    rstd = lax.rsqrt(var + NORM_EPS)
    return centred * rstd, rstd


def norm_back(d_hat, hat, rstd):
    m1 = jnp.sum(d_hat, -1, keepdims=True) * (1.0 / D)
    m2 = jnp.sum(d_hat * hat, -1, keepdims=True) * (1.0 / D)
    return rstd * (d_hat - m1 - hat * m2)


def compute(step, patch_ref, meta_ref, loss_ref, T, x, h, a, at, mix, prob, o, h1, a2, hid, slope, h2, dh, dyb):
    G = T
    dmix = mix

    def section(ref, start, c, groups):
        return ref.at[pl.ds(start, groups * c)].reshape(groups, c, 16, 128)

    def cols(start, c, groups, j):
        part = section(T, start, c, groups)
        return jnp.concatenate([part[:, 2 * j + k].reshape(groups * 16, 128) for k in range(2)], axis=1)

    def put_cols(start, c, groups, j, value):
        low = value.astype(BF16)
        part = section(G, start, c, groups)
        for k in range(2):
            part[:, 2 * j + k] = low[:, k * 128 : (k + 1) * 128].reshape(groups, 16, 128)

    def row_of(start, k):
        return jnp.concatenate([T[start + j][k : k + 1, :] for j in range(6)], axis=1).astype(F32)

    def lanes(j):
        return pl.ds(pl.multiple_of(j * BLK, BLK), BLK)

    def rows(i):
        return pl.ds(pl.multiple_of(i * STEP_ROWS, STEP_ROWS), STEP_ROWS)

    steps = TOK // STEP_ROWS
    step("start")
    for i in range(2):
        x[pl.ds(i * ROWS, 192), :] = patch_ref[i, pl.ds(0, 192), :]
        x[pl.ds(i * ROWS + 192, 16), :] = jnp.concatenate([patch_ref[i, pl.ds(192, 4), :], jnp.zeros((12, D), BF16)], axis=0)

    real = lax.broadcasted_iota(jnp.int32, (ROWS, 128), 0) < P_SIZE
    for j in range(3):
        acc = dot(x[...], cols(T_E, 6, 48, j))
        p = cols(T_POS, 6, 13, j).astype(F32)
        p = jnp.where(lax.broadcasted_iota(jnp.int32, (ROWS, BLK), 0) < P_SIZE, p, 0.0)
        for i in range(2):
            h[pl.ds(i * ROWS, ROWS), pl.ds(j * BLK, BLK)] = acc[i * ROWS : (i + 1) * ROWS] + p

    step("embedded")
    gain1, shift1, gain2, shift2 = (row_of(T_NORM, k) for k in range(4))

    def norm_one(i, carry):
        hat, unused = stats(h[rows(i), :])
        a[rows(i), :] = (hat * gain1 + shift1).astype(BF16)
        return carry

    lax.fori_loop(0, steps, norm_one, 0)

    step("qkv")
    def mix_block(j, carry):
        mix[:, lanes(j)] = dot(a[...], cols(T_QKV, 18, 48, j)).astype(BF16)
        return carry

    lax.fori_loop(0, 9, mix_block, 0)

    first_half = lax.broadcasted_iota(jnp.int32, (ROWS, 128), 1) < HEAD_DIM
    key_ok = lax.broadcasted_iota(jnp.int32, (ROWS, ROWS), 1) < P_SIZE
    zero = jnp.zeros((ROWS, 128), BF16)

    def qkv_of(n):
        i = lax.div(n, 6)
        p = lax.rem(n, 6)
        r = pl.ds(pl.multiple_of(i * ROWS, ROWS), ROWS)
        ls = [pl.ds(pl.multiple_of(p * 128 + D * k, 128), 128) for k in range(3)]
        return r, ls

    def attend(n, carry):
        r, ls = qkv_of(n)
        q, k, v = (mix[r, l] for l in ls)
        q = q * jnp.asarray(0.125, BF16)
        outs = []
        for e in range(2):
            mask = first_half if e == 0 else jnp.logical_not(first_half)
            s = dot_t(jnp.where(mask, q, zero), k)
            s = jnp.where(key_ok, s, -jnp.inf)
            top = jnp.max(s, -1, keepdims=True)
            ex = jnp.exp(s - top)
            pr = (ex / jnp.sum(ex, -1, keepdims=True)).astype(BF16)
            prob[n * 2 + e] = pr
            outs.append(dot(pr, v))
        o[r, ls[0]] = jnp.where(first_half, outs[0], outs[1]).astype(BF16)
        return carry

    for part in range(4):
        step("attend%d" % part)
        lax.fori_loop(3 * part, 3 * part + 3, attend, 0)
    step("attended")
    for j in range(3):
        h1[:, pl.ds(j * BLK, BLK)] = h[:, pl.ds(j * BLK, BLK)] + dot(o[...], cols(T_OUT, 6, 48, j))

    def norm_two(i, carry):
        hat, unused = stats(h1[rows(i), :])
        a2[rows(i), :] = (hat * gain2 + shift2).astype(BF16)
        return carry

    lax.fori_loop(0, steps, norm_two, 0)

    step("up")
    def up_block(j, carry):
        u = dot(a2[...], cols(T_IN, 24, 48, j))
        phi = 0.5 * (1.0 + lax.erf(u * ROOT_HALF))
        pdf = jnp.exp(-0.5 * u * u) * INV_ROOT_TWO_PI
        hid[:, lanes(j)] = (u * phi).astype(BF16)
        slope[:, lanes(j)] = (phi + u * pdf).astype(BF16)
        return carry

    lax.fori_loop(0, 12, up_block, 0)
    step("down")
    for j in range(3):
        h2[:, pl.ds(j * BLK, BLK)] = h1[:, pl.ds(j * BLK, BLK)] + dot(hid[...], cols(T_FO, 6, 192, j))

    step("pool")
    gain_end, shift_end = (row_of(T_POS + 72, 4 + k) for k in range(2))
    means = []
    for i in range(2):

        def pool_step(n, carry):
            hat, unused = stats(h2[pl.ds(pl.multiple_of(i * ROWS + n * 16, 16), 16), :])
            ok = lax.broadcasted_iota(jnp.int32, (16, D), 0) + n * 16 < P_SIZE
            hat = jnp.where(ok, hat, 0.0)
            return carry + hat[:8] + hat[8:]

        total = lax.fori_loop(0, 13, pool_step, jnp.zeros((8, D), F32))
        means.append(jnp.sum(total, 0, keepdims=True) * (1.0 / P_SIZE))
    mean_hat = jnp.concatenate(means + [jnp.zeros((14, D), F32)], axis=0)
    two = lax.broadcasted_iota(jnp.int32, (16, D), 0) < 2
    pooled = jnp.where(two, mean_hat * gain_end + shift_end, 0.0).astype(BF16)
    logits = jnp.concatenate([dot(pooled, cols(T_HEAD, 8, 48, j)) for j in range(4)], axis=1)
    lane = lax.broadcasted_iota(jnp.int32, (16, 1024), 1)
    lane_f = lane.astype(F32)
    inside = lane < CLS
    logits = jnp.where(inside, logits, -1e30)
    top = jnp.max(logits, -1, keepdims=True)
    total = jnp.sum(jnp.where(inside, jnp.exp(logits - top), 0.0), -1, keepdims=True)
    logp = logits - top - jnp.log(total)
    meta = meta_ref[...]
    pad14 = jnp.zeros((14, 1), F32)
    label = jnp.concatenate([meta[0:2, 0:1], pad14], axis=0)
    scale = jnp.concatenate([meta[2:4, 0:1], pad14], axis=0)
    valid = jnp.concatenate([meta[4:6, 0:1], pad14], axis=0)
    target = jnp.where(lane_f == label, 1.0 - SMOOTHING, 0.0) + SMOOTHING / CLS
    values = -jnp.sum(jnp.where(inside, target * logp, 0.0), -1, keepdims=True)
    loss_ref[...] = jnp.broadcast_to(jnp.sum(values * valid, 0, keepdims=True), (8, 128))
    d_logits = jnp.where(inside, scale * (jnp.exp(logp) - target), 0.0).astype(BF16)
    d_pooled = jnp.zeros((16, D), F32)
    for j in range(4):
        w = cols(T_HEAD, 8, 48, j)
        d_pooled = d_pooled + dot_t(d_logits[:, j * BLK : (j + 1) * BLK], w)
        put_cols(T_HEAD, 8, 48, j, t_dot(pooled, d_logits[:, j * BLK : (j + 1) * BLK]))
    d_gain_end = jnp.sum(d_pooled * mean_hat, 0, keepdims=True)
    d_shift_end = jnp.sum(d_pooled, 0, keepdims=True)
    for i in range(2):
        d_hat = d_pooled[i : i + 1, :] * (1.0 / P_SIZE) * gain_end

        def end_step(n, carry):
            r = pl.ds(pl.multiple_of(i * ROWS + n * 16, 16), 16)
            hat, rstd = stats(h2[r, :])
            ok = lax.broadcasted_iota(jnp.int32, (16, D), 0) + n * 16 < P_SIZE
            d = jnp.where(ok, norm_back(jnp.broadcast_to(d_hat, (16, D)), hat, rstd), 0.0)
            dh[r, :] = d
            dyb[r, :] = d.astype(BF16)
            return carry

        lax.fori_loop(0, 13, end_step, 0)

    step("backward")
    at[...] = a2[...].T
    da = h2

    def down_block(j, carry):
        dy = dyb[...]
        d_w = t_dot(hid[:, lanes(j)], dy).astype(BF16)
        part = section(T, T_FO + j * 96, 6, 16)
        w = jnp.concatenate([part[:, k].reshape(BLK, 128) for k in range(6)], axis=1)
        hid[:, lanes(j)] = (dot_t(dy, w) * slope[:, lanes(j)].astype(F32)).astype(BF16)
        for k in range(6):
            part[:, k] = d_w[:, k * 128 : (k + 1) * 128].reshape(16, 16, 128)
        return carry

    G[pl.ds(4212, 12)] = jnp.zeros((12, 16, 128), BF16)
    lax.fori_loop(0, 8, down_block, 0)
    step("fc_out0")
    lax.fori_loop(8, 12, down_block, 0)
    step("fc_out1")
    da[...] = jnp.zeros((TOK, D), F32)

    def up_back(j, carry):
        d_u = hid[:, lanes(j)]
        da[...] += dot_t(d_u, cols(T_IN, 24, 48, j))
        put_cols(T_IN, 24, 48, j, dot(at[...], d_u))
        return carry

    for part in range(4):
        lax.fori_loop(3 * part, 3 * part + 3, up_back, 0)
        step("fc_in%d" % part)

    def back_two(i, carry):
        dg, ds = carry
        hat, rstd = stats(h1[rows(i), :])
        d = da[rows(i), :]
        new = dh[rows(i), :] + norm_back(d * gain2, hat, rstd)
        dh[rows(i), :] = new
        dyb[rows(i), :] = new.astype(BF16)
        return dg + jnp.sum((d * hat).reshape(4, 8, D), 0), ds + jnp.sum(d.reshape(4, 8, D), 0)

    none = jnp.zeros((8, D), F32)
    d_gain2, d_shift2 = lax.fori_loop(0, steps, back_two, (none, none))

    step("normed2")
    at[...] = o[...].T
    da[...] = jnp.zeros((TOK, D), F32)
    for j in range(3):
        dz = dyb[:, pl.ds(j * BLK, BLK)]
        da[...] += dot_t(dz, cols(T_OUT, 6, 48, j))
        put_cols(T_OUT, 6, 48, j, dot(at[...], dz))
    o[...] = da[...].astype(BF16)

    step("out")
    def attend_back(n, carry):
        r, ls = qkv_of(n)
        q, k, v = (mix[r, l] for l in ls)
        q = q * jnp.asarray(0.125, BF16)
        k8 = k * jnp.asarray(0.125, BF16)
        do = o[r, ls[0]]
        dq, dk, dv = [], [], []
        for e in range(2):
            mask = first_half if e == 0 else jnp.logical_not(first_half)
            pr = prob[n * 2 + e]
            dv.append(t_dot(pr, do))
            dp = dot_t(jnp.where(mask, do, zero), v)
            prf = pr.astype(F32)
            row = jnp.sum(prf * dp, -1, keepdims=True)
            ds = (prf * (dp - row)).astype(BF16)
            dq.append(dot(ds, k8))
            dk.append(t_dot(ds, q))
        for l, pair in zip(ls, (dq, dk, dv)):
            dmix[r, l] = jnp.where(first_half, pair[0], pair[1]).astype(BF16)
        return carry

    for part in range(4):
        lax.fori_loop(3 * part, 3 * part + 3, attend_back, 0)
        step("back%d" % part)

    at[...] = a[...].T
    da[...] = jnp.zeros((TOK, D), F32)

    def qkv_block(j, carry):
        d = dmix[:, lanes(j)]
        da[...] += dot_t(d, cols(T_QKV, 18, 48, j))
        put_cols(T_QKV, 18, 48, j, dot(at[...], d))
        return carry

    lax.fori_loop(0, 9, qkv_block, 0)

    step("qkv_back")
    def back_one(i, carry):
        dg, ds = carry
        hat, rstd = stats(h[rows(i), :])
        d = da[rows(i), :]
        new = dh[rows(i), :] + norm_back(d * gain1, hat, rstd)
        dh[rows(i), :] = new
        dyb[rows(i), :] = new.astype(BF16)
        return dg + jnp.sum((d * hat).reshape(4, 8, D), 0), ds + jnp.sum(d.reshape(4, 8, D), 0)

    d_gain1, d_shift1 = lax.fori_loop(0, steps, back_one, (none, none))
    d_norms = jnp.concatenate([jnp.sum(d, 0, keepdims=True) for d in (d_gain1, d_shift1, d_gain2, d_shift2)] + [jnp.zeros((12, D), F32)], axis=0).astype(BF16)
    for j in range(6):
        G[T_NORM + j] = d_norms[:, j * 128 : (j + 1) * 128]
    step("norms")
    at[...] = x[...].T
    row_id = lax.broadcasted_iota(jnp.int32, (ROWS, BLK), 0)
    for j in range(3):
        put_cols(T_E, 6, 48, j, dot(at[...], dyb[:, pl.ds(j * BLK, BLK)]))
        c = pl.ds(j * BLK, BLK)
        s = slice(j * BLK, (j + 1) * BLK)
        d_pos = dh[pl.ds(0, ROWS), c] + dh[pl.ds(ROWS, ROWS), c]
        d_pos = jnp.where(row_id < P_SIZE, d_pos, 0.0)
        d_pos = jnp.where(row_id == P_SIZE, jnp.broadcast_to(d_gain_end[:, s], (ROWS, BLK)), d_pos)
        d_pos = jnp.where(row_id == P_SIZE + 1, jnp.broadcast_to(d_shift_end[:, s], (ROWS, BLK)), d_pos)
        put_cols(T_POS, 6, 13, j, d_pos)
    step("embed")


FORWARD = {
    "start": ((0, 0), (1, 0), (0, 1), (0, 2), (1, 1), (2, 0), (0, 3), (1, 2), (0, 4), (2, 1), (3, 0), (0, 5)),
    "embedded": ((1, 3), (2, 2), (3, 1)),
    "qkv": ((1, 4), (1, 5), (3, 2)),
    "attend0": ((2, 3),),
    "attend1": ((3, 3), (2, 4)),
    "attend2": ((3, 4),),
    "up": ((2, 5),),
    "down": ((3, 5),),
}
BACKWARD = {
    "fc_out0": ((3, 0, 0),),
    "fc_out1": ((3, 1, 0), (3, 0, 1)),
    "fc_in0": ((3, 1, 1),),
    "fc_in1": ((3, 0, 2),),
    "fc_in2": ((3, 1, 2), (3, 0, 3)),
    "fc_in3": ((2, 0, 0), (2, 1, 0), (3, 1, 3)),
    "normed2": ((3, 0, 4), (3, 1, 4), (2, 0, 1)),
    "out": ((2, 1, 1), (3, 0, 5)),
    "back0": ((2, 0, 2), (2, 1, 2), (3, 1, 5)),
    "back1": ((2, 0, 3), (2, 1, 3)),
    "back2": ((2, 0, 4), (2, 1, 4)),
    "back3": ((2, 0, 5), (2, 1, 5)),
    "qkv_back": ((1, 0, 0), (1, 1, 0)),
    "norms": ((0, 1, 0), (1, 0, 1), (1, 1, 1)),
    "embed": ((0, 0, 0), (0, 1, 1), (1, 0, 2), (1, 1, 2), (0, 0, 1), (1, 0, 3), (1, 1, 3), (0, 1, 2), (0, 0, 2), (1, 0, 4), (1, 1, 4), (0, 1, 3), (0, 0, 3), (1, 0, 5), (1, 1, 5), (0, 1, 4), (0, 0, 4), (0, 1, 5), (0, 0, 5)),
}


def grads_kernel(w_ref, patch_ref, meta_ref, red_ref, loss_out, T, R, RA, RB, g_send, g_recv, r_send, r_recv, LS, l_send, l_recv, patch_in, meta_in, loss, *rest):
    gather_refs, compute_refs, out_sem = rest[:12], rest[12:-1], rest[-1]
    links = Links(T, R, RA, RB, g_send, g_recv, r_send, r_recv)
    xl, b, z, a, y = links.xl, links.b, links.z, links.a, links.y
    swap = a != b
    mirror = device(xl, b, a, z, y)
    units_here, finish_start = start_gather(links, w_ref, patch_ref, meta_ref, T, patch_in, meta_in, *gather_refs)

    def loss_send(src, dst, target):
        links.go(LS.at[src], LS.at[dst], l_send.at[dst], l_recv.at[dst], target)

    def loss_wait(*slots):
        for k in slots:
            links.landed(LS.at[k], l_send.at[k], l_recv.at[k])

    def loss_step(n):
        if n == 0:
            LS[0] = loss[...]
            loss_send(0, 1, links.sibling)
        elif n == 1:
            loss_wait(1)
            LS[8] = LS[0] + LS[1]
            loss_send(8, 2, links.at_y(1))
            loss_send(8, 3, links.at_y(3))
        elif n == 2:
            loss_wait(2, 3)
            loss_send(2, 4, links.at_y(1))
        elif n == 3:
            loss_wait(4)
            LS[9] = (LS[8] + LS[4]) + (LS[2] + LS[3])
            loss_send(9, 5, links.at_z(1))
            loss_send(9, 6, links.at_z(3))
        elif n == 4:
            loss_wait(5, 6)
            loss_send(5, 7, links.at_z(1))
        elif n == 5:
            loss_wait(7)
            LS[10] = (LS[9] + LS[7]) + (LS[5] + LS[6])

            @pl.when(swap)
            def _():
                loss_swap.start()

        else:

            @pl.when(swap)
            def _():
                loss_swap.wait()
                loss_out[...] = LS[11]

            @pl.when(jnp.logical_not(swap))
            def _():
                loss_out[...] = LS[10]

    loss_swap = pltpu.make_async_remote_copy(src_ref=LS.at[10], dst_ref=LS.at[11], send_sem=l_send.at[11], recv_sem=l_recv.at[11], device_id=mirror, device_id_type=MESH)
    losses = {"fc_out0": 0, "fc_in0": 1, "fc_in2": 2, "normed2": 3, "back0": 4, "back2": 5, "qkv_back": 6}

    def step(name):
        if name == "pool":
            links.sent()
        for item in FORWARD.get(name, ()):
            if item[1] == 0:
                units_here(item[0])
            links.gather_step(*item)
        if name == "start":
            finish_start()
        for item in BACKWARD.get(name, ()):
            links.reduce_step(*item)
        if name in losses:
            loss_step(losses[name])

    compute(step, patch_in, meta_in, loss, T, *compute_refs)
    mine = T.reshape(ROUNDS, 32, UNIT, 16, 128).at[:, z * 8 + b * 4 + y]
    out = pltpu.make_async_copy(mine, red_ref, out_sem)
    out.start()
    links.sent()
    out.wait()


def grads(weights, patches, meta):
    hbm = pl.BlockSpec(memory_space=pl.ANY)
    vmem = pl.BlockSpec(memory_space=pltpu.VMEM)
    V = pltpu.VMEM
    dma = pltpu.SemaphoreType.DMA
    return pl.pallas_call(
        grads_kernel,
        out_shape=(jax.ShapeDtypeStruct((ROUNDS, UNIT, 16, 128), BF16), jax.ShapeDtypeStruct((8, 128), F32)),
        in_specs=[hbm] * 3,
        out_specs=(hbm, vmem),
        scratch_shapes=[
            V((NTILES, 16, 128), BF16),
            V((ROUNDS, 4, 4, UNIT, 16, 128), BF16),
            V((6, ROUNDS, 2, UNIT, 16, 128), BF16),
            V((6, ROUNDS, 3, 16, 128), BF16),
            dma((96,)),
            dma((96,)),
            dma((104,)),
            dma((104,)),
            V((12, 8, 128), F32),
            dma((12,)),
            dma((12,)),
            V(patches.shape, BF16),
            V((8, 128), F32),
            V((8, 128), F32),
            V((FROWS, 128), F32),
            V((128, 128), F32),
            V((LO, 128), BF16),
            V((HI, 128), BF16),
            V((HI, 128), BF16),
            V((LO, 128), BF16),
            V((SLOT, 16, 128), BF16),
            dma((4,)),
            dma((4,)),
            dma((4,)),
            dma((ROUNDS,)),
            dma((ROUNDS,)),
            V((TOK, D), BF16),
            V((TOK, D), F32),
            V((TOK, D), BF16),
            V((D, TOK), BF16),
            V((TOK, 3 * D), BF16),
            V((24, ROWS, ROWS), BF16),
            V((TOK, D), BF16),
            V((TOK, D), F32),
            V((TOK, D), BF16),
            V((TOK, FF), BF16),
            V((TOK, FF), BF16),
            V((TOK, D), F32),
            V((TOK, D), F32),
            V((TOK, D), BF16),
            dma,
        ],
        compiler_params=pltpu.CompilerParams(collective_id=0, has_side_effects=True, vmem_limit_bytes=60 * 1024 * 1024),
        name="grads",
    )(weights, patches, meta)


EDGE = 24
FRONT = 768
BACK_ROWS = FRONT + SHARD + 640 + 6
PADDED = 2112
STEP = 10
EDGE_UNITS = 4
WINDOW = ROUNDS + 2 * EDGE_UNITS
BETA_ONE = 0.9
BETA_TWO = 0.95
ADAM_EPS = 1e-08
DECAY = 0.05
INNER_RATE = 0.01
OUTER_RATE = 0.7
OUTER_MU = 0.9


def update_kernel(
    red_ref, w_ref, first_ref, second_ref, mom_ref,
    avg_out, mom_out, new_out, first_out, second_out,
    red, window, flat, headrows, w, first, second, mom, upd, low, low2, pair, pair2, total, total2,
    load_sem, x_send, x_recv, o_send, e_send, w_recv,
):
    xl, b, z, a, y = coords()
    fs = z * 8 + a * 4 + y
    holder = z * 8 + b * 4 + y
    sibling = device(xl, a, 1 - b, z, y)
    across = device(1 - xl, a, b, z, y)
    extra = [pltpu.make_async_copy(src, dst, load_sem.at[i]) for i, (src, dst) in enumerate(((w_ref, w), (first_ref, first), (second_ref, second), (mom_ref, mom)))]
    load = pltpu.make_async_copy(red_ref, red, load_sem.at[4])
    load.start()
    for copy in extra:
        copy.start()

    barrier = pltpu.get_barrier_semaphore()

    def greet(target):
        pl.semaphore_signal(barrier, inc=1, device_id=target, device_id_type=MESH)

    greet(sibling)
    greet(across)
    first_unit = ROUNDS * fs - EDGE_UNITS

    def window_unit(p):
        k = first_unit + p
        d = lax.rem(k + 32, 32)
        inside = jnp.logical_and(k >= 0, k < 32 * ROUNDS)
        mine = jnp.logical_and(a == b, d == holder)
        return inside, mine, device(xl, b, lax.rem(lax.div(d, 4), 2), lax.div(d, 8), lax.rem(d, 4))

    def greet_holder(p, carry):
        inside, mine, source = window_unit(p)

        @pl.when(jnp.logical_and(inside, jnp.logical_not(mine)))
        def _():
            greet(source)

        return carry

    lax.fori_loop(0, WINDOW, greet_holder, 0)

    def held_unit(j):
        k = 32 * j + holder
        q = lax.div(k, ROUNDS)
        r = lax.rem(k, ROUNDS)
        shift = jnp.where(r < EDGE_UNITS, -1, jnp.where(r >= ROUNDS - EDGE_UNITS, 1, 0))
        near = jnp.logical_and(shift != 0, jnp.logical_and(q + shift >= 0, q + shift < NSLOT))
        return k, q, jnp.where(near, q + shift, q), near

    def to_owner(j, k, s, send):
        p = k - (ROUNDS * s - EDGE_UNITS)
        src = red.at[j]
        dst = window.at[pl.ds(UNIT * p, UNIT)]
        sa = lax.rem(lax.div(s, 4), 2)
        mine = jnp.logical_and(a == b, s == fs)
        target = device(xl, sa, a, lax.div(s, 8), lax.rem(s, 4))
        away = pltpu.make_async_remote_copy(src_ref=src, dst_ref=dst, send_sem=send.at[j], recv_sem=w_recv.at[p], device_id=target, device_id_type=MESH)
        here = pltpu.make_async_copy(src, dst, load_sem.at[10])
        return mine, away, here

    def count(j, n):
        k, q, s, near = held_unit(j)
        first_away = jnp.logical_not(jnp.logical_and(a == b, q == fs))
        second_away = jnp.logical_and(near, jnp.logical_not(jnp.logical_and(a == b, s == fs)))
        return n + jnp.where(first_away, 1, 0) + jnp.where(second_away, 1, 0)

    outgoing = lax.fori_loop(0, ROUNDS, count, 2)
    pl.semaphore_wait(barrier, outgoing)
    load.wait()

    def give(j, carry):
        k, q, s, near = held_unit(j)
        mine, away, here = to_owner(j, k, q, o_send)

        @pl.when(mine)
        def _():
            here.start()

        @pl.when(jnp.logical_not(mine))
        def _():
            away.start()

        mine2, away2, here2 = to_owner(j, k, s, e_send)

        @pl.when(jnp.logical_and(near, mine2))
        def _():
            here2.start()

        @pl.when(jnp.logical_and(near, jnp.logical_not(mine2)))
        def _():
            away2.start()

        return carry

    lax.fori_loop(0, ROUNDS, give, 0)

    def given(j, carry):
        k, q, s, near = held_unit(j)
        mine, away, here = to_owner(j, k, q, o_send)

        @pl.when(jnp.logical_not(mine))
        def _():
            away.wait_send()

        mine2, away2, here2 = to_owner(j, k, s, e_send)

        @pl.when(jnp.logical_and(near, jnp.logical_not(mine2)))
        def _():
            away2.wait_send()

        return carry

    def clear(i, carry):
        flat[pl.ds(pl.multiple_of(i * 32, 32), 32), :] = jnp.zeros((32, 128), F32)
        return carry

    lax.fori_loop(0, BACK_ROWS // 32, clear, 0)

    def got(p, carry):
        inside, mine, source = window_unit(p)
        place = window.at[pl.ds(UNIT * p, UNIT)]

        @pl.when(jnp.logical_and(inside, mine))
        def _():
            pltpu.make_async_copy(place, place, load_sem.at[10]).wait()

        @pl.when(jnp.logical_and(inside, jnp.logical_not(mine)))
        def _():
            pltpu.make_async_remote_copy(src_ref=place, dst_ref=place, send_sem=x_send.at[0], recv_sem=w_recv.at[p], device_id=sibling, device_id_type=MESH).wait_recv()

        return carry

    lax.fori_loop(0, WINDOW, got, 0)
    for copy in extra:
        copy.wait()
    sends = []

    def go(src, dst, send, recv, k, target):
        copy = pltpu.make_async_remote_copy(src_ref=src, dst_ref=dst, send_sem=send.at[k], recv_sem=recv.at[k], device_id=target, device_id_type=MESH)
        copy.start()
        sends.append(copy)

    def arrive(dst, recv, k):
        pltpu.make_async_remote_copy(src_ref=dst, dst_ref=dst, send_sem=x_send.at[k], recv_sem=recv.at[k], device_id=sibling, device_id_type=MESH).wait_recv()

    low_tile = SLOT * fs - EDGE
    high_tile = SLOT * fs + SLOT + EDGE
    origin = SHARD * fs - FRONT
    for index, (base, c, groups, per, start) in enumerate(SECTIONS):
        if index == 1:
            lane = lax.broadcasted_iota(jnp.int32, (8, 128), 1)
            g0 = lax.div(jnp.maximum(SHARD * fs - base, 0), per)
            g1 = lax.div(jnp.maximum(SHARD * (fs + 1) - base, 0) + per - 1, per)

            def head_group(g, carry):
                t = start + g * 8 - low_tile
                for j in range(8):
                    headrows[pl.ds(j, 16, stride=8), :] = window[t + j].astype(F32)
                row = base + per * g - origin
                for i in range(16):
                    q, s = divmod(1000 * i, 128)
                    value = headrows[pl.ds(i * 8, 8), :]
                    if s:
                        value = pltpu.roll(value, s, 1)
                        flat[pl.ds(row + q, 8), :] += jnp.where(lane >= s, value, 0.0)
                        flat[pl.ds(row + q + 1, 8), :] += jnp.where(lane < s, value, 0.0)
                    else:
                        flat[pl.ds(row + q, 8), :] += value
                return carry

            lax.fori_loop(jnp.minimum(g0, groups), jnp.minimum(g1, groups), head_group, 0)
        else:

            def tile(t, carry):
                g = lax.div(t - start, c)
                j = lax.rem(t - start, c)
                flat[pl.ds(base + 16 * c * g + j - origin, 16, stride=c), :] = window[t - low_tile].astype(F32)
                return carry

            lax.fori_loop(jnp.maximum(low_tile, start), jnp.minimum(high_tile, start + c * groups), tile, 0)

    fix_one = 1.0 / (1.0 - BETA_ONE**STEP)
    fix_two = 1.0 / (1.0 - BETA_TWO**STEP)

    def in_rows(fn, lo, hi, step=32):
        def body(i, carry):
            fn(pl.multiple_of(i * step, step), step)
            return carry

        n = (hi - lo) // step
        lax.fori_loop(lo // step, lo // step + n, body, 0)
        if lo + n * step < hi:
            fn(lo + n * step, hi - lo - n * step)

    def adam(r, n):
        grad = flat[pl.ds(FRONT + r, n), :]
        m = BETA_ONE * first[pl.ds(r, n), :] + (1.0 - BETA_ONE) * grad
        s = BETA_TWO * second[pl.ds(r, n), :] + (1.0 - BETA_TWO) * grad * grad
        first[pl.ds(r, n), :] = m
        second[pl.ds(r, n), :] = s
        u = (m * fix_one) / (jnp.sqrt(s * fix_two) + ADAM_EPS)
        upd[pl.ds(r, n), :] = u

    in_rows(adam, 0, SHARD)
    upd[pl.ds(SHARD, PADDED - SHARD), :] = jnp.zeros((PADDED - SHARD, 128), F32)
    outs = [pltpu.make_async_copy(src, dst, load_sem.at[5 + i]) for i, (src, dst) in enumerate(((first, first_out), (second, second_out)))]
    for copy in outs:
        copy.start()

    def lower(r, n):
        low[pl.ds(r, n), :] = upd[pl.ds(r, n), :].astype(BF16)

    in_rows(lower, 0, PADDED)
    go(low, low2, x_send, x_recv, 0, sibling)
    arrive(low2, x_recv, 0)
    half = PADDED // 2

    def pairs(r, n):
        at = pl.ds(pl.multiple_of(b * half + r, 16), n)
        pair[pl.ds(r, n), :] = low[at, :] + low2[at, :]

    in_rows(pairs, 0, half)
    go(pair, pair2, x_send, x_recv, 1, across)
    arrive(pair2, x_recv, 1)

    def fours(r, n):
        total[pl.ds(r, n), :] = pair[pl.ds(r, n), :].astype(F32) + pair2[pl.ds(r, n), :].astype(F32)

    in_rows(fours, 0, half)
    go(total, total2, x_send, x_recv, 2, sibling)

    def outer(source, shift):
        def rows_of(r, n):
            at = pl.ds(shift + r, n)
            t = source[pl.ds(r, n), :]
            old = w[at, :]
            averaged = INNER_RATE * (t * 0.25 + DECAY * old)
            momentum = OUTER_MU * mom[at, :] + averaged
            upd[at, :] = averaged
            mom[at, :] = momentum
            w[at, :] = old - OUTER_RATE * (averaged + OUTER_MU * momentum)

        return rows_of

    def both(here, there):
        in_rows(outer(here, 0), 0, half)
        in_rows(outer(there, half), 0, SHARD - half)

    arrive(total2, x_recv, 2)

    @pl.when(b == 0)
    def _():
        both(total, total2)

    @pl.when(b == 1)
    def _():
        both(total2, total)

    final = [(upd.at[pl.ds(0, SHARD)], avg_out), (mom, mom_out), (w, new_out)]
    final = [pltpu.make_async_copy(src, dst, load_sem.at[7 + i]) for i, (src, dst) in enumerate(final)]
    for copy in final:
        copy.start()
    for copy in sends:
        copy.wait_send()
    lax.fori_loop(0, ROUNDS, given, 0)
    for copy in outs + final:
        copy.wait()


def update(red, weights, first, second, momentum):
    hbm = pl.BlockSpec(memory_space=pl.ANY)
    V = pltpu.VMEM
    flat = jax.ShapeDtypeStruct((SHARD, 128), F32)
    dma = pltpu.SemaphoreType.DMA
    return pl.pallas_call(
        update_kernel,
        out_shape=(flat,) * 5,
        in_specs=[hbm] * 5,
        out_specs=(hbm,) * 5,
        scratch_shapes=[
            V((ROUNDS, UNIT, 16, 128), BF16),
            V((EDGE + SLOT + EDGE, 16, 128), BF16),
            V((BACK_ROWS, 128), F32),
            V((128, 128), F32),
            V((SHARD, 128), F32),
            V((SHARD, 128), F32),
            V((SHARD, 128), F32),
            V((SHARD, 128), F32),
            V((PADDED, 128), F32),
            V((PADDED, 128), BF16),
            V((PADDED, 128), BF16),
            V((PADDED // 2, 128), BF16),
            V((PADDED // 2, 128), BF16),
            V((PADDED // 2, 128), F32),
            V((PADDED // 2, 128), F32),
            dma((11,)),
            dma((3,)),
            dma((3,)),
            dma((ROUNDS,)),
            dma((ROUNDS,)),
            dma((WINDOW,)),
        ],
        compiler_params=pltpu.CompilerParams(collective_id=1, has_side_effects=True, vmem_limit_bytes=60 * 1024 * 1024),
        name="update",
    )(red, weights, first, second, momentum)


def move_kernel(*refs):
    one, two, out_one, out_two, buf_one, buf_two, sem = refs

    def rows(ref):
        return ref.reshape(SHARD, 128) if ref.shape[0] == 1 else ref

    ins = [pltpu.make_async_copy(rows(src), dst, sem.at[i]) for i, (src, dst) in enumerate(((one, buf_one), (two, buf_two)))]
    outs = [pltpu.make_async_copy(src, rows(dst), sem.at[2 + i]) for i, (src, dst) in enumerate(((buf_one, out_one), (buf_two, out_two)))]
    for copy in ins:
        copy.start()
    for i in range(2):
        ins[i].wait()
        outs[i].start()
    for copy in outs:
        copy.wait()


def move(one, two, shape, name):
    hbm = pl.BlockSpec(memory_space=pl.ANY)
    shape = jax.ShapeDtypeStruct(shape, F32)
    rows = pltpu.VMEM((SHARD, 128), F32)
    return pl.pallas_call(
        move_kernel,
        out_shape=(shape,) * 2,
        in_specs=[hbm] * 2,
        out_specs=(hbm,) * 2,
        scratch_shapes=[rows, rows, pltpu.SemaphoreType.DMA((4,))],
        compiler_params=pltpu.CompilerParams(vmem_limit_bytes=60 * 1024 * 1024),
        name=name,
    )(one, two)


def body(patches, labels, counts, weights, first_moments, second_moments, outer_momentum):
    rank = lax.axis_index("fsdp")
    total_count = jnp.sum(counts[0, 0]).astype(jnp.float32)
    valid = (rank < counts[0, 0]).astype(jnp.float32)
    fields = jnp.concatenate([labels[0, 0, :, 0].astype(jnp.float32), valid / total_count, valid, jnp.zeros((2,), jnp.float32)])
    meta = jnp.broadcast_to(fields[:, None], (8, 128))
    flat = weights.reshape(SHARD, 128)
    first, second = move(first_moments, second_moments, (SHARD, 128), "as_rows")
    reduced, losses = grads(flat, patches.reshape(2, P_SIZE, D), meta)
    averaged, momentum, new_weights, first, second = update(reduced, flat, first, second, outer_momentum.reshape(SHARD, 128))
    first, second = move(first, second, (1, SHARD * 128), "as_flat")
    return (
        averaged.reshape(-1),
        momentum.reshape(-1),
        new_weights.reshape(-1),
        first,
        second,
        losses[:1, :1],
    )


def solution(mesh):
    placed = (
        P("rep", None, None, "fsdp", None, None),
        P("rep", None, None, "fsdp"),
        P("rep", None, None),
        P("fsdp"),
        P("rep", "fsdp"),
        P("rep", "fsdp"),
        P("fsdp"),
    )
    return jax.shard_map(
        body,
        mesh=mesh,
        in_specs=placed,
        out_specs=(
            P("fsdp"),
            P("fsdp"),
            P("fsdp"),
            P("rep", "fsdp"),
            P("rep", "fsdp"),
            P("rep", None),
        ),
        check_vma=False,
    )
```

```python
from functools import partial

import jax
import jax.numpy as jnp
from jax import lax
from jax.experimental import pallas as pl
from jax.experimental.pallas import tpu as pltpu
from jax.sharding import PartitionSpec as P

SHARD = 2098
SLOT = 132
HALF = 66
QUART = 33
NSLOT = 32
ROUNDS = 22
UNIT = 6
STAGES = ((0, 4), (4, 10), (10, 16), (16, 22))
SECTIONS = []
_t = 0
for _base, _c, _g, _rpg in ((0, 6, 61, 96), (5796, 8, 48, 125), (11796, 6, 1, 96), (11820, 18, 48, 288), (25644, 6, 48, 96), (30252, 24, 48, 384), (48684, 6, 192, 96)):
    SECTIONS.append((_base, _c, _g, _rpg, _t))
    _t += _c * _g
NTILE = _t
HI = 352
LO = 224
MARGIN = 512
FROWS = 3072
HEAD_ROWS = 16
MESH = pl.DeviceIdType.MESH


def coords():
    rep = lax.axis_index("rep")
    fs = lax.axis_index("fsdp")
    return lax.div(rep, 2), lax.rem(rep, 2), lax.div(fs, 8), lax.rem(lax.div(fs, 4), 2), lax.rem(fs, 4)


def device(xl, xh, core, z, y):
    return {"rep": xl * 2 + core, "fsdp": z * 8 + xh * 4 + y}


def flat_device(xl, core, s):
    return device(xl, lax.rem(lax.div(s, 4), 2), core, lax.div(s, 8), lax.rem(s, 4))


class Links:

    def __init__(self, T, R, RA, RB, g_send, g_recv, r_send, r_recv):
        self.xl, self.b, self.z, self.a, self.y = coords()
        self.T5 = T.reshape(ROUNDS, 4, 2, 4, UNIT, 16, 128)
        self.R, self.RA, self.RB = R, RA, RB
        self.g_send, self.g_recv, self.r_send, self.r_recv = g_send, g_recv, r_send, r_recv
        self.pending = []
        self.sibling = device(self.xl, self.a, 1 - self.b, self.z, self.y)

    def at_y(self, k):
        return device(self.xl, self.a, self.b, self.z, lax.rem(self.y + k, 4))

    def at_z(self, k):
        return device(self.xl, self.a, self.b, lax.rem(self.z + k, 4), self.y)

    def go(self, src, dst, send, recv, target):
        copy = pltpu.make_async_remote_copy(src_ref=src, dst_ref=dst, send_sem=send, recv_sem=recv, device_id=target, device_id_type=MESH)
        copy.start()
        self.pending.append(copy)

    def landed(self, dst, send, recv):
        pltpu.make_async_remote_copy(src_ref=dst, dst_ref=dst, send_sem=send, recv_sem=recv, device_id=self.sibling, device_id_type=MESH).wait_recv()

    def sent(self):
        for copy in self.pending:
            copy.wait_send()
        self.pending = []

    def span(self, i, h):
        lo, hi = STAGES[i]
        n = (hi - lo) // 2
        return pl.ds(lo + h * n, n)

    def first_axis(self, h, k):
        return (self.at_y if h == 0 else self.at_z)(k)

    def second_axis(self, h, k):
        return (self.at_z if h == 0 else self.at_y)(k)

    def one(self, i, h, k, q=None):
        rd = self.span(i, h)
        t = pl.ds(0, UNIT) if q is None else pl.ds(3 * q, 3)
        if h == 0:
            return self.T5.at[rd, self.z, self.b, lax.rem(self.y + k, 4), t]
        return self.T5.at[rd, lax.rem(self.z + k, 4), self.b, self.y, t]

    def row(self, i, h, k, core=None, p=None):
        rd = self.span(i, h)
        core = self.b if core is None else core
        t = pl.ds(0, 4) if p is None else pl.ds(2 * p, 2)
        if h == 0:
            return self.T5.at[rd, lax.rem(self.z + k, 4), core, t]
        return self.T5.at[rd, t, core, lax.rem(self.y + k, 4)]

    def gsem(self, i, h, k):
        n = (i * 2 + h) * 12 + k
        return self.g_send.at[n], self.g_recv.at[n]

    def gather_go(self, i, h, k, view, target):
        self.go(view, view, *self.gsem(i, h, k), target)

    def gather_wait(self, i, h, k, view):
        self.landed(view, *self.gsem(i, h, k))

    def gather_step(self, i, step):
        for h in range(2):
            if step == 0:
                self.gather_go(i, h, 0, self.one(i, h, 0), self.first_axis(h, 1))
                self.gather_go(i, h, 1, self.one(i, h, 0), self.first_axis(h, 3))
            elif step == 1:
                self.gather_wait(i, h, 0, self.one(i, h, 3))
                self.gather_go(i, h, 2, self.one(i, h, 3, 0), self.first_axis(h, 1))
                self.gather_wait(i, h, 1, self.one(i, h, 1))
                self.gather_go(i, h, 3, self.one(i, h, 1, 1), self.first_axis(h, 3))
            elif step == 2:
                self.gather_wait(i, h, 2, self.one(i, h, 2, 0))
                self.gather_wait(i, h, 3, self.one(i, h, 2, 1))
                self.gather_go(i, h, 4, self.row(i, h, 0), self.second_axis(h, 1))
                self.gather_go(i, h, 5, self.row(i, h, 0), self.second_axis(h, 3))
                self.gather_go(i, h, 8, self.row(i, h, 0), self.sibling)
            elif step == 3:
                self.gather_wait(i, h, 4, self.row(i, h, 3))
                self.gather_go(i, h, 6, self.row(i, h, 3, p=0), self.second_axis(h, 1))
                self.gather_go(i, h, 9, self.row(i, h, 3), self.sibling)
                self.gather_wait(i, h, 5, self.row(i, h, 1))
                self.gather_go(i, h, 7, self.row(i, h, 1, p=1), self.second_axis(h, 3))
                self.gather_go(i, h, 10, self.row(i, h, 1), self.sibling)
            elif step == 4:
                self.gather_wait(i, h, 6, self.row(i, h, 2, p=0))
                self.gather_wait(i, h, 7, self.row(i, h, 2, p=1))
                self.gather_go(i, h, 11, self.row(i, h, 2), self.sibling)
            else:
                for k, offset in ((8, 0), (9, 3), (10, 1), (11, 2)):
                    self.gather_wait(i, h, k, self.row(i, h, offset, core=1 - self.b))

    def rsem(self, i, h, k):
        n = (i * 2 + h) * 13 + k
        return self.r_send.at[n], self.r_recv.at[n]

    def cell(self, i, h, k, q):
        rd = self.span(i, h)
        t = pl.ds(3 * q, 3)
        if h == 0:
            return self.T5.at[rd, self.z, self.b, lax.rem(self.y + k, 4), t]
        return self.T5.at[rd, lax.rem(self.z + k, 4), self.b, self.y, t]

    def add(self, dst, *sources, inner=()):
        n = dst.shape[0]

        def one(r, carry):
            for k in range(inner) if inner else (None,):
                at = (r,) if k is None else (r, k)
                if len(sources) == 1:
                    dst[at] = dst[at] + sources[0][at]
                else:
                    total = dst[at].astype(jnp.float32)
                    for source in sources:
                        total = total + source[at].astype(jnp.float32)
                    dst[at] = total.astype(jnp.bfloat16)
            return carry

        lax.fori_loop(0, n, one, 0)

    def reduce_step(self, i, h, step):
        rd = self.span(i, h)
        T5 = self.T5

        def send_a(k, ka, p, shift):
            self.go(self.row(i, h, ka, p=p), self.RA.at[k, rd], *self.rsem(i, h, 1 + k), self.second_axis(h, shift))

        def wait_a(k):
            self.landed(self.RA.at[k, rd], *self.rsem(i, h, 1 + k))

        def send_b(k, kb, q, shift):
            self.go(self.cell(i, h, kb, q), self.RB.at[k, rd], *self.rsem(i, h, 7 + k), self.first_axis(h, shift))

        def wait_b(k):
            self.landed(self.RB.at[k, rd], *self.rsem(i, h, 7 + k))

        if step == 0:
            self.go(T5.at[rd, :, 1 - self.b], self.R.at[rd], *self.rsem(i, h, 0), self.sibling)
        elif step == 1:
            self.landed(self.R.at[rd], *self.rsem(i, h, 0))
            mine, theirs = T5.at[rd, :, self.b], self.R.at[rd]
            n = mine.shape[0]

            def both(r, carry):
                q = lax.div(r, 4)
                w = lax.rem(r, 4)
                for k in range(4):
                    mine[q, w, k] = mine[q, w, k] + theirs[q, w, k]
                return carry

            lax.fori_loop(0, 4 * n, both, 0)
            send_a(0, 2, 0, 1)
            send_a(1, 2, 1, 3)
            send_a(2, 1, 1, 1)
            send_a(3, 3, 0, 3)
        elif step == 2:
            wait_a(0)
            self.add(self.row(i, h, 1, p=0), self.RA.at[0, rd], inner=2)
            send_a(4, 1, 0, 1)
            wait_a(1)
            self.add(self.row(i, h, 3, p=1), self.RA.at[1, rd], inner=2)
            send_a(5, 3, 1, 3)
        elif step == 3:
            for k in (2, 3, 4, 5):
                wait_a(k)
            self.add(self.row(i, h, 0, p=0), self.RA.at[3, rd], self.RA.at[4, rd], inner=2)
            self.add(self.row(i, h, 0, p=1), self.RA.at[2, rd], self.RA.at[5, rd], inner=2)
            send_b(0, 2, 0, 1)
            send_b(1, 2, 1, 3)
            send_b(2, 1, 1, 1)
            send_b(3, 3, 0, 3)
        elif step == 4:
            wait_b(0)
            self.add(self.cell(i, h, 1, 0), self.RB.at[0, rd])
            send_b(4, 1, 0, 1)
            wait_b(1)
            self.add(self.cell(i, h, 3, 1), self.RB.at[1, rd])
            send_b(5, 3, 1, 3)
        else:
            for k in (2, 3, 4, 5):
                wait_b(k)
            self.add(self.cell(i, h, 0, 0), self.RB.at[3, rd], self.RB.at[4, rd])
            self.add(self.cell(i, h, 0, 1), self.RB.at[2, rd], self.RB.at[5, rd])


def start_gather(links, w_ref, patch_ref, labels_ref, counts_ref, T, patch_in, meta_in, meta_ref, flat, headrows, lob, hib, rlo, rhi, slot, local_sem, x_send, x_recv, u_send, u_recv):
    xl, b, z, a, y = links.xl, links.b, links.z, links.a, links.y
    fs = z * 8 + a * 4 + y
    swap = a != b
    xo = lax.rem(xl + a + b, 2)
    holder = z * 8 + b * 4 + y
    up = flat_device(xl, b, lax.rem(fs + 1, NSLOT))
    down = flat_device(xl, b, lax.rem(fs + NSLOT - 1, NSLOT))
    mirror = device(xl, b, a, z, y)
    load = pltpu.make_async_copy(w_ref, flat.at[pl.ds(MARGIN, SHARD)], local_sem.at[0])
    load.start()
    barrier = pltpu.get_barrier_semaphore()
    total = (counts_ref[0] + counts_ref[1]).astype(jnp.float32)
    for m in range(2):
        valid = jnp.full((1, 128), jnp.where(fs < counts_ref[m], 1.0, 0.0), jnp.float32)
        meta_ref[m : m + 1, :] = jnp.full((1, 128), labels_ref[m].astype(jnp.float32), jnp.float32)
        meta_ref[2 + m : 3 + m, :] = valid / jnp.full((1, 128), total, jnp.float32)
        meta_ref[4 + m : 5 + m, :] = valid
    meta_ref[6:8, :] = jnp.zeros((2, 128), jnp.float32)

    def greet(target):
        pl.semaphore_signal(barrier, inc=1, device_id=target, device_id_type=MESH)

    for target in (up, down, links.at_y(1), links.at_y(3), links.at_z(1), links.at_z(3), links.sibling):
        greet(target)

    @pl.when(swap)
    def _():
        greet(mirror)

    own_index = lax.rem(fs * 11, NSLOT)
    keeps = jnp.logical_and(a == b, own_index < ROUNDS)

    def greet_source(j, carry):
        s = lax.div(32 * j + holder, ROUNDS)
        sa = lax.rem(lax.div(s, 4), 2)

        @pl.when(jnp.logical_not(jnp.logical_and(keeps, s == fs)))
        def _():
            greet(device(lax.rem(xl + sa + a, 2), sa, a, lax.div(s, 8), lax.rem(s, 4)))

        return carry

    lax.fori_loop(0, ROUNDS, greet_source, 0)
    pl.semaphore_wait(barrier, 7 + ROUNDS + jnp.where(swap, 1, 0) - jnp.where(keeps, 1, 0))
    load.wait()

    def remote(src, dst, k, target):
        return pltpu.make_async_remote_copy(src_ref=src, dst_ref=dst, send_sem=x_send.at[k], recv_sem=x_recv.at[k], device_id=target, device_id_type=MESH)

    hib[...] = flat[pl.ds(MARGIN + SHARD - HI, HI), :].astype(jnp.bfloat16)
    to_up = remote(hib, rlo, 0, up)
    to_up.start()
    lob[...] = flat[pl.ds(MARGIN, LO), :].astype(jnp.bfloat16)
    to_down = remote(lob, rhi, 1, down)
    to_down.start()
    patch_swap = remote(patch_ref, patch_in, 2, mirror)
    meta_swap = remote(meta_ref, meta_in, 3, mirror)
    patch_keep = pltpu.make_async_copy(patch_ref, patch_in, local_sem.at[1])
    meta_keep = pltpu.make_async_copy(meta_ref, meta_in, local_sem.at[2])
    first = ROUNDS * fs
    origin = SHARD * fs - MARGIN

    def unit_copy(i):
        k = first + i
        d = lax.rem(k, 32)
        src = slot.at[pl.ds(UNIT * i, UNIT)]
        dst = T.at[pl.ds(UNIT * k, UNIT)]
        target = device(xo, b, lax.rem(lax.div(d, 4), 2), lax.div(d, 8), lax.rem(d, 4))
        mine = jnp.logical_and(keeps, i == own_index)
        away = pltpu.make_async_remote_copy(src_ref=src, dst_ref=dst, send_sem=u_send.at[i], recv_sem=u_recv.at[lax.div(k, 32)], device_id=target, device_id_type=MESH)
        return mine, away, (src, dst)

    def send_unit(i):
        mine, away, (src, dst) = unit_copy(i)

        @pl.when(mine)
        def _():
            pltpu.make_async_copy(src, dst, local_sem.at[3]).start()

        @pl.when(jnp.logical_not(mine))
        def _():
            away.start()

    lane = lax.broadcasted_iota(jnp.int32, (8, 128), 1)

    def head_group(g, base, per, start):
        row = base + per * g - origin
        for i in range(16):
            q, s = divmod(1000 * i, 128)
            one = flat[pl.ds(row + q, 8), :]
            if s:
                two = flat[pl.ds(row + q + 1, 8), :]
                one = jnp.where(lane < 128 - s, pltpu.roll(one, 128 - s, 1), pltpu.roll(two, 128 - s, 1))
            headrows[pl.ds(i * 8, 8), :] = one
        for j in range(8):
            t = start + g * 8 + j - UNIT * first

            @pl.when(jnp.logical_and(t >= 0, t < SLOT))
            def _():
                slot[t] = headrows[pl.ds(j, 16, stride=8), :].astype(jnp.bfloat16)

    def inside(row, rows):
        return jnp.logical_and(row >= MARGIN, row + rows <= MARGIN + SHARD)

    def convert(near):
        for index, (base, c, groups, per, start) in enumerate(SECTIONS):
            lo = jnp.maximum(UNIT * first, start)
            hi = jnp.minimum(UNIT * first + SLOT, start + c * groups)
            if index == 1:

                def group(g, carry):
                    @pl.when(inside(base + per * g - origin, per + 1) == near)
                    def _():
                        head_group(g, base, per, start)

                    return carry

                lax.fori_loop(lax.div(jnp.maximum(lo, start) - start, 8), lax.div(jnp.maximum(hi, start) - start + 7, 8), group, 0)
                if not near:

                    def deal(u, carry):
                        send_unit(u - first)
                        return carry

                    lax.fori_loop(lax.div(lo, UNIT), lax.div(hi, UNIT), deal, 0)
            else:

                def unit(u, carry):
                    t = UNIT * u - start
                    g = lax.div(t, c)
                    row = base + 16 * c * g + lax.rem(t, c) - origin

                    @pl.when(inside(row, 15 * c + UNIT) == near)
                    def _():
                        for k in range(UNIT):
                            slot[UNIT * (u - first) + k] = flat[pl.ds(row + k, 16, stride=c), :].astype(jnp.bfloat16)
                        send_unit(u - first)

                    return carry

                lax.fori_loop(lax.div(lo, UNIT), lax.div(hi, UNIT), unit, 0)

    convert(True)
    to_up.wait_recv()
    flat[pl.ds(MARGIN - HI, HI), :] = rlo[...].astype(jnp.float32)
    to_down.wait_recv()
    flat[pl.ds(MARGIN + SHARD, LO), :] = rhi[...].astype(jnp.float32)
    convert(False)

    @pl.when(fs == NSLOT - 1)
    def _():
        slot[pl.ds(SLOT - 12, 12)] = jnp.zeros((12, 16, 128), jnp.bfloat16)
        send_unit(ROUNDS - 2)
        send_unit(ROUNDS - 1)

    @pl.when(swap)
    def _():
        patch_swap.start()
        meta_swap.start()

    @pl.when(jnp.logical_not(swap))
    def _():
        patch_keep.start()
        meta_keep.start()

    def units_here(i):
        def wait(j, carry):
            place = T.at[pl.ds(UNIT * (32 * j + holder), UNIT)]
            mine = jnp.logical_and(keeps, lax.div(32 * j + holder, ROUNDS) == fs)

            @pl.when(mine)
            def _():
                pltpu.make_async_copy(place, place, local_sem.at[3]).wait()

            @pl.when(jnp.logical_not(mine))
            def _():
                pltpu.make_async_remote_copy(src_ref=place, dst_ref=place, send_sem=u_send.at[0], recv_sem=u_recv.at[j], device_id=links.sibling, device_id_type=MESH).wait_recv()

            return carry

        lax.fori_loop(*STAGES[i], wait, 0)

    def finish_start():
        def wait(i, carry):
            mine, away, unused = unit_copy(i)

            @pl.when(jnp.logical_not(mine))
            def _():
                away.wait_send()

            return carry

        lax.fori_loop(0, ROUNDS, wait, 0)
        to_up.wait_send()
        to_down.wait_send()

        @pl.when(swap)
        def _():
            patch_swap.wait()
            meta_swap.wait()

        @pl.when(jnp.logical_not(swap))
        def _():
            patch_keep.wait()
            meta_keep.wait()

    return units_here, finish_start


D = 768
HEADS = 12
HEAD_DIM = 64
FF = 3072
CLS = 1000
P_SIZE = 196
ROWS = 208
TOK = 2 * ROWS
NORM_EPS = 1e-06
SMOOTHING = 0.1
NTILES = 4224
T_E, T_HEAD, T_NORM, T_QKV, T_OUT, T_IN, T_FO = 0, 366, 750, 756, 1620, 1908, 3060
T_POS = 288
BLK = 256
BLOCKS = ((0, 96), (96, 112), (208, 96), (304, 112))
F32 = jnp.float32
BF16 = jnp.bfloat16
ROOT_HALF = 0.7071067811865476
INV_ROOT_TWO_PI = 0.3989422804014327


def dot(x, w):
    return lax.dot_general(x, w, (((1,), (0,)), ((), ())), preferred_element_type=F32)


def dot_t(x, w):
    return lax.dot_general(x, w, (((1,), (1,)), ((), ())), preferred_element_type=F32)


def t_dot(x, w):
    return lax.dot_general(x, w, (((0,), (0,)), ((), ())), preferred_element_type=F32)


def stats(x, keep, r, k):
    mean = jnp.sum(x, -1, keepdims=True) * (1.0 / D)
    centred = x - mean
    var = jnp.sum(centred * centred, -1, keepdims=True) * (1.0 / D)
    rstd = lax.rsqrt(var + NORM_EPS)
    keep[r, k : k + 1] = mean
    keep[r, k + 1 : k + 2] = rstd
    return centred * rstd


def kept(x, keep, r, k):
    rstd = keep[r, k + 1 : k + 2]
    return (x - keep[r, k : k + 1]) * rstd, rstd


def norm_back(d_hat, hat, rstd):
    m1 = jnp.sum(d_hat, -1, keepdims=True) * (1.0 / D)
    m2 = jnp.sum(d_hat * hat, -1, keepdims=True) * (1.0 / D)
    return rstd * (d_hat - m1 - hat * m2)


def compute(step, patch_ref, meta_ref, loss_ref, T, x, h, a, at, mix, prob, o, h1, a2, hid, slope, h2, dh, dyb, keep):
    G = T
    dmix = mix

    def section(ref, start, c, groups):
        return ref.at[pl.ds(start, groups * c)].reshape(groups, c, 16, 128)

    def cols(start, c, groups, j):
        part = section(T, start, c, groups)
        return jnp.concatenate([part[:, 2 * j + k].reshape(groups * 16, 128) for k in range(2)], axis=1)

    def put_cols(start, c, groups, j, value):
        low = value.astype(BF16)
        part = section(G, start, c, groups)
        for k in range(2):
            part[:, 2 * j + k] = low[:, k * 128 : (k + 1) * 128].reshape(groups, 16, 128)

    def row_of(start, k):
        return jnp.concatenate([T[start + j][k : k + 1, :] for j in range(6)], axis=1).astype(F32)

    def lanes(j):
        return pl.ds(pl.multiple_of(j * BLK, BLK), BLK)

    step("start")
    for i in range(2):
        x[pl.ds(i * ROWS, 192), :] = patch_ref[i, pl.ds(0, 192), :]
        x[pl.ds(i * ROWS + 192, 16), :] = jnp.concatenate([patch_ref[i, pl.ds(192, 4), :], jnp.zeros((12, D), BF16)], axis=0)

    real = lax.broadcasted_iota(jnp.int32, (ROWS, 128), 0) < P_SIZE
    for j in range(3):
        acc = dot(x[...], cols(T_E, 6, 48, j))
        p = cols(T_POS, 6, 13, j).astype(F32)
        p = jnp.where(lax.broadcasted_iota(jnp.int32, (ROWS, BLK), 0) < P_SIZE, p, 0.0)
        for i in range(2):
            h[pl.ds(i * ROWS, ROWS), pl.ds(j * BLK, BLK)] = acc[i * ROWS : (i + 1) * ROWS] + p

    step("embedded")
    gain1, shift1, gain2, shift2 = (row_of(T_NORM, k) for k in range(4))

    for at_row, n in BLOCKS:
        r = pl.ds(at_row, n)
        a[r, :] = (stats(h[r, :], keep, r, 0) * gain1 + shift1).astype(BF16)

    step("qkv")
    def wide_cols(start, c, groups, j):
        return jnp.concatenate([cols(start, c, groups, 3 * j + k) for k in range(3)], axis=1)

    def wide_lanes(j):
        return pl.ds(pl.multiple_of(j * D, D), D)

    def mix_block(j, carry):
        mix[:, wide_lanes(j)] = dot(a[...], wide_cols(T_QKV, 18, 48, j)).astype(BF16)
        return carry

    lax.fori_loop(0, 3, mix_block, 0)

    first_half = lax.broadcasted_iota(jnp.int32, (ROWS, 128), 1) < HEAD_DIM
    key_ok = lax.broadcasted_iota(jnp.int32, (ROWS, ROWS), 0) < P_SIZE
    first_rows = lax.broadcasted_iota(jnp.int32, (128, ROWS), 0) < HEAD_DIM
    halves = (first_half, jnp.logical_not(first_half))
    zero = jnp.zeros((ROWS, 128), BF16)

    def split(block):
        return jnp.concatenate([jnp.where(first_half, block, zero), jnp.where(first_half, zero, block)], axis=0)

    def heads_of(p, i):
        r = pl.ds(i * ROWS, ROWS)
        return r, [pl.ds(pl.multiple_of(p * 128 + D * k, 128), 128) for k in range(3)]

    def attend(p, carry):
        for i in range(2):
            r, ls = heads_of(p, i)
            q, k, v = (mix[r, l] for l in ls)
            q = q * jnp.asarray(0.125, BF16)
            vt = v.T
            outs = []
            for e in range(2):
                s = dot_t(jnp.where(halves[e], k, zero), q)
                s = jnp.where(key_ok, s, -jnp.inf)
                ex = jnp.exp(s - jnp.max(s, 0, keepdims=True))
                pr = (ex * (1.0 / jnp.sum(ex, 0, keepdims=True))).astype(BF16)
                prob[p * 2 + i, e] = pr
                outs.append(dot(vt, pr))
            o[r, ls[0]] = jnp.where(first_rows, outs[0], outs[1]).astype(BF16).T
        return carry

    parts = ((0, 2), (2, 3), (3, 5), (5, 6))
    for part in range(4):
        step("attend%d" % part)
        lax.fori_loop(*parts[part], attend, 0)
    step("attended")
    for j in range(3):
        h1[:, pl.ds(j * BLK, BLK)] = h[:, pl.ds(j * BLK, BLK)] + dot(o[...], cols(T_OUT, 6, 48, j))

    for at_row, n in BLOCKS:
        r = pl.ds(at_row, n)
        a2[r, :] = (stats(h1[r, :], keep, r, 2) * gain2 + shift2).astype(BF16)

    step("up")
    def up_block(j, carry):
        u = dot(a2[...], wide_cols(T_IN, 24, 48, j))
        phi = 0.5 * (1.0 + lax.erf(u * ROOT_HALF))
        pdf = jnp.exp(-0.5 * u * u) * INV_ROOT_TWO_PI
        hid[:, wide_lanes(j)] = (u * phi).astype(BF16)
        slope[:, wide_lanes(j)] = (phi + u * pdf).astype(BF16)
        return carry

    lax.fori_loop(0, 4, up_block, 0)
    step("down")
    for j in range(3):
        h2[:, pl.ds(j * BLK, BLK)] = h1[:, pl.ds(j * BLK, BLK)] + dot(hid[...], cols(T_FO, 6, 192, j))

    step("pool")
    gain_end, shift_end = (row_of(T_POS + 72, 4 + k) for k in range(2))
    means = []
    last_rows = lax.broadcasted_iota(jnp.int32, (112, D), 0) < P_SIZE - 96
    for i in range(2):
        total = jnp.zeros((8, D), F32)
        for at_row, n in BLOCKS[2 * i : 2 * i + 2]:
            r = pl.ds(at_row, n)
            hat = stats(h2[r, :], keep, r, 4)
            if n == 112:
                hat = jnp.where(last_rows, hat, 0.0)
            total = total + jnp.sum(hat.reshape(n // 8, 8, D), 0)
        means.append(jnp.sum(total, 0, keepdims=True) * (1.0 / P_SIZE))
    mean_hat = jnp.concatenate(means + [jnp.zeros((14, D), F32)], axis=0)
    two = lax.broadcasted_iota(jnp.int32, (16, D), 0) < 2
    pooled = jnp.where(two, mean_hat * gain_end + shift_end, 0.0).astype(BF16)
    logits = jnp.concatenate([dot(pooled, cols(T_HEAD, 8, 48, j)) for j in range(4)], axis=1)
    lane = lax.broadcasted_iota(jnp.int32, (16, 1024), 1)
    lane_f = lane.astype(F32)
    inside = lane < CLS
    logits = jnp.where(inside, logits, -1e30)
    top = jnp.max(logits, -1, keepdims=True)
    total = jnp.sum(jnp.where(inside, jnp.exp(logits - top), 0.0), -1, keepdims=True)
    logp = logits - top - jnp.log(total)
    meta = meta_ref[...]
    pad14 = jnp.zeros((14, 1), F32)
    label = jnp.concatenate([meta[0:2, 0:1], pad14], axis=0)
    scale = jnp.concatenate([meta[2:4, 0:1], pad14], axis=0)
    valid = jnp.concatenate([meta[4:6, 0:1], pad14], axis=0)
    target = jnp.where(lane_f == label, 1.0 - SMOOTHING, 0.0) + SMOOTHING / CLS
    values = -jnp.sum(jnp.where(inside, target * logp, 0.0), -1, keepdims=True)
    loss_ref[...] = jnp.broadcast_to(jnp.sum(values * valid, 0, keepdims=True), (8, 128))
    d_logits = jnp.where(inside, scale * (jnp.exp(logp) - target), 0.0).astype(BF16)
    d_pooled = jnp.zeros((16, D), F32)
    for j in range(4):
        w = cols(T_HEAD, 8, 48, j)
        d_pooled = d_pooled + dot_t(d_logits[:, j * BLK : (j + 1) * BLK], w)
        put_cols(T_HEAD, 8, 48, j, t_dot(pooled, d_logits[:, j * BLK : (j + 1) * BLK]))
    d_gain_end = jnp.sum(d_pooled * mean_hat, 0, keepdims=True)
    d_shift_end = jnp.sum(d_pooled, 0, keepdims=True)
    for i in range(2):
        d_hat = d_pooled[i : i + 1, :] * (1.0 / P_SIZE) * gain_end

        m1 = jnp.sum(d_hat, -1, keepdims=True) * (1.0 / D)
        for at_row, n in BLOCKS[2 * i : 2 * i + 2]:
            r = pl.ds(at_row, n)
            hat, rstd = kept(h2[r, :], keep, r, 4)
            m2 = jnp.sum(d_hat * hat, -1, keepdims=True) * (1.0 / D)
            d = rstd * ((d_hat - m1) - hat * m2)
            if n == 112:
                d = jnp.where(last_rows, d, 0.0)
            dh[r, :] = d
            dyb[r, :] = d.astype(BF16)

    step("backward")
    at[...] = a2[...].T
    da = h2

    wide = D // 16

    def down_block(j, carry):
        part = section(T, T_FO + j * wide * 6, 6, wide)
        w = jnp.concatenate([part[:, k].reshape(D, 128) for k in range(6)], axis=1)
        dy = dyb[...]
        d_w = t_dot(hid[:, wide_lanes(j)], dy).astype(BF16)
        hid[:, wide_lanes(j)] = (dot_t(dy, w) * slope[:, wide_lanes(j)].astype(F32)).astype(BF16)
        for k in range(6):
            part[:, k] = d_w[:, k * 128 : (k + 1) * 128].reshape(wide, 16, 128)
        return carry

    G[pl.ds(4212, 12)] = jnp.zeros((12, 16, 128), BF16)
    lax.fori_loop(0, 3, down_block, 0)
    step("fc_out0")
    lax.fori_loop(3, 4, down_block, 0)
    step("fc_out1")
    def row_block(start, c, j):
        part = section(T, start + j * 16 * c, c, 16)
        return jnp.concatenate([part[:, k].reshape(BLK, 128) for k in range(c)], axis=1)

    def put_rows(start, c, j, first, value):
        part = section(G, start + j * 16 * c, c, 16)
        low = value.astype(BF16)
        for k in range(value.shape[1] // 128):
            part[:, first + k] = low[:, k * 128 : (k + 1) * 128].reshape(16, 16, 128)

    for j in range(3):
        da[:, pl.ds(j * BLK, BLK)] = dot_t(hid[...], row_block(T_IN, 24, j))
    step("fc_in0")
    for j in range(3):
        for k in range(4):
            put_rows(T_IN, 24, j, 6 * k, dot(at[pl.ds(j * BLK, BLK), :], hid[:, pl.ds(k * D, D)]))
        step("fc_in%d" % (j + 1))

    def norm_grads(inputs, column, gain):
        dg, ds = jnp.zeros((8, D), F32), jnp.zeros((8, D), F32)
        for at_row, n in BLOCKS:
            r = pl.ds(at_row, n)
            hat, rstd = kept(inputs[r, :], keep, r, column)
            d = da[r, :]
            new = dh[r, :] + norm_back(d * gain, hat, rstd)
            dh[r, :] = new
            dyb[r, :] = new.astype(BF16)
            dg = dg + jnp.sum((d * hat).reshape(n // 8, 8, D), 0)
            ds = ds + jnp.sum(d.reshape(n // 8, 8, D), 0)
        return dg, ds

    d_gain2, d_shift2 = norm_grads(h1, 2, gain2)

    step("normed2")
    at[...] = o[...].T
    for j in range(3):
        o[:, pl.ds(j * BLK, BLK)] = dot_t(dyb[...], row_block(T_OUT, 6, j)).astype(BF16)
    for j in range(3):
        put_rows(T_OUT, 6, j, 0, dot(at[pl.ds(j * BLK, BLK), :], dyb[...]))

    step("out")
    def attend_back(p, carry):
        for i in range(2):
            r, ls = heads_of(p, i)
            q, k, v = (mix[r, l] for l in ls)
            q = q * jnp.asarray(0.125, BF16)
            k8 = k * jnp.asarray(0.125, BF16)
            kt = k8.T
            do = o[r, ls[0]]
            pr = prob[p * 2 + i]
            dv = dot(pr.reshape(TOK, ROWS), do)
            dp = dot_t(split(v), do).reshape(2, ROWS, ROWS)
            prf = pr.astype(F32)
            row = jnp.sum(prf * dp, 1, keepdims=True)
            ds = (prf * (dp - row)).astype(BF16)
            dq = [dot(kt[HEAD_DIM * e : HEAD_DIM * (e + 1)], ds[e]) for e in range(2)]
            dk = dot(ds.reshape(TOK, ROWS), q)
            dmix[r, ls[0]] = jnp.concatenate(dq, axis=0).astype(BF16).T
            dmix[r, ls[1]] = jnp.where(first_half, dk[:ROWS], dk[ROWS:]).astype(BF16)
            dmix[r, ls[2]] = jnp.where(first_half, dv[:ROWS], dv[ROWS:]).astype(BF16)
        return carry

    for part in range(4):
        lax.fori_loop(*parts[part], attend_back, 0)
        step("back%d" % part)

    at[...] = a[...].T
    for j in range(3):
        da[:, pl.ds(j * BLK, BLK)] = dot_t(dmix[...], row_block(T_QKV, 18, j))
    for j in range(3):
        for k in range(3):
            put_rows(T_QKV, 18, j, 6 * k, dot(at[pl.ds(j * BLK, BLK), :], dmix[:, pl.ds(k * D, D)]))
    step("qkv_back")
    d_gain1, d_shift1 = norm_grads(h, 0, gain1)
    d_norms = jnp.concatenate([jnp.sum(d, 0, keepdims=True) for d in (d_gain1, d_shift1, d_gain2, d_shift2)] + [jnp.zeros((12, D), F32)], axis=0).astype(BF16)
    for j in range(6):
        G[T_NORM + j] = d_norms[:, j * 128 : (j + 1) * 128]
    step("norms")
    at[...] = x[...].T
    row_id = lax.broadcasted_iota(jnp.int32, (ROWS, BLK), 0)
    for j in range(3):
        put_cols(T_E, 6, 48, j, dot(at[...], dyb[:, pl.ds(j * BLK, BLK)]))
        c = pl.ds(j * BLK, BLK)
        s = slice(j * BLK, (j + 1) * BLK)
        d_pos = dh[pl.ds(0, ROWS), c] + dh[pl.ds(ROWS, ROWS), c]
        d_pos = jnp.where(row_id < P_SIZE, d_pos, 0.0)
        d_pos = jnp.where(row_id == P_SIZE, jnp.broadcast_to(d_gain_end[:, s], (ROWS, BLK)), d_pos)
        d_pos = jnp.where(row_id == P_SIZE + 1, jnp.broadcast_to(d_shift_end[:, s], (ROWS, BLK)), d_pos)
        put_cols(T_POS, 6, 13, j, d_pos)
    step("embed")


FORWARD = {
    "start": ((0, 0), (1, 0), (0, 1), (0, 2), (1, 1), (2, 0), (0, 3), (1, 2), (0, 4), (2, 1), (3, 0), (0, 5)),
    "embedded": ((1, 3), (2, 2), (3, 1)),
    "qkv": ((1, 4), (1, 5), (3, 2)),
    "attend0": ((2, 3),),
    "attend1": ((3, 3), (2, 4)),
    "attend2": ((3, 4),),
    "up": ((2, 5),),
    "down": ((3, 5),),
}
BACKWARD = {
    "fc_out0": ((3, 0, 0),),
    "fc_out1": ((3, 1, 0), (3, 0, 1)),
    "fc_in0": ((3, 1, 1),),
    "fc_in1": ((3, 0, 2),),
    "fc_in2": ((2, 0, 0), (3, 1, 2)),
    "fc_in3": ((2, 1, 0), (2, 0, 1), (3, 0, 3)),
    "normed2": ((2, 1, 1), (3, 1, 3)),
    "out": ((3, 0, 4), (2, 0, 2), (3, 1, 4)),
    "back0": ((2, 1, 2), (3, 0, 5)),
    "back1": ((2, 0, 3), (3, 1, 5)),
    "back2": ((2, 1, 3),),
    "back3": ((2, 0, 4), (2, 1, 4)),
    "qkv_back": ((1, 0, 0), (1, 1, 0), (2, 0, 5), (2, 1, 5)),
    "norms": ((0, 1, 0), (1, 0, 1), (1, 1, 1)),
    "embed": ((0, 0, 0), (0, 1, 1), (0, 0, 1), (1, 0, 2), (1, 1, 2), (0, 1, 2), (0, 0, 2), (1, 0, 3), (1, 1, 3), (0, 1, 3), (0, 0, 3), (1, 0, 4), (1, 1, 4), (0, 1, 4), (0, 0, 4), (1, 0, 5), (1, 1, 5), (0, 1, 5), (0, 0, 5)),
}


def grads_kernel(w_ref, patch_ref, labels_ref, counts_ref, red_ref, loss_out, T, R, RA, RB, g_send, g_recv, r_send, r_recv, LS, l_send, l_recv, patch_in, meta_in, meta, loss, *rest):
    gather_refs, compute_refs, out_sem = rest[:12], rest[12:-1], rest[-1]
    links = Links(T, R, RA, RB, g_send, g_recv, r_send, r_recv)
    xl, b, z, a, y = links.xl, links.b, links.z, links.a, links.y
    swap = a != b
    mirror = device(xl, b, a, z, y)
    units_here, finish_start = start_gather(links, w_ref, patch_ref, labels_ref, counts_ref, T, patch_in, meta_in, meta, *gather_refs)

    def loss_send(src, dst, target):
        links.go(LS.at[src], LS.at[dst], l_send.at[dst], l_recv.at[dst], target)

    def loss_wait(*slots):
        for k in slots:
            links.landed(LS.at[k], l_send.at[k], l_recv.at[k])

    def loss_step(n):
        if n == 0:
            LS[0] = loss[...]
            loss_send(0, 1, links.sibling)
        elif n == 1:
            loss_wait(1)
            LS[8] = LS[0] + LS[1]
            loss_send(8, 2, links.at_y(1))
            loss_send(8, 3, links.at_y(3))
        elif n == 2:
            loss_wait(2, 3)
            loss_send(2, 4, links.at_y(1))
        elif n == 3:
            loss_wait(4)
            LS[9] = (LS[8] + LS[4]) + (LS[2] + LS[3])
            loss_send(9, 5, links.at_z(1))
            loss_send(9, 6, links.at_z(3))
        elif n == 4:
            loss_wait(5, 6)
            loss_send(5, 7, links.at_z(1))
        elif n == 5:
            loss_wait(7)
            LS[10] = (LS[9] + LS[7]) + (LS[5] + LS[6])

            @pl.when(swap)
            def _():
                loss_swap.start()

        else:

            @pl.when(swap)
            def _():
                loss_swap.wait()
                loss_out[...] = LS[11]

            @pl.when(jnp.logical_not(swap))
            def _():
                loss_out[...] = LS[10]

    loss_swap = pltpu.make_async_remote_copy(src_ref=LS.at[10], dst_ref=LS.at[11], send_sem=l_send.at[11], recv_sem=l_recv.at[11], device_id=mirror, device_id_type=MESH)
    losses = {"fc_out0": 0, "fc_in0": 1, "fc_in2": 2, "normed2": 3, "back0": 4, "back2": 5, "qkv_back": 6}

    def step(name):
        if name == "pool":
            links.sent()
        for item in FORWARD.get(name, ()):
            if item[1] == 0:
                units_here(item[0])
            links.gather_step(*item)
        if name == "start":
            finish_start()
        for item in BACKWARD.get(name, ()):
            links.reduce_step(*item)
        if name in losses:
            loss_step(losses[name])

    compute(step, patch_in, meta_in, loss, T, *compute_refs)
    mine = T.reshape(ROUNDS, 32, UNIT, 16, 128).at[:, z * 8 + b * 4 + y]
    out = pltpu.make_async_copy(mine, red_ref, out_sem)
    out.start()
    links.sent()
    out.wait()


def grads(weights, patches, labels, counts):
    hbm = pl.BlockSpec(memory_space=pl.ANY)
    vmem = pl.BlockSpec(memory_space=pltpu.VMEM)
    V = pltpu.VMEM
    dma = pltpu.SemaphoreType.DMA
    return pl.pallas_call(
        grads_kernel,
        out_shape=(jax.ShapeDtypeStruct((ROUNDS, UNIT, 16, 128), BF16), jax.ShapeDtypeStruct((8, 128), F32)),
        in_specs=[hbm] * 2 + [pl.BlockSpec(memory_space=pltpu.SMEM)] * 2,
        out_specs=(hbm, vmem),
        scratch_shapes=[
            V((NTILES, 16, 128), BF16),
            V((ROUNDS, 4, 4, UNIT, 16, 128), BF16),
            V((6, ROUNDS, 2, UNIT, 16, 128), BF16),
            V((6, ROUNDS, 3, 16, 128), BF16),
            dma((96,)),
            dma((96,)),
            dma((104,)),
            dma((104,)),
            V((12, 8, 128), F32),
            dma((12,)),
            dma((12,)),
            V(patches.shape, BF16),
            V((8, 128), F32),
            V((8, 128), F32),
            V((8, 128), F32),
            V((FROWS, 128), F32),
            V((128, 128), F32),
            V((LO, 128), BF16),
            V((HI, 128), BF16),
            V((HI, 128), BF16),
            V((LO, 128), BF16),
            V((SLOT, 16, 128), BF16),
            dma((4,)),
            dma((4,)),
            dma((4,)),
            dma((ROUNDS,)),
            dma((ROUNDS,)),
            V((TOK, D), BF16),
            V((TOK, D), F32),
            V((TOK, D), BF16),
            V((D, TOK), BF16),
            V((TOK, 3 * D), BF16),
            V((12, 2, ROWS, ROWS), BF16),
            V((TOK, D), BF16),
            V((TOK, D), F32),
            V((TOK, D), BF16),
            V((TOK, FF), BF16),
            V((TOK, FF), BF16),
            V((TOK, D), F32),
            V((TOK, D), F32),
            V((TOK, D), BF16),
            V((TOK, 128), F32),
            dma,
        ],
        compiler_params=pltpu.CompilerParams(collective_id=0, has_side_effects=True, vmem_limit_bytes=60 * 1024 * 1024),
        name="grads",
    )(weights, patches, labels, counts)


EDGE = 24
FRONT = 768
BACK_ROWS = FRONT + SHARD + 640 + 6
PADDED = 2112
STEP = 10
EDGE_UNITS = 4
WINDOW = ROUNDS + 2 * EDGE_UNITS
BETA_ONE = 0.9
BETA_TWO = 0.95
ADAM_EPS = 1e-08
DECAY = 0.05
INNER_RATE = 0.01
OUTER_RATE = 0.7
OUTER_MU = 0.9


def update_kernel(
    red_ref, w_ref, first_ref, second_ref, mom_ref,
    avg_out, mom_out, new_out, first_out, second_out,
    red, window, flat, headrows, w, first, second, mom, upd, low, low2, pair, pair2, total, total2,
    load_sem, x_send, x_recv, o_send, e_send, w_recv,
):
    xl, b, z, a, y = coords()
    fs = z * 8 + a * 4 + y
    holder = z * 8 + b * 4 + y
    sibling = device(xl, a, 1 - b, z, y)
    across = device(1 - xl, a, b, z, y)
    extra = [pltpu.make_async_copy(src, dst, load_sem.at[i]) for i, (src, dst) in enumerate(((w_ref, w), (first_ref, first), (second_ref, second), (mom_ref, mom)))]
    load = pltpu.make_async_copy(red_ref, red, load_sem.at[4])
    load.start()
    for copy in extra:
        copy.start()

    barrier = pltpu.get_barrier_semaphore()

    def greet(target):
        pl.semaphore_signal(barrier, inc=1, device_id=target, device_id_type=MESH)

    greet(sibling)
    greet(across)
    first_unit = ROUNDS * fs - EDGE_UNITS

    def window_unit(p):
        k = first_unit + p
        d = lax.rem(k + 32, 32)
        inside = jnp.logical_and(k >= 0, k < 32 * ROUNDS)
        mine = jnp.logical_and(a == b, d == holder)
        return inside, mine, device(xl, b, lax.rem(lax.div(d, 4), 2), lax.div(d, 8), lax.rem(d, 4))

    def greet_holder(p, carry):
        inside, mine, source = window_unit(p)

        @pl.when(jnp.logical_and(inside, jnp.logical_not(mine)))
        def _():
            greet(source)

        return carry

    lax.fori_loop(0, WINDOW, greet_holder, 0)

    def held_unit(j):
        k = 32 * j + holder
        q = lax.div(k, ROUNDS)
        r = lax.rem(k, ROUNDS)
        shift = jnp.where(r < EDGE_UNITS, -1, jnp.where(r >= ROUNDS - EDGE_UNITS, 1, 0))
        near = jnp.logical_and(shift != 0, jnp.logical_and(q + shift >= 0, q + shift < NSLOT))
        return k, q, jnp.where(near, q + shift, q), near

    def to_owner(j, k, s, send):
        p = k - (ROUNDS * s - EDGE_UNITS)
        src = red.at[j]
        dst = window.at[pl.ds(UNIT * p, UNIT)]
        sa = lax.rem(lax.div(s, 4), 2)
        mine = jnp.logical_and(a == b, s == fs)
        target = device(xl, sa, a, lax.div(s, 8), lax.rem(s, 4))
        away = pltpu.make_async_remote_copy(src_ref=src, dst_ref=dst, send_sem=send.at[j], recv_sem=w_recv.at[p], device_id=target, device_id_type=MESH)
        here = pltpu.make_async_copy(src, dst, load_sem.at[10])
        return mine, away, here

    def count(j, n):
        k, q, s, near = held_unit(j)
        first_away = jnp.logical_not(jnp.logical_and(a == b, q == fs))
        second_away = jnp.logical_and(near, jnp.logical_not(jnp.logical_and(a == b, s == fs)))
        return n + jnp.where(first_away, 1, 0) + jnp.where(second_away, 1, 0)

    outgoing = lax.fori_loop(0, ROUNDS, count, 2)
    pl.semaphore_wait(barrier, outgoing)
    load.wait()

    def give(j, carry):
        k, q, s, near = held_unit(j)
        mine, away, here = to_owner(j, k, q, o_send)

        @pl.when(mine)
        def _():
            here.start()

        @pl.when(jnp.logical_not(mine))
        def _():
            away.start()

        mine2, away2, here2 = to_owner(j, k, s, e_send)

        @pl.when(jnp.logical_and(near, mine2))
        def _():
            here2.start()

        @pl.when(jnp.logical_and(near, jnp.logical_not(mine2)))
        def _():
            away2.start()

        return carry

    lax.fori_loop(0, ROUNDS, give, 0)

    def given(j, carry):
        k, q, s, near = held_unit(j)
        mine, away, here = to_owner(j, k, q, o_send)

        @pl.when(jnp.logical_not(mine))
        def _():
            away.wait_send()

        mine2, away2, here2 = to_owner(j, k, s, e_send)

        @pl.when(jnp.logical_and(near, jnp.logical_not(mine2)))
        def _():
            away2.wait_send()

        return carry

    def clear(i, carry):
        flat[pl.ds(pl.multiple_of(i * 32, 32), 32), :] = jnp.zeros((32, 128), F32)
        return carry

    lax.fori_loop(0, BACK_ROWS // 32, clear, 0)

    def got(p, carry):
        inside, mine, source = window_unit(p)
        place = window.at[pl.ds(UNIT * p, UNIT)]

        @pl.when(jnp.logical_and(inside, mine))
        def _():
            pltpu.make_async_copy(place, place, load_sem.at[10]).wait()

        @pl.when(jnp.logical_and(inside, jnp.logical_not(mine)))
        def _():
            pltpu.make_async_remote_copy(src_ref=place, dst_ref=place, send_sem=x_send.at[0], recv_sem=w_recv.at[p], device_id=sibling, device_id_type=MESH).wait_recv()

        return carry

    lax.fori_loop(0, WINDOW, got, 0)
    for copy in extra:
        copy.wait()
    sends = []

    def go(src, dst, send, recv, k, target):
        copy = pltpu.make_async_remote_copy(src_ref=src, dst_ref=dst, send_sem=send.at[k], recv_sem=recv.at[k], device_id=target, device_id_type=MESH)
        copy.start()
        sends.append(copy)

    def arrive(dst, recv, k):
        pltpu.make_async_remote_copy(src_ref=dst, dst_ref=dst, send_sem=x_send.at[k], recv_sem=recv.at[k], device_id=sibling, device_id_type=MESH).wait_recv()

    low_tile = SLOT * fs - EDGE
    high_tile = SLOT * fs + SLOT + EDGE
    origin = SHARD * fs - FRONT
    for index, (base, c, groups, per, start) in enumerate(SECTIONS):
        if index == 1:
            lane = lax.broadcasted_iota(jnp.int32, (8, 128), 1)
            g0 = lax.div(jnp.maximum(SHARD * fs - base, 0), per)
            g1 = lax.div(jnp.maximum(SHARD * (fs + 1) - base, 0) + per - 1, per)

            def head_group(g, carry):
                t = start + g * 8 - low_tile
                for j in range(8):
                    headrows[pl.ds(j, 16, stride=8), :] = window[t + j].astype(F32)
                row = base + per * g - origin
                for i in range(16):
                    q, s = divmod(1000 * i, 128)
                    value = headrows[pl.ds(i * 8, 8), :]
                    if s:
                        value = pltpu.roll(value, s, 1)
                        flat[pl.ds(row + q, 8), :] += jnp.where(lane >= s, value, 0.0)
                        flat[pl.ds(row + q + 1, 8), :] += jnp.where(lane < s, value, 0.0)
                    else:
                        flat[pl.ds(row + q, 8), :] += value
                return carry

            lax.fori_loop(jnp.minimum(g0, groups), jnp.minimum(g1, groups), head_group, 0)
        else:

            def unit(n, carry):
                t = UNIT * n - start
                row = base + 16 * c * lax.div(t, c) + lax.rem(t, c) - origin
                for m in range(UNIT):
                    flat[pl.ds(row + m, 16, stride=c), :] = window[UNIT * n - low_tile + m].astype(F32)
                return carry

            lax.fori_loop(lax.div(jnp.maximum(low_tile, start), UNIT), lax.div(jnp.minimum(high_tile, start + c * groups), UNIT), unit, 0)

    fix_one = 1.0 / (1.0 - BETA_ONE**STEP)
    fix_two = 1.0 / (1.0 - BETA_TWO**STEP)

    def in_rows(fn, lo, hi, step=32):
        def body(i, carry):
            fn(pl.multiple_of(i * step, step), step)
            return carry

        n = (hi - lo) // step
        lax.fori_loop(lo // step, lo // step + n, body, 0)
        if lo + n * step < hi:
            fn(lo + n * step, hi - lo - n * step)

    def adam(r, n):
        grad = flat[pl.ds(FRONT + r, n), :]
        m = BETA_ONE * first[pl.ds(r, n), :] + (1.0 - BETA_ONE) * grad
        s = BETA_TWO * second[pl.ds(r, n), :] + (1.0 - BETA_TWO) * grad * grad
        first[pl.ds(r, n), :] = m
        second[pl.ds(r, n), :] = s
        u = (m * fix_one) / (jnp.sqrt(s * fix_two) + ADAM_EPS)
        upd[pl.ds(r, n), :] = u

    in_rows(adam, 0, SHARD)
    upd[pl.ds(SHARD, PADDED - SHARD), :] = jnp.zeros((PADDED - SHARD, 128), F32)
    outs = [pltpu.make_async_copy(src, dst, load_sem.at[5 + i]) for i, (src, dst) in enumerate(((first, first_out), (second, second_out)))]
    for copy in outs:
        copy.start()

    def lower(r, n):
        low[pl.ds(r, n), :] = upd[pl.ds(r, n), :].astype(BF16)

    in_rows(lower, 0, PADDED)
    go(low, low2, x_send, x_recv, 0, sibling)
    arrive(low2, x_recv, 0)
    half = PADDED // 2

    def pairs(r, n):
        at = pl.ds(pl.multiple_of(b * half + r, 16), n)
        pair[pl.ds(r, n), :] = low[at, :] + low2[at, :]

    in_rows(pairs, 0, half)
    go(pair, pair2, x_send, x_recv, 1, across)
    arrive(pair2, x_recv, 1)

    def fours(r, n):
        total[pl.ds(r, n), :] = pair[pl.ds(r, n), :].astype(F32) + pair2[pl.ds(r, n), :].astype(F32)

    in_rows(fours, 0, half)
    go(total, total2, x_send, x_recv, 2, sibling)

    def outer(source, shift):
        def rows_of(r, n):
            at = pl.ds(shift + r, n)
            t = source[pl.ds(r, n), :]
            old = w[at, :]
            averaged = INNER_RATE * (t * 0.25 + DECAY * old)
            momentum = OUTER_MU * mom[at, :] + averaged
            upd[at, :] = averaged
            mom[at, :] = momentum
            w[at, :] = old - OUTER_RATE * (averaged + OUTER_MU * momentum)

        return rows_of

    def both(here, there):
        in_rows(outer(here, 0), 0, half)
        in_rows(outer(there, half), 0, SHARD - half)

    arrive(total2, x_recv, 2)

    @pl.when(b == 0)
    def _():
        both(total, total2)

    @pl.when(b == 1)
    def _():
        both(total2, total)

    final = [(upd.at[pl.ds(0, SHARD)], avg_out), (mom, mom_out), (w, new_out)]
    final = [pltpu.make_async_copy(src, dst, load_sem.at[7 + i]) for i, (src, dst) in enumerate(final)]
    for copy in final:
        copy.start()
    for copy in sends:
        copy.wait_send()
    lax.fori_loop(0, ROUNDS, given, 0)
    for copy in outs + final:
        copy.wait()


def update(red, weights, first, second, momentum):
    hbm = pl.BlockSpec(memory_space=pl.ANY)
    V = pltpu.VMEM
    flat = jax.ShapeDtypeStruct((SHARD, 128), F32)
    dma = pltpu.SemaphoreType.DMA
    return pl.pallas_call(
        update_kernel,
        out_shape=(flat,) * 5,
        in_specs=[hbm] * 5,
        out_specs=(hbm,) * 5,
        scratch_shapes=[
            V((ROUNDS, UNIT, 16, 128), BF16),
            V((EDGE + SLOT + EDGE, 16, 128), BF16),
            V((BACK_ROWS, 128), F32),
            V((128, 128), F32),
            V((SHARD, 128), F32),
            V((SHARD, 128), F32),
            V((SHARD, 128), F32),
            V((SHARD, 128), F32),
            V((PADDED, 128), F32),
            V((PADDED, 128), BF16),
            V((PADDED, 128), BF16),
            V((PADDED // 2, 128), BF16),
            V((PADDED // 2, 128), BF16),
            V((PADDED // 2, 128), F32),
            V((PADDED // 2, 128), F32),
            dma((11,)),
            dma((3,)),
            dma((3,)),
            dma((ROUNDS,)),
            dma((ROUNDS,)),
            dma((WINDOW,)),
        ],
        compiler_params=pltpu.CompilerParams(collective_id=1, has_side_effects=True, vmem_limit_bytes=60 * 1024 * 1024),
        name="update",
    )(red, weights, first, second, momentum)


def move_kernel(*refs):
    one, two, out_one, out_two, buf_one, buf_two, sem = refs

    def rows(ref):
        return ref.reshape(SHARD, 128) if ref.shape[0] == 1 else ref

    ins = [pltpu.make_async_copy(rows(src), dst, sem.at[i]) for i, (src, dst) in enumerate(((one, buf_one), (two, buf_two)))]
    outs = [pltpu.make_async_copy(src, rows(dst), sem.at[2 + i]) for i, (src, dst) in enumerate(((buf_one, out_one), (buf_two, out_two)))]
    for copy in ins:
        copy.start()
    for i in range(2):
        ins[i].wait()
        outs[i].start()
    for copy in outs:
        copy.wait()


def move(one, two, shape, name):
    hbm = pl.BlockSpec(memory_space=pl.ANY)
    shape = jax.ShapeDtypeStruct(shape, F32)
    rows = pltpu.VMEM((SHARD, 128), F32)
    return pl.pallas_call(
        move_kernel,
        out_shape=(shape,) * 2,
        in_specs=[hbm] * 2,
        out_specs=(hbm,) * 2,
        scratch_shapes=[rows, rows, pltpu.SemaphoreType.DMA((4,))],
        compiler_params=pltpu.CompilerParams(vmem_limit_bytes=60 * 1024 * 1024),
        name=name,
    )(one, two)


def body(patches, labels, counts, weights, first_moments, second_moments, outer_momentum):
    flat = weights.reshape(SHARD, 128)
    first, second = move(first_moments, second_moments, (SHARD, 128), "as_rows")
    reduced, losses = grads(flat, patches.reshape(2, P_SIZE, D), labels.reshape(2), counts.reshape(2))
    averaged, momentum, new_weights, first, second = update(reduced, flat, first, second, outer_momentum.reshape(SHARD, 128))
    first, second = move(first, second, (1, SHARD * 128), "as_flat")
    return (
        averaged.reshape(-1),
        momentum.reshape(-1),
        new_weights.reshape(-1),
        first,
        second,
        losses[:1, :1],
    )


def solution(mesh):
    placed = (
        P("rep", None, None, "fsdp", None, None),
        P("rep", None, None, "fsdp"),
        P("rep", None, None),
        P("fsdp"),
        P("rep", "fsdp"),
        P("rep", "fsdp"),
        P("fsdp"),
    )
    return jax.shard_map(
        body,
        mesh=mesh,
        in_specs=placed,
        out_specs=(
            P("fsdp"),
            P("fsdp"),
            P("fsdp"),
            P("rep", "fsdp"),
            P("rep", "fsdp"),
            P("rep", None),
        ),
        check_vma=False,
    )
```

```python
from functools import partial

import jax
import jax.numpy as jnp
from jax import lax
from jax.experimental import pallas as pl
from jax.experimental.pallas import tpu as pltpu
from jax.sharding import PartitionSpec as P

SHARD = 2098
SLOT = 132
HALF = 66
QUART = 33
NSLOT = 32
ROUNDS = 22
UNIT = 6
STAGES = ((0, 4), (4, 10), (10, 16), (16, 22))
SECTIONS = []
_t = 0
for _base, _c, _g, _rpg in ((0, 6, 61, 96), (5796, 8, 48, 125), (11796, 6, 1, 96), (11820, 18, 48, 288), (25644, 6, 48, 96), (30252, 24, 48, 384), (48684, 6, 192, 96)):
    SECTIONS.append((_base, _c, _g, _rpg, _t))
    _t += _c * _g
NTILE = _t
HI = 352
LO = 224
MARGIN = 512
FROWS = 3072
HEAD_ROWS = 16
MESH = pl.DeviceIdType.MESH


def coords():
    rep = lax.axis_index("rep")
    fs = lax.axis_index("fsdp")
    return lax.div(rep, 2), lax.rem(rep, 2), lax.div(fs, 8), lax.rem(lax.div(fs, 4), 2), lax.rem(fs, 4)


def device(xl, xh, core, z, y):
    return {"rep": xl * 2 + core, "fsdp": z * 8 + xh * 4 + y}


def flat_device(xl, core, s):
    return device(xl, lax.rem(lax.div(s, 4), 2), core, lax.div(s, 8), lax.rem(s, 4))


class Links:

    def __init__(self, T, R, RA, RB, g_send, g_recv, r_send, r_recv):
        self.xl, self.b, self.z, self.a, self.y = coords()
        self.T5 = T.reshape(ROUNDS, 4, 2, 4, UNIT, 16, 128)
        self.R, self.RA, self.RB = R, RA, RB
        self.g_send, self.g_recv, self.r_send, self.r_recv = g_send, g_recv, r_send, r_recv
        self.pending = []
        self.sibling = device(self.xl, self.a, 1 - self.b, self.z, self.y)

    def at_y(self, k):
        return device(self.xl, self.a, self.b, self.z, lax.rem(self.y + k, 4))

    def at_z(self, k):
        return device(self.xl, self.a, self.b, lax.rem(self.z + k, 4), self.y)

    def go(self, src, dst, send, recv, target):
        copy = pltpu.make_async_remote_copy(src_ref=src, dst_ref=dst, send_sem=send, recv_sem=recv, device_id=target, device_id_type=MESH)
        copy.start()
        self.pending.append(copy)

    def landed(self, dst, send, recv):
        pltpu.make_async_remote_copy(src_ref=dst, dst_ref=dst, send_sem=send, recv_sem=recv, device_id=self.sibling, device_id_type=MESH).wait_recv()

    def sent(self):
        for copy in self.pending:
            copy.wait_send()
        self.pending = []

    def span(self, i, h):
        lo, hi = STAGES[i]
        n = (hi - lo) // 2
        return pl.ds(lo + h * n, n)

    def first_axis(self, h, k):
        return (self.at_y if h == 0 else self.at_z)(k)

    def second_axis(self, h, k):
        return (self.at_z if h == 0 else self.at_y)(k)

    def one(self, i, h, k, q=None):
        rd = self.span(i, h)
        t = pl.ds(0, UNIT) if q is None else pl.ds(3 * q, 3)
        if h == 0:
            return self.T5.at[rd, self.z, self.b, lax.rem(self.y + k, 4), t]
        return self.T5.at[rd, lax.rem(self.z + k, 4), self.b, self.y, t]

    def row(self, i, h, k, core=None, p=None):
        rd = self.span(i, h)
        core = self.b if core is None else core
        t = pl.ds(0, 4) if p is None else pl.ds(2 * p, 2)
        if h == 0:
            return self.T5.at[rd, lax.rem(self.z + k, 4), core, t]
        return self.T5.at[rd, t, core, lax.rem(self.y + k, 4)]

    def gsem(self, i, h, k):
        n = (i * 2 + h) * 12 + k
        return self.g_send.at[n], self.g_recv.at[n]

    def gather_go(self, i, h, k, view, target):
        self.go(view, view, *self.gsem(i, h, k), target)

    def gather_wait(self, i, h, k, view):
        self.landed(view, *self.gsem(i, h, k))

    def gather_step(self, i, step):
        for h in range(2):
            if step == 0:
                self.gather_go(i, h, 0, self.one(i, h, 0), self.first_axis(h, 1))
                self.gather_go(i, h, 1, self.one(i, h, 0), self.first_axis(h, 3))
            elif step == 1:
                self.gather_wait(i, h, 0, self.one(i, h, 3))
                self.gather_go(i, h, 2, self.one(i, h, 3, 0), self.first_axis(h, 1))
                self.gather_wait(i, h, 1, self.one(i, h, 1))
                self.gather_go(i, h, 3, self.one(i, h, 1, 1), self.first_axis(h, 3))
            elif step == 2:
                self.gather_wait(i, h, 2, self.one(i, h, 2, 0))
                self.gather_wait(i, h, 3, self.one(i, h, 2, 1))
                self.gather_go(i, h, 4, self.row(i, h, 0), self.second_axis(h, 1))
                self.gather_go(i, h, 5, self.row(i, h, 0), self.second_axis(h, 3))
                self.gather_go(i, h, 8, self.row(i, h, 0), self.sibling)
            elif step == 3:
                self.gather_wait(i, h, 4, self.row(i, h, 3))
                self.gather_go(i, h, 6, self.row(i, h, 3, p=0), self.second_axis(h, 1))
                self.gather_go(i, h, 9, self.row(i, h, 3), self.sibling)
                self.gather_wait(i, h, 5, self.row(i, h, 1))
                self.gather_go(i, h, 7, self.row(i, h, 1, p=1), self.second_axis(h, 3))
                self.gather_go(i, h, 10, self.row(i, h, 1), self.sibling)
            elif step == 4:
                self.gather_wait(i, h, 6, self.row(i, h, 2, p=0))
                self.gather_wait(i, h, 7, self.row(i, h, 2, p=1))
                self.gather_go(i, h, 11, self.row(i, h, 2), self.sibling)
            else:
                for k, offset in ((8, 0), (9, 3), (10, 1), (11, 2)):
                    self.gather_wait(i, h, k, self.row(i, h, offset, core=1 - self.b))

    def rsem(self, i, h, k):
        n = (i * 2 + h) * 13 + k
        return self.r_send.at[n], self.r_recv.at[n]

    def cell(self, i, h, k, q):
        rd = self.span(i, h)
        t = pl.ds(3 * q, 3)
        if h == 0:
            return self.T5.at[rd, self.z, self.b, lax.rem(self.y + k, 4), t]
        return self.T5.at[rd, lax.rem(self.z + k, 4), self.b, self.y, t]

    def add(self, dst, *sources, inner=()):
        n = dst.shape[0]

        def one(r, carry):
            for k in range(inner) if inner else (None,):
                at = (r,) if k is None else (r, k)
                if len(sources) == 1:
                    dst[at] = dst[at] + sources[0][at]
                else:
                    total = dst[at].astype(jnp.float32)
                    for source in sources:
                        total = total + source[at].astype(jnp.float32)
                    dst[at] = total.astype(jnp.bfloat16)
            return carry

        lax.fori_loop(0, n, one, 0)

    def reduce_step(self, i, h, step):
        rd = self.span(i, h)
        T5 = self.T5

        def send_a(k, ka, p, shift):
            self.go(self.row(i, h, ka, p=p), self.RA.at[k, rd], *self.rsem(i, h, 1 + k), self.second_axis(h, shift))

        def wait_a(k):
            self.landed(self.RA.at[k, rd], *self.rsem(i, h, 1 + k))

        def send_b(k, kb, q, shift):
            self.go(self.cell(i, h, kb, q), self.RB.at[k, rd], *self.rsem(i, h, 7 + k), self.first_axis(h, shift))

        def wait_b(k):
            self.landed(self.RB.at[k, rd], *self.rsem(i, h, 7 + k))

        if step == 0:
            self.go(T5.at[rd, :, 1 - self.b], self.R.at[rd], *self.rsem(i, h, 0), self.sibling)
        elif step == 1:
            self.landed(self.R.at[rd], *self.rsem(i, h, 0))
            mine, theirs = T5.at[rd, :, self.b], self.R.at[rd]
            n = mine.shape[0]

            def both(r, carry):
                q = lax.div(r, 4)
                w = lax.rem(r, 4)
                for k in range(4):
                    mine[q, w, k] = mine[q, w, k] + theirs[q, w, k]
                return carry

            lax.fori_loop(0, 4 * n, both, 0)
            send_a(0, 2, 0, 1)
            send_a(1, 2, 1, 3)
            send_a(2, 1, 1, 1)
            send_a(3, 3, 0, 3)
        elif step == 2:
            wait_a(0)
            self.add(self.row(i, h, 1, p=0), self.RA.at[0, rd], inner=2)
            send_a(4, 1, 0, 1)
            wait_a(1)
            self.add(self.row(i, h, 3, p=1), self.RA.at[1, rd], inner=2)
            send_a(5, 3, 1, 3)
        elif step == 3:
            for k in (2, 3, 4, 5):
                wait_a(k)
            self.add(self.row(i, h, 0, p=0), self.RA.at[3, rd], self.RA.at[4, rd], inner=2)
            self.add(self.row(i, h, 0, p=1), self.RA.at[2, rd], self.RA.at[5, rd], inner=2)
            send_b(0, 2, 0, 1)
            send_b(1, 2, 1, 3)
            send_b(2, 1, 1, 1)
            send_b(3, 3, 0, 3)
        elif step == 4:
            wait_b(0)
            self.add(self.cell(i, h, 1, 0), self.RB.at[0, rd])
            send_b(4, 1, 0, 1)
            wait_b(1)
            self.add(self.cell(i, h, 3, 1), self.RB.at[1, rd])
            send_b(5, 3, 1, 3)
        else:
            for k in (2, 3, 4, 5):
                wait_b(k)
            self.add(self.cell(i, h, 0, 0), self.RB.at[3, rd], self.RB.at[4, rd])
            self.add(self.cell(i, h, 0, 1), self.RB.at[2, rd], self.RB.at[5, rd])


def start_gather(links, w_ref, patch_ref, labels_ref, counts_ref, T, patch_in, meta_in, meta_ref, flat, headrows, lob, hib, rlo, rhi, slot, local_sem, x_send, x_recv, u_send, u_recv):
    xl, b, z, a, y = links.xl, links.b, links.z, links.a, links.y
    fs = z * 8 + a * 4 + y
    swap = a != b
    xo = lax.rem(xl + a + b, 2)
    holder = z * 8 + b * 4 + y
    up = flat_device(xl, b, lax.rem(fs + 1, NSLOT))
    down = flat_device(xl, b, lax.rem(fs + NSLOT - 1, NSLOT))
    mirror = device(xl, b, a, z, y)
    load = pltpu.make_async_copy(w_ref, flat.at[pl.ds(MARGIN, SHARD)], local_sem.at[0])
    load.start()
    barrier = pltpu.get_barrier_semaphore()
    total = (counts_ref[0] + counts_ref[1]).astype(jnp.float32)
    for m in range(2):
        valid = jnp.full((1, 128), jnp.where(fs < counts_ref[m], 1.0, 0.0), jnp.float32)
        meta_ref[m : m + 1, :] = jnp.full((1, 128), labels_ref[m].astype(jnp.float32), jnp.float32)
        meta_ref[2 + m : 3 + m, :] = valid / jnp.full((1, 128), total, jnp.float32)
        meta_ref[4 + m : 5 + m, :] = valid
    meta_ref[6:8, :] = jnp.zeros((2, 128), jnp.float32)

    def greet(target):
        pl.semaphore_signal(barrier, inc=1, device_id=target, device_id_type=MESH)

    for target in (up, down, links.at_y(1), links.at_y(3), links.at_z(1), links.at_z(3), links.sibling):
        greet(target)

    @pl.when(swap)
    def _():
        greet(mirror)

    own_index = lax.rem(fs * 11, NSLOT)
    keeps = jnp.logical_and(a == b, own_index < ROUNDS)

    def greet_source(j, carry):
        s = lax.div(32 * j + holder, ROUNDS)
        sa = lax.rem(lax.div(s, 4), 2)

        @pl.when(jnp.logical_not(jnp.logical_and(keeps, s == fs)))
        def _():
            greet(device(lax.rem(xl + sa + a, 2), sa, a, lax.div(s, 8), lax.rem(s, 4)))

        return carry

    lax.fori_loop(0, ROUNDS, greet_source, 0)
    pl.semaphore_wait(barrier, 7 + ROUNDS + jnp.where(swap, 1, 0) - jnp.where(keeps, 1, 0))
    load.wait()

    def remote(src, dst, k, target):
        return pltpu.make_async_remote_copy(src_ref=src, dst_ref=dst, send_sem=x_send.at[k], recv_sem=x_recv.at[k], device_id=target, device_id_type=MESH)

    hib[...] = flat[pl.ds(MARGIN + SHARD - HI, HI), :].astype(jnp.bfloat16)
    to_up = remote(hib, rlo, 0, up)
    to_up.start()
    lob[...] = flat[pl.ds(MARGIN, LO), :].astype(jnp.bfloat16)
    to_down = remote(lob, rhi, 1, down)
    to_down.start()
    patch_swap = remote(patch_ref, patch_in, 2, mirror)
    meta_swap = remote(meta_ref, meta_in, 3, mirror)
    patch_keep = pltpu.make_async_copy(patch_ref, patch_in, local_sem.at[1])
    meta_keep = pltpu.make_async_copy(meta_ref, meta_in, local_sem.at[2])
    first = ROUNDS * fs
    origin = SHARD * fs - MARGIN

    def unit_copy(i):
        k = first + i
        d = lax.rem(k, 32)
        src = slot.at[pl.ds(UNIT * i, UNIT)]
        dst = T.at[pl.ds(UNIT * k, UNIT)]
        target = device(xo, b, lax.rem(lax.div(d, 4), 2), lax.div(d, 8), lax.rem(d, 4))
        mine = jnp.logical_and(keeps, i == own_index)
        away = pltpu.make_async_remote_copy(src_ref=src, dst_ref=dst, send_sem=u_send.at[i], recv_sem=u_recv.at[lax.div(k, 32)], device_id=target, device_id_type=MESH)
        return mine, away, (src, dst)

    def send_unit(i):
        mine, away, (src, dst) = unit_copy(i)

        @pl.when(mine)
        def _():
            pltpu.make_async_copy(src, dst, local_sem.at[3]).start()

        @pl.when(jnp.logical_not(mine))
        def _():
            away.start()

    lane = lax.broadcasted_iota(jnp.int32, (8, 128), 1)

    def head_group(g, base, per, start):
        row = base + per * g - origin
        for i in range(16):
            q, s = divmod(1000 * i, 128)
            one = flat[pl.ds(row + q, 8), :]
            if s:
                two = flat[pl.ds(row + q + 1, 8), :]
                one = jnp.where(lane < 128 - s, pltpu.roll(one, 128 - s, 1), pltpu.roll(two, 128 - s, 1))
            headrows[pl.ds(i * 8, 8), :] = one
        for j in range(8):
            t = start + g * 8 + j - UNIT * first

            @pl.when(jnp.logical_and(t >= 0, t < SLOT))
            def _():
                slot[t] = headrows[pl.ds(j, 16, stride=8), :].astype(jnp.bfloat16)

    def inside(row, rows):
        return jnp.logical_and(row >= MARGIN, row + rows <= MARGIN + SHARD)

    def convert(near):
        for index, (base, c, groups, per, start) in enumerate(SECTIONS):
            lo = jnp.maximum(UNIT * first, start)
            hi = jnp.minimum(UNIT * first + SLOT, start + c * groups)
            if index == 1:

                def group(g, carry):
                    @pl.when(inside(base + per * g - origin, per + 1) == near)
                    def _():
                        head_group(g, base, per, start)

                    return carry

                lax.fori_loop(lax.div(jnp.maximum(lo, start) - start, 8), lax.div(jnp.maximum(hi, start) - start + 7, 8), group, 0)
                if not near:

                    def deal(u, carry):
                        send_unit(u - first)
                        return carry

                    lax.fori_loop(lax.div(lo, UNIT), lax.div(hi, UNIT), deal, 0)
            else:

                def unit(u, carry):
                    t = UNIT * u - start
                    g = lax.div(t, c)
                    row = base + 16 * c * g + lax.rem(t, c) - origin

                    @pl.when(inside(row, 15 * c + UNIT) == near)
                    def _():
                        for k in range(UNIT):
                            slot[UNIT * (u - first) + k] = flat[pl.ds(row + k, 16, stride=c), :].astype(jnp.bfloat16)
                        send_unit(u - first)

                    return carry

                lax.fori_loop(lax.div(lo, UNIT), lax.div(hi, UNIT), unit, 0)

    convert(True)
    to_up.wait_recv()
    flat[pl.ds(MARGIN - HI, HI), :] = rlo[...].astype(jnp.float32)
    to_down.wait_recv()
    flat[pl.ds(MARGIN + SHARD, LO), :] = rhi[...].astype(jnp.float32)
    convert(False)

    @pl.when(fs == NSLOT - 1)
    def _():
        slot[pl.ds(SLOT - 12, 12)] = jnp.zeros((12, 16, 128), jnp.bfloat16)
        send_unit(ROUNDS - 2)
        send_unit(ROUNDS - 1)

    @pl.when(swap)
    def _():
        patch_swap.start()
        meta_swap.start()

    @pl.when(jnp.logical_not(swap))
    def _():
        patch_keep.start()
        meta_keep.start()

    def units_here(i):
        def wait(j, carry):
            place = T.at[pl.ds(UNIT * (32 * j + holder), UNIT)]
            mine = jnp.logical_and(keeps, lax.div(32 * j + holder, ROUNDS) == fs)

            @pl.when(mine)
            def _():
                pltpu.make_async_copy(place, place, local_sem.at[3]).wait()

            @pl.when(jnp.logical_not(mine))
            def _():
                pltpu.make_async_remote_copy(src_ref=place, dst_ref=place, send_sem=u_send.at[0], recv_sem=u_recv.at[j], device_id=links.sibling, device_id_type=MESH).wait_recv()

            return carry

        lax.fori_loop(*STAGES[i], wait, 0)

    def finish_start():
        def wait(i, carry):
            mine, away, unused = unit_copy(i)

            @pl.when(jnp.logical_not(mine))
            def _():
                away.wait_send()

            return carry

        lax.fori_loop(0, ROUNDS, wait, 0)
        to_up.wait_send()
        to_down.wait_send()

        @pl.when(swap)
        def _():
            patch_swap.wait()
            meta_swap.wait()

        @pl.when(jnp.logical_not(swap))
        def _():
            patch_keep.wait()
            meta_keep.wait()

    return units_here, finish_start


D = 768
HEADS = 12
HEAD_DIM = 64
FF = 3072
CLS = 1000
P_SIZE = 196
ROWS = 208
TOK = 2 * ROWS
NORM_EPS = 1e-06
SMOOTHING = 0.1
NTILES = 4224
T_E, T_HEAD, T_NORM, T_QKV, T_OUT, T_IN, T_FO = 0, 366, 750, 756, 1620, 1908, 3060
T_POS = 288
BLK = 256
BLOCKS = ((0, 96), (96, 112), (208, 96), (304, 112))
F32 = jnp.float32
BF16 = jnp.bfloat16
ROOT_HALF = 0.7071067811865476
INV_ROOT_TWO_PI = 0.3989422804014327


def dot(x, w):
    return lax.dot_general(x, w, (((1,), (0,)), ((), ())), preferred_element_type=F32)


def dot_t(x, w):
    return lax.dot_general(x, w, (((1,), (1,)), ((), ())), preferred_element_type=F32)


def t_dot(x, w):
    return lax.dot_general(x, w, (((0,), (0,)), ((), ())), preferred_element_type=F32)


def stats(x, keep, r, k):
    mean = jnp.sum(x, -1, keepdims=True) * (1.0 / D)
    centred = x - mean
    var = jnp.sum(centred * centred, -1, keepdims=True) * (1.0 / D)
    rstd = lax.rsqrt(var + NORM_EPS)
    keep[r, k : k + 1] = mean
    keep[r, k + 1 : k + 2] = rstd
    return centred * rstd


def kept(x, keep, r, k):
    rstd = keep[r, k + 1 : k + 2]
    return (x - keep[r, k : k + 1]) * rstd, rstd


def norm_back(d_hat, hat, rstd):
    m1 = jnp.sum(d_hat, -1, keepdims=True) * (1.0 / D)
    m2 = jnp.sum(d_hat * hat, -1, keepdims=True) * (1.0 / D)
    return rstd * (d_hat - m1 - hat * m2)


def compute(step, patch_ref, meta_ref, loss_ref, T, x, h, a, at, mix, prob, o, h1, a2, hid, slope, h2, dh, dyb, keep):
    G = T
    dmix = mix

    def section(ref, start, c, groups):
        return ref.at[pl.ds(start, groups * c)].reshape(groups, c, 16, 128)

    def cols(start, c, groups, j):
        part = section(T, start, c, groups)
        return jnp.concatenate([part[:, 2 * j + k].reshape(groups * 16, 128) for k in range(2)], axis=1)

    def put_cols(start, c, groups, j, value):
        low = value.astype(BF16)
        part = section(G, start, c, groups)
        for k in range(2):
            part[:, 2 * j + k] = low[:, k * 128 : (k + 1) * 128].reshape(groups, 16, 128)

    def row_of(start, k):
        return jnp.concatenate([T[start + j][k : k + 1, :] for j in range(6)], axis=1).astype(F32)

    def lanes(j):
        return pl.ds(pl.multiple_of(j * BLK, BLK), BLK)

    step("start")
    for i in range(2):
        x[pl.ds(i * ROWS, 192), :] = patch_ref[i, pl.ds(0, 192), :]
        x[pl.ds(i * ROWS + 192, 16), :] = jnp.concatenate([patch_ref[i, pl.ds(192, 4), :], jnp.zeros((12, D), BF16)], axis=0)

    real = lax.broadcasted_iota(jnp.int32, (ROWS, 128), 0) < P_SIZE
    for j in range(3):
        acc = dot(x[...], cols(T_E, 6, 48, j))
        p = cols(T_POS, 6, 13, j).astype(F32)
        p = jnp.where(lax.broadcasted_iota(jnp.int32, (ROWS, BLK), 0) < P_SIZE, p, 0.0)
        for i in range(2):
            h[pl.ds(i * ROWS, ROWS), pl.ds(j * BLK, BLK)] = acc[i * ROWS : (i + 1) * ROWS] + p

    step("embedded")
    gain1, shift1, gain2, shift2 = (row_of(T_NORM, k) for k in range(4))

    for at_row, n in BLOCKS:
        r = pl.ds(at_row, n)
        a[r, :] = (stats(h[r, :], keep, r, 0) * gain1 + shift1).astype(BF16)

    step("qkv")
    def wide_cols(start, c, groups, j):
        return jnp.concatenate([cols(start, c, groups, 3 * j + k) for k in range(3)], axis=1)

    def wide_lanes(j):
        return pl.ds(pl.multiple_of(j * D, D), D)

    def mix_block(j, carry):
        mix[:, wide_lanes(j)] = dot(a[...], wide_cols(T_QKV, 18, 48, j)).astype(BF16)
        return carry

    lax.fori_loop(0, 3, mix_block, 0)

    first_half = lax.broadcasted_iota(jnp.int32, (ROWS, 128), 1) < HEAD_DIM
    key_ok = lax.broadcasted_iota(jnp.int32, (ROWS, ROWS), 0) < P_SIZE
    first_rows = lax.broadcasted_iota(jnp.int32, (128, ROWS), 0) < HEAD_DIM
    halves = (first_half, jnp.logical_not(first_half))
    zero = jnp.zeros((ROWS, 128), BF16)

    def split(block):
        return jnp.concatenate([jnp.where(first_half, block, zero), jnp.where(first_half, zero, block)], axis=0)

    def heads_of(p, i):
        r = pl.ds(i * ROWS, ROWS)
        return r, [pl.ds(pl.multiple_of(p * 128 + D * k, 128), 128) for k in range(3)]

    def attend(p, carry):
        for i in range(2):
            r, ls = heads_of(p, i)
            q, k, v = (mix[r, l] for l in ls)
            q = q * jnp.asarray(0.125, BF16)
            vt = v.T
            outs = []
            for e in range(2):
                s = dot_t(jnp.where(halves[e], k, zero), q)
                s = jnp.where(key_ok, s, -jnp.inf)
                ex = jnp.exp(s - jnp.max(s, 0, keepdims=True))
                pr = (ex * (1.0 / jnp.sum(ex, 0, keepdims=True))).astype(BF16)
                prob[p * 2 + i, e] = pr
                outs.append(dot(vt, pr))
            o[r, ls[0]] = jnp.where(first_rows, outs[0], outs[1]).astype(BF16).T
        return carry

    parts = ((0, 2), (2, 3), (3, 5), (5, 6))
    for part in range(4):
        step("attend%d" % part)
        lax.fori_loop(*parts[part], attend, 0)
    step("attended")
    for j in range(3):
        h1[:, pl.ds(j * BLK, BLK)] = h[:, pl.ds(j * BLK, BLK)] + dot(o[...], cols(T_OUT, 6, 48, j))

    for at_row, n in BLOCKS:
        r = pl.ds(at_row, n)
        a2[r, :] = (stats(h1[r, :], keep, r, 2) * gain2 + shift2).astype(BF16)

    step("up")
    def up_block(j, carry):
        u = dot(a2[...], wide_cols(T_IN, 24, 48, j))
        phi = 0.5 * (1.0 + lax.erf(u * ROOT_HALF))
        pdf = jnp.exp(-0.5 * u * u) * INV_ROOT_TWO_PI
        hid[:, wide_lanes(j)] = (u * phi).astype(BF16)
        slope[:, wide_lanes(j)] = (phi + u * pdf).astype(BF16)
        return carry

    lax.fori_loop(0, 4, up_block, 0)
    step("down")
    for j in range(3):
        h2[:, pl.ds(j * BLK, BLK)] = h1[:, pl.ds(j * BLK, BLK)] + dot(hid[...], cols(T_FO, 6, 192, j))

    step("pool")
    gain_end, shift_end = (row_of(T_POS + 72, 4 + k) for k in range(2))
    means = []
    last_rows = lax.broadcasted_iota(jnp.int32, (112, D), 0) < P_SIZE - 96
    for i in range(2):
        total = jnp.zeros((8, D), F32)
        for at_row, n in BLOCKS[2 * i : 2 * i + 2]:
            r = pl.ds(at_row, n)
            hat = stats(h2[r, :], keep, r, 4)
            if n == 112:
                hat = jnp.where(last_rows, hat, 0.0)
            total = total + jnp.sum(hat.reshape(n // 8, 8, D), 0)
        means.append(jnp.sum(total, 0, keepdims=True) * (1.0 / P_SIZE))
    mean_hat = jnp.concatenate(means + [jnp.zeros((14, D), F32)], axis=0)
    two = lax.broadcasted_iota(jnp.int32, (16, D), 0) < 2
    pooled = jnp.where(two, mean_hat * gain_end + shift_end, 0.0).astype(BF16)
    logits = jnp.concatenate([dot(pooled, cols(T_HEAD, 8, 48, j)) for j in range(4)], axis=1)
    lane = lax.broadcasted_iota(jnp.int32, (16, 1024), 1)
    lane_f = lane.astype(F32)
    inside = lane < CLS
    logits = jnp.where(inside, logits, -1e30)
    top = jnp.max(logits, -1, keepdims=True)
    total = jnp.sum(jnp.where(inside, jnp.exp(logits - top), 0.0), -1, keepdims=True)
    logp = logits - top - jnp.log(total)
    meta = meta_ref[...]
    pad14 = jnp.zeros((14, 1), F32)
    label = jnp.concatenate([meta[0:2, 0:1], pad14], axis=0)
    scale = jnp.concatenate([meta[2:4, 0:1], pad14], axis=0)
    valid = jnp.concatenate([meta[4:6, 0:1], pad14], axis=0)
    target = jnp.where(lane_f == label, 1.0 - SMOOTHING, 0.0) + SMOOTHING / CLS
    values = -jnp.sum(jnp.where(inside, target * logp, 0.0), -1, keepdims=True)
    loss_ref[...] = jnp.broadcast_to(jnp.sum(values * valid, 0, keepdims=True), (8, 128))
    d_logits = jnp.where(inside, scale * (jnp.exp(logp) - target), 0.0).astype(BF16)
    d_pooled = jnp.zeros((16, D), F32)
    for j in range(4):
        w = cols(T_HEAD, 8, 48, j)
        d_pooled = d_pooled + dot_t(d_logits[:, j * BLK : (j + 1) * BLK], w)
        put_cols(T_HEAD, 8, 48, j, t_dot(pooled, d_logits[:, j * BLK : (j + 1) * BLK]))
    d_gain_end = jnp.sum(d_pooled * mean_hat, 0, keepdims=True)
    d_shift_end = jnp.sum(d_pooled, 0, keepdims=True)
    for i in range(2):
        d_hat = d_pooled[i : i + 1, :] * (1.0 / P_SIZE) * gain_end

        m1 = jnp.sum(d_hat, -1, keepdims=True) * (1.0 / D)
        for at_row, n in BLOCKS[2 * i : 2 * i + 2]:
            r = pl.ds(at_row, n)
            hat, rstd = kept(h2[r, :], keep, r, 4)
            m2 = jnp.sum(d_hat * hat, -1, keepdims=True) * (1.0 / D)
            d = rstd * ((d_hat - m1) - hat * m2)
            if n == 112:
                d = jnp.where(last_rows, d, 0.0)
            dh[r, :] = d
            dyb[r, :] = d.astype(BF16)

    step("backward")
    at[...] = a2[...].T
    da = h2

    wide = D // 16

    def down_block(j, carry):
        part = section(T, T_FO + j * wide * 6, 6, wide)
        w = jnp.concatenate([part[:, k].reshape(D, 128) for k in range(6)], axis=1)
        dy = dyb[...]
        d_w = t_dot(hid[:, wide_lanes(j)], dy).astype(BF16)
        hid[:, wide_lanes(j)] = (dot_t(dy, w) * slope[:, wide_lanes(j)].astype(F32)).astype(BF16)
        for k in range(6):
            part[:, k] = d_w[:, k * 128 : (k + 1) * 128].reshape(wide, 16, 128)
        return carry

    G[pl.ds(4212, 12)] = jnp.zeros((12, 16, 128), BF16)
    lax.fori_loop(0, 3, down_block, 0)
    step("fc_out0")
    lax.fori_loop(3, 4, down_block, 0)
    step("fc_out1")
    def row_block(start, c, j):
        part = section(T, start + j * 16 * c, c, 16)
        return jnp.concatenate([part[:, k].reshape(BLK, 128) for k in range(c)], axis=1)

    def put_rows(start, c, j, first, value):
        part = section(G, start + j * 16 * c, c, 16)
        low = value.astype(BF16)
        for k in range(value.shape[1] // 128):
            part[:, first + k] = low[:, k * 128 : (k + 1) * 128].reshape(16, 16, 128)

    for j in range(3):
        da[:, pl.ds(j * BLK, BLK)] = dot_t(hid[...], row_block(T_IN, 24, j))
    step("fc_in0")
    for j in range(3):
        for k in range(4):
            put_rows(T_IN, 24, j, 6 * k, dot(at[pl.ds(j * BLK, BLK), :], hid[:, pl.ds(k * D, D)]))
        step("fc_in%d" % (j + 1))

    def norm_grads(inputs, column, gain):
        dg, ds = jnp.zeros((8, D), F32), jnp.zeros((8, D), F32)
        for at_row, n in BLOCKS:
            r = pl.ds(at_row, n)
            hat, rstd = kept(inputs[r, :], keep, r, column)
            d = da[r, :]
            new = dh[r, :] + norm_back(d * gain, hat, rstd)
            dh[r, :] = new
            dyb[r, :] = new.astype(BF16)
            dg = dg + jnp.sum((d * hat).reshape(n // 8, 8, D), 0)
            ds = ds + jnp.sum(d.reshape(n // 8, 8, D), 0)
        return dg, ds

    d_gain2, d_shift2 = norm_grads(h1, 2, gain2)

    step("normed2")
    at[...] = o[...].T
    for j in range(3):
        o[:, pl.ds(j * BLK, BLK)] = dot_t(dyb[...], row_block(T_OUT, 6, j)).astype(BF16)
    for j in range(3):
        put_rows(T_OUT, 6, j, 0, dot(at[pl.ds(j * BLK, BLK), :], dyb[...]))

    step("out")
    def attend_back(p, carry):
        for i in range(2):
            r, ls = heads_of(p, i)
            q, k, v = (mix[r, l] for l in ls)
            q = q * jnp.asarray(0.125, BF16)
            k8 = k * jnp.asarray(0.125, BF16)
            kt = k8.T
            do = o[r, ls[0]]
            pr = prob[p * 2 + i]
            dv = dot(pr.reshape(TOK, ROWS), do)
            dp = dot_t(split(v), do).reshape(2, ROWS, ROWS)
            prf = pr.astype(F32)
            row = jnp.sum(prf * dp, 1, keepdims=True)
            ds = (prf * (dp - row)).astype(BF16)
            dq = [dot(kt[HEAD_DIM * e : HEAD_DIM * (e + 1)], ds[e]) for e in range(2)]
            dk = dot(ds.reshape(TOK, ROWS), q)
            dmix[r, ls[0]] = jnp.concatenate(dq, axis=0).astype(BF16).T
            dmix[r, ls[1]] = jnp.where(first_half, dk[:ROWS], dk[ROWS:]).astype(BF16)
            dmix[r, ls[2]] = jnp.where(first_half, dv[:ROWS], dv[ROWS:]).astype(BF16)
        return carry

    for part in range(4):
        lax.fori_loop(*parts[part], attend_back, 0)
        step("back%d" % part)

    at[...] = a[...].T
    for j in range(3):
        da[:, pl.ds(j * BLK, BLK)] = dot_t(dmix[...], row_block(T_QKV, 18, j))
    for j in range(3):
        for k in range(3):
            put_rows(T_QKV, 18, j, 6 * k, dot(at[pl.ds(j * BLK, BLK), :], dmix[:, pl.ds(k * D, D)]))
    step("qkv_back")
    d_gain1, d_shift1 = norm_grads(h, 0, gain1)
    d_norms = jnp.concatenate([jnp.sum(d, 0, keepdims=True) for d in (d_gain1, d_shift1, d_gain2, d_shift2)] + [jnp.zeros((12, D), F32)], axis=0).astype(BF16)
    for j in range(6):
        G[T_NORM + j] = d_norms[:, j * 128 : (j + 1) * 128]
    step("norms")
    at[...] = x[...].T
    row_id = lax.broadcasted_iota(jnp.int32, (ROWS, BLK), 0)
    for j in range(3):
        put_cols(T_E, 6, 48, j, dot(at[...], dyb[:, pl.ds(j * BLK, BLK)]))
        c = pl.ds(j * BLK, BLK)
        s = slice(j * BLK, (j + 1) * BLK)
        d_pos = dh[pl.ds(0, ROWS), c] + dh[pl.ds(ROWS, ROWS), c]
        d_pos = jnp.where(row_id < P_SIZE, d_pos, 0.0)
        d_pos = jnp.where(row_id == P_SIZE, jnp.broadcast_to(d_gain_end[:, s], (ROWS, BLK)), d_pos)
        d_pos = jnp.where(row_id == P_SIZE + 1, jnp.broadcast_to(d_shift_end[:, s], (ROWS, BLK)), d_pos)
        put_cols(T_POS, 6, 13, j, d_pos)
    step("embed")


FORWARD = {
    "start": ((0, 0), (1, 0), (0, 1), (0, 2), (1, 1), (2, 0), (0, 3), (1, 2), (0, 4), (2, 1), (3, 0), (0, 5)),
    "embedded": ((1, 3), (2, 2), (3, 1)),
    "qkv": ((1, 4), (1, 5), (3, 2)),
    "attend0": ((2, 3),),
    "attend1": ((3, 3), (2, 4)),
    "attend2": ((3, 4),),
    "up": ((2, 5),),
    "down": ((3, 5),),
}
BACKWARD = {
    "fc_out0": ((3, 0, 0),),
    "fc_out1": ((3, 1, 0), (3, 0, 1)),
    "fc_in0": ((3, 1, 1),),
    "fc_in2": ((2, 0, 0),),
    "fc_in3": ((2, 1, 0), (2, 0, 1)),
    "normed2": ((2, 1, 1),),
    "out": ((3, 0, 2), (3, 1, 2)),
    "back3": ((2, 0, 2), (2, 1, 2)),
    "qkv_back": ((1, 0, 0), (1, 1, 0), (1, 0, 1), (1, 1, 1), (3, 0, 3), (3, 1, 3)),
    "norms": ((0, 1, 0),),
    "embed": (
        (0, 0, 0), (0, 1, 1), (0, 0, 1), (2, 0, 3), (2, 1, 3), (1, 0, 2), (1, 1, 2), (3, 0, 4), (3, 1, 4), (0, 1, 2), (0, 0, 2), (2, 0, 4), (2, 1, 4),
        (1, 0, 3), (1, 1, 3), (3, 0, 5), (3, 1, 5), (0, 1, 3), (0, 0, 3), (2, 0, 5), (2, 1, 5), (1, 0, 4), (1, 1, 4), (0, 1, 4), (0, 0, 4), (1, 0, 5), (1, 1, 5), (0, 1, 5), (0, 0, 5),
    ),
}


def grads_kernel(w_ref, patch_ref, labels_ref, counts_ref, red_ref, loss_out, T, R, RA, RB, g_send, g_recv, r_send, r_recv, LS, l_send, l_recv, patch_in, meta_in, meta, loss, *rest):
    gather_refs, compute_refs, out_sem = rest[:12], rest[12:-1], rest[-1]
    links = Links(T, R, RA, RB, g_send, g_recv, r_send, r_recv)
    xl, b, z, a, y = links.xl, links.b, links.z, links.a, links.y
    swap = a != b
    mirror = device(xl, b, a, z, y)
    units_here, finish_start = start_gather(links, w_ref, patch_ref, labels_ref, counts_ref, T, patch_in, meta_in, meta, *gather_refs)

    def loss_send(src, dst, target):
        links.go(LS.at[src], LS.at[dst], l_send.at[dst], l_recv.at[dst], target)

    def loss_wait(*slots):
        for k in slots:
            links.landed(LS.at[k], l_send.at[k], l_recv.at[k])

    def loss_step(n):
        if n == 0:
            LS[0] = loss[...]
            loss_send(0, 1, links.sibling)
        elif n == 1:
            loss_wait(1)
            LS[8] = LS[0] + LS[1]
            loss_send(8, 2, links.at_y(1))
            loss_send(8, 3, links.at_y(3))
        elif n == 2:
            loss_wait(2, 3)
            loss_send(2, 4, links.at_y(1))
        elif n == 3:
            loss_wait(4)
            LS[9] = (LS[8] + LS[4]) + (LS[2] + LS[3])
            loss_send(9, 5, links.at_z(1))
            loss_send(9, 6, links.at_z(3))
        elif n == 4:
            loss_wait(5, 6)
            loss_send(5, 7, links.at_z(1))
        elif n == 5:
            loss_wait(7)
            LS[10] = (LS[9] + LS[7]) + (LS[5] + LS[6])

            @pl.when(swap)
            def _():
                loss_swap.start()

        else:

            @pl.when(swap)
            def _():
                loss_swap.wait()
                loss_out[...] = LS[11]

            @pl.when(jnp.logical_not(swap))
            def _():
                loss_out[...] = LS[10]

    loss_swap = pltpu.make_async_remote_copy(src_ref=LS.at[10], dst_ref=LS.at[11], send_sem=l_send.at[11], recv_sem=l_recv.at[11], device_id=mirror, device_id_type=MESH)
    losses = {"fc_out0": 0, "fc_in0": 1, "fc_in2": 2, "normed2": 3, "back0": 4, "back2": 5, "qkv_back": 6}

    def step(name):
        if name == "pool":
            links.sent()
        for item in FORWARD.get(name, ()):
            if item[1] == 0:
                units_here(item[0])
            links.gather_step(*item)
        if name == "start":
            finish_start()
        for item in BACKWARD.get(name, ()):
            links.reduce_step(*item)
        if name in losses:
            loss_step(losses[name])

    compute(step, patch_in, meta_in, loss, T, *compute_refs)
    mine = T.reshape(ROUNDS, 32, UNIT, 16, 128).at[:, z * 8 + b * 4 + y]
    out = pltpu.make_async_copy(mine, red_ref, out_sem)
    out.start()
    links.sent()
    out.wait()


def grads(weights, patches, labels, counts):
    hbm = pl.BlockSpec(memory_space=pl.ANY)
    vmem = pl.BlockSpec(memory_space=pltpu.VMEM)
    V = pltpu.VMEM
    dma = pltpu.SemaphoreType.DMA
    return pl.pallas_call(
        grads_kernel,
        out_shape=(jax.ShapeDtypeStruct((ROUNDS, UNIT, 16, 128), BF16), jax.ShapeDtypeStruct((8, 128), F32)),
        in_specs=[hbm] * 2 + [pl.BlockSpec(memory_space=pltpu.SMEM)] * 2,
        out_specs=(hbm, vmem),
        scratch_shapes=[
            V((NTILES, 16, 128), BF16),
            V((ROUNDS, 4, 4, UNIT, 16, 128), BF16),
            V((6, ROUNDS, 2, UNIT, 16, 128), BF16),
            V((6, ROUNDS, 3, 16, 128), BF16),
            dma((96,)),
            dma((96,)),
            dma((104,)),
            dma((104,)),
            V((12, 8, 128), F32),
            dma((12,)),
            dma((12,)),
            V(patches.shape, BF16),
            V((8, 128), F32),
            V((8, 128), F32),
            V((8, 128), F32),
            V((FROWS, 128), F32),
            V((128, 128), F32),
            V((LO, 128), BF16),
            V((HI, 128), BF16),
            V((HI, 128), BF16),
            V((LO, 128), BF16),
            V((SLOT, 16, 128), BF16),
            dma((4,)),
            dma((4,)),
            dma((4,)),
            dma((ROUNDS,)),
            dma((ROUNDS,)),
            V((TOK, D), BF16),
            V((TOK, D), F32),
            V((TOK, D), BF16),
            V((D, TOK), BF16),
            V((TOK, 3 * D), BF16),
            V((12, 2, ROWS, ROWS), BF16),
            V((TOK, D), BF16),
            V((TOK, D), F32),
            V((TOK, D), BF16),
            V((TOK, FF), BF16),
            V((TOK, FF), BF16),
            V((TOK, D), F32),
            V((TOK, D), F32),
            V((TOK, D), BF16),
            V((TOK, 128), F32),
            dma,
        ],
        compiler_params=pltpu.CompilerParams(collective_id=0, has_side_effects=True, vmem_limit_bytes=60 * 1024 * 1024),
        name="grads",
    )(weights, patches, labels, counts)


EDGE = 24
FRONT = 768
BACK_ROWS = FRONT + SHARD + 640 + 6
PADDED = 2112
STEP = 10
EDGE_UNITS = 4
WINDOW = ROUNDS + 2 * EDGE_UNITS
BETA_ONE = 0.9
BETA_TWO = 0.95
ADAM_EPS = 1e-08
DECAY = 0.05
INNER_RATE = 0.01
OUTER_RATE = 0.7
OUTER_MU = 0.9


def update_kernel(
    red_ref, first_ref, second_ref,
    sum_out, first_out, second_out,
    red, window, flat, headrows, first_row, second_row, first, second, upd, low, low2, pair, pair2, total, total2,
    load_sem, x_send, x_recv, o_send, e_send, w_recv,
):
    xl, b, z, a, y = coords()
    fs = z * 8 + a * 4 + y
    holder = z * 8 + b * 4 + y
    sibling = device(xl, a, 1 - b, z, y)
    across = device(1 - xl, a, b, z, y)
    extra = [pltpu.make_async_copy(src, dst, load_sem.at[i]) for i, (src, dst) in enumerate(((first_ref, first_row), (second_ref, second_row)))]
    load = pltpu.make_async_copy(red_ref, red, load_sem.at[4])
    load.start()
    for copy in extra:
        copy.start()

    barrier = pltpu.get_barrier_semaphore()

    def greet(target):
        pl.semaphore_signal(barrier, inc=1, device_id=target, device_id_type=MESH)

    greet(sibling)
    greet(across)
    first_unit = ROUNDS * fs - EDGE_UNITS

    def window_unit(p):
        k = first_unit + p
        d = lax.rem(k + 32, 32)
        inside = jnp.logical_and(k >= 0, k < 32 * ROUNDS)
        mine = jnp.logical_and(a == b, d == holder)
        return inside, mine, device(xl, b, lax.rem(lax.div(d, 4), 2), lax.div(d, 8), lax.rem(d, 4))

    def greet_holder(p, carry):
        inside, mine, source = window_unit(p)

        @pl.when(jnp.logical_and(inside, jnp.logical_not(mine)))
        def _():
            greet(source)

        return carry

    lax.fori_loop(0, WINDOW, greet_holder, 0)

    def held_unit(j):
        k = 32 * j + holder
        q = lax.div(k, ROUNDS)
        r = lax.rem(k, ROUNDS)
        shift = jnp.where(r < EDGE_UNITS, -1, jnp.where(r >= ROUNDS - EDGE_UNITS, 1, 0))
        near = jnp.logical_and(shift != 0, jnp.logical_and(q + shift >= 0, q + shift < NSLOT))
        return k, q, jnp.where(near, q + shift, q), near

    def to_owner(j, k, s, send):
        p = k - (ROUNDS * s - EDGE_UNITS)
        src = red.at[j]
        dst = window.at[pl.ds(UNIT * p, UNIT)]
        sa = lax.rem(lax.div(s, 4), 2)
        mine = jnp.logical_and(a == b, s == fs)
        target = device(xl, sa, a, lax.div(s, 8), lax.rem(s, 4))
        away = pltpu.make_async_remote_copy(src_ref=src, dst_ref=dst, send_sem=send.at[j], recv_sem=w_recv.at[p], device_id=target, device_id_type=MESH)
        here = pltpu.make_async_copy(src, dst, load_sem.at[10])
        return mine, away, here

    def count(j, n):
        k, q, s, near = held_unit(j)
        first_away = jnp.logical_not(jnp.logical_and(a == b, q == fs))
        second_away = jnp.logical_and(near, jnp.logical_not(jnp.logical_and(a == b, s == fs)))
        return n + jnp.where(first_away, 1, 0) + jnp.where(second_away, 1, 0)

    outgoing = lax.fori_loop(0, ROUNDS, count, 2)
    pl.semaphore_wait(barrier, outgoing)
    load.wait()

    def give(j, carry):
        k, q, s, near = held_unit(j)
        mine, away, here = to_owner(j, k, q, o_send)

        @pl.when(mine)
        def _():
            here.start()

        @pl.when(jnp.logical_not(mine))
        def _():
            away.start()

        mine2, away2, here2 = to_owner(j, k, s, e_send)

        @pl.when(jnp.logical_and(near, mine2))
        def _():
            here2.start()

        @pl.when(jnp.logical_and(near, jnp.logical_not(mine2)))
        def _():
            away2.start()

        return carry

    lax.fori_loop(0, ROUNDS, give, 0)

    def given(j, carry):
        k, q, s, near = held_unit(j)
        mine, away, here = to_owner(j, k, q, o_send)

        @pl.when(jnp.logical_not(mine))
        def _():
            away.wait_send()

        mine2, away2, here2 = to_owner(j, k, s, e_send)

        @pl.when(jnp.logical_and(near, jnp.logical_not(mine2)))
        def _():
            away2.wait_send()

        return carry

    def clear(i, carry):
        flat[pl.ds(pl.multiple_of(i * 32, 32), 32), :] = jnp.zeros((32, 128), F32)
        return carry

    lax.fori_loop(0, BACK_ROWS // 32, clear, 0)

    for copy in extra:
        copy.wait()
    for source, rows_of in ((first_row, first), (second_row, second)):

        def eight(i, carry):
            rows_of[pl.ds(pl.multiple_of(i * 8, 8), 8), :] = source[0, pl.ds(pl.multiple_of(i * 1024, 1024), 1024)].reshape(8, 128)
            return carry

        whole = SHARD // 8
        lax.fori_loop(0, whole, eight, 0, unroll=2)
        rows_of[pl.ds(whole * 8, SHARD - whole * 8), :] = source[0, pl.ds(whole * 1024, (SHARD - whole * 8) * 128)].reshape(SHARD - whole * 8, 128)

    def got(p, carry):
        inside, mine, source = window_unit(p)
        place = window.at[pl.ds(UNIT * p, UNIT)]

        @pl.when(jnp.logical_and(inside, mine))
        def _():
            pltpu.make_async_copy(place, place, load_sem.at[10]).wait()

        @pl.when(jnp.logical_and(inside, jnp.logical_not(mine)))
        def _():
            pltpu.make_async_remote_copy(src_ref=place, dst_ref=place, send_sem=x_send.at[0], recv_sem=w_recv.at[p], device_id=sibling, device_id_type=MESH).wait_recv()

        return carry

    lax.fori_loop(0, WINDOW, got, 0)
    sends = []

    def go(src, dst, send, recv, k, target):
        copy = pltpu.make_async_remote_copy(src_ref=src, dst_ref=dst, send_sem=send.at[k], recv_sem=recv.at[k], device_id=target, device_id_type=MESH)
        copy.start()
        sends.append(copy)

    def arrive(dst, recv, k):
        pltpu.make_async_remote_copy(src_ref=dst, dst_ref=dst, send_sem=x_send.at[k], recv_sem=recv.at[k], device_id=sibling, device_id_type=MESH).wait_recv()

    low_tile = SLOT * fs - EDGE
    high_tile = SLOT * fs + SLOT + EDGE
    origin = SHARD * fs - FRONT
    for index, (base, c, groups, per, start) in enumerate(SECTIONS):
        if index == 1:
            lane = lax.broadcasted_iota(jnp.int32, (8, 128), 1)
            g0 = lax.div(jnp.maximum(SHARD * fs - base, 0), per)
            g1 = lax.div(jnp.maximum(SHARD * (fs + 1) - base, 0) + per - 1, per)

            def head_group(g, carry):
                t = start + g * 8 - low_tile
                for j in range(8):
                    headrows[pl.ds(j, 16, stride=8), :] = window[t + j].astype(F32)
                row = base + per * g - origin
                for i in range(16):
                    q, s = divmod(1000 * i, 128)
                    value = headrows[pl.ds(i * 8, 8), :]
                    if s:
                        value = pltpu.roll(value, s, 1)
                        flat[pl.ds(row + q, 8), :] += jnp.where(lane >= s, value, 0.0)
                        flat[pl.ds(row + q + 1, 8), :] += jnp.where(lane < s, value, 0.0)
                    else:
                        flat[pl.ds(row + q, 8), :] += value
                return carry

            lax.fori_loop(jnp.minimum(g0, groups), jnp.minimum(g1, groups), head_group, 0)
        else:

            def unit(n, carry):
                t = UNIT * n - start
                row = base + 16 * c * lax.div(t, c) + lax.rem(t, c) - origin
                for m in range(UNIT):
                    flat[pl.ds(row + m, 16, stride=c), :] = window[UNIT * n - low_tile + m].astype(F32)
                return carry

            lax.fori_loop(lax.div(jnp.maximum(low_tile, start), UNIT), lax.div(jnp.minimum(high_tile, start + c * groups), UNIT), unit, 0)

    fix_one = 1.0 / (1.0 - BETA_ONE**STEP)
    fix_two = 1.0 / (1.0 - BETA_TWO**STEP)

    def in_rows(fn, lo, hi, step=32):
        def body(i, carry):
            fn(pl.multiple_of(i * step, step), step)
            return carry

        n = (hi - lo) // step
        lax.fori_loop(lo // step, lo // step + n, body, 0)
        if lo + n * step < hi:
            fn(lo + n * step, hi - lo - n * step)

    def adam(r, n):
        grad = flat[pl.ds(FRONT + r, n), :]
        m = BETA_ONE * first[pl.ds(r, n), :] + (1.0 - BETA_ONE) * grad
        s = BETA_TWO * second[pl.ds(r, n), :] + (1.0 - BETA_TWO) * grad * grad
        first[pl.ds(r, n), :] = m
        second[pl.ds(r, n), :] = s
        u = (m * fix_one) / (jnp.sqrt(s * fix_two) + ADAM_EPS)
        upd[pl.ds(r, n), :] = u

    in_rows(adam, 0, SHARD)
    upd[pl.ds(SHARD, PADDED - SHARD), :] = jnp.zeros((PADDED - SHARD, 128), F32)
    outs = [pltpu.make_async_copy(src, dst, load_sem.at[5 + i]) for i, (src, dst) in enumerate(((first, first_out), (second, second_out)))]
    for copy in outs:
        copy.start()

    def lower(r, n):
        low[pl.ds(r, n), :] = upd[pl.ds(r, n), :].astype(BF16)

    in_rows(lower, 0, PADDED)
    go(low, low2, x_send, x_recv, 0, sibling)
    arrive(low2, x_recv, 0)
    half = PADDED // 2

    def pairs(r, n):
        at = pl.ds(pl.multiple_of(b * half + r, 16), n)
        pair[pl.ds(r, n), :] = low[at, :] + low2[at, :]

    in_rows(pairs, 0, half)
    go(pair, pair2, x_send, x_recv, 1, across)
    arrive(pair2, x_recv, 1)

    def fours(r, n):
        total[pl.ds(r, n), :] = pair[pl.ds(r, n), :].astype(F32) + pair2[pl.ds(r, n), :].astype(F32)

    in_rows(fours, 0, half)
    go(total, total2, x_send, x_recv, 2, sibling)

    arrive(total2, x_recv, 2)
    other = half - b * half
    final = [(total, sum_out.at[pl.ds(pl.multiple_of(b * half, 16), half)]), (total2, sum_out.at[pl.ds(pl.multiple_of(other, 16), half)])]
    final = [pltpu.make_async_copy(src, dst, load_sem.at[7 + i]) for i, (src, dst) in enumerate(final)]
    for copy in final:
        copy.start()
    for copy in sends:
        copy.wait_send()
    lax.fori_loop(0, ROUNDS, given, 0)
    for copy in outs + final:
        copy.wait()


def update(red, first, second):
    hbm = pl.BlockSpec(memory_space=pl.ANY)
    V = pltpu.VMEM
    flat = jax.ShapeDtypeStruct((SHARD, 128), F32)
    dma = pltpu.SemaphoreType.DMA
    return pl.pallas_call(
        update_kernel,
        out_shape=(jax.ShapeDtypeStruct((PADDED, 128), F32), flat, flat),
        in_specs=[hbm] * 3,
        out_specs=(hbm,) * 3,
        scratch_shapes=[
            V((ROUNDS, UNIT, 16, 128), BF16),
            V((EDGE + SLOT + EDGE, 16, 128), BF16),
            V((BACK_ROWS, 128), F32),
            V((128, 128), F32),
            V((1, SHARD * 128), F32),
            V((1, SHARD * 128), F32),
            V((SHARD, 128), F32),
            V((SHARD, 128), F32),
            V((PADDED, 128), F32),
            V((PADDED, 128), BF16),
            V((PADDED, 128), BF16),
            V((PADDED // 2, 128), BF16),
            V((PADDED // 2, 128), BF16),
            V((PADDED // 2, 128), F32),
            V((PADDED // 2, 128), F32),
            dma((11,)),
            dma((3,)),
            dma((3,)),
            dma((ROUNDS,)),
            dma((ROUNDS,)),
            dma((WINDOW,)),
        ],
        compiler_params=pltpu.CompilerParams(collective_id=1, has_side_effects=True, vmem_limit_bytes=60 * 1024 * 1024),
        name="update",
    )(red, first, second)


def finish_kernel(
    sum_ref, w_ref, mom_ref, first_ref, second_ref, loss_ref,
    avg_out, mom_out, new_out, first_out, second_out, loss_out,
    total, w, mom, first, second, averaged, sem, out_sem,
):
    cut = PADDED // 2
    pieces = [pl.ds(0, cut), pl.ds(cut, SHARD - cut)]
    loads = []
    for i, at in enumerate(pieces):
        loads.append([pltpu.make_async_copy(src.at[at], dst.at[at], sem.at[3 * i + k]) for k, (src, dst) in enumerate(((sum_ref, total), (w_ref, w), (mom_ref, mom)))])
    moments = [pltpu.make_async_copy(src, dst, sem.at[6 + i]) for i, (src, dst) in enumerate(((first_ref, first), (second_ref, second)))]
    for copy in loads[0] + loads[1] + moments:
        copy.start()
    outs = []

    def send(src, dst):
        copy = pltpu.make_async_copy(src, dst, out_sem.at[len(outs)])
        copy.start()
        outs.append(copy)

    loss_out[...] = loss_ref[0:1, 0:1]

    def outer(r, n):
        at = pl.ds(r, n)
        old = w[at, :]
        mean = INNER_RATE * (total[at, :] * 0.25 + DECAY * old)
        momentum = OUTER_MU * mom[at, :] + mean
        averaged[at, :] = mean
        mom[at, :] = momentum
        w[at, :] = old - OUTER_RATE * (mean + OUTER_MU * momentum)

    def block(i, carry):
        outer(pl.multiple_of(i * 96, 96), 96)
        return carry

    for i, at in enumerate(pieces):
        for copy in loads[i]:
            copy.wait()
        if i == 0:
            lax.fori_loop(0, cut // 96, block, 0)
        else:
            lax.fori_loop(cut // 96, SHARD // 96, block, 0)
            outer(SHARD // 96 * 96, SHARD - SHARD // 96 * 96)
        for src, dst in ((averaged, avg_out), (mom, mom_out), (w, new_out)):
            send(src.at[at], dst.at[at])
        if i == 0:
            for copy, src, dst in zip(moments, (first, second), (first_out, second_out)):
                copy.wait()
                send(src, dst.reshape(SHARD, 128))
    for copy in outs:
        copy.wait()


def finish(total, weights, momentum, first, second, loss):
    hbm = pl.BlockSpec(memory_space=pl.ANY)
    vmem = pl.BlockSpec(memory_space=pltpu.VMEM)
    V = pltpu.VMEM
    rows = jax.ShapeDtypeStruct((SHARD, 128), F32)
    row = jax.ShapeDtypeStruct((1, SHARD * 128), F32)
    return pl.pallas_call(
        finish_kernel,
        out_shape=(rows,) * 3 + (row,) * 2 + (jax.ShapeDtypeStruct((1, 1), F32),),
        in_specs=[hbm] * 5 + [vmem],
        out_specs=(hbm,) * 5 + (vmem,),
        scratch_shapes=[V((PADDED, 128), F32)] + [V((SHARD, 128), F32)] * 5 + [pltpu.SemaphoreType.DMA((8,)), pltpu.SemaphoreType.DMA((8,))],
        compiler_params=pltpu.CompilerParams(vmem_limit_bytes=60 * 1024 * 1024),
        name="finish",
    )(total, weights, momentum, first, second, loss)


def body(patches, labels, counts, weights, first_moments, second_moments, outer_momentum):
    flat = weights.reshape(SHARD, 128)
    reduced, loss = grads(flat, patches.reshape(2, P_SIZE, D), labels.reshape(2), counts.reshape(2))
    total, first, second = update(reduced, first_moments, second_moments)
    averaged, momentum, new_weights, first, second, loss = finish(total, flat, outer_momentum.reshape(SHARD, 128), first, second, loss)
    return (
        averaged.reshape(-1),
        momentum.reshape(-1),
        new_weights.reshape(-1),
        first,
        second,
        loss,
    )


def solution(mesh):
    placed = (
        P("rep", None, None, "fsdp", None, None),
        P("rep", None, None, "fsdp"),
        P("rep", None, None),
        P("fsdp"),
        P("rep", "fsdp"),
        P("rep", "fsdp"),
        P("fsdp"),
    )
    return jax.shard_map(
        body,
        mesh=mesh,
        in_specs=placed,
        out_specs=(
            P("fsdp"),
            P("fsdp"),
            P("fsdp"),
            P("rep", "fsdp"),
            P("rep", "fsdp"),
            P("rep", None),
        ),
        check_vma=False,
    )
```

```python
from functools import partial

import jax
import jax.numpy as jnp
from jax import lax
from jax.experimental import pallas as pl
from jax.experimental.pallas import tpu as pltpu
from jax.sharding import PartitionSpec as P

SHARD = 2098
SLOT = 132
HALF = 66
QUART = 33
NSLOT = 32
ROUNDS = 22
UNIT = 6
STAGES = ((0, 4), (4, 10), (10, 16), (16, 22))
SECTIONS = []
_t = 0
for _base, _c, _g, _rpg in ((0, 6, 61, 96), (5796, 8, 48, 125), (11796, 6, 1, 96), (11820, 18, 48, 288), (25644, 6, 48, 96), (30252, 24, 48, 384), (48684, 6, 192, 96)):
    SECTIONS.append((_base, _c, _g, _rpg, _t))
    _t += _c * _g
NTILE = _t
HI = 352
LO = 224
MARGIN = 512
FROWS = 3072
HEAD_ROWS = 16
MESH = pl.DeviceIdType.MESH


def coords():
    rep = lax.axis_index("rep")
    fs = lax.axis_index("fsdp")
    return lax.div(rep, 2), lax.rem(rep, 2), lax.div(fs, 8), lax.rem(lax.div(fs, 4), 2), lax.rem(fs, 4)


def device(xl, xh, core, z, y):
    return {"rep": xl * 2 + core, "fsdp": z * 8 + xh * 4 + y}


def flat_device(xl, core, s):
    return device(xl, lax.rem(lax.div(s, 4), 2), core, lax.div(s, 8), lax.rem(s, 4))


class Links:

    def __init__(self, T, R, RA, RB, g_send, g_recv, r_send, r_recv):
        self.xl, self.b, self.z, self.a, self.y = coords()
        self.T5 = T.reshape(ROUNDS, 4, 2, 4, UNIT, 16, 128)
        self.R, self.RA, self.RB = R, RA, RB
        self.g_send, self.g_recv, self.r_send, self.r_recv = g_send, g_recv, r_send, r_recv
        self.pending = []
        self.sibling = device(self.xl, self.a, 1 - self.b, self.z, self.y)

    def at_y(self, k):
        return device(self.xl, self.a, self.b, self.z, lax.rem(self.y + k, 4))

    def at_z(self, k):
        return device(self.xl, self.a, self.b, lax.rem(self.z + k, 4), self.y)

    def at_x(self, k):
        a = lax.rem(self.a + (self.xl if k == 1 else 1 - self.xl), 2)
        return device(1 - self.xl, a, self.b, self.z, self.y)

    def go(self, src, dst, send, recv, target):
        copy = pltpu.make_async_remote_copy(src_ref=src, dst_ref=dst, send_sem=send, recv_sem=recv, device_id=target, device_id_type=MESH)
        copy.start()
        self.pending.append(copy)

    def landed(self, dst, send, recv):
        pltpu.make_async_remote_copy(src_ref=dst, dst_ref=dst, send_sem=send, recv_sem=recv, device_id=self.sibling, device_id_type=MESH).wait_recv()

    def sent(self):
        for copy in self.pending:
            copy.wait_send()
        self.pending = []

    def span(self, i, h):
        lo, hi = STAGES[i]
        n = (hi - lo) // 2
        return pl.ds(lo + h * n, n)

    def first_axis(self, h, k):
        return (self.at_y if h == 0 else self.at_z)(k)

    def second_axis(self, h, k):
        return (self.at_z if h == 0 else self.at_y)(k)

    def gathered(self, i, h):
        lo, hi = STAGES[i]
        n = (hi - lo) // 2
        if i == 0:
            return pl.ds(lo + h * n, n)
        return pl.ds(lo + h * n + self.xl, 2)

    def single(self, i, h, own):
        lo, hi = STAGES[i]
        parity = self.xl if own else 1 - self.xl
        return pl.ds(lo + h * ((hi - lo) // 2) + 2 * parity, 1)

    def one(self, i, h, k, q=None):
        rd = self.gathered(i, h)
        t = pl.ds(0, UNIT) if q is None else pl.ds(3 * q, 3)
        if h == 0:
            return self.T5.at[rd, self.z, self.b, lax.rem(self.y + k, 4), t]
        return self.T5.at[rd, lax.rem(self.z + k, 4), self.b, self.y, t]

    def row(self, rd, h, k, core=None, p=None):
        core = self.b if core is None else core
        t = pl.ds(0, 4) if p is None else pl.ds(2 * p, 2)
        if h == 0:
            return self.T5.at[rd, lax.rem(self.z + k, 4), core, t]
        return self.T5.at[rd, t, core, lax.rem(self.y + k, 4)]

    def gsem(self, i, h, k):
        n = (i * 2 + h) * 24 + k
        return self.g_send.at[n], self.g_recv.at[n]

    def gather_go(self, i, h, k, view, target):
        self.go(view, view, *self.gsem(i, h, k), target)

    def gather_wait(self, i, h, k, view):
        self.landed(view, *self.gsem(i, h, k))

    def share(self, i, h, m, k):
        self.gather_go(i, h, 8 + m, self.row(self.gathered(i, h), h, k), self.sibling)
        if i > 0:
            rd = self.single(i, h, True)
            self.gather_go(i, h, 12 + m, self.row(rd, h, k, p=0), self.at_x(1))
            self.gather_go(i, h, 16 + m, self.row(rd, h, k, p=1), self.at_x(3))

    def gather_step(self, i, step):
        for h in range(2):
            rd = self.gathered(i, h)
            if step == 0:
                self.gather_go(i, h, 0, self.one(i, h, 0), self.first_axis(h, 1))
                self.gather_go(i, h, 1, self.one(i, h, 0), self.first_axis(h, 3))
            elif step == 1:
                self.gather_wait(i, h, 0, self.one(i, h, 3))
                self.gather_go(i, h, 2, self.one(i, h, 3, 0), self.first_axis(h, 1))
                self.gather_wait(i, h, 1, self.one(i, h, 1))
                self.gather_go(i, h, 3, self.one(i, h, 1, 1), self.first_axis(h, 3))
            elif step == 2:
                self.gather_wait(i, h, 2, self.one(i, h, 2, 0))
                self.gather_wait(i, h, 3, self.one(i, h, 2, 1))
                self.gather_go(i, h, 4, self.row(rd, h, 0), self.second_axis(h, 1))
                self.gather_go(i, h, 5, self.row(rd, h, 0), self.second_axis(h, 3))
                self.share(i, h, 0, 0)
            elif step == 3:
                self.gather_wait(i, h, 4, self.row(rd, h, 3))
                self.gather_go(i, h, 6, self.row(rd, h, 3, p=0), self.second_axis(h, 1))
                self.share(i, h, 1, 3)
                self.gather_wait(i, h, 5, self.row(rd, h, 1))
                self.gather_go(i, h, 7, self.row(rd, h, 1, p=1), self.second_axis(h, 3))
                self.share(i, h, 2, 1)
            elif step == 4:
                self.gather_wait(i, h, 6, self.row(rd, h, 2, p=0))
                self.gather_wait(i, h, 7, self.row(rd, h, 2, p=1))
                self.share(i, h, 3, 2)
            elif step == 5:
                if i > 0:
                    other = self.single(i, h, False)
                    for m, k in enumerate((0, 3, 1, 2)):
                        self.gather_wait(i, h, 12 + m, self.row(other, h, k, p=0))
                        self.gather_wait(i, h, 16 + m, self.row(other, h, k, p=1))
                        self.gather_go(i, h, 20 + m, self.row(other, h, k), self.sibling)
            else:
                for m, k in enumerate((0, 3, 1, 2)):
                    self.gather_wait(i, h, 8 + m, self.row(rd, h, k, core=1 - self.b))
                    if i > 0:
                        self.gather_wait(i, h, 20 + m, self.row(self.single(i, h, False), h, k, core=1 - self.b))

    def rsem(self, i, h, k):
        n = (i * 2 + h) * 13 + k
        return self.r_send.at[n], self.r_recv.at[n]

    def cell(self, i, h, k, q):
        rd = self.span(i, h)
        t = pl.ds(3 * q, 3)
        if h == 0:
            return self.T5.at[rd, self.z, self.b, lax.rem(self.y + k, 4), t]
        return self.T5.at[rd, lax.rem(self.z + k, 4), self.b, self.y, t]

    def add(self, dst, *sources, inner=()):
        n = dst.shape[0]

        def one(r, carry):
            for k in range(inner) if inner else (None,):
                at = (r,) if k is None else (r, k)
                if len(sources) == 1:
                    dst[at] = dst[at] + sources[0][at]
                else:
                    total = dst[at].astype(jnp.float32)
                    for source in sources:
                        total = total + source[at].astype(jnp.float32)
                    dst[at] = total.astype(jnp.bfloat16)
            return carry

        lax.fori_loop(0, n, one, 0)

    def reduce_step(self, i, h, step):
        rd = self.span(i, h)
        T5 = self.T5

        def send_a(k, ka, p, shift):
            self.go(self.row(rd, h, ka, p=p), self.RA.at[k, rd], *self.rsem(i, h, 1 + k), self.second_axis(h, shift))

        def wait_a(k):
            self.landed(self.RA.at[k, rd], *self.rsem(i, h, 1 + k))

        def send_b(k, kb, q, shift):
            self.go(self.cell(i, h, kb, q), self.RB.at[k, rd], *self.rsem(i, h, 7 + k), self.first_axis(h, shift))

        def wait_b(k):
            self.landed(self.RB.at[k, rd], *self.rsem(i, h, 7 + k))

        if step == 0:
            self.go(T5.at[rd, :, 1 - self.b], self.R.at[rd], *self.rsem(i, h, 0), self.sibling)
        elif step == 1:
            self.landed(self.R.at[rd], *self.rsem(i, h, 0))
            mine, theirs = T5.at[rd, :, self.b], self.R.at[rd]
            n = mine.shape[0]

            def both(r, carry):
                q = lax.div(r, 4)
                w = lax.rem(r, 4)
                for k in range(4):
                    mine[q, w, k] = mine[q, w, k] + theirs[q, w, k]
                return carry

            lax.fori_loop(0, 4 * n, both, 0)
            send_a(0, 2, 0, 1)
            send_a(1, 2, 1, 3)
            send_a(2, 1, 1, 1)
            send_a(3, 3, 0, 3)
        elif step == 2:
            wait_a(0)
            self.add(self.row(rd, h, 1, p=0), self.RA.at[0, rd], inner=2)
            send_a(4, 1, 0, 1)
            wait_a(1)
            self.add(self.row(rd, h, 3, p=1), self.RA.at[1, rd], inner=2)
            send_a(5, 3, 1, 3)
        elif step == 3:
            for k in (2, 3, 4, 5):
                wait_a(k)
            self.add(self.row(rd, h, 0, p=0), self.RA.at[3, rd], self.RA.at[4, rd], inner=2)
            self.add(self.row(rd, h, 0, p=1), self.RA.at[2, rd], self.RA.at[5, rd], inner=2)
            send_b(0, 2, 0, 1)
            send_b(1, 2, 1, 3)
            send_b(2, 1, 1, 1)
            send_b(3, 3, 0, 3)
        elif step == 4:
            wait_b(0)
            self.add(self.cell(i, h, 1, 0), self.RB.at[0, rd])
            send_b(4, 1, 0, 1)
            wait_b(1)
            self.add(self.cell(i, h, 3, 1), self.RB.at[1, rd])
            send_b(5, 3, 1, 3)
        else:
            for k in (2, 3, 4, 5):
                wait_b(k)
            self.add(self.cell(i, h, 0, 0), self.RB.at[3, rd], self.RB.at[4, rd])
            self.add(self.cell(i, h, 0, 1), self.RB.at[2, rd], self.RB.at[5, rd])


def start_gather(links, w_ref, patch_ref, labels_ref, counts_ref, T, patch_in, meta_in, meta_ref, flat, headrows, lob, hib, rlo, rhi, slot, local_sem, x_send, x_recv, u_send, u_recv):
    xl, b, z, a, y = links.xl, links.b, links.z, links.a, links.y
    fs = z * 8 + a * 4 + y
    swap = a != b
    xo = lax.rem(xl + a + b, 2)
    holder = z * 8 + b * 4 + y
    up = flat_device(xl, b, lax.rem(fs + 1, NSLOT))
    down = flat_device(xl, b, lax.rem(fs + NSLOT - 1, NSLOT))
    mirror = device(xl, b, a, z, y)
    load = pltpu.make_async_copy(w_ref, flat.at[pl.ds(MARGIN, SHARD)], local_sem.at[0])
    load.start()
    barrier = pltpu.get_barrier_semaphore()
    total = (counts_ref[0] + counts_ref[1]).astype(jnp.float32)
    for m in range(2):
        valid = jnp.full((1, 128), jnp.where(fs < counts_ref[m], 1.0, 0.0), jnp.float32)
        meta_ref[m : m + 1, :] = jnp.full((1, 128), labels_ref[m].astype(jnp.float32), jnp.float32)
        meta_ref[2 + m : 3 + m, :] = valid / jnp.full((1, 128), total, jnp.float32)
        meta_ref[4 + m : 5 + m, :] = valid
    meta_ref[6:8, :] = jnp.zeros((2, 128), jnp.float32)

    def greet(target):
        pl.semaphore_signal(barrier, inc=1, device_id=target, device_id_type=MESH)

    def wanted(j, parity):
        return jnp.logical_or(j < STAGES[0][1], lax.rem(j + 3 - STAGES[0][1] % 3, 3) != 2 * (1 - parity))

    for target in (up, down, links.at_x(1), links.at_x(3), links.at_y(1), links.at_y(3), links.at_z(1), links.at_z(3), links.sibling):
        greet(target)

    @pl.when(swap)
    def _():
        greet(mirror)

    own_index = lax.rem(fs * 11, NSLOT)
    keeps = jnp.logical_and(a == b, own_index < ROUNDS)

    def greet_source(j, carry):
        s = lax.div(32 * j + holder, ROUNDS)
        sa = lax.rem(lax.div(s, 4), 2)

        @pl.when(jnp.logical_and(wanted(j, xl), jnp.logical_not(jnp.logical_and(keeps, s == fs))))
        def _():
            greet(device(lax.rem(xl + sa + a, 2), sa, a, lax.div(s, 8), lax.rem(s, 4)))

        return carry

    lax.fori_loop(0, ROUNDS, greet_source, 0)
    def unit_goes(i):
        there = wanted(lax.div(ROUNDS * fs + i, 32), xo)
        stays = jnp.logical_and(keeps, i == own_index)
        return jnp.logical_and(there, jnp.logical_not(stays)), jnp.logical_and(there, stays)

    outgoing = lax.fori_loop(0, ROUNDS, lambda i, n: n + jnp.where(unit_goes(i)[0], 1, 0), 9)
    pl.semaphore_wait(barrier, outgoing + jnp.where(swap, 1, 0))
    load.wait()

    def remote(src, dst, k, target):
        return pltpu.make_async_remote_copy(src_ref=src, dst_ref=dst, send_sem=x_send.at[k], recv_sem=x_recv.at[k], device_id=target, device_id_type=MESH)

    hib[...] = flat[pl.ds(MARGIN + SHARD - HI, HI), :].astype(jnp.bfloat16)
    to_up = remote(hib, rlo, 0, up)
    to_up.start()
    lob[...] = flat[pl.ds(MARGIN, LO), :].astype(jnp.bfloat16)
    to_down = remote(lob, rhi, 1, down)
    to_down.start()
    patch_swap = remote(patch_ref, patch_in, 2, mirror)
    meta_swap = remote(meta_ref, meta_in, 3, mirror)
    patch_keep = pltpu.make_async_copy(patch_ref, patch_in, local_sem.at[1])
    meta_keep = pltpu.make_async_copy(meta_ref, meta_in, local_sem.at[2])
    first = ROUNDS * fs
    origin = SHARD * fs - MARGIN

    def unit_copy(i):
        k = first + i
        d = lax.rem(k, 32)
        src = slot.at[pl.ds(UNIT * i, UNIT)]
        dst = T.at[pl.ds(UNIT * k, UNIT)]
        target = device(xo, b, lax.rem(lax.div(d, 4), 2), lax.div(d, 8), lax.rem(d, 4))
        away = pltpu.make_async_remote_copy(src_ref=src, dst_ref=dst, send_sem=u_send.at[i], recv_sem=u_recv.at[lax.div(k, 32)], device_id=target, device_id_type=MESH)
        return away, (src, dst)

    def send_unit(i):
        away, (src, dst) = unit_copy(i)
        goes, stays = unit_goes(i)

        @pl.when(stays)
        def _():
            pltpu.make_async_copy(src, dst, local_sem.at[3]).start()

        @pl.when(goes)
        def _():
            away.start()

    lane = lax.broadcasted_iota(jnp.int32, (8, 128), 1)

    def head_group(g, base, per, start):
        row = base + per * g - origin
        for i in range(16):
            q, s = divmod(1000 * i, 128)
            one = flat[pl.ds(row + q, 8), :]
            if s:
                two = flat[pl.ds(row + q + 1, 8), :]
                one = jnp.where(lane < 128 - s, pltpu.roll(one, 128 - s, 1), pltpu.roll(two, 128 - s, 1))
            headrows[pl.ds(i * 8, 8), :] = one
        for j in range(8):
            t = start + g * 8 + j - UNIT * first

            @pl.when(jnp.logical_and(t >= 0, t < SLOT))
            def _():
                slot[t] = headrows[pl.ds(j, 16, stride=8), :].astype(jnp.bfloat16)

    def inside(row, rows):
        return jnp.logical_and(row >= MARGIN, row + rows <= MARGIN + SHARD)

    def convert(near):
        for index, (base, c, groups, per, start) in enumerate(SECTIONS):
            lo = jnp.maximum(UNIT * first, start)
            hi = jnp.minimum(UNIT * first + SLOT, start + c * groups)
            if index == 1:

                def group(g, carry):
                    @pl.when(inside(base + per * g - origin, per + 1) == near)
                    def _():
                        head_group(g, base, per, start)

                    return carry

                lax.fori_loop(lax.div(jnp.maximum(lo, start) - start, 8), lax.div(jnp.maximum(hi, start) - start + 7, 8), group, 0)
                if not near:

                    def deal(u, carry):
                        send_unit(u - first)
                        return carry

                    lax.fori_loop(lax.div(lo, UNIT), lax.div(hi, UNIT), deal, 0)
            else:

                def unit(u, carry):
                    t = UNIT * u - start
                    g = lax.div(t, c)
                    row = base + 16 * c * g + lax.rem(t, c) - origin

                    @pl.when(inside(row, 15 * c + UNIT) == near)
                    def _():
                        for k in range(UNIT):
                            slot[UNIT * (u - first) + k] = flat[pl.ds(row + k, 16, stride=c), :].astype(jnp.bfloat16)
                        send_unit(u - first)

                    return carry

                lax.fori_loop(lax.div(lo, UNIT), lax.div(hi, UNIT), unit, 0)

    convert(True)
    to_up.wait_recv()
    flat[pl.ds(MARGIN - HI, HI), :] = rlo[...].astype(jnp.float32)
    to_down.wait_recv()
    flat[pl.ds(MARGIN + SHARD, LO), :] = rhi[...].astype(jnp.float32)
    convert(False)

    @pl.when(fs == NSLOT - 1)
    def _():
        slot[pl.ds(SLOT - 12, 12)] = jnp.zeros((12, 16, 128), jnp.bfloat16)
        send_unit(ROUNDS - 2)
        send_unit(ROUNDS - 1)

    @pl.when(swap)
    def _():
        patch_swap.start()
        meta_swap.start()

    @pl.when(jnp.logical_not(swap))
    def _():
        patch_keep.start()
        meta_keep.start()

    def units_here(i):
        def wait(j, carry):
            place = T.at[pl.ds(UNIT * (32 * j + holder), UNIT)]
            mine = jnp.logical_and(keeps, lax.div(32 * j + holder, ROUNDS) == fs)

            @pl.when(jnp.logical_and(wanted(j, xl), mine))
            def _():
                pltpu.make_async_copy(place, place, local_sem.at[3]).wait()

            @pl.when(jnp.logical_and(wanted(j, xl), jnp.logical_not(mine)))
            def _():
                pltpu.make_async_remote_copy(src_ref=place, dst_ref=place, send_sem=u_send.at[0], recv_sem=u_recv.at[j], device_id=links.sibling, device_id_type=MESH).wait_recv()

            return carry

        lax.fori_loop(*STAGES[i], wait, 0)

    def finish_start():
        def wait(i, carry):
            away, unused = unit_copy(i)

            @pl.when(unit_goes(i)[0])
            def _():
                away.wait_send()

            return carry

        lax.fori_loop(0, ROUNDS, wait, 0)
        to_up.wait_send()
        to_down.wait_send()

        @pl.when(swap)
        def _():
            patch_swap.wait()
            meta_swap.wait()

        @pl.when(jnp.logical_not(swap))
        def _():
            patch_keep.wait()
            meta_keep.wait()

    return units_here, finish_start


D = 768
HEADS = 12
HEAD_DIM = 64
FF = 3072
CLS = 1000
P_SIZE = 196
ROWS = 208
TOK = 2 * ROWS
NORM_EPS = 1e-06
SMOOTHING = 0.1
NTILES = 4224
T_E, T_HEAD, T_NORM, T_QKV, T_OUT, T_IN, T_FO = 0, 366, 750, 756, 1620, 1908, 3060
T_POS = 288
BLK = 256
BLOCKS = ((0, 96), (96, 112), (208, 96), (304, 112))
F32 = jnp.float32
BF16 = jnp.bfloat16
ROOT_HALF = 0.7071067811865476
INV_ROOT_TWO_PI = 0.3989422804014327


def dot(x, w):
    return lax.dot_general(x, w, (((1,), (0,)), ((), ())), preferred_element_type=F32)


def dot_t(x, w):
    return lax.dot_general(x, w, (((1,), (1,)), ((), ())), preferred_element_type=F32)


def t_dot(x, w):
    return lax.dot_general(x, w, (((0,), (0,)), ((), ())), preferred_element_type=F32)


def stats(x, keep, r, k):
    mean = jnp.sum(x, -1, keepdims=True) * (1.0 / D)
    centred = x - mean
    var = jnp.sum(centred * centred, -1, keepdims=True) * (1.0 / D)
    rstd = lax.rsqrt(var + NORM_EPS)
    keep[r, k : k + 1] = mean
    keep[r, k + 1 : k + 2] = rstd
    return centred * rstd


def kept(x, keep, r, k):
    rstd = keep[r, k + 1 : k + 2]
    return (x - keep[r, k : k + 1]) * rstd, rstd


def norm_back(d_hat, hat, rstd):
    m1 = jnp.sum(d_hat, -1, keepdims=True) * (1.0 / D)
    m2 = jnp.sum(d_hat * hat, -1, keepdims=True) * (1.0 / D)
    return rstd * (d_hat - m1 - hat * m2)


def compute(step, patch_ref, meta_ref, loss_ref, T, x, h, a, at, mix, prob, o, h1, a2, hid, slope, h2, dh, dyb, keep):
    G = T
    dmix = mix

    def section(ref, start, c, groups):
        return ref.at[pl.ds(start, groups * c)].reshape(groups, c, 16, 128)

    def cols(start, c, groups, j):
        part = section(T, start, c, groups)
        return jnp.concatenate([part[:, 2 * j + k].reshape(groups * 16, 128) for k in range(2)], axis=1)

    def put_cols(start, c, groups, j, value):
        low = value.astype(BF16)
        part = section(G, start, c, groups)
        for k in range(2):
            part[:, 2 * j + k] = low[:, k * 128 : (k + 1) * 128].reshape(groups, 16, 128)

    def row_of(start, k):
        return jnp.concatenate([T[start + j][k : k + 1, :] for j in range(6)], axis=1).astype(F32)

    def lanes(j):
        return pl.ds(pl.multiple_of(j * BLK, BLK), BLK)

    step("start")
    for i in range(2):
        x[pl.ds(i * ROWS, 192), :] = patch_ref[i, pl.ds(0, 192), :]
        x[pl.ds(i * ROWS + 192, 16), :] = jnp.concatenate([patch_ref[i, pl.ds(192, 4), :], jnp.zeros((12, D), BF16)], axis=0)

    real = lax.broadcasted_iota(jnp.int32, (ROWS, 128), 0) < P_SIZE
    for j in range(3):
        acc = dot(x[...], cols(T_E, 6, 48, j))
        p = cols(T_POS, 6, 13, j).astype(F32)
        p = jnp.where(lax.broadcasted_iota(jnp.int32, (ROWS, BLK), 0) < P_SIZE, p, 0.0)
        for i in range(2):
            h[pl.ds(i * ROWS, ROWS), pl.ds(j * BLK, BLK)] = acc[i * ROWS : (i + 1) * ROWS] + p

    step("embedded")
    gain1, shift1, gain2, shift2 = (row_of(T_NORM, k) for k in range(4))

    for at_row, n in BLOCKS:
        r = pl.ds(at_row, n)
        a[r, :] = (stats(h[r, :], keep, r, 0) * gain1 + shift1).astype(BF16)

    step("qkv")
    def wide_cols(start, c, groups, j):
        return jnp.concatenate([cols(start, c, groups, 3 * j + k) for k in range(3)], axis=1)

    def wide_lanes(j):
        return pl.ds(pl.multiple_of(j * D, D), D)

    def mix_block(j, carry):
        mix[:, wide_lanes(j)] = dot(a[...], wide_cols(T_QKV, 18, 48, j)).astype(BF16)
        return carry

    lax.fori_loop(0, 3, mix_block, 0)

    first_half = lax.broadcasted_iota(jnp.int32, (ROWS, 128), 1) < HEAD_DIM
    key_ok = lax.broadcasted_iota(jnp.int32, (ROWS, ROWS), 0) < P_SIZE
    first_rows = lax.broadcasted_iota(jnp.int32, (128, ROWS), 0) < HEAD_DIM
    halves = (first_half, jnp.logical_not(first_half))
    zero = jnp.zeros((ROWS, 128), BF16)

    def split(block):
        return jnp.concatenate([jnp.where(first_half, block, zero), jnp.where(first_half, zero, block)], axis=0)

    def heads_of(p, i):
        r = pl.ds(i * ROWS, ROWS)
        return r, [pl.ds(pl.multiple_of(p * 128 + D * k, 128), 128) for k in range(3)]

    def attend(p, carry):
        for i in range(2):
            r, ls = heads_of(p, i)
            q, k, v = (mix[r, l] for l in ls)
            q = q * jnp.asarray(0.125, BF16)
            vt = v.T
            outs = []
            for e in range(2):
                s = dot_t(jnp.where(halves[e], k, zero), q)
                s = jnp.where(key_ok, s, -jnp.inf)
                ex = jnp.exp(s - jnp.max(s, 0, keepdims=True))
                pr = (ex * (1.0 / jnp.sum(ex, 0, keepdims=True))).astype(BF16)
                prob[p * 2 + i, e] = pr
                outs.append(dot(vt, pr))
            o[r, ls[0]] = jnp.where(first_rows, outs[0], outs[1]).astype(BF16).T
        return carry

    parts = ((0, 2), (2, 3), (3, 5), (5, 6))
    for part in range(4):
        step("attend%d" % part)
        lax.fori_loop(*parts[part], attend, 0)
    step("attended")
    for j in range(3):
        h1[:, pl.ds(j * BLK, BLK)] = h[:, pl.ds(j * BLK, BLK)] + dot(o[...], cols(T_OUT, 6, 48, j))

    for at_row, n in BLOCKS:
        r = pl.ds(at_row, n)
        a2[r, :] = (stats(h1[r, :], keep, r, 2) * gain2 + shift2).astype(BF16)

    step("up")
    def up_block(j, carry):
        u = dot(a2[...], wide_cols(T_IN, 24, 48, j))
        phi = 0.5 * (1.0 + lax.erf(u * ROOT_HALF))
        pdf = jnp.exp(-0.5 * u * u) * INV_ROOT_TWO_PI
        hid[:, wide_lanes(j)] = (u * phi).astype(BF16)
        slope[:, wide_lanes(j)] = (phi + u * pdf).astype(BF16)
        return carry

    lax.fori_loop(0, 4, up_block, 0)
    step("down")
    for j in range(3):
        h2[:, pl.ds(j * BLK, BLK)] = h1[:, pl.ds(j * BLK, BLK)] + dot(hid[...], cols(T_FO, 6, 192, j))

    step("pool")
    gain_end, shift_end = (row_of(T_POS + 72, 4 + k) for k in range(2))
    means = []
    last_rows = lax.broadcasted_iota(jnp.int32, (112, D), 0) < P_SIZE - 96
    for i in range(2):
        total = jnp.zeros((8, D), F32)
        for at_row, n in BLOCKS[2 * i : 2 * i + 2]:
            r = pl.ds(at_row, n)
            hat = stats(h2[r, :], keep, r, 4)
            if n == 112:
                hat = jnp.where(last_rows, hat, 0.0)
            total = total + jnp.sum(hat.reshape(n // 8, 8, D), 0)
        means.append(jnp.sum(total, 0, keepdims=True) * (1.0 / P_SIZE))
    mean_hat = jnp.concatenate(means + [jnp.zeros((14, D), F32)], axis=0)
    two = lax.broadcasted_iota(jnp.int32, (16, D), 0) < 2
    pooled = jnp.where(two, mean_hat * gain_end + shift_end, 0.0).astype(BF16)
    logits = jnp.concatenate([dot(pooled, cols(T_HEAD, 8, 48, j)) for j in range(4)], axis=1)
    lane = lax.broadcasted_iota(jnp.int32, (16, 1024), 1)
    lane_f = lane.astype(F32)
    inside = lane < CLS
    logits = jnp.where(inside, logits, -1e30)
    top = jnp.max(logits, -1, keepdims=True)
    total = jnp.sum(jnp.where(inside, jnp.exp(logits - top), 0.0), -1, keepdims=True)
    logp = logits - top - jnp.log(total)
    meta = meta_ref[...]
    pad14 = jnp.zeros((14, 1), F32)
    label = jnp.concatenate([meta[0:2, 0:1], pad14], axis=0)
    scale = jnp.concatenate([meta[2:4, 0:1], pad14], axis=0)
    valid = jnp.concatenate([meta[4:6, 0:1], pad14], axis=0)
    target = jnp.where(lane_f == label, 1.0 - SMOOTHING, 0.0) + SMOOTHING / CLS
    values = -jnp.sum(jnp.where(inside, target * logp, 0.0), -1, keepdims=True)
    loss_ref[...] = jnp.broadcast_to(jnp.sum(values * valid, 0, keepdims=True), (8, 128))
    d_logits = jnp.where(inside, scale * (jnp.exp(logp) - target), 0.0).astype(BF16)
    d_pooled = jnp.zeros((16, D), F32)
    for j in range(4):
        w = cols(T_HEAD, 8, 48, j)
        d_pooled = d_pooled + dot_t(d_logits[:, j * BLK : (j + 1) * BLK], w)
        put_cols(T_HEAD, 8, 48, j, t_dot(pooled, d_logits[:, j * BLK : (j + 1) * BLK]))
    d_gain_end = jnp.sum(d_pooled * mean_hat, 0, keepdims=True)
    d_shift_end = jnp.sum(d_pooled, 0, keepdims=True)
    for i in range(2):
        d_hat = d_pooled[i : i + 1, :] * (1.0 / P_SIZE) * gain_end

        m1 = jnp.sum(d_hat, -1, keepdims=True) * (1.0 / D)
        for at_row, n in BLOCKS[2 * i : 2 * i + 2]:
            r = pl.ds(at_row, n)
            hat, rstd = kept(h2[r, :], keep, r, 4)
            m2 = jnp.sum(d_hat * hat, -1, keepdims=True) * (1.0 / D)
            d = rstd * ((d_hat - m1) - hat * m2)
            if n == 112:
                d = jnp.where(last_rows, d, 0.0)
            dh[r, :] = d
            dyb[r, :] = d.astype(BF16)

    step("backward")
    at[...] = a2[...].T
    da = h2

    wide = D // 16

    def down_block(j, carry):
        part = section(T, T_FO + j * wide * 6, 6, wide)
        w = jnp.concatenate([part[:, k].reshape(D, 128) for k in range(6)], axis=1)
        dy = dyb[...]
        d_w = t_dot(hid[:, wide_lanes(j)], dy).astype(BF16)
        hid[:, wide_lanes(j)] = (dot_t(dy, w) * slope[:, wide_lanes(j)].astype(F32)).astype(BF16)
        for k in range(6):
            part[:, k] = d_w[:, k * 128 : (k + 1) * 128].reshape(wide, 16, 128)
        return carry

    G[pl.ds(4212, 12)] = jnp.zeros((12, 16, 128), BF16)
    lax.fori_loop(0, 3, down_block, 0)
    step("fc_out0")
    lax.fori_loop(3, 4, down_block, 0)
    step("fc_out1")
    def row_block(start, c, j):
        part = section(T, start + j * 16 * c, c, 16)
        return jnp.concatenate([part[:, k].reshape(BLK, 128) for k in range(c)], axis=1)

    def put_rows(start, c, j, first, value):
        part = section(G, start + j * 16 * c, c, 16)
        low = value.astype(BF16)
        for k in range(value.shape[1] // 128):
            part[:, first + k] = low[:, k * 128 : (k + 1) * 128].reshape(16, 16, 128)

    for j in range(3):
        da[:, pl.ds(j * BLK, BLK)] = dot_t(hid[...], row_block(T_IN, 24, j))
    step("fc_in0")
    for j in range(3):
        for k in range(4):
            put_rows(T_IN, 24, j, 6 * k, dot(at[pl.ds(j * BLK, BLK), :], hid[:, pl.ds(k * D, D)]))
        step("fc_in%d" % (j + 1))

    def norm_grads(inputs, column, gain):
        dg, ds = jnp.zeros((8, D), F32), jnp.zeros((8, D), F32)
        for at_row, n in BLOCKS:
            r = pl.ds(at_row, n)
            hat, rstd = kept(inputs[r, :], keep, r, column)
            d = da[r, :]
            new = dh[r, :] + norm_back(d * gain, hat, rstd)
            dh[r, :] = new
            dyb[r, :] = new.astype(BF16)
            dg = dg + jnp.sum((d * hat).reshape(n // 8, 8, D), 0)
            ds = ds + jnp.sum(d.reshape(n // 8, 8, D), 0)
        return dg, ds

    d_gain2, d_shift2 = norm_grads(h1, 2, gain2)

    step("normed2")
    at[...] = o[...].T
    for j in range(3):
        o[:, pl.ds(j * BLK, BLK)] = dot_t(dyb[...], row_block(T_OUT, 6, j)).astype(BF16)
    for j in range(3):
        put_rows(T_OUT, 6, j, 0, dot(at[pl.ds(j * BLK, BLK), :], dyb[...]))

    step("out")
    def attend_back(p, carry):
        for i in range(2):
            r, ls = heads_of(p, i)
            q, k, v = (mix[r, l] for l in ls)
            q = q * jnp.asarray(0.125, BF16)
            k8 = k * jnp.asarray(0.125, BF16)
            kt = k8.T
            do = o[r, ls[0]]
            pr = prob[p * 2 + i]
            dv = dot(pr.reshape(TOK, ROWS), do)
            dp = dot_t(split(v), do).reshape(2, ROWS, ROWS)
            prf = pr.astype(F32)
            row = jnp.sum(prf * dp, 1, keepdims=True)
            ds = (prf * (dp - row)).astype(BF16)
            dq = [dot(kt[HEAD_DIM * e : HEAD_DIM * (e + 1)], ds[e]) for e in range(2)]
            dk = dot(ds.reshape(TOK, ROWS), q)
            dmix[r, ls[0]] = jnp.concatenate(dq, axis=0).astype(BF16).T
            dmix[r, ls[1]] = jnp.where(first_half, dk[:ROWS], dk[ROWS:]).astype(BF16)
            dmix[r, ls[2]] = jnp.where(first_half, dv[:ROWS], dv[ROWS:]).astype(BF16)
        return carry

    for part in range(4):
        lax.fori_loop(*parts[part], attend_back, 0)
        step("back%d" % part)

    at[...] = a[...].T
    for j in range(3):
        da[:, pl.ds(j * BLK, BLK)] = dot_t(dmix[...], row_block(T_QKV, 18, j))
    for j in range(3):
        for k in range(3):
            put_rows(T_QKV, 18, j, 6 * k, dot(at[pl.ds(j * BLK, BLK), :], dmix[:, pl.ds(k * D, D)]))
    step("qkv_back")
    d_gain1, d_shift1 = norm_grads(h, 0, gain1)
    d_norms = jnp.concatenate([jnp.sum(d, 0, keepdims=True) for d in (d_gain1, d_shift1, d_gain2, d_shift2)] + [jnp.zeros((12, D), F32)], axis=0).astype(BF16)
    for j in range(6):
        G[T_NORM + j] = d_norms[:, j * 128 : (j + 1) * 128]
    step("norms")
    at[...] = x[...].T
    row_id = lax.broadcasted_iota(jnp.int32, (ROWS, BLK), 0)
    for j in range(3):
        put_cols(T_E, 6, 48, j, dot(at[...], dyb[:, pl.ds(j * BLK, BLK)]))
        c = pl.ds(j * BLK, BLK)
        s = slice(j * BLK, (j + 1) * BLK)
        d_pos = dh[pl.ds(0, ROWS), c] + dh[pl.ds(ROWS, ROWS), c]
        d_pos = jnp.where(row_id < P_SIZE, d_pos, 0.0)
        d_pos = jnp.where(row_id == P_SIZE, jnp.broadcast_to(d_gain_end[:, s], (ROWS, BLK)), d_pos)
        d_pos = jnp.where(row_id == P_SIZE + 1, jnp.broadcast_to(d_shift_end[:, s], (ROWS, BLK)), d_pos)
        put_cols(T_POS, 6, 13, j, d_pos)
    step("embed")


FORWARD = {
    "start": ((0, 0), (1, 0), (0, 1), (0, 2), (1, 1), (2, 0), (0, 3), (1, 2), (0, 4), (2, 1), (3, 0), (1, 3), (0, 6)),
    "embedded": ((2, 2), (3, 1)),
    "qkv": ((1, 4), (3, 2), (2, 3), (1, 5), (2, 4), (1, 6)),
    "attend0": ((3, 3),),
    "attend1": ((3, 4), (2, 5)),
    "up": ((2, 6), (3, 5)),
    "down": ((3, 6),),
}
BACKWARD = {
    "fc_out0": ((3, 0, 0),),
    "fc_out1": ((3, 1, 0), (3, 0, 1)),
    "fc_in0": ((3, 1, 1),),
    "fc_in2": ((2, 0, 0),),
    "fc_in3": ((2, 1, 0), (2, 0, 1)),
    "normed2": ((2, 1, 1),),
    "back1": ((3, 0, 2), (3, 1, 2)),
    "qkv_back": ((1, 0, 0), (1, 1, 0), (2, 0, 2), (2, 1, 2), (1, 0, 1), (1, 1, 1), (3, 0, 3), (3, 1, 3)),
    "norms": ((0, 1, 0),),
    "embed": (
        (0, 0, 0), (0, 1, 1), (0, 0, 1), (3, 0, 4), (3, 1, 4), (2, 0, 3), (2, 1, 3), (1, 0, 2), (1, 1, 2), (3, 0, 5), (3, 1, 5), (2, 0, 4), (2, 1, 4),
        (0, 1, 2), (0, 0, 2), (1, 0, 3), (1, 1, 3), (2, 0, 5), (2, 1, 5), (0, 1, 3), (0, 0, 3), (1, 0, 4), (1, 1, 4), (0, 1, 4), (0, 0, 4), (1, 0, 5), (1, 1, 5), (0, 1, 5), (0, 0, 5),
    ),
}


def grads_kernel(w_ref, patch_ref, labels_ref, counts_ref, red_ref, loss_out, T, R, RA, RB, g_send, g_recv, r_send, r_recv, LS, l_send, l_recv, patch_in, meta_in, meta, loss, *rest):
    gather_refs, compute_refs, out_sem = rest[:12], rest[12:-1], rest[-1]
    links = Links(T, R, RA, RB, g_send, g_recv, r_send, r_recv)
    xl, b, z, a, y = links.xl, links.b, links.z, links.a, links.y
    swap = a != b
    mirror = device(xl, b, a, z, y)
    units_here, finish_start = start_gather(links, w_ref, patch_ref, labels_ref, counts_ref, T, patch_in, meta_in, meta, *gather_refs)

    def loss_send(src, dst, target):
        links.go(LS.at[src], LS.at[dst], l_send.at[dst], l_recv.at[dst], target)

    def loss_wait(*slots):
        for k in slots:
            links.landed(LS.at[k], l_send.at[k], l_recv.at[k])

    def loss_step(n):
        if n == 0:
            LS[0] = loss[...]
            loss_send(0, 1, links.sibling)
        elif n == 1:
            loss_wait(1)
            LS[8] = LS[0] + LS[1]
            loss_send(8, 2, links.at_y(1))
            loss_send(8, 3, links.at_y(3))
        elif n == 2:
            loss_wait(2, 3)
            loss_send(2, 4, links.at_y(1))
        elif n == 3:
            loss_wait(4)
            LS[9] = (LS[8] + LS[4]) + (LS[2] + LS[3])
            loss_send(9, 5, links.at_z(1))
            loss_send(9, 6, links.at_z(3))
        elif n == 4:
            loss_wait(5, 6)
            loss_send(5, 7, links.at_z(1))
        elif n == 5:
            loss_wait(7)
            LS[10] = (LS[9] + LS[7]) + (LS[5] + LS[6])

            @pl.when(swap)
            def _():
                loss_swap.start()

        else:

            @pl.when(swap)
            def _():
                loss_swap.wait()
                loss_out[...] = LS[11]

            @pl.when(jnp.logical_not(swap))
            def _():
                loss_out[...] = LS[10]

    loss_swap = pltpu.make_async_remote_copy(src_ref=LS.at[10], dst_ref=LS.at[11], send_sem=l_send.at[11], recv_sem=l_recv.at[11], device_id=mirror, device_id_type=MESH)
    losses = {"fc_out0": 0, "fc_in0": 1, "fc_in2": 2, "normed2": 3, "back0": 4, "back2": 5, "qkv_back": 6}

    def step(name):
        if name == "pool":
            links.sent()
        for item in FORWARD.get(name, ()):
            if item[1] == 0:
                units_here(item[0])
            links.gather_step(*item)
        if name == "start":
            finish_start()
        for item in BACKWARD.get(name, ()):
            links.reduce_step(*item)
        if name in losses:
            loss_step(losses[name])

    compute(step, patch_in, meta_in, loss, T, *compute_refs)
    mine = T.reshape(ROUNDS, 32, UNIT, 16, 128).at[:, z * 8 + b * 4 + y]
    out = pltpu.make_async_copy(mine, red_ref, out_sem)
    out.start()
    links.sent()
    out.wait()


def grads(weights, patches, labels, counts):
    hbm = pl.BlockSpec(memory_space=pl.ANY)
    vmem = pl.BlockSpec(memory_space=pltpu.VMEM)
    V = pltpu.VMEM
    dma = pltpu.SemaphoreType.DMA
    return pl.pallas_call(
        grads_kernel,
        out_shape=(jax.ShapeDtypeStruct((ROUNDS, UNIT, 16, 128), BF16), jax.ShapeDtypeStruct((8, 128), F32)),
        in_specs=[hbm] * 2 + [pl.BlockSpec(memory_space=pltpu.SMEM)] * 2,
        out_specs=(hbm, vmem),
        scratch_shapes=[
            V((NTILES, 16, 128), BF16),
            V((ROUNDS, 4, 4, UNIT, 16, 128), BF16),
            V((6, ROUNDS, 2, UNIT, 16, 128), BF16),
            V((6, ROUNDS, 3, 16, 128), BF16),
            dma((192,)),
            dma((192,)),
            dma((104,)),
            dma((104,)),
            V((12, 8, 128), F32),
            dma((12,)),
            dma((12,)),
            V(patches.shape, BF16),
            V((8, 128), F32),
            V((8, 128), F32),
            V((8, 128), F32),
            V((FROWS, 128), F32),
            V((128, 128), F32),
            V((LO, 128), BF16),
            V((HI, 128), BF16),
            V((HI, 128), BF16),
            V((LO, 128), BF16),
            V((SLOT, 16, 128), BF16),
            dma((4,)),
            dma((4,)),
            dma((4,)),
            dma((ROUNDS,)),
            dma((ROUNDS,)),
            V((TOK, D), BF16),
            V((TOK, D), F32),
            V((TOK, D), BF16),
            V((D, TOK), BF16),
            V((TOK, 3 * D), BF16),
            V((12, 2, ROWS, ROWS), BF16),
            V((TOK, D), BF16),
            V((TOK, D), F32),
            V((TOK, D), BF16),
            V((TOK, FF), BF16),
            V((TOK, FF), BF16),
            V((TOK, D), F32),
            V((TOK, D), F32),
            V((TOK, D), BF16),
            V((TOK, 128), F32),
            dma,
        ],
        compiler_params=pltpu.CompilerParams(collective_id=0, has_side_effects=True, vmem_limit_bytes=60 * 1024 * 1024),
        name="grads",
    )(weights, patches, labels, counts)


EDGE = 24
FRONT = 768
BACK_ROWS = FRONT + SHARD + 640 + 6
PADDED = 2112
STEP = 10
EDGE_UNITS = 4
WINDOW = ROUNDS + 2 * EDGE_UNITS
BETA_ONE = 0.9
BETA_TWO = 0.95
ADAM_EPS = 1e-08
DECAY = 0.05
INNER_RATE = 0.01
OUTER_RATE = 0.7
OUTER_MU = 0.9


def update_kernel(
    red_ref, first_ref, second_ref,
    sum_out, first_out, second_out,
    red, window, flat, headrows, first_row, second_row, first, second, upd, low, low2, pair, pair2, total, total2,
    load_sem, x_send, x_recv, o_send, e_send, w_recv,
):
    xl, b, z, a, y = coords()
    fs = z * 8 + a * 4 + y
    holder = z * 8 + b * 4 + y
    sibling = device(xl, a, 1 - b, z, y)
    across = device(1 - xl, a, b, z, y)
    extra = [pltpu.make_async_copy(src, dst, load_sem.at[i]) for i, (src, dst) in enumerate(((first_ref, first_row), (second_ref, second_row)))]
    load = pltpu.make_async_copy(red_ref, red, load_sem.at[4])
    load.start()
    for copy in extra:
        copy.start()

    barrier = pltpu.get_barrier_semaphore()

    def greet(target):
        pl.semaphore_signal(barrier, inc=1, device_id=target, device_id_type=MESH)

    greet(sibling)
    greet(across)
    first_unit = ROUNDS * fs - EDGE_UNITS

    def window_unit(p):
        k = first_unit + p
        d = lax.rem(k + 32, 32)
        inside = jnp.logical_and(k >= 0, k < 32 * ROUNDS)
        mine = jnp.logical_and(a == b, d == holder)
        return inside, mine, device(xl, b, lax.rem(lax.div(d, 4), 2), lax.div(d, 8), lax.rem(d, 4))

    def greet_holder(p, carry):
        inside, mine, source = window_unit(p)

        @pl.when(jnp.logical_and(inside, jnp.logical_not(mine)))
        def _():
            greet(source)

        return carry

    lax.fori_loop(0, WINDOW, greet_holder, 0)

    def held_unit(j):
        k = 32 * j + holder
        q = lax.div(k, ROUNDS)
        r = lax.rem(k, ROUNDS)
        shift = jnp.where(r < EDGE_UNITS, -1, jnp.where(r >= ROUNDS - EDGE_UNITS, 1, 0))
        near = jnp.logical_and(shift != 0, jnp.logical_and(q + shift >= 0, q + shift < NSLOT))
        return k, q, jnp.where(near, q + shift, q), near

    def to_owner(j, k, s, send):
        p = k - (ROUNDS * s - EDGE_UNITS)
        src = red.at[j]
        dst = window.at[pl.ds(UNIT * p, UNIT)]
        sa = lax.rem(lax.div(s, 4), 2)
        mine = jnp.logical_and(a == b, s == fs)
        target = device(xl, sa, a, lax.div(s, 8), lax.rem(s, 4))
        away = pltpu.make_async_remote_copy(src_ref=src, dst_ref=dst, send_sem=send.at[j], recv_sem=w_recv.at[p], device_id=target, device_id_type=MESH)
        here = pltpu.make_async_copy(src, dst, load_sem.at[10])
        return mine, away, here

    def count(j, n):
        k, q, s, near = held_unit(j)
        first_away = jnp.logical_not(jnp.logical_and(a == b, q == fs))
        second_away = jnp.logical_and(near, jnp.logical_not(jnp.logical_and(a == b, s == fs)))
        return n + jnp.where(first_away, 1, 0) + jnp.where(second_away, 1, 0)

    outgoing = lax.fori_loop(0, ROUNDS, count, 2)
    pl.semaphore_wait(barrier, outgoing)
    load.wait()

    def give(j, carry):
        k, q, s, near = held_unit(j)
        mine, away, here = to_owner(j, k, q, o_send)

        @pl.when(mine)
        def _():
            here.start()

        @pl.when(jnp.logical_not(mine))
        def _():
            away.start()

        mine2, away2, here2 = to_owner(j, k, s, e_send)

        @pl.when(jnp.logical_and(near, mine2))
        def _():
            here2.start()

        @pl.when(jnp.logical_and(near, jnp.logical_not(mine2)))
        def _():
            away2.start()

        return carry

    lax.fori_loop(0, ROUNDS, give, 0)

    def given(j, carry):
        k, q, s, near = held_unit(j)
        mine, away, here = to_owner(j, k, q, o_send)

        @pl.when(jnp.logical_not(mine))
        def _():
            away.wait_send()

        mine2, away2, here2 = to_owner(j, k, s, e_send)

        @pl.when(jnp.logical_and(near, jnp.logical_not(mine2)))
        def _():
            away2.wait_send()

        return carry

    def clear(i, carry):
        flat[pl.ds(pl.multiple_of(i * 32, 32), 32), :] = jnp.zeros((32, 128), F32)
        return carry

    lax.fori_loop(0, BACK_ROWS // 32, clear, 0)

    for copy in extra:
        copy.wait()
    for source, rows_of in ((first_row, first), (second_row, second)):

        def eight(i, carry):
            rows_of[pl.ds(pl.multiple_of(i * 8, 8), 8), :] = source[0, pl.ds(pl.multiple_of(i * 1024, 1024), 1024)].reshape(8, 128)
            return carry

        whole = SHARD // 8
        lax.fori_loop(0, whole, eight, 0, unroll=2)
        rows_of[pl.ds(whole * 8, SHARD - whole * 8), :] = source[0, pl.ds(whole * 1024, (SHARD - whole * 8) * 128)].reshape(SHARD - whole * 8, 128)

    def got(p, carry):
        inside, mine, source = window_unit(p)
        place = window.at[pl.ds(UNIT * p, UNIT)]

        @pl.when(jnp.logical_and(inside, mine))
        def _():
            pltpu.make_async_copy(place, place, load_sem.at[10]).wait()

        @pl.when(jnp.logical_and(inside, jnp.logical_not(mine)))
        def _():
            pltpu.make_async_remote_copy(src_ref=place, dst_ref=place, send_sem=x_send.at[0], recv_sem=w_recv.at[p], device_id=sibling, device_id_type=MESH).wait_recv()

        return carry

    lax.fori_loop(0, WINDOW, got, 0)
    sends = []

    def go(src, dst, send, recv, k, target):
        copy = pltpu.make_async_remote_copy(src_ref=src, dst_ref=dst, send_sem=send.at[k], recv_sem=recv.at[k], device_id=target, device_id_type=MESH)
        copy.start()
        sends.append(copy)

    def arrive(dst, recv, k):
        pltpu.make_async_remote_copy(src_ref=dst, dst_ref=dst, send_sem=x_send.at[k], recv_sem=recv.at[k], device_id=sibling, device_id_type=MESH).wait_recv()

    low_tile = SLOT * fs - EDGE
    high_tile = SLOT * fs + SLOT + EDGE
    origin = SHARD * fs - FRONT
    for index, (base, c, groups, per, start) in enumerate(SECTIONS):
        if index == 1:
            lane = lax.broadcasted_iota(jnp.int32, (8, 128), 1)
            g0 = lax.div(jnp.maximum(SHARD * fs - base, 0), per)
            g1 = lax.div(jnp.maximum(SHARD * (fs + 1) - base, 0) + per - 1, per)

            def head_group(g, carry):
                t = start + g * 8 - low_tile
                for j in range(8):
                    headrows[pl.ds(j, 16, stride=8), :] = window[t + j].astype(F32)
                row = base + per * g - origin
                for i in range(16):
                    q, s = divmod(1000 * i, 128)
                    value = headrows[pl.ds(i * 8, 8), :]
                    if s:
                        value = pltpu.roll(value, s, 1)
                        flat[pl.ds(row + q, 8), :] += jnp.where(lane >= s, value, 0.0)
                        flat[pl.ds(row + q + 1, 8), :] += jnp.where(lane < s, value, 0.0)
                    else:
                        flat[pl.ds(row + q, 8), :] += value
                return carry

            lax.fori_loop(jnp.minimum(g0, groups), jnp.minimum(g1, groups), head_group, 0)
        else:

            def unit(n, carry):
                t = UNIT * n - start
                row = base + 16 * c * lax.div(t, c) + lax.rem(t, c) - origin
                for m in range(UNIT):
                    flat[pl.ds(row + m, 16, stride=c), :] = window[UNIT * n - low_tile + m].astype(F32)
                return carry

            lax.fori_loop(lax.div(jnp.maximum(low_tile, start), UNIT), lax.div(jnp.minimum(high_tile, start + c * groups), UNIT), unit, 0)

    fix_one = 1.0 / (1.0 - BETA_ONE**STEP)
    fix_two = 1.0 / (1.0 - BETA_TWO**STEP)

    def in_rows(fn, lo, hi, step=32):
        def body(i, carry):
            fn(pl.multiple_of(i * step, step), step)
            return carry

        n = (hi - lo) // step
        lax.fori_loop(lo // step, lo // step + n, body, 0)
        if lo + n * step < hi:
            fn(lo + n * step, hi - lo - n * step)

    def adam(r, n):
        grad = flat[pl.ds(FRONT + r, n), :]
        m = BETA_ONE * first[pl.ds(r, n), :] + (1.0 - BETA_ONE) * grad
        s = BETA_TWO * second[pl.ds(r, n), :] + (1.0 - BETA_TWO) * grad * grad
        first[pl.ds(r, n), :] = m
        second[pl.ds(r, n), :] = s
        u = (m * fix_one) / (jnp.sqrt(s * fix_two) + ADAM_EPS)
        upd[pl.ds(r, n), :] = u

    in_rows(adam, 0, SHARD)
    upd[pl.ds(SHARD, PADDED - SHARD), :] = jnp.zeros((PADDED - SHARD, 128), F32)
    outs = [pltpu.make_async_copy(src, dst, load_sem.at[5 + i]) for i, (src, dst) in enumerate(((first, first_out), (second, second_out)))]
    for copy in outs:
        copy.start()

    def lower(r, n):
        low[pl.ds(r, n), :] = upd[pl.ds(r, n), :].astype(BF16)

    in_rows(lower, 0, PADDED)
    go(low, low2, x_send, x_recv, 0, sibling)
    arrive(low2, x_recv, 0)
    half = PADDED // 2

    def pairs(r, n):
        at = pl.ds(pl.multiple_of(b * half + r, 16), n)
        pair[pl.ds(r, n), :] = low[at, :] + low2[at, :]

    in_rows(pairs, 0, half)
    go(pair, pair2, x_send, x_recv, 1, across)
    arrive(pair2, x_recv, 1)

    def fours(r, n):
        total[pl.ds(r, n), :] = pair[pl.ds(r, n), :].astype(F32) + pair2[pl.ds(r, n), :].astype(F32)

    in_rows(fours, 0, half)
    go(total, total2, x_send, x_recv, 2, sibling)

    arrive(total2, x_recv, 2)
    other = half - b * half
    final = [(total, sum_out.at[pl.ds(pl.multiple_of(b * half, 16), half)]), (total2, sum_out.at[pl.ds(pl.multiple_of(other, 16), half)])]
    final = [pltpu.make_async_copy(src, dst, load_sem.at[7 + i]) for i, (src, dst) in enumerate(final)]
    for copy in final:
        copy.start()
    for copy in sends:
        copy.wait_send()
    lax.fori_loop(0, ROUNDS, given, 0)
    for copy in outs + final:
        copy.wait()


def update(red, first, second):
    hbm = pl.BlockSpec(memory_space=pl.ANY)
    V = pltpu.VMEM
    flat = jax.ShapeDtypeStruct((SHARD, 128), F32)
    dma = pltpu.SemaphoreType.DMA
    return pl.pallas_call(
        update_kernel,
        out_shape=(jax.ShapeDtypeStruct((PADDED, 128), F32), flat, flat),
        in_specs=[hbm] * 3,
        out_specs=(hbm,) * 3,
        scratch_shapes=[
            V((ROUNDS, UNIT, 16, 128), BF16),
            V((EDGE + SLOT + EDGE, 16, 128), BF16),
            V((BACK_ROWS, 128), F32),
            V((128, 128), F32),
            V((1, SHARD * 128), F32),
            V((1, SHARD * 128), F32),
            V((SHARD, 128), F32),
            V((SHARD, 128), F32),
            V((PADDED, 128), F32),
            V((PADDED, 128), BF16),
            V((PADDED, 128), BF16),
            V((PADDED // 2, 128), BF16),
            V((PADDED // 2, 128), BF16),
            V((PADDED // 2, 128), F32),
            V((PADDED // 2, 128), F32),
            dma((11,)),
            dma((3,)),
            dma((3,)),
            dma((ROUNDS,)),
            dma((ROUNDS,)),
            dma((WINDOW,)),
        ],
        compiler_params=pltpu.CompilerParams(collective_id=1, has_side_effects=True, vmem_limit_bytes=60 * 1024 * 1024),
        name="update",
    )(red, first, second)


def finish_kernel(
    sum_ref, w_ref, mom_ref, first_ref, second_ref, loss_ref,
    avg_out, mom_out, new_out, first_out, second_out, loss_out,
    total, w, mom, first, second, averaged, sem, out_sem,
):
    cut = PADDED // 2
    pieces = [pl.ds(0, cut), pl.ds(cut, SHARD - cut)]
    loads = []
    for i, at in enumerate(pieces):
        loads.append([pltpu.make_async_copy(src.at[at], dst.at[at], sem.at[3 * i + k]) for k, (src, dst) in enumerate(((sum_ref, total), (w_ref, w), (mom_ref, mom)))])
    moments = [pltpu.make_async_copy(src, dst, sem.at[6 + i]) for i, (src, dst) in enumerate(((first_ref, first), (second_ref, second)))]
    for copy in loads[0] + loads[1] + moments:
        copy.start()
    outs = []

    def send(src, dst):
        copy = pltpu.make_async_copy(src, dst, out_sem.at[len(outs)])
        copy.start()
        outs.append(copy)

    loss_out[...] = loss_ref[0:1, 0:1]

    def outer(r, n):
        at = pl.ds(r, n)
        old = w[at, :]
        mean = INNER_RATE * (total[at, :] * 0.25 + DECAY * old)
        momentum = OUTER_MU * mom[at, :] + mean
        averaged[at, :] = mean
        mom[at, :] = momentum
        w[at, :] = old - OUTER_RATE * (mean + OUTER_MU * momentum)

    def block(i, carry):
        outer(pl.multiple_of(i * 96, 96), 96)
        return carry

    for i, at in enumerate(pieces):
        for copy in loads[i]:
            copy.wait()
        if i == 0:
            lax.fori_loop(0, cut // 96, block, 0)
        else:
            lax.fori_loop(cut // 96, SHARD // 96, block, 0)
            outer(SHARD // 96 * 96, SHARD - SHARD // 96 * 96)
        for src, dst in ((averaged, avg_out), (mom, mom_out), (w, new_out)):
            send(src.at[at], dst.at[at])
        if i == 0:
            for copy, src, dst in zip(moments, (first, second), (first_out, second_out)):
                copy.wait()
                send(src, dst.reshape(SHARD, 128))
    for copy in outs:
        copy.wait()


def finish(total, weights, momentum, first, second, loss):
    hbm = pl.BlockSpec(memory_space=pl.ANY)
    vmem = pl.BlockSpec(memory_space=pltpu.VMEM)
    V = pltpu.VMEM
    rows = jax.ShapeDtypeStruct((SHARD, 128), F32)
    row = jax.ShapeDtypeStruct((1, SHARD * 128), F32)
    return pl.pallas_call(
        finish_kernel,
        out_shape=(rows,) * 3 + (row,) * 2 + (jax.ShapeDtypeStruct((1, 1), F32),),
        in_specs=[hbm] * 5 + [vmem],
        out_specs=(hbm,) * 5 + (vmem,),
        scratch_shapes=[V((PADDED, 128), F32)] + [V((SHARD, 128), F32)] * 5 + [pltpu.SemaphoreType.DMA((8,)), pltpu.SemaphoreType.DMA((8,))],
        compiler_params=pltpu.CompilerParams(vmem_limit_bytes=60 * 1024 * 1024),
        name="finish",
    )(total, weights, momentum, first, second, loss)


def body(patches, labels, counts, weights, first_moments, second_moments, outer_momentum):
    flat = weights.reshape(SHARD, 128)
    reduced, loss = grads(flat, patches.reshape(2, P_SIZE, D), labels.reshape(2), counts.reshape(2))
    total, first, second = update(reduced, first_moments, second_moments)
    averaged, momentum, new_weights, first, second, loss = finish(total, flat, outer_momentum.reshape(SHARD, 128), first, second, loss)
    return (
        averaged.reshape(-1),
        momentum.reshape(-1),
        new_weights.reshape(-1),
        first,
        second,
        loss,
    )


def solution(mesh):
    placed = (
        P("rep", None, None, "fsdp", None, None),
        P("rep", None, None, "fsdp"),
        P("rep", None, None),
        P("fsdp"),
        P("rep", "fsdp"),
        P("rep", "fsdp"),
        P("fsdp"),
    )
    return jax.shard_map(
        body,
        mesh=mesh,
        in_specs=placed,
        out_specs=(
            P("fsdp"),
            P("fsdp"),
            P("fsdp"),
            P("rep", "fsdp"),
            P("rep", "fsdp"),
            P("rep", None),
        ),
        check_vma=False,
    )
```

```python
from functools import partial

import jax
import jax.numpy as jnp
from jax import lax
from jax.experimental import pallas as pl
from jax.experimental.pallas import tpu as pltpu
from jax.sharding import PartitionSpec as P

SHARD = 2098
SLOT = 132
HALF = 66
QUART = 33
NSLOT = 32
ROUNDS = 22
UNIT = 6
STAGES = ((0, 4), (4, 10), (10, 16), (16, 22))
SECTIONS = []
_t = 0
for _base, _c, _g, _rpg in ((0, 6, 61, 96), (5796, 8, 48, 125), (11796, 6, 1, 96), (11820, 18, 48, 288), (25644, 6, 48, 96), (30252, 24, 48, 384), (48684, 6, 192, 96)):
    SECTIONS.append((_base, _c, _g, _rpg, _t))
    _t += _c * _g
NTILE = _t
HI = 352
LO = 224
MARGIN = 512
FROWS = 3072
HEAD_ROWS = 16
MESH = pl.DeviceIdType.MESH


def coords():
    rep = lax.axis_index("rep")
    fs = lax.axis_index("fsdp")
    return lax.div(rep, 2), lax.rem(rep, 2), lax.div(fs, 8), lax.rem(lax.div(fs, 4), 2), lax.rem(fs, 4)


def device(xl, xh, core, z, y):
    return {"rep": xl * 2 + core, "fsdp": z * 8 + xh * 4 + y}


def flat_device(xl, core, s):
    return device(xl, lax.rem(lax.div(s, 4), 2), core, lax.div(s, 8), lax.rem(s, 4))


class Links:

    def __init__(self, T, R, RA, RB, g_send, g_recv, r_send, r_recv):
        self.xl, self.b, self.z, self.a, self.y = coords()
        self.T5 = T.reshape(ROUNDS, 4, 2, 4, UNIT, 16, 128)
        self.R, self.RA, self.RB = R, RA, RB
        self.g_send, self.g_recv, self.r_send, self.r_recv = g_send, g_recv, r_send, r_recv
        self.pending = []
        self.sibling = device(self.xl, self.a, 1 - self.b, self.z, self.y)

    def at_y(self, k):
        return device(self.xl, self.a, self.b, self.z, lax.rem(self.y + k, 4))

    def at_z(self, k):
        return device(self.xl, self.a, self.b, lax.rem(self.z + k, 4), self.y)

    def at_x(self, k):
        a = lax.rem(self.a + (self.xl if k == 1 else 1 - self.xl), 2)
        return device(1 - self.xl, a, self.b, self.z, self.y)

    def go(self, src, dst, send, recv, target):
        copy = pltpu.make_async_remote_copy(src_ref=src, dst_ref=dst, send_sem=send, recv_sem=recv, device_id=target, device_id_type=MESH)
        copy.start()
        self.pending.append(copy)

    def landed(self, dst, send, recv):
        pltpu.make_async_remote_copy(src_ref=dst, dst_ref=dst, send_sem=send, recv_sem=recv, device_id=self.sibling, device_id_type=MESH).wait_recv()

    def sent(self):
        for copy in self.pending:
            copy.wait_send()
        self.pending = []

    def span(self, i, h):
        lo, hi = STAGES[i]
        n = (hi - lo) // 2
        return pl.ds(lo + h * n, n)

    def first_axis(self, h, k):
        return (self.at_y if h == 0 else self.at_z)(k)

    def second_axis(self, h, k):
        return (self.at_z if h == 0 else self.at_y)(k)

    def gathered(self, i, h):
        lo, hi = STAGES[i]
        n = (hi - lo) // 2
        if i == 0:
            return pl.ds(lo + h * n, n)
        return pl.ds(lo + h * n + self.xl, 2)

    def single(self, i, h, own):
        lo, hi = STAGES[i]
        parity = self.xl if own else 1 - self.xl
        return pl.ds(lo + h * ((hi - lo) // 2) + 2 * parity, 1)

    def one(self, i, h, k, q=None):
        rd = self.gathered(i, h)
        t = pl.ds(0, UNIT) if q is None else pl.ds(3 * q, 3)
        if h == 0:
            return self.T5.at[rd, self.z, self.b, lax.rem(self.y + k, 4), t]
        return self.T5.at[rd, lax.rem(self.z + k, 4), self.b, self.y, t]

    def row(self, rd, h, k, core=None, p=None):
        core = self.b if core is None else core
        t = pl.ds(0, 4) if p is None else pl.ds(2 * p, 2)
        if h == 0:
            return self.T5.at[rd, lax.rem(self.z + k, 4), core, t]
        return self.T5.at[rd, t, core, lax.rem(self.y + k, 4)]

    def gsem(self, i, h, k):
        n = (i * 2 + h) * 24 + k
        return self.g_send.at[n], self.g_recv.at[n]

    def gather_go(self, i, h, k, view, target):
        self.go(view, view, *self.gsem(i, h, k), target)

    def gather_wait(self, i, h, k, view):
        self.landed(view, *self.gsem(i, h, k))

    def share(self, i, h, m, k):
        self.gather_go(i, h, 8 + m, self.row(self.gathered(i, h), h, k), self.sibling)
        if i > 0:
            rd = self.single(i, h, True)
            self.gather_go(i, h, 12 + m, self.row(rd, h, k, p=0), self.at_x(1))
            self.gather_go(i, h, 16 + m, self.row(rd, h, k, p=1), self.at_x(3))

    def gather_step(self, i, step):
        for h in range(2):
            rd = self.gathered(i, h)
            if step == 0:
                self.gather_go(i, h, 0, self.one(i, h, 0), self.first_axis(h, 1))
                self.gather_go(i, h, 1, self.one(i, h, 0), self.first_axis(h, 3))
            elif step == 1:
                self.gather_wait(i, h, 0, self.one(i, h, 3))
                self.gather_go(i, h, 2, self.one(i, h, 3, 0), self.first_axis(h, 1))
                self.gather_wait(i, h, 1, self.one(i, h, 1))
                self.gather_go(i, h, 3, self.one(i, h, 1, 1), self.first_axis(h, 3))
            elif step == 2:
                self.gather_wait(i, h, 2, self.one(i, h, 2, 0))
                self.gather_wait(i, h, 3, self.one(i, h, 2, 1))
                self.gather_go(i, h, 4, self.row(rd, h, 0), self.second_axis(h, 1))
                self.gather_go(i, h, 5, self.row(rd, h, 0), self.second_axis(h, 3))
                self.share(i, h, 0, 0)
            elif step == 3:
                self.gather_wait(i, h, 4, self.row(rd, h, 3))
                self.gather_go(i, h, 6, self.row(rd, h, 3, p=0), self.second_axis(h, 1))
                self.share(i, h, 1, 3)
                self.gather_wait(i, h, 5, self.row(rd, h, 1))
                self.gather_go(i, h, 7, self.row(rd, h, 1, p=1), self.second_axis(h, 3))
                self.share(i, h, 2, 1)
            elif step == 4:
                self.gather_wait(i, h, 6, self.row(rd, h, 2, p=0))
                self.gather_wait(i, h, 7, self.row(rd, h, 2, p=1))
                self.share(i, h, 3, 2)
            elif step == 5:
                if i > 0:
                    other = self.single(i, h, False)
                    for m, k in enumerate((0, 3, 1, 2)):
                        self.gather_wait(i, h, 12 + m, self.row(other, h, k, p=0))
                        self.gather_wait(i, h, 16 + m, self.row(other, h, k, p=1))
                        self.gather_go(i, h, 20 + m, self.row(other, h, k), self.sibling)
            else:
                for m, k in enumerate((0, 3, 1, 2)):
                    self.gather_wait(i, h, 8 + m, self.row(rd, h, k, core=1 - self.b))
                    if i > 0:
                        self.gather_wait(i, h, 20 + m, self.row(self.single(i, h, False), h, k, core=1 - self.b))

    def rsem(self, i, h, k):
        n = (i * 2 + h) * 13 + k
        return self.r_send.at[n], self.r_recv.at[n]

    def cell(self, i, h, k, q):
        rd = self.span(i, h)
        t = pl.ds(3 * q, 3)
        if h == 0:
            return self.T5.at[rd, self.z, self.b, lax.rem(self.y + k, 4), t]
        return self.T5.at[rd, lax.rem(self.z + k, 4), self.b, self.y, t]

    def add(self, dst, *sources, inner=()):
        n = dst.shape[0]

        def one(r, carry):
            for k in range(inner) if inner else (None,):
                at = (r,) if k is None else (r, k)
                if len(sources) == 1:
                    dst[at] = dst[at] + sources[0][at]
                else:
                    total = dst[at].astype(jnp.float32)
                    for source in sources:
                        total = total + source[at].astype(jnp.float32)
                    dst[at] = total.astype(jnp.bfloat16)
            return carry

        lax.fori_loop(0, n, one, 0)

    def reduce_step(self, i, h, step):
        rd = self.span(i, h)
        T5 = self.T5

        def send_a(k, ka, p, shift):
            self.go(self.row(rd, h, ka, p=p), self.RA.at[k, rd], *self.rsem(i, h, 1 + k), self.second_axis(h, shift))

        def wait_a(k):
            self.landed(self.RA.at[k, rd], *self.rsem(i, h, 1 + k))

        def send_b(k, kb, q, shift):
            self.go(self.cell(i, h, kb, q), self.RB.at[k, rd], *self.rsem(i, h, 7 + k), self.first_axis(h, shift))

        def wait_b(k):
            self.landed(self.RB.at[k, rd], *self.rsem(i, h, 7 + k))

        if step == 0:
            self.go(T5.at[rd, :, 1 - self.b], self.R.at[rd], *self.rsem(i, h, 0), self.sibling)
        elif step == 1:
            self.landed(self.R.at[rd], *self.rsem(i, h, 0))
            mine, theirs = T5.at[rd, :, self.b], self.R.at[rd]
            n = mine.shape[0]

            def both(r, carry):
                q = lax.div(r, 4)
                w = lax.rem(r, 4)
                for k in range(4):
                    mine[q, w, k] = mine[q, w, k] + theirs[q, w, k]
                return carry

            lax.fori_loop(0, 4 * n, both, 0)
            send_a(0, 2, 0, 1)
            send_a(1, 2, 1, 3)
            send_a(2, 1, 1, 1)
            send_a(3, 3, 0, 3)
        elif step == 2:
            wait_a(0)
            self.add(self.row(rd, h, 1, p=0), self.RA.at[0, rd], inner=2)
            send_a(4, 1, 0, 1)
            wait_a(1)
            self.add(self.row(rd, h, 3, p=1), self.RA.at[1, rd], inner=2)
            send_a(5, 3, 1, 3)
        elif step == 3:
            for k in (2, 3, 4, 5):
                wait_a(k)
            self.add(self.row(rd, h, 0, p=0), self.RA.at[3, rd], self.RA.at[4, rd], inner=2)
            self.add(self.row(rd, h, 0, p=1), self.RA.at[2, rd], self.RA.at[5, rd], inner=2)
            send_b(0, 2, 0, 1)
            send_b(1, 2, 1, 3)
            send_b(2, 1, 1, 1)
            send_b(3, 3, 0, 3)
        elif step == 4:
            wait_b(0)
            self.add(self.cell(i, h, 1, 0), self.RB.at[0, rd])
            send_b(4, 1, 0, 1)
            wait_b(1)
            self.add(self.cell(i, h, 3, 1), self.RB.at[1, rd])
            send_b(5, 3, 1, 3)
        else:
            for k in (2, 3, 4, 5):
                wait_b(k)
            self.add(self.cell(i, h, 0, 0), self.RB.at[3, rd], self.RB.at[4, rd])
            self.add(self.cell(i, h, 0, 1), self.RB.at[2, rd], self.RB.at[5, rd])


def start_gather(links, w_ref, patch_ref, labels_ref, counts_ref, T, patch_in, meta_in, meta_ref, flat, headrows, lob, hib, rlo, rhi, slot, local_sem, x_send, x_recv, u_send, u_recv):
    xl, b, z, a, y = links.xl, links.b, links.z, links.a, links.y
    fs = z * 8 + a * 4 + y
    swap = a != b
    xo = lax.rem(xl + a + b, 2)
    holder = z * 8 + b * 4 + y
    up = flat_device(xl, b, lax.rem(fs + 1, NSLOT))
    down = flat_device(xl, b, lax.rem(fs + NSLOT - 1, NSLOT))
    mirror = device(xl, b, a, z, y)
    load = pltpu.make_async_copy(w_ref, flat.at[pl.ds(MARGIN, SHARD)], local_sem.at[0])
    load.start()
    barrier = pltpu.get_barrier_semaphore()
    total = (counts_ref[0] + counts_ref[1]).astype(jnp.float32)
    for m in range(2):
        valid = jnp.full((1, 128), jnp.where(fs < counts_ref[m], 1.0, 0.0), jnp.float32)
        meta_ref[m : m + 1, :] = jnp.full((1, 128), labels_ref[m].astype(jnp.float32), jnp.float32)
        meta_ref[2 + m : 3 + m, :] = valid / jnp.full((1, 128), total, jnp.float32)
        meta_ref[4 + m : 5 + m, :] = valid
    meta_ref[6:8, :] = jnp.zeros((2, 128), jnp.float32)

    def greet(target):
        pl.semaphore_signal(barrier, inc=1, device_id=target, device_id_type=MESH)

    def wanted(j, parity):
        return jnp.logical_or(j < STAGES[0][1], lax.rem(j + 3 - STAGES[0][1] % 3, 3) != 2 * (1 - parity))

    for target in (up, down, links.at_x(1), links.at_x(3), links.at_y(1), links.at_y(3), links.at_z(1), links.at_z(3), links.sibling):
        greet(target)

    @pl.when(swap)
    def _():
        greet(mirror)

    own_index = lax.rem(fs * 11, NSLOT)
    keeps = jnp.logical_and(a == b, own_index < ROUNDS)

    def greet_source(j, carry):
        s = lax.div(32 * j + holder, ROUNDS)
        sa = lax.rem(lax.div(s, 4), 2)

        @pl.when(jnp.logical_and(wanted(j, xl), jnp.logical_not(jnp.logical_and(keeps, s == fs))))
        def _():
            greet(device(lax.rem(xl + sa + a, 2), sa, a, lax.div(s, 8), lax.rem(s, 4)))

        return carry

    lax.fori_loop(0, ROUNDS, greet_source, 0)
    def unit_goes(i):
        there = wanted(lax.div(ROUNDS * fs + i, 32), xo)
        stays = jnp.logical_and(keeps, i == own_index)
        return jnp.logical_and(there, jnp.logical_not(stays)), jnp.logical_and(there, stays)

    outgoing = lax.fori_loop(0, ROUNDS, lambda i, n: n + jnp.where(unit_goes(i)[0], 1, 0), 9)
    pl.semaphore_wait(barrier, outgoing + jnp.where(swap, 1, 0))
    load.wait()

    def remote(src, dst, k, target):
        return pltpu.make_async_remote_copy(src_ref=src, dst_ref=dst, send_sem=x_send.at[k], recv_sem=x_recv.at[k], device_id=target, device_id_type=MESH)

    hib[...] = flat[pl.ds(MARGIN + SHARD - HI, HI), :].astype(jnp.bfloat16)
    to_up = remote(hib, rlo, 0, up)
    to_up.start()
    lob[...] = flat[pl.ds(MARGIN, LO), :].astype(jnp.bfloat16)
    to_down = remote(lob, rhi, 1, down)
    to_down.start()
    patch_swap = remote(patch_ref, patch_in, 2, mirror)
    meta_swap = remote(meta_ref, meta_in, 3, mirror)
    patch_keep = pltpu.make_async_copy(patch_ref, patch_in, local_sem.at[1])
    meta_keep = pltpu.make_async_copy(meta_ref, meta_in, local_sem.at[2])
    first = ROUNDS * fs
    origin = SHARD * fs - MARGIN

    def unit_copy(i):
        k = first + i
        d = lax.rem(k, 32)
        src = slot.at[pl.ds(UNIT * i, UNIT)]
        dst = T.at[pl.ds(UNIT * k, UNIT)]
        target = device(xo, b, lax.rem(lax.div(d, 4), 2), lax.div(d, 8), lax.rem(d, 4))
        away = pltpu.make_async_remote_copy(src_ref=src, dst_ref=dst, send_sem=u_send.at[i], recv_sem=u_recv.at[lax.div(k, 32)], device_id=target, device_id_type=MESH)
        return away, (src, dst)

    def send_unit(i):
        away, (src, dst) = unit_copy(i)
        goes, stays = unit_goes(i)

        @pl.when(stays)
        def _():
            pltpu.make_async_copy(src, dst, local_sem.at[3]).start()

        @pl.when(goes)
        def _():
            away.start()

    lane = lax.broadcasted_iota(jnp.int32, (8, 128), 1)

    def head_group(g, base, per, start):
        row = base + per * g - origin
        for i in range(16):
            q, s = divmod(1000 * i, 128)
            one = flat[pl.ds(row + q, 8), :]
            if s:
                two = flat[pl.ds(row + q + 1, 8), :]
                one = jnp.where(lane < 128 - s, pltpu.roll(one, 128 - s, 1), pltpu.roll(two, 128 - s, 1))
            headrows[pl.ds(i * 8, 8), :] = one
        for j in range(8):
            t = start + g * 8 + j - UNIT * first

            @pl.when(jnp.logical_and(t >= 0, t < SLOT))
            def _():
                slot[t] = headrows[pl.ds(j, 16, stride=8), :].astype(jnp.bfloat16)

    def inside(row, rows):
        return jnp.logical_and(row >= MARGIN, row + rows <= MARGIN + SHARD)

    def convert(near):
        for index, (base, c, groups, per, start) in enumerate(SECTIONS):
            lo = jnp.maximum(UNIT * first, start)
            hi = jnp.minimum(UNIT * first + SLOT, start + c * groups)
            if index == 1:

                def group(g, carry):
                    @pl.when(inside(base + per * g - origin, per + 1) == near)
                    def _():
                        head_group(g, base, per, start)

                    return carry

                lax.fori_loop(lax.div(jnp.maximum(lo, start) - start, 8), lax.div(jnp.maximum(hi, start) - start + 7, 8), group, 0)
                if not near:

                    def deal(u, carry):
                        send_unit(u - first)
                        return carry

                    lax.fori_loop(lax.div(lo, UNIT), lax.div(hi, UNIT), deal, 0)
            else:

                def unit(u, carry):
                    t = UNIT * u - start
                    g = lax.div(t, c)
                    row = base + 16 * c * g + lax.rem(t, c) - origin

                    @pl.when(inside(row, 15 * c + UNIT) == near)
                    def _():
                        for k in range(UNIT):
                            slot[UNIT * (u - first) + k] = flat[pl.ds(row + k, 16, stride=c), :].astype(jnp.bfloat16)
                        send_unit(u - first)

                    return carry

                lax.fori_loop(lax.div(lo, UNIT), lax.div(hi, UNIT), unit, 0)

    convert(True)
    to_up.wait_recv()
    flat[pl.ds(MARGIN - HI, HI), :] = rlo[...].astype(jnp.float32)
    to_down.wait_recv()
    flat[pl.ds(MARGIN + SHARD, LO), :] = rhi[...].astype(jnp.float32)
    convert(False)

    @pl.when(fs == NSLOT - 1)
    def _():
        slot[pl.ds(SLOT - 12, 12)] = jnp.zeros((12, 16, 128), jnp.bfloat16)
        send_unit(ROUNDS - 2)
        send_unit(ROUNDS - 1)

    @pl.when(swap)
    def _():
        patch_swap.start()
        meta_swap.start()

    @pl.when(jnp.logical_not(swap))
    def _():
        patch_keep.start()
        meta_keep.start()

    def units_here(i):
        def wait(j, carry):
            place = T.at[pl.ds(UNIT * (32 * j + holder), UNIT)]
            mine = jnp.logical_and(keeps, lax.div(32 * j + holder, ROUNDS) == fs)

            @pl.when(jnp.logical_and(wanted(j, xl), mine))
            def _():
                pltpu.make_async_copy(place, place, local_sem.at[3]).wait()

            @pl.when(jnp.logical_and(wanted(j, xl), jnp.logical_not(mine)))
            def _():
                pltpu.make_async_remote_copy(src_ref=place, dst_ref=place, send_sem=u_send.at[0], recv_sem=u_recv.at[j], device_id=links.sibling, device_id_type=MESH).wait_recv()

            return carry

        lax.fori_loop(*STAGES[i], wait, 0)

    def finish_start():
        def wait(i, carry):
            away, unused = unit_copy(i)

            @pl.when(unit_goes(i)[0])
            def _():
                away.wait_send()

            return carry

        lax.fori_loop(0, ROUNDS, wait, 0)
        to_up.wait_send()
        to_down.wait_send()

        @pl.when(swap)
        def _():
            patch_swap.wait()
            meta_swap.wait()

        @pl.when(jnp.logical_not(swap))
        def _():
            patch_keep.wait()
            meta_keep.wait()

    return units_here, finish_start


D = 768
HEADS = 12
HEAD_DIM = 64
FF = 3072
CLS = 1000
P_SIZE = 196
ROWS = 208
TOK = 2 * ROWS
NORM_EPS = 1e-06
SMOOTHING = 0.1
NTILES = 4224
T_E, T_HEAD, T_NORM, T_QKV, T_OUT, T_IN, T_FO = 0, 366, 750, 756, 1620, 1908, 3060
T_POS = 288
BLK = 256
BLOCKS = ((0, 96), (96, 112), (208, 96), (304, 112))
F32 = jnp.float32
BF16 = jnp.bfloat16
ROOT_HALF = 0.7071067811865476
INV_ROOT_TWO_PI = 0.3989422804014327


def dot(x, w):
    return lax.dot_general(x, w, (((1,), (0,)), ((), ())), preferred_element_type=F32)


def dot_t(x, w):
    return lax.dot_general(x, w, (((1,), (1,)), ((), ())), preferred_element_type=F32)


def t_dot(x, w):
    return lax.dot_general(x, w, (((0,), (0,)), ((), ())), preferred_element_type=F32)


def stats(x, keep, r, k):
    mean = jnp.sum(x, -1, keepdims=True) * (1.0 / D)
    centred = x - mean
    var = jnp.sum(centred * centred, -1, keepdims=True) * (1.0 / D)
    rstd = lax.rsqrt(var + NORM_EPS)
    keep[r, k : k + 1] = mean
    keep[r, k + 1 : k + 2] = rstd
    return centred * rstd


def kept(x, keep, r, k):
    rstd = keep[r, k + 1 : k + 2]
    return (x - keep[r, k : k + 1]) * rstd, rstd


def norm_back(d_hat, hat, rstd):
    m1 = jnp.sum(d_hat, -1, keepdims=True) * (1.0 / D)
    m2 = jnp.sum(d_hat * hat, -1, keepdims=True) * (1.0 / D)
    return rstd * (d_hat - m1 - hat * m2)


def compute(step, patch_ref, meta_ref, loss_ref, T, x, h, a, at, mix, prob, o, h1, a2, hid, slope, h2, dh, dyb, keep):
    G = T
    dmix = mix

    def section(ref, start, c, groups):
        return ref.at[pl.ds(start, groups * c)].reshape(groups, c, 16, 128)

    def cols(start, c, groups, j):
        part = section(T, start, c, groups)
        return jnp.concatenate([part[:, 2 * j + k].reshape(groups * 16, 128) for k in range(2)], axis=1)

    def put_cols(start, c, groups, j, value):
        low = value.astype(BF16)
        part = section(G, start, c, groups)
        for k in range(2):
            part[:, 2 * j + k] = low[:, k * 128 : (k + 1) * 128].reshape(groups, 16, 128)

    def row_of(start, k):
        return jnp.concatenate([T[start + j][k : k + 1, :] for j in range(6)], axis=1).astype(F32)

    def lanes(j):
        return pl.ds(pl.multiple_of(j * BLK, BLK), BLK)

    step("start")
    for i in range(2):
        x[pl.ds(i * ROWS, 192), :] = patch_ref[i, pl.ds(0, 192), :]
        x[pl.ds(i * ROWS + 192, 16), :] = jnp.concatenate([patch_ref[i, pl.ds(192, 4), :], jnp.zeros((12, D), BF16)], axis=0)

    real = lax.broadcasted_iota(jnp.int32, (ROWS, 128), 0) < P_SIZE
    for j in range(3):
        acc = dot(x[...], cols(T_E, 6, 48, j))
        p = cols(T_POS, 6, 13, j).astype(F32)
        p = jnp.where(lax.broadcasted_iota(jnp.int32, (ROWS, BLK), 0) < P_SIZE, p, 0.0)
        for i in range(2):
            h[pl.ds(i * ROWS, ROWS), pl.ds(j * BLK, BLK)] = acc[i * ROWS : (i + 1) * ROWS] + p

    step("embedded")
    gain1, shift1, gain2, shift2 = (row_of(T_NORM, k) for k in range(4))

    for at_row, n in BLOCKS:
        r = pl.ds(at_row, n)
        a[r, :] = (stats(h[r, :], keep, r, 0) * gain1 + shift1).astype(BF16)

    step("qkv")
    def wide_cols(start, c, groups, j):
        return jnp.concatenate([cols(start, c, groups, 3 * j + k) for k in range(3)], axis=1)

    def wide_lanes(j):
        return pl.ds(pl.multiple_of(j * D, D), D)

    def mix_block(j, carry):
        mix[:, wide_lanes(j)] = dot(a[...], wide_cols(T_QKV, 18, 48, j)).astype(BF16)
        return carry

    lax.fori_loop(0, 3, mix_block, 0)

    first_half = lax.broadcasted_iota(jnp.int32, (ROWS, 128), 1) < HEAD_DIM
    key_ok = lax.broadcasted_iota(jnp.int32, (ROWS, ROWS), 0) < P_SIZE
    first_rows = lax.broadcasted_iota(jnp.int32, (128, ROWS), 0) < HEAD_DIM
    halves = (first_half, jnp.logical_not(first_half))
    zero = jnp.zeros((ROWS, 128), BF16)

    def split(block):
        return jnp.concatenate([jnp.where(first_half, block, zero), jnp.where(first_half, zero, block)], axis=0)

    def heads_of(p, i):
        r = pl.ds(i * ROWS, ROWS)
        return r, [pl.ds(pl.multiple_of(p * 128 + D * k, 128), 128) for k in range(3)]

    def attend(p, carry):
        for i in range(2):
            r, ls = heads_of(p, i)
            q, k, v = (mix[r, l] for l in ls)
            q = q * jnp.asarray(0.125, BF16)
            vt = v.T
            outs = []
            for e in range(2):
                s = dot_t(jnp.where(halves[e], k, zero), q)
                s = jnp.where(key_ok, s, -jnp.inf)
                ex = jnp.exp(s - jnp.max(s, 0, keepdims=True))
                pr = (ex * (1.0 / jnp.sum(ex, 0, keepdims=True))).astype(BF16)
                prob[p * 2 + i, e] = pr
                outs.append(dot(vt, pr))
            o[r, ls[0]] = jnp.where(first_rows, outs[0], outs[1]).astype(BF16).T
        return carry

    parts = ((0, 2), (2, 3), (3, 5), (5, 6))
    for part in range(4):
        step("attend%d" % part)
        lax.fori_loop(*parts[part], attend, 0)
    step("attended")
    for j in range(3):
        h1[:, pl.ds(j * BLK, BLK)] = h[:, pl.ds(j * BLK, BLK)] + dot(o[...], cols(T_OUT, 6, 48, j))

    for at_row, n in BLOCKS:
        r = pl.ds(at_row, n)
        a2[r, :] = (stats(h1[r, :], keep, r, 2) * gain2 + shift2).astype(BF16)

    step("up")
    def up_block(j, carry):
        u = dot(a2[...], wide_cols(T_IN, 24, 48, j))
        phi = 0.5 * (1.0 + lax.erf(u * ROOT_HALF))
        pdf = jnp.exp(-0.5 * u * u) * INV_ROOT_TWO_PI
        hid[:, wide_lanes(j)] = (u * phi).astype(BF16)
        slope[:, wide_lanes(j)] = (phi + u * pdf).astype(BF16)
        return carry

    lax.fori_loop(0, 4, up_block, 0)
    step("down")
    for j in range(3):
        h2[:, pl.ds(j * BLK, BLK)] = h1[:, pl.ds(j * BLK, BLK)] + dot(hid[...], cols(T_FO, 6, 192, j))

    step("pool")
    gain_end, shift_end = (row_of(T_POS + 72, 4 + k) for k in range(2))
    means = []
    last_rows = lax.broadcasted_iota(jnp.int32, (112, D), 0) < P_SIZE - 96
    for i in range(2):
        total = jnp.zeros((8, D), F32)
        for at_row, n in BLOCKS[2 * i : 2 * i + 2]:
            r = pl.ds(at_row, n)
            hat = stats(h2[r, :], keep, r, 4)
            if n == 112:
                hat = jnp.where(last_rows, hat, 0.0)
            total = total + jnp.sum(hat.reshape(n // 8, 8, D), 0)
        means.append(jnp.sum(total, 0, keepdims=True) * (1.0 / P_SIZE))
    mean_hat = jnp.concatenate(means + [jnp.zeros((14, D), F32)], axis=0)
    two = lax.broadcasted_iota(jnp.int32, (16, D), 0) < 2
    pooled = jnp.where(two, mean_hat * gain_end + shift_end, 0.0).astype(BF16)
    logits = jnp.concatenate([dot(pooled, cols(T_HEAD, 8, 48, j)) for j in range(4)], axis=1)
    lane = lax.broadcasted_iota(jnp.int32, (16, 1024), 1)
    lane_f = lane.astype(F32)
    inside = lane < CLS
    logits = jnp.where(inside, logits, -1e30)
    top = jnp.max(logits, -1, keepdims=True)
    total = jnp.sum(jnp.where(inside, jnp.exp(logits - top), 0.0), -1, keepdims=True)
    logp = logits - top - jnp.log(total)
    meta = meta_ref[...]
    pad14 = jnp.zeros((14, 1), F32)
    label = jnp.concatenate([meta[0:2, 0:1], pad14], axis=0)
    scale = jnp.concatenate([meta[2:4, 0:1], pad14], axis=0)
    valid = jnp.concatenate([meta[4:6, 0:1], pad14], axis=0)
    target = jnp.where(lane_f == label, 1.0 - SMOOTHING, 0.0) + SMOOTHING / CLS
    values = -jnp.sum(jnp.where(inside, target * logp, 0.0), -1, keepdims=True)
    loss_ref[...] = jnp.broadcast_to(jnp.sum(values * valid, 0, keepdims=True), (8, 128))
    d_logits = jnp.where(inside, scale * (jnp.exp(logp) - target), 0.0).astype(BF16)
    d_pooled = jnp.zeros((16, D), F32)
    for j in range(4):
        w = cols(T_HEAD, 8, 48, j)
        d_pooled = d_pooled + dot_t(d_logits[:, j * BLK : (j + 1) * BLK], w)
        put_cols(T_HEAD, 8, 48, j, t_dot(pooled, d_logits[:, j * BLK : (j + 1) * BLK]))
    d_gain_end = jnp.sum(d_pooled * mean_hat, 0, keepdims=True)
    d_shift_end = jnp.sum(d_pooled, 0, keepdims=True)
    for i in range(2):
        d_hat = d_pooled[i : i + 1, :] * (1.0 / P_SIZE) * gain_end

        m1 = jnp.sum(d_hat, -1, keepdims=True) * (1.0 / D)
        for at_row, n in BLOCKS[2 * i : 2 * i + 2]:
            r = pl.ds(at_row, n)
            hat, rstd = kept(h2[r, :], keep, r, 4)
            m2 = jnp.sum(d_hat * hat, -1, keepdims=True) * (1.0 / D)
            d = rstd * ((d_hat - m1) - hat * m2)
            if n == 112:
                d = jnp.where(last_rows, d, 0.0)
            dh[r, :] = d
            dyb[r, :] = d.astype(BF16)

    step("backward")
    at[...] = a2[...].T
    da = h2

    wide = D // 16

    def down_block(j, carry):
        part = section(T, T_FO + j * wide * 6, 6, wide)
        w = jnp.concatenate([part[:, k].reshape(D, 128) for k in range(6)], axis=1)
        dy = dyb[...]
        d_w = t_dot(hid[:, wide_lanes(j)], dy).astype(BF16)
        hid[:, wide_lanes(j)] = (dot_t(dy, w) * slope[:, wide_lanes(j)].astype(F32)).astype(BF16)
        for k in range(6):
            part[:, k] = d_w[:, k * 128 : (k + 1) * 128].reshape(wide, 16, 128)
        return carry

    G[pl.ds(4212, 12)] = jnp.zeros((12, 16, 128), BF16)
    lax.fori_loop(0, 3, down_block, 0)
    step("fc_out0")
    lax.fori_loop(3, 4, down_block, 0)
    step("fc_out1")
    def row_block(start, c, j):
        part = section(T, start + j * 16 * c, c, 16)
        return jnp.concatenate([part[:, k].reshape(BLK, 128) for k in range(c)], axis=1)

    def put_rows(start, c, j, first, value):
        part = section(G, start + j * 16 * c, c, 16)
        low = value.astype(BF16)
        for k in range(value.shape[1] // 128):
            part[:, first + k] = low[:, k * 128 : (k + 1) * 128].reshape(16, 16, 128)

    for j in range(3):
        da[:, pl.ds(j * BLK, BLK)] = dot_t(hid[...], row_block(T_IN, 24, j))
    step("fc_in0")
    for j in range(3):
        for k in range(4):
            put_rows(T_IN, 24, j, 6 * k, dot(at[pl.ds(j * BLK, BLK), :], hid[:, pl.ds(k * D, D)]))
        step("fc_in%d" % (j + 1))

    def norm_grads(inputs, column, gain):
        dg, ds = jnp.zeros((8, D), F32), jnp.zeros((8, D), F32)
        for at_row, n in BLOCKS:
            r = pl.ds(at_row, n)
            hat, rstd = kept(inputs[r, :], keep, r, column)
            d = da[r, :]
            new = dh[r, :] + norm_back(d * gain, hat, rstd)
            dh[r, :] = new
            dyb[r, :] = new.astype(BF16)
            dg = dg + jnp.sum((d * hat).reshape(n // 8, 8, D), 0)
            ds = ds + jnp.sum(d.reshape(n // 8, 8, D), 0)
        return dg, ds

    d_gain2, d_shift2 = norm_grads(h1, 2, gain2)

    step("normed2")
    at[...] = o[...].T
    for j in range(3):
        o[:, pl.ds(j * BLK, BLK)] = dot_t(dyb[...], row_block(T_OUT, 6, j)).astype(BF16)
    for j in range(3):
        put_rows(T_OUT, 6, j, 0, dot(at[pl.ds(j * BLK, BLK), :], dyb[...]))

    step("out")
    def attend_back(p, carry):
        for i in range(2):
            r, ls = heads_of(p, i)
            q, k, v = (mix[r, l] for l in ls)
            q = q * jnp.asarray(0.125, BF16)
            k8 = k * jnp.asarray(0.125, BF16)
            kt = k8.T
            do = o[r, ls[0]]
            pr = prob[p * 2 + i]
            dv = dot(pr.reshape(TOK, ROWS), do)
            dp = dot_t(split(v), do).reshape(2, ROWS, ROWS)
            prf = pr.astype(F32)
            row = jnp.sum(prf * dp, 1, keepdims=True)
            ds = (prf * (dp - row)).astype(BF16)
            dq = [dot(kt[HEAD_DIM * e : HEAD_DIM * (e + 1)], ds[e]) for e in range(2)]
            dk = dot(ds.reshape(TOK, ROWS), q)
            dmix[r, ls[0]] = jnp.concatenate(dq, axis=0).astype(BF16).T
            dmix[r, ls[1]] = jnp.where(first_half, dk[:ROWS], dk[ROWS:]).astype(BF16)
            dmix[r, ls[2]] = jnp.where(first_half, dv[:ROWS], dv[ROWS:]).astype(BF16)
        return carry

    for part in range(4):
        lax.fori_loop(*parts[part], attend_back, 0)
        step("back%d" % part)

    at[...] = a[...].T
    for j in range(3):
        da[:, pl.ds(j * BLK, BLK)] = dot_t(dmix[...], row_block(T_QKV, 18, j))
    for j in range(3):
        for k in range(3):
            put_rows(T_QKV, 18, j, 6 * k, dot(at[pl.ds(j * BLK, BLK), :], dmix[:, pl.ds(k * D, D)]))
    step("qkv_back")
    d_gain1, d_shift1 = norm_grads(h, 0, gain1)
    d_norms = jnp.concatenate([jnp.sum(d, 0, keepdims=True) for d in (d_gain1, d_shift1, d_gain2, d_shift2)] + [jnp.zeros((12, D), F32)], axis=0).astype(BF16)
    for j in range(6):
        G[T_NORM + j] = d_norms[:, j * 128 : (j + 1) * 128]
    step("norms")
    at[...] = x[...].T
    row_id = lax.broadcasted_iota(jnp.int32, (ROWS, BLK), 0)
    for j in range(3):
        put_cols(T_E, 6, 48, j, dot(at[...], dyb[:, pl.ds(j * BLK, BLK)]))
        c = pl.ds(j * BLK, BLK)
        s = slice(j * BLK, (j + 1) * BLK)
        d_pos = dh[pl.ds(0, ROWS), c] + dh[pl.ds(ROWS, ROWS), c]
        d_pos = jnp.where(row_id < P_SIZE, d_pos, 0.0)
        d_pos = jnp.where(row_id == P_SIZE, jnp.broadcast_to(d_gain_end[:, s], (ROWS, BLK)), d_pos)
        d_pos = jnp.where(row_id == P_SIZE + 1, jnp.broadcast_to(d_shift_end[:, s], (ROWS, BLK)), d_pos)
        put_cols(T_POS, 6, 13, j, d_pos)
    step("embed")


FORWARD = {
    "start": (
        (0, 0), (1, 0), (2, 0), (3, 0), (0, 1), (2, 1), (1, 1), (0, 2), (1, 2), (0, 3), (1, 3), (2, 2),
        (1, 4), (0, 4), (0, 6), (3, 1), (2, 3),
    ),
    "embedded": ((1, 5), (3, 2),),
    "qkv": ((1, 6),),
    "attend0": ((2, 4),),
    "attend2": ((3, 3),),
    "attend3": ((2, 5),),
    "up": ((2, 6), (3, 4),),
    "down": ((3, 5), (3, 6),),
}
BACKWARD = {
    "fc_out0": ((3, 0, 0),),
    "fc_out1": ((3, 1, 0), (3, 0, 1)),
    "fc_in0": ((3, 1, 1),),
    "fc_in2": ((2, 0, 0),),
    "fc_in3": ((2, 1, 0), (2, 0, 1)),
    "normed2": ((2, 1, 1),),
    "back1": ((3, 0, 2), (3, 1, 2)),
    "qkv_back": ((1, 0, 0), (1, 1, 0), (2, 0, 2), (2, 1, 2), (1, 0, 1), (1, 1, 1), (3, 0, 3), (3, 1, 3)),
    "norms": ((0, 1, 0),),
    "embed": (
        (0, 0, 0), (0, 1, 1), (0, 0, 1), (3, 0, 4), (3, 1, 4), (2, 0, 3), (2, 1, 3), (1, 0, 2), (1, 1, 2), (3, 0, 5), (3, 1, 5), (2, 0, 4), (2, 1, 4),
        (0, 1, 2), (0, 0, 2), (1, 0, 3), (1, 1, 3), (2, 0, 5), (2, 1, 5), (0, 1, 3), (0, 0, 3), (1, 0, 4), (1, 1, 4), (0, 1, 4), (0, 0, 4), (1, 0, 5), (1, 1, 5), (0, 1, 5), (0, 0, 5),
    ),
}


def grads_kernel(w_ref, patch_ref, labels_ref, counts_ref, red_ref, loss_out, T, R, RA, RB, g_send, g_recv, r_send, r_recv, LS, l_send, l_recv, patch_in, meta_in, meta, loss, *rest):
    gather_refs, compute_refs, out_sem = rest[:12], rest[12:-1], rest[-1]
    links = Links(T, R, RA, RB, g_send, g_recv, r_send, r_recv)
    xl, b, z, a, y = links.xl, links.b, links.z, links.a, links.y
    swap = a != b
    mirror = device(xl, b, a, z, y)
    units_here, finish_start = start_gather(links, w_ref, patch_ref, labels_ref, counts_ref, T, patch_in, meta_in, meta, *gather_refs)

    def loss_send(src, dst, target):
        links.go(LS.at[src], LS.at[dst], l_send.at[dst], l_recv.at[dst], target)

    def loss_wait(*slots):
        for k in slots:
            links.landed(LS.at[k], l_send.at[k], l_recv.at[k])

    def loss_step(n):
        if n == 0:
            LS[0] = loss[...]
            loss_send(0, 1, links.sibling)
        elif n == 1:
            loss_wait(1)
            LS[8] = LS[0] + LS[1]
            loss_send(8, 2, links.at_y(1))
            loss_send(8, 3, links.at_y(3))
        elif n == 2:
            loss_wait(2, 3)
            loss_send(2, 4, links.at_y(1))
        elif n == 3:
            loss_wait(4)
            LS[9] = (LS[8] + LS[4]) + (LS[2] + LS[3])
            loss_send(9, 5, links.at_z(1))
            loss_send(9, 6, links.at_z(3))
        elif n == 4:
            loss_wait(5, 6)
            loss_send(5, 7, links.at_z(1))
        elif n == 5:
            loss_wait(7)
            LS[10] = (LS[9] + LS[7]) + (LS[5] + LS[6])

            @pl.when(swap)
            def _():
                loss_swap.start()

        else:

            @pl.when(swap)
            def _():
                loss_swap.wait()
                loss_out[...] = LS[11]

            @pl.when(jnp.logical_not(swap))
            def _():
                loss_out[...] = LS[10]

    loss_swap = pltpu.make_async_remote_copy(src_ref=LS.at[10], dst_ref=LS.at[11], send_sem=l_send.at[11], recv_sem=l_recv.at[11], device_id=mirror, device_id_type=MESH)
    losses = {"fc_out0": 0, "fc_in2": 1, "out": 2, "back1": 3, "back3": 4, "norms": 5}

    def step(name):
        if name == "pool":
            links.sent()
        for item in FORWARD.get(name, ()):
            if item[1] == 0:
                units_here(item[0])
            links.gather_step(*item)
        if name == "start":
            finish_start()
        for item in BACKWARD.get(name, ()):
            links.reduce_step(*item)
        if name in losses:
            loss_step(losses[name])

    compute(step, patch_in, meta_in, loss, T, *compute_refs)
    loss_step(6)
    mine = T.reshape(ROUNDS, 32, UNIT, 16, 128).at[:, z * 8 + b * 4 + y]
    out = pltpu.make_async_copy(mine, red_ref, out_sem)
    out.start()
    links.sent()
    out.wait()


def grads(weights, patches, labels, counts):
    hbm = pl.BlockSpec(memory_space=pl.ANY)
    vmem = pl.BlockSpec(memory_space=pltpu.VMEM)
    V = pltpu.VMEM
    dma = pltpu.SemaphoreType.DMA
    return pl.pallas_call(
        grads_kernel,
        out_shape=(jax.ShapeDtypeStruct((ROUNDS, UNIT, 16, 128), BF16), jax.ShapeDtypeStruct((8, 128), F32)),
        in_specs=[hbm] * 2 + [pl.BlockSpec(memory_space=pltpu.SMEM)] * 2,
        out_specs=(hbm, vmem),
        scratch_shapes=[
            V((NTILES, 16, 128), BF16),
            V((ROUNDS, 4, 4, UNIT, 16, 128), BF16),
            V((6, ROUNDS, 2, UNIT, 16, 128), BF16),
            V((6, ROUNDS, 3, 16, 128), BF16),
            dma((192,)),
            dma((192,)),
            dma((104,)),
            dma((104,)),
            V((12, 8, 128), F32),
            dma((12,)),
            dma((12,)),
            V(patches.shape, BF16),
            V((8, 128), F32),
            V((8, 128), F32),
            V((8, 128), F32),
            V((FROWS, 128), F32),
            V((128, 128), F32),
            V((LO, 128), BF16),
            V((HI, 128), BF16),
            V((HI, 128), BF16),
            V((LO, 128), BF16),
            V((SLOT, 16, 128), BF16),
            dma((4,)),
            dma((4,)),
            dma((4,)),
            dma((ROUNDS,)),
            dma((ROUNDS,)),
            V((TOK, D), BF16),
            V((TOK, D), F32),
            V((TOK, D), BF16),
            V((D, TOK), BF16),
            V((TOK, 3 * D), BF16),
            V((12, 2, ROWS, ROWS), BF16),
            V((TOK, D), BF16),
            V((TOK, D), F32),
            V((TOK, D), BF16),
            V((TOK, FF), BF16),
            V((TOK, FF), BF16),
            V((TOK, D), F32),
            V((TOK, D), F32),
            V((TOK, D), BF16),
            V((TOK, 128), F32),
            dma,
        ],
        compiler_params=pltpu.CompilerParams(collective_id=0, has_side_effects=True, vmem_limit_bytes=60 * 1024 * 1024),
        name="grads",
    )(weights, patches, labels, counts)


EDGE = 24
FRONT = 768
BACK_ROWS = FRONT + SHARD + 640 + 6
PADDED = 2112
STEP = 10
EDGE_UNITS = 4
WINDOW = ROUNDS + 2 * EDGE_UNITS
BETA_ONE = 0.9
BETA_TWO = 0.95
ADAM_EPS = 1e-08
DECAY = 0.05
INNER_RATE = 0.01
OUTER_RATE = 0.7
OUTER_MU = 0.9


def update_kernel(
    red_ref, first_ref, second_ref,
    sum_out, first_out, second_out,
    red, window, flat, headrows, first_row, second_row, first, second, low, low2, pair, pair2, total, total2,
    load_sem, x_send, x_recv, o_send, e_send, w_recv,
):
    xl, b, z, a, y = coords()
    fs = z * 8 + a * 4 + y
    holder = z * 8 + b * 4 + y
    sibling = device(xl, a, 1 - b, z, y)
    across = device(1 - xl, a, b, z, y)
    extra = [pltpu.make_async_copy(src, dst, load_sem.at[i]) for i, (src, dst) in enumerate(((first_ref, first_row), (second_ref, second_row)))]
    load = pltpu.make_async_copy(red_ref, red, load_sem.at[4])
    load.start()
    for copy in extra:
        copy.start()

    barrier = pltpu.get_barrier_semaphore()

    def greet(target):
        pl.semaphore_signal(barrier, inc=1, device_id=target, device_id_type=MESH)

    greet(sibling)
    greet(across)
    first_unit = ROUNDS * fs - EDGE_UNITS

    def window_unit(p):
        k = first_unit + p
        d = lax.rem(k + 32, 32)
        inside = jnp.logical_and(k >= 0, k < 32 * ROUNDS)
        mine = jnp.logical_and(a == b, d == holder)
        return inside, mine, device(xl, b, lax.rem(lax.div(d, 4), 2), lax.div(d, 8), lax.rem(d, 4))

    def greet_holder(p, carry):
        inside, mine, source = window_unit(p)

        @pl.when(jnp.logical_and(inside, jnp.logical_not(mine)))
        def _():
            greet(source)

        return carry

    lax.fori_loop(0, WINDOW, greet_holder, 0)

    def held_unit(j):
        k = 32 * j + holder
        q = lax.div(k, ROUNDS)
        r = lax.rem(k, ROUNDS)
        shift = jnp.where(r < EDGE_UNITS, -1, jnp.where(r >= ROUNDS - EDGE_UNITS, 1, 0))
        near = jnp.logical_and(shift != 0, jnp.logical_and(q + shift >= 0, q + shift < NSLOT))
        return k, q, jnp.where(near, q + shift, q), near

    def to_owner(j, k, s, send):
        p = k - (ROUNDS * s - EDGE_UNITS)
        src = red.at[j]
        dst = window.at[pl.ds(UNIT * p, UNIT)]
        sa = lax.rem(lax.div(s, 4), 2)
        mine = jnp.logical_and(a == b, s == fs)
        target = device(xl, sa, a, lax.div(s, 8), lax.rem(s, 4))
        away = pltpu.make_async_remote_copy(src_ref=src, dst_ref=dst, send_sem=send.at[j], recv_sem=w_recv.at[p], device_id=target, device_id_type=MESH)
        here = pltpu.make_async_copy(src, dst, load_sem.at[10])
        return mine, away, here

    def count(j, n):
        k, q, s, near = held_unit(j)
        first_away = jnp.logical_not(jnp.logical_and(a == b, q == fs))
        second_away = jnp.logical_and(near, jnp.logical_not(jnp.logical_and(a == b, s == fs)))
        return n + jnp.where(first_away, 1, 0) + jnp.where(second_away, 1, 0)

    outgoing = lax.fori_loop(0, ROUNDS, count, 2)
    pl.semaphore_wait(barrier, outgoing)
    load.wait()

    def give(j, carry):
        k, q, s, near = held_unit(j)
        mine, away, here = to_owner(j, k, q, o_send)

        @pl.when(mine)
        def _():
            here.start()

        @pl.when(jnp.logical_not(mine))
        def _():
            away.start()

        mine2, away2, here2 = to_owner(j, k, s, e_send)

        @pl.when(jnp.logical_and(near, mine2))
        def _():
            here2.start()

        @pl.when(jnp.logical_and(near, jnp.logical_not(mine2)))
        def _():
            away2.start()

        return carry

    lax.fori_loop(0, ROUNDS, give, 0)

    def given(j, carry):
        k, q, s, near = held_unit(j)
        mine, away, here = to_owner(j, k, q, o_send)

        @pl.when(jnp.logical_not(mine))
        def _():
            away.wait_send()

        mine2, away2, here2 = to_owner(j, k, s, e_send)

        @pl.when(jnp.logical_and(near, jnp.logical_not(mine2)))
        def _():
            away2.wait_send()

        return carry

    def clear(i, carry):
        flat[pl.ds(pl.multiple_of(i * 32, 32), 32), :] = jnp.zeros((32, 128), F32)
        return carry

    lax.fori_loop(0, BACK_ROWS // 32, clear, 0)

    for copy in extra:
        copy.wait()
    for source, rows_of in ((first_row, first), (second_row, second)):

        def eight(i, carry):
            rows_of[pl.ds(pl.multiple_of(i * 8, 8), 8), :] = source[0, pl.ds(pl.multiple_of(i * 1024, 1024), 1024)].reshape(8, 128)
            return carry

        whole = SHARD // 8
        lax.fori_loop(0, whole, eight, 0, unroll=2)
        rows_of[pl.ds(whole * 8, SHARD - whole * 8), :] = source[0, pl.ds(whole * 1024, (SHARD - whole * 8) * 128)].reshape(SHARD - whole * 8, 128)

    def got(p, carry):
        inside, mine, source = window_unit(p)
        place = window.at[pl.ds(UNIT * p, UNIT)]

        @pl.when(jnp.logical_and(inside, mine))
        def _():
            pltpu.make_async_copy(place, place, load_sem.at[10]).wait()

        @pl.when(jnp.logical_and(inside, jnp.logical_not(mine)))
        def _():
            pltpu.make_async_remote_copy(src_ref=place, dst_ref=place, send_sem=x_send.at[0], recv_sem=w_recv.at[p], device_id=sibling, device_id_type=MESH).wait_recv()

        return carry

    lax.fori_loop(0, WINDOW, got, 0)
    sends = []

    def go(src, dst, send, recv, k, target):
        copy = pltpu.make_async_remote_copy(src_ref=src, dst_ref=dst, send_sem=send.at[k], recv_sem=recv.at[k], device_id=target, device_id_type=MESH)
        copy.start()
        sends.append(copy)

    def arrive(dst, recv, k):
        pltpu.make_async_remote_copy(src_ref=dst, dst_ref=dst, send_sem=x_send.at[k], recv_sem=recv.at[k], device_id=sibling, device_id_type=MESH).wait_recv()

    low_tile = SLOT * fs - EDGE
    high_tile = SLOT * fs + SLOT + EDGE
    origin = SHARD * fs - FRONT
    for index, (base, c, groups, per, start) in enumerate(SECTIONS):
        if index == 1:
            lane = lax.broadcasted_iota(jnp.int32, (8, 128), 1)
            g0 = lax.div(jnp.maximum(SHARD * fs - base, 0), per)
            g1 = lax.div(jnp.maximum(SHARD * (fs + 1) - base, 0) + per - 1, per)

            def head_group(g, carry):
                t = start + g * 8 - low_tile
                for j in range(8):
                    headrows[pl.ds(j, 16, stride=8), :] = window[t + j].astype(F32)
                row = base + per * g - origin
                for i in range(16):
                    q, s = divmod(1000 * i, 128)
                    value = headrows[pl.ds(i * 8, 8), :]
                    if s:
                        value = pltpu.roll(value, s, 1)
                        flat[pl.ds(row + q, 8), :] += jnp.where(lane >= s, value, 0.0)
                        flat[pl.ds(row + q + 1, 8), :] += jnp.where(lane < s, value, 0.0)
                    else:
                        flat[pl.ds(row + q, 8), :] += value
                return carry

            lax.fori_loop(jnp.minimum(g0, groups), jnp.minimum(g1, groups), head_group, 0)
        else:

            def unit(n, carry):
                t = UNIT * n - start
                row = base + 16 * c * lax.div(t, c) + lax.rem(t, c) - origin
                for m in range(UNIT):
                    flat[pl.ds(row + m, 16, stride=c), :] = window[UNIT * n - low_tile + m].astype(F32)
                return carry

            lax.fori_loop(lax.div(jnp.maximum(low_tile, start), UNIT), lax.div(jnp.minimum(high_tile, start + c * groups), UNIT), unit, 0)

    fix_one = 1.0 / (1.0 - BETA_ONE**STEP)
    fix_two = 1.0 / (1.0 - BETA_TWO**STEP)

    half = PADDED // 2
    step = 96
    for rows_of in (first, second):
        rows_of[pl.ds(SHARD, PADDED - SHARD), :] = jnp.zeros((PADDED - SHARD, 128), F32)

    def in_half(fn):
        def rows_step(i, carry):
            fn(pl.multiple_of(i * step, step), step)
            return carry

        lax.fori_loop(0, half // step, rows_step, 0)

    def adam_half(q):
        def adam(r, n):
            at = pl.ds(pl.multiple_of(q * half + r, 16), n)
            grad = flat[pl.ds(pl.multiple_of(FRONT + q * half + r, 16), n), :]
            m = BETA_ONE * first[at, :] + (1.0 - BETA_ONE) * grad
            s = BETA_TWO * second[at, :] + (1.0 - BETA_TWO) * grad * grad
            first[at, :] = m
            second[at, :] = s
            low[at, :] = ((m * fix_one) / (jnp.sqrt(s * fix_two) + ADAM_EPS)).astype(BF16)

        in_half(adam)

    adam_half(1 - b)
    go(low.at[pl.ds(pl.multiple_of((1 - b) * half, 16), half)], low2, x_send, x_recv, 0, sibling)
    adam_half(b)
    outs = [pltpu.make_async_copy(src.at[pl.ds(0, SHARD)], dst, load_sem.at[5 + i]) for i, (src, dst) in enumerate(((first, first_out), (second, second_out)))]
    for copy in outs:
        copy.start()
    arrive(low2, x_recv, 0)

    def pairs(r, n):
        pair[pl.ds(r, n), :] = low[pl.ds(pl.multiple_of(b * half + r, 16), n), :] + low2[pl.ds(r, n), :]

    in_half(pairs)
    go(pair, pair2, x_send, x_recv, 1, across)
    arrive(pair2, x_recv, 1)

    def fours(r, n):
        total[pl.ds(r, n), :] = pair[pl.ds(r, n), :].astype(F32) + pair2[pl.ds(r, n), :].astype(F32)

    in_half(fours)
    go(total, total2, x_send, x_recv, 2, sibling)

    arrive(total2, x_recv, 2)
    other = half - b * half
    final = [(total, sum_out.at[pl.ds(pl.multiple_of(b * half, 16), half)]), (total2, sum_out.at[pl.ds(pl.multiple_of(other, 16), half)])]
    final = [pltpu.make_async_copy(src, dst, load_sem.at[7 + i]) for i, (src, dst) in enumerate(final)]
    for copy in final:
        copy.start()
    for copy in sends:
        copy.wait_send()
    lax.fori_loop(0, ROUNDS, given, 0)
    for copy in outs + final:
        copy.wait()


def update(red, first, second):
    hbm = pl.BlockSpec(memory_space=pl.ANY)
    V = pltpu.VMEM
    flat = jax.ShapeDtypeStruct((SHARD, 128), F32)
    dma = pltpu.SemaphoreType.DMA
    return pl.pallas_call(
        update_kernel,
        out_shape=(jax.ShapeDtypeStruct((PADDED, 128), F32), flat, flat),
        in_specs=[hbm] * 3,
        out_specs=(hbm,) * 3,
        scratch_shapes=[
            V((ROUNDS, UNIT, 16, 128), BF16),
            V((EDGE + SLOT + EDGE, 16, 128), BF16),
            V((BACK_ROWS, 128), F32),
            V((128, 128), F32),
            V((1, SHARD * 128), F32),
            V((1, SHARD * 128), F32),
            V((PADDED, 128), F32),
            V((PADDED, 128), F32),
            V((PADDED, 128), BF16),
            V((PADDED // 2, 128), BF16),
            V((PADDED // 2, 128), BF16),
            V((PADDED // 2, 128), BF16),
            V((PADDED // 2, 128), F32),
            V((PADDED // 2, 128), F32),
            dma((11,)),
            dma((3,)),
            dma((3,)),
            dma((ROUNDS,)),
            dma((ROUNDS,)),
            dma((WINDOW,)),
        ],
        compiler_params=pltpu.CompilerParams(collective_id=1, has_side_effects=True, vmem_limit_bytes=60 * 1024 * 1024),
        name="update",
    )(red, first, second)


def finish_kernel(
    sum_ref, w_ref, mom_ref, first_ref, second_ref, loss_ref,
    avg_out, mom_out, new_out, first_out, second_out, loss_out,
    total, w, mom, first, second, averaged, sem, out_sem,
):
    cut = PADDED // 2
    pieces = [pl.ds(0, cut), pl.ds(cut, SHARD - cut)]
    loads = []
    for i, at in enumerate(pieces):
        loads.append([pltpu.make_async_copy(src.at[at], dst.at[at], sem.at[3 * i + k]) for k, (src, dst) in enumerate(((sum_ref, total), (w_ref, w), (mom_ref, mom)))])
    moments = [pltpu.make_async_copy(src, dst, sem.at[6 + i]) for i, (src, dst) in enumerate(((first_ref, first), (second_ref, second)))]
    for copy in loads[0] + loads[1] + moments:
        copy.start()
    outs = []

    def send(src, dst):
        copy = pltpu.make_async_copy(src, dst, out_sem.at[len(outs)])
        copy.start()
        outs.append(copy)

    loss_out[...] = loss_ref[0:1, 0:1]

    def outer(r, n):
        at = pl.ds(r, n)
        old = w[at, :]
        mean = INNER_RATE * (total[at, :] * 0.25 + DECAY * old)
        momentum = OUTER_MU * mom[at, :] + mean
        averaged[at, :] = mean
        mom[at, :] = momentum
        w[at, :] = old - OUTER_RATE * (mean + OUTER_MU * momentum)

    def block(i, carry):
        outer(pl.multiple_of(i * 96, 96), 96)
        return carry

    for i, at in enumerate(pieces):
        for copy in loads[i]:
            copy.wait()
        if i == 0:
            lax.fori_loop(0, cut // 96, block, 0)
        else:
            lax.fori_loop(cut // 96, SHARD // 96, block, 0)
            outer(SHARD // 96 * 96, SHARD - SHARD // 96 * 96)
        for src, dst in ((averaged, avg_out), (mom, mom_out), (w, new_out)):
            send(src.at[at], dst.at[at])
        if i == 0:
            for copy, src, dst in zip(moments, (first, second), (first_out, second_out)):
                copy.wait()
                send(src, dst.reshape(SHARD, 128))
    for copy in outs:
        copy.wait()


def finish(total, weights, momentum, first, second, loss):
    hbm = pl.BlockSpec(memory_space=pl.ANY)
    vmem = pl.BlockSpec(memory_space=pltpu.VMEM)
    V = pltpu.VMEM
    rows = jax.ShapeDtypeStruct((SHARD, 128), F32)
    row = jax.ShapeDtypeStruct((1, SHARD * 128), F32)
    return pl.pallas_call(
        finish_kernel,
        out_shape=(rows,) * 3 + (row,) * 2 + (jax.ShapeDtypeStruct((1, 1), F32),),
        in_specs=[hbm] * 5 + [vmem],
        out_specs=(hbm,) * 5 + (vmem,),
        scratch_shapes=[V((PADDED, 128), F32)] + [V((SHARD, 128), F32)] * 5 + [pltpu.SemaphoreType.DMA((8,)), pltpu.SemaphoreType.DMA((8,))],
        compiler_params=pltpu.CompilerParams(vmem_limit_bytes=60 * 1024 * 1024),
        name="finish",
    )(total, weights, momentum, first, second, loss)


def body(patches, labels, counts, weights, first_moments, second_moments, outer_momentum):
    flat = weights.reshape(SHARD, 128)
    reduced, loss = grads(flat, patches.reshape(2, P_SIZE, D), labels.reshape(2), counts.reshape(2))
    total, first, second = update(reduced, first_moments, second_moments)
    averaged, momentum, new_weights, first, second, loss = finish(total, flat, outer_momentum.reshape(SHARD, 128), first, second, loss)
    return (
        averaged.reshape(-1),
        momentum.reshape(-1),
        new_weights.reshape(-1),
        first,
        second,
        loss,
    )


def solution(mesh):
    placed = (
        P("rep", None, None, "fsdp", None, None),
        P("rep", None, None, "fsdp"),
        P("rep", None, None),
        P("fsdp"),
        P("rep", "fsdp"),
        P("rep", "fsdp"),
        P("fsdp"),
    )
    return jax.shard_map(
        body,
        mesh=mesh,
        in_specs=placed,
        out_specs=(
            P("fsdp"),
            P("fsdp"),
            P("fsdp"),
            P("rep", "fsdp"),
            P("rep", "fsdp"),
            P("rep", None),
        ),
        check_vma=False,
    )
```

```python
from functools import partial

import jax
import jax.numpy as jnp
from jax import lax
from jax.experimental import pallas as pl
from jax.experimental.pallas import tpu as pltpu
from jax.sharding import PartitionSpec as P

SHARD = 2098
SLOT = 132
HALF = 66
QUART = 33
NSLOT = 32
ROUNDS = 22
UNIT = 6
STAGES = ((0, 4), (4, 10), (10, 16), (16, 22))
SECTIONS = []
_t = 0
for _base, _c, _g, _rpg in ((0, 6, 61, 96), (5796, 8, 48, 125), (11796, 6, 1, 96), (11820, 18, 48, 288), (25644, 6, 48, 96), (30252, 24, 48, 384), (48684, 6, 192, 96)):
    SECTIONS.append((_base, _c, _g, _rpg, _t))
    _t += _c * _g
NTILE = _t
HI = 352
LO = 224
MARGIN = 512
FROWS = 3072
HEAD_ROWS = 16
MESH = pl.DeviceIdType.MESH


def coords():
    rep = lax.axis_index("rep")
    fs = lax.axis_index("fsdp")
    return lax.div(rep, 2), lax.rem(rep, 2), lax.div(fs, 8), lax.rem(lax.div(fs, 4), 2), lax.rem(fs, 4)


def device(xl, xh, core, z, y):
    return {"rep": xl * 2 + core, "fsdp": z * 8 + xh * 4 + y}


def flat_device(xl, core, s):
    return device(xl, lax.rem(lax.div(s, 4), 2), core, lax.div(s, 8), lax.rem(s, 4))


class Links:

    def __init__(self, T, R, RA, RB, g_send, g_recv, r_send, r_recv):
        self.xl, self.b, self.z, self.a, self.y = coords()
        self.T5 = T.reshape(ROUNDS, 4, 2, 4, UNIT, 16, 128)
        self.R, self.RA, self.RB = R, RA, RB
        self.g_send, self.g_recv, self.r_send, self.r_recv = g_send, g_recv, r_send, r_recv
        self.pending = []
        self.sibling = device(self.xl, self.a, 1 - self.b, self.z, self.y)

    def at_y(self, k):
        return device(self.xl, self.a, self.b, self.z, lax.rem(self.y + k, 4))

    def at_z(self, k):
        return device(self.xl, self.a, self.b, lax.rem(self.z + k, 4), self.y)

    def at_x(self, k):
        a = lax.rem(self.a + (self.xl if k == 1 else 1 - self.xl), 2)
        return device(1 - self.xl, a, self.b, self.z, self.y)

    def go(self, src, dst, send, recv, target):
        copy = pltpu.make_async_remote_copy(src_ref=src, dst_ref=dst, send_sem=send, recv_sem=recv, device_id=target, device_id_type=MESH)
        copy.start()
        self.pending.append(copy)

    def landed(self, dst, send, recv):
        pltpu.make_async_remote_copy(src_ref=dst, dst_ref=dst, send_sem=send, recv_sem=recv, device_id=self.sibling, device_id_type=MESH).wait_recv()

    def sent(self):
        for copy in self.pending:
            copy.wait_send()
        self.pending = []

    def span(self, i, h):
        lo, hi = STAGES[i]
        n = (hi - lo) // 2
        return pl.ds(lo + h * n, n)

    def first_axis(self, h, k):
        return (self.at_y if h == 0 else self.at_z)(k)

    def second_axis(self, h, k):
        return (self.at_z if h == 0 else self.at_y)(k)

    def gathered(self, i, h):
        lo, hi = STAGES[i]
        n = (hi - lo) // 2
        if i == 0:
            return pl.ds(lo + h * n, n)
        return pl.ds(lo + h * n + self.xl, 2)

    def single(self, i, h, own):
        lo, hi = STAGES[i]
        parity = self.xl if own else 1 - self.xl
        return pl.ds(lo + h * ((hi - lo) // 2) + 2 * parity, 1)

    def one(self, i, h, k, q=None):
        rd = self.gathered(i, h)
        t = pl.ds(0, UNIT) if q is None else pl.ds(3 * q, 3)
        if h == 0:
            return self.T5.at[rd, self.z, self.b, lax.rem(self.y + k, 4), t]
        return self.T5.at[rd, lax.rem(self.z + k, 4), self.b, self.y, t]

    def row(self, rd, h, k, core=None, p=None):
        core = self.b if core is None else core
        t = pl.ds(0, 4) if p is None else pl.ds(2 * p, 2)
        if h == 0:
            return self.T5.at[rd, lax.rem(self.z + k, 4), core, t]
        return self.T5.at[rd, t, core, lax.rem(self.y + k, 4)]

    def gsem(self, i, h, k):
        n = (i * 2 + h) * 24 + k
        return self.g_send.at[n], self.g_recv.at[n]

    def gather_go(self, i, h, k, view, target):
        self.go(view, view, *self.gsem(i, h, k), target)

    def gather_wait(self, i, h, k, view):
        self.landed(view, *self.gsem(i, h, k))

    def share(self, i, h, m, k):
        self.gather_go(i, h, 8 + m, self.row(self.gathered(i, h), h, k), self.sibling)
        if i > 0:
            rd = self.single(i, h, True)
            self.gather_go(i, h, 12 + m, self.row(rd, h, k, p=0), self.at_x(1))
            self.gather_go(i, h, 16 + m, self.row(rd, h, k, p=1), self.at_x(3))

    def gather_step(self, i, step):
        for h in range(2):
            rd = self.gathered(i, h)
            if step == 0:
                self.gather_go(i, h, 0, self.one(i, h, 0), self.first_axis(h, 1))
                self.gather_go(i, h, 1, self.one(i, h, 0), self.first_axis(h, 3))
            elif step == 1:
                self.gather_wait(i, h, 0, self.one(i, h, 3))
                self.gather_go(i, h, 2, self.one(i, h, 3, 0), self.first_axis(h, 1))
                self.gather_wait(i, h, 1, self.one(i, h, 1))
                self.gather_go(i, h, 3, self.one(i, h, 1, 1), self.first_axis(h, 3))
            elif step == 2:
                self.gather_wait(i, h, 2, self.one(i, h, 2, 0))
                self.gather_wait(i, h, 3, self.one(i, h, 2, 1))
                self.gather_go(i, h, 4, self.row(rd, h, 0), self.second_axis(h, 1))
                self.gather_go(i, h, 5, self.row(rd, h, 0), self.second_axis(h, 3))
                self.share(i, h, 0, 0)
            elif step == 3:
                self.gather_wait(i, h, 4, self.row(rd, h, 3))
                self.gather_go(i, h, 6, self.row(rd, h, 3, p=0), self.second_axis(h, 1))
                self.share(i, h, 1, 3)
                self.gather_wait(i, h, 5, self.row(rd, h, 1))
                self.gather_go(i, h, 7, self.row(rd, h, 1, p=1), self.second_axis(h, 3))
                self.share(i, h, 2, 1)
            elif step == 4:
                self.gather_wait(i, h, 6, self.row(rd, h, 2, p=0))
                self.gather_wait(i, h, 7, self.row(rd, h, 2, p=1))
                self.share(i, h, 3, 2)
            elif step == 5:
                if i > 0:
                    other = self.single(i, h, False)
                    for m, k in enumerate((0, 3, 1, 2)):
                        self.gather_wait(i, h, 12 + m, self.row(other, h, k, p=0))
                        self.gather_wait(i, h, 16 + m, self.row(other, h, k, p=1))
                        self.gather_go(i, h, 20 + m, self.row(other, h, k), self.sibling)
            else:
                for m, k in enumerate((0, 3, 1, 2)):
                    self.gather_wait(i, h, 8 + m, self.row(rd, h, k, core=1 - self.b))
                    if i > 0:
                        self.gather_wait(i, h, 20 + m, self.row(self.single(i, h, False), h, k, core=1 - self.b))

    def rsem(self, i, h, k):
        n = (i * 2 + h) * 13 + k
        return self.r_send.at[n], self.r_recv.at[n]

    def cell(self, i, h, k, q):
        rd = self.span(i, h)
        t = pl.ds(3 * q, 3)
        if h == 0:
            return self.T5.at[rd, self.z, self.b, lax.rem(self.y + k, 4), t]
        return self.T5.at[rd, lax.rem(self.z + k, 4), self.b, self.y, t]

    def add(self, dst, *sources, inner=()):
        n = dst.shape[0]

        def one(r, carry):
            for k in range(inner) if inner else (None,):
                at = (r,) if k is None else (r, k)
                if len(sources) == 1:
                    dst[at] = dst[at] + sources[0][at]
                else:
                    total = dst[at].astype(jnp.float32)
                    for source in sources:
                        total = total + source[at].astype(jnp.float32)
                    dst[at] = total.astype(jnp.bfloat16)
            return carry

        lax.fori_loop(0, n, one, 0)

    def reduce_step(self, i, h, step):
        rd = self.span(i, h)
        T5 = self.T5

        def send_a(k, ka, p, shift):
            self.go(self.row(rd, h, ka, p=p), self.RA.at[k, rd], *self.rsem(i, h, 1 + k), self.second_axis(h, shift))

        def wait_a(k):
            self.landed(self.RA.at[k, rd], *self.rsem(i, h, 1 + k))

        def send_b(k, kb, q, shift):
            self.go(self.cell(i, h, kb, q), self.RB.at[k, rd], *self.rsem(i, h, 7 + k), self.first_axis(h, shift))

        def wait_b(k):
            self.landed(self.RB.at[k, rd], *self.rsem(i, h, 7 + k))

        if step == 0:
            self.go(T5.at[rd, :, 1 - self.b], self.R.at[rd], *self.rsem(i, h, 0), self.sibling)
        elif step == 1:
            self.landed(self.R.at[rd], *self.rsem(i, h, 0))
            mine, theirs = T5.at[rd, :, self.b], self.R.at[rd]
            n = mine.shape[0]

            def both(r, carry):
                q = lax.div(r, 4)
                w = lax.rem(r, 4)
                for k in range(4):
                    mine[q, w, k] = mine[q, w, k] + theirs[q, w, k]
                return carry

            lax.fori_loop(0, 4 * n, both, 0)
            send_a(0, 2, 0, 1)
            send_a(1, 2, 1, 3)
            send_a(2, 1, 1, 1)
            send_a(3, 3, 0, 3)
        elif step == 2:
            wait_a(0)
            self.add(self.row(rd, h, 1, p=0), self.RA.at[0, rd], inner=2)
            send_a(4, 1, 0, 1)
            wait_a(1)
            self.add(self.row(rd, h, 3, p=1), self.RA.at[1, rd], inner=2)
            send_a(5, 3, 1, 3)
        elif step == 3:
            for k in (2, 3, 4, 5):
                wait_a(k)
            self.add(self.row(rd, h, 0, p=0), self.RA.at[3, rd], self.RA.at[4, rd], inner=2)
            self.add(self.row(rd, h, 0, p=1), self.RA.at[2, rd], self.RA.at[5, rd], inner=2)
            send_b(0, 2, 0, 1)
            send_b(1, 2, 1, 3)
            send_b(2, 1, 1, 1)
            send_b(3, 3, 0, 3)
        elif step == 4:
            wait_b(0)
            self.add(self.cell(i, h, 1, 0), self.RB.at[0, rd])
            send_b(4, 1, 0, 1)
            wait_b(1)
            self.add(self.cell(i, h, 3, 1), self.RB.at[1, rd])
            send_b(5, 3, 1, 3)
        else:
            for k in (2, 3, 4, 5):
                wait_b(k)
            self.add(self.cell(i, h, 0, 0), self.RB.at[3, rd], self.RB.at[4, rd])
            self.add(self.cell(i, h, 0, 1), self.RB.at[2, rd], self.RB.at[5, rd])


def start_gather(links, w_ref, patch_ref, labels_ref, counts_ref, T, patch_in, meta_in, meta_ref, flat, headrows, lob, hib, rlo, rhi, slot, local_sem, x_send, x_recv, u_send, u_recv):
    xl, b, z, a, y = links.xl, links.b, links.z, links.a, links.y
    fs = z * 8 + a * 4 + y
    swap = a != b
    xo = lax.rem(xl + a + b, 2)
    holder = z * 8 + b * 4 + y
    up = flat_device(xl, b, lax.rem(fs + 1, NSLOT))
    down = flat_device(xl, b, lax.rem(fs + NSLOT - 1, NSLOT))
    mirror = device(xl, b, a, z, y)
    load = pltpu.make_async_copy(w_ref, flat.at[pl.ds(MARGIN, SHARD)], local_sem.at[0])
    load.start()
    barrier = pltpu.get_barrier_semaphore()
    total = (counts_ref[0] + counts_ref[1]).astype(jnp.float32)
    for m in range(2):
        valid = jnp.full((1, 128), jnp.where(fs < counts_ref[m], 1.0, 0.0), jnp.float32)
        meta_ref[m : m + 1, :] = jnp.full((1, 128), labels_ref[m].astype(jnp.float32), jnp.float32)
        meta_ref[2 + m : 3 + m, :] = valid / jnp.full((1, 128), total, jnp.float32)
        meta_ref[4 + m : 5 + m, :] = valid
    meta_ref[6:8, :] = jnp.zeros((2, 128), jnp.float32)

    def greet(target):
        pl.semaphore_signal(barrier, inc=1, device_id=target, device_id_type=MESH)

    def wanted(j, parity):
        return jnp.logical_or(j < STAGES[0][1], lax.rem(j + 3 - STAGES[0][1] % 3, 3) != 2 * (1 - parity))

    for target in (up, down, links.at_x(1), links.at_x(3), links.at_y(1), links.at_y(3), links.at_z(1), links.at_z(3), links.sibling):
        greet(target)

    @pl.when(swap)
    def _():
        greet(mirror)

    own_index = lax.rem(fs * 11, NSLOT)
    keeps = jnp.logical_and(a == b, own_index < ROUNDS)

    def greet_source(j, carry):
        s = lax.div(32 * j + holder, ROUNDS)
        sa = lax.rem(lax.div(s, 4), 2)

        @pl.when(jnp.logical_and(wanted(j, xl), jnp.logical_not(jnp.logical_and(keeps, s == fs))))
        def _():
            greet(device(lax.rem(xl + sa + a, 2), sa, a, lax.div(s, 8), lax.rem(s, 4)))

        return carry

    lax.fori_loop(0, ROUNDS, greet_source, 0)
    def unit_goes(i):
        there = wanted(lax.div(ROUNDS * fs + i, 32), xo)
        stays = jnp.logical_and(keeps, i == own_index)
        return jnp.logical_and(there, jnp.logical_not(stays)), jnp.logical_and(there, stays)

    outgoing = lax.fori_loop(0, ROUNDS, lambda i, n: n + jnp.where(unit_goes(i)[0], 1, 0), 9)
    pl.semaphore_wait(barrier, outgoing + jnp.where(swap, 1, 0))
    load.wait()

    def remote(src, dst, k, target):
        return pltpu.make_async_remote_copy(src_ref=src, dst_ref=dst, send_sem=x_send.at[k], recv_sem=x_recv.at[k], device_id=target, device_id_type=MESH)

    hib[...] = flat[pl.ds(MARGIN + SHARD - HI, HI), :].astype(jnp.bfloat16)
    to_up = remote(hib, rlo, 0, up)
    to_up.start()
    lob[...] = flat[pl.ds(MARGIN, LO), :].astype(jnp.bfloat16)
    to_down = remote(lob, rhi, 1, down)
    to_down.start()
    patch_swap = remote(patch_ref, patch_in, 2, mirror)
    meta_swap = remote(meta_ref, meta_in, 3, mirror)
    patch_keep = pltpu.make_async_copy(patch_ref, patch_in, local_sem.at[1])
    meta_keep = pltpu.make_async_copy(meta_ref, meta_in, local_sem.at[2])
    first = ROUNDS * fs
    origin = SHARD * fs - MARGIN

    def unit_copy(i):
        k = first + i
        d = lax.rem(k, 32)
        src = slot.at[pl.ds(UNIT * i, UNIT)]
        dst = T.at[pl.ds(UNIT * k, UNIT)]
        target = device(xo, b, lax.rem(lax.div(d, 4), 2), lax.div(d, 8), lax.rem(d, 4))
        away = pltpu.make_async_remote_copy(src_ref=src, dst_ref=dst, send_sem=u_send.at[i], recv_sem=u_recv.at[lax.div(k, 32)], device_id=target, device_id_type=MESH)
        return away, (src, dst)

    def send_unit(i):
        away, (src, dst) = unit_copy(i)
        goes, stays = unit_goes(i)

        @pl.when(stays)
        def _():
            pltpu.make_async_copy(src, dst, local_sem.at[3]).start()

        @pl.when(goes)
        def _():
            away.start()

    lane = lax.broadcasted_iota(jnp.int32, (8, 128), 1)

    def head_group(g, base, per, start):
        row = base + per * g - origin
        for i in range(16):
            q, s = divmod(1000 * i, 128)
            one = flat[pl.ds(row + q, 8), :]
            if s:
                two = flat[pl.ds(row + q + 1, 8), :]
                one = jnp.where(lane < 128 - s, pltpu.roll(one, 128 - s, 1), pltpu.roll(two, 128 - s, 1))
            headrows[pl.ds(i * 8, 8), :] = one
        for j in range(8):
            t = start + g * 8 + j - UNIT * first

            @pl.when(jnp.logical_and(t >= 0, t < SLOT))
            def _():
                slot[t] = headrows[pl.ds(j, 16, stride=8), :].astype(jnp.bfloat16)

    def inside(row, rows):
        return jnp.logical_and(row >= MARGIN, row + rows <= MARGIN + SHARD)

    def convert(near):
        for index, (base, c, groups, per, start) in enumerate(SECTIONS):
            lo = jnp.maximum(UNIT * first, start)
            hi = jnp.minimum(UNIT * first + SLOT, start + c * groups)
            if index == 1:

                def group(g, carry):
                    @pl.when(inside(base + per * g - origin, per + 1) == near)
                    def _():
                        head_group(g, base, per, start)

                    return carry

                lax.fori_loop(lax.div(jnp.maximum(lo, start) - start, 8), lax.div(jnp.maximum(hi, start) - start + 7, 8), group, 0)
                if not near:

                    def deal(u, carry):
                        send_unit(u - first)
                        return carry

                    lax.fori_loop(lax.div(lo, UNIT), lax.div(hi, UNIT), deal, 0)
            else:

                def unit(u, carry):
                    t = UNIT * u - start
                    g = lax.div(t, c)
                    row = base + 16 * c * g + lax.rem(t, c) - origin

                    @pl.when(inside(row, 15 * c + UNIT) == near)
                    def _():
                        for k in range(UNIT):
                            slot[UNIT * (u - first) + k] = flat[pl.ds(row + k, 16, stride=c), :].astype(jnp.bfloat16)
                        send_unit(u - first)

                    return carry

                lax.fori_loop(lax.div(lo, UNIT), lax.div(hi, UNIT), unit, 0)

    convert(True)
    to_up.wait_recv()
    flat[pl.ds(MARGIN - HI, HI), :] = rlo[...].astype(jnp.float32)
    to_down.wait_recv()
    flat[pl.ds(MARGIN + SHARD, LO), :] = rhi[...].astype(jnp.float32)
    convert(False)

    @pl.when(fs == NSLOT - 1)
    def _():
        slot[pl.ds(SLOT - 12, 12)] = jnp.zeros((12, 16, 128), jnp.bfloat16)
        send_unit(ROUNDS - 2)
        send_unit(ROUNDS - 1)

    @pl.when(swap)
    def _():
        patch_swap.start()
        meta_swap.start()

    @pl.when(jnp.logical_not(swap))
    def _():
        patch_keep.start()
        meta_keep.start()

    def units_here(i):
        def wait(j, carry):
            place = T.at[pl.ds(UNIT * (32 * j + holder), UNIT)]
            mine = jnp.logical_and(keeps, lax.div(32 * j + holder, ROUNDS) == fs)

            @pl.when(jnp.logical_and(wanted(j, xl), mine))
            def _():
                pltpu.make_async_copy(place, place, local_sem.at[3]).wait()

            @pl.when(jnp.logical_and(wanted(j, xl), jnp.logical_not(mine)))
            def _():
                pltpu.make_async_remote_copy(src_ref=place, dst_ref=place, send_sem=u_send.at[0], recv_sem=u_recv.at[j], device_id=links.sibling, device_id_type=MESH).wait_recv()

            return carry

        lax.fori_loop(*STAGES[i], wait, 0)

    def finish_start():
        def wait(i, carry):
            away, unused = unit_copy(i)

            @pl.when(unit_goes(i)[0])
            def _():
                away.wait_send()

            return carry

        lax.fori_loop(0, ROUNDS, wait, 0)
        to_up.wait_send()
        to_down.wait_send()

        @pl.when(swap)
        def _():
            patch_swap.wait()
            meta_swap.wait()

        @pl.when(jnp.logical_not(swap))
        def _():
            patch_keep.wait()
            meta_keep.wait()

    return units_here, finish_start


D = 768
HEADS = 12
HEAD_DIM = 64
FF = 3072
CLS = 1000
P_SIZE = 196
ROWS = 208
TOK = 2 * ROWS
NORM_EPS = 1e-06
SMOOTHING = 0.1
NTILES = 4224
T_E, T_HEAD, T_NORM, T_QKV, T_OUT, T_IN, T_FO = 0, 366, 750, 756, 1620, 1908, 3060
T_POS = 288
BLK = 256
BLOCKS = ((0, 96), (96, 112), (208, 96), (304, 112))
F32 = jnp.float32
BF16 = jnp.bfloat16
ROOT_HALF = 0.7071067811865476
INV_ROOT_TWO_PI = 0.3989422804014327


def dot(x, w):
    return lax.dot_general(x, w, (((1,), (0,)), ((), ())), preferred_element_type=F32)


def dot_t(x, w):
    return lax.dot_general(x, w, (((1,), (1,)), ((), ())), preferred_element_type=F32)


def t_dot(x, w):
    return lax.dot_general(x, w, (((0,), (0,)), ((), ())), preferred_element_type=F32)


def stats(x, keep, r, k):
    mean = jnp.sum(x, -1, keepdims=True) * (1.0 / D)
    centred = x - mean
    var = jnp.sum(centred * centred, -1, keepdims=True) * (1.0 / D)
    rstd = lax.rsqrt(var + NORM_EPS)
    keep[r, k : k + 1] = mean
    keep[r, k + 1 : k + 2] = rstd
    return centred * rstd


def kept(x, keep, r, k):
    rstd = keep[r, k + 1 : k + 2]
    return (x - keep[r, k : k + 1]) * rstd, rstd


def norm_back(d_hat, hat, rstd):
    m1 = jnp.sum(d_hat, -1, keepdims=True) * (1.0 / D)
    m2 = jnp.sum(d_hat * hat, -1, keepdims=True) * (1.0 / D)
    return rstd * (d_hat - m1 - hat * m2)


def compute(step, patch_ref, meta_ref, loss_ref, T, x, h, a, at, mix, prob, o, h1, a2, hid, slope, h2, dh, dyb, keep):
    G = T
    dmix = mix

    def section(ref, start, c, groups):
        return ref.at[pl.ds(start, groups * c)].reshape(groups, c, 16, 128)

    def cols(start, c, groups, j):
        part = section(T, start, c, groups)
        return jnp.concatenate([part[:, 2 * j + k].reshape(groups * 16, 128) for k in range(2)], axis=1)

    def put_cols(start, c, groups, j, value):
        low = value.astype(BF16)
        part = section(G, start, c, groups)
        for k in range(2):
            part[:, 2 * j + k] = low[:, k * 128 : (k + 1) * 128].reshape(groups, 16, 128)

    def row_of(start, k):
        return jnp.concatenate([T[start + j][k : k + 1, :] for j in range(6)], axis=1).astype(F32)

    def lanes(j):
        return pl.ds(pl.multiple_of(j * BLK, BLK), BLK)

    step("start")
    for i in range(2):
        x[pl.ds(i * ROWS, 192), :] = patch_ref[i, pl.ds(0, 192), :]
        x[pl.ds(i * ROWS + 192, 16), :] = jnp.concatenate([patch_ref[i, pl.ds(192, 4), :], jnp.zeros((12, D), BF16)], axis=0)

    real = lax.broadcasted_iota(jnp.int32, (ROWS, 128), 0) < P_SIZE
    for j in range(3):
        acc = dot(x[...], cols(T_E, 6, 48, j))
        p = cols(T_POS, 6, 13, j).astype(F32)
        p = jnp.where(lax.broadcasted_iota(jnp.int32, (ROWS, BLK), 0) < P_SIZE, p, 0.0)
        for i in range(2):
            h[pl.ds(i * ROWS, ROWS), pl.ds(j * BLK, BLK)] = acc[i * ROWS : (i + 1) * ROWS] + p

    step("embedded")
    gain1, shift1, gain2, shift2 = (row_of(T_NORM, k) for k in range(4))

    for at_row, n in BLOCKS:
        r = pl.ds(at_row, n)
        a[r, :] = (stats(h[r, :], keep, r, 0) * gain1 + shift1).astype(BF16)

    step("qkv")
    def wide_cols(start, c, groups, j):
        return jnp.concatenate([cols(start, c, groups, 3 * j + k) for k in range(3)], axis=1)

    def wide_lanes(j):
        return pl.ds(pl.multiple_of(j * D, D), D)

    def mix_block(j, carry):
        mix[:, wide_lanes(j)] = dot(a[...], wide_cols(T_QKV, 18, 48, j)).astype(BF16)
        return carry

    lax.fori_loop(0, 3, mix_block, 0)

    first_half = lax.broadcasted_iota(jnp.int32, (ROWS, 128), 1) < HEAD_DIM
    key_ok = lax.broadcasted_iota(jnp.int32, (ROWS, ROWS), 0) < P_SIZE
    first_rows = lax.broadcasted_iota(jnp.int32, (128, ROWS), 0) < HEAD_DIM
    halves = (first_half, jnp.logical_not(first_half))
    zero = jnp.zeros((ROWS, 128), BF16)

    def split(block):
        return jnp.concatenate([jnp.where(first_half, block, zero), jnp.where(first_half, zero, block)], axis=0)

    def heads_of(p, i):
        r = pl.ds(i * ROWS, ROWS)
        return r, [pl.ds(pl.multiple_of(p * 128 + D * k, 128), 128) for k in range(3)]

    def attend(p, carry):
        for i in range(2):
            r, ls = heads_of(p, i)
            q, k, v = (mix[r, l] for l in ls)
            q = q * jnp.asarray(0.125, BF16)
            vt = v.T
            outs = []
            for e in range(2):
                s = dot_t(jnp.where(halves[e], k, zero), q)
                s = jnp.where(key_ok, s, -jnp.inf)
                ex = jnp.exp(s - jnp.max(s, 0, keepdims=True))
                pr = (ex * (1.0 / jnp.sum(ex, 0, keepdims=True))).astype(BF16)
                prob[p * 2 + i, e] = pr
                outs.append(dot(vt, pr))
            o[r, ls[0]] = jnp.where(first_rows, outs[0], outs[1]).astype(BF16).T
        return carry

    parts = ((0, 2), (2, 3), (3, 5), (5, 6))
    for part in range(4):
        step("attend%d" % part)
        lax.fori_loop(*parts[part], attend, 0)
    step("attended")
    for j in range(3):
        h1[:, pl.ds(j * BLK, BLK)] = h[:, pl.ds(j * BLK, BLK)] + dot(o[...], cols(T_OUT, 6, 48, j))

    for at_row, n in BLOCKS:
        r = pl.ds(at_row, n)
        a2[r, :] = (stats(h1[r, :], keep, r, 2) * gain2 + shift2).astype(BF16)

    step("up")
    def up_block(j, carry):
        u = dot(a2[...], wide_cols(T_IN, 24, 48, j))
        phi = 0.5 * (1.0 + lax.erf(u * ROOT_HALF))
        pdf = jnp.exp(-0.5 * u * u) * INV_ROOT_TWO_PI
        hid[:, wide_lanes(j)] = (u * phi).astype(BF16)
        slope[:, wide_lanes(j)] = (phi + u * pdf).astype(BF16)
        return carry

    lax.fori_loop(0, 4, up_block, 0)
    step("down")
    for j in range(3):
        h2[:, pl.ds(j * BLK, BLK)] = h1[:, pl.ds(j * BLK, BLK)] + dot(hid[...], cols(T_FO, 6, 192, j))

    step("pool")
    gain_end, shift_end = (row_of(T_POS + 72, 4 + k) for k in range(2))
    means = []
    last_rows = lax.broadcasted_iota(jnp.int32, (112, D), 0) < P_SIZE - 96
    for i in range(2):
        total = jnp.zeros((8, D), F32)
        for at_row, n in BLOCKS[2 * i : 2 * i + 2]:
            r = pl.ds(at_row, n)
            hat = stats(h2[r, :], keep, r, 4)
            if n == 112:
                hat = jnp.where(last_rows, hat, 0.0)
            total = total + jnp.sum(hat.reshape(n // 8, 8, D), 0)
        means.append(jnp.sum(total, 0, keepdims=True) * (1.0 / P_SIZE))
    mean_hat = jnp.concatenate(means + [jnp.zeros((14, D), F32)], axis=0)
    two = lax.broadcasted_iota(jnp.int32, (16, D), 0) < 2
    pooled = jnp.where(two, mean_hat * gain_end + shift_end, 0.0).astype(BF16)
    logits = jnp.concatenate([dot(pooled, cols(T_HEAD, 8, 48, j)) for j in range(4)], axis=1)
    lane = lax.broadcasted_iota(jnp.int32, (16, 1024), 1)
    lane_f = lane.astype(F32)
    inside = lane < CLS
    logits = jnp.where(inside, logits, -1e30)
    top = jnp.max(logits, -1, keepdims=True)
    total = jnp.sum(jnp.where(inside, jnp.exp(logits - top), 0.0), -1, keepdims=True)
    logp = logits - top - jnp.log(total)
    meta = meta_ref[...]
    pad14 = jnp.zeros((14, 1), F32)
    label = jnp.concatenate([meta[0:2, 0:1], pad14], axis=0)
    scale = jnp.concatenate([meta[2:4, 0:1], pad14], axis=0)
    valid = jnp.concatenate([meta[4:6, 0:1], pad14], axis=0)
    target = jnp.where(lane_f == label, 1.0 - SMOOTHING, 0.0) + SMOOTHING / CLS
    values = -jnp.sum(jnp.where(inside, target * logp, 0.0), -1, keepdims=True)
    loss_ref[...] = jnp.broadcast_to(jnp.sum(values * valid, 0, keepdims=True), (8, 128))
    d_logits = jnp.where(inside, scale * (jnp.exp(logp) - target), 0.0).astype(BF16)
    d_pooled = jnp.zeros((16, D), F32)
    for j in range(4):
        w = cols(T_HEAD, 8, 48, j)
        d_pooled = d_pooled + dot_t(d_logits[:, j * BLK : (j + 1) * BLK], w)
        put_cols(T_HEAD, 8, 48, j, t_dot(pooled, d_logits[:, j * BLK : (j + 1) * BLK]))
    d_gain_end = jnp.sum(d_pooled * mean_hat, 0, keepdims=True)
    d_shift_end = jnp.sum(d_pooled, 0, keepdims=True)
    for i in range(2):
        d_hat = d_pooled[i : i + 1, :] * (1.0 / P_SIZE) * gain_end

        m1 = jnp.sum(d_hat, -1, keepdims=True) * (1.0 / D)
        for at_row, n in BLOCKS[2 * i : 2 * i + 2]:
            r = pl.ds(at_row, n)
            hat, rstd = kept(h2[r, :], keep, r, 4)
            m2 = jnp.sum(d_hat * hat, -1, keepdims=True) * (1.0 / D)
            d = rstd * ((d_hat - m1) - hat * m2)
            if n == 112:
                d = jnp.where(last_rows, d, 0.0)
            dh[r, :] = d
            dyb[r, :] = d.astype(BF16)

    step("backward")
    at[...] = a2[...].T
    da = h2

    wide = D // 16

    def down_block(j, carry):
        part = section(T, T_FO + j * wide * 6, 6, wide)
        w = jnp.concatenate([part[:, k].reshape(D, 128) for k in range(6)], axis=1)
        dy = dyb[...]
        d_w = t_dot(hid[:, wide_lanes(j)], dy).astype(BF16)
        hid[:, wide_lanes(j)] = (dot_t(dy, w) * slope[:, wide_lanes(j)].astype(F32)).astype(BF16)
        for k in range(6):
            part[:, k] = d_w[:, k * 128 : (k + 1) * 128].reshape(wide, 16, 128)
        return carry

    G[pl.ds(4212, 12)] = jnp.zeros((12, 16, 128), BF16)
    lax.fori_loop(0, 3, down_block, 0)
    step("fc_out0")
    lax.fori_loop(3, 4, down_block, 0)
    step("fc_out1")
    def row_block(start, c, j):
        part = section(T, start + j * 16 * c, c, 16)
        return jnp.concatenate([part[:, k].reshape(BLK, 128) for k in range(c)], axis=1)

    def put_rows(start, c, j, first, value):
        part = section(G, start + j * 16 * c, c, 16)
        low = value.astype(BF16)
        for k in range(value.shape[1] // 128):
            part[:, first + k] = low[:, k * 128 : (k + 1) * 128].reshape(16, 16, 128)

    for j in range(3):
        da[:, pl.ds(j * BLK, BLK)] = dot_t(hid[...], row_block(T_IN, 24, j))
    step("fc_in0")
    for j in range(3):
        for k in range(4):
            put_rows(T_IN, 24, j, 6 * k, dot(at[pl.ds(j * BLK, BLK), :], hid[:, pl.ds(k * D, D)]))
        step("fc_in%d" % (j + 1))

    def norm_grads(inputs, column, gain):
        dg, ds = jnp.zeros((8, D), F32), jnp.zeros((8, D), F32)
        for at_row, n in BLOCKS:
            r = pl.ds(at_row, n)
            hat, rstd = kept(inputs[r, :], keep, r, column)
            d = da[r, :]
            new = dh[r, :] + norm_back(d * gain, hat, rstd)
            dh[r, :] = new
            dyb[r, :] = new.astype(BF16)
            dg = dg + jnp.sum((d * hat).reshape(n // 8, 8, D), 0)
            ds = ds + jnp.sum(d.reshape(n // 8, 8, D), 0)
        return dg, ds

    d_gain2, d_shift2 = norm_grads(h1, 2, gain2)

    step("normed2")
    at[...] = o[...].T
    for j in range(3):
        o[:, pl.ds(j * BLK, BLK)] = dot_t(dyb[...], row_block(T_OUT, 6, j)).astype(BF16)
    for j in range(3):
        put_rows(T_OUT, 6, j, 0, dot(at[pl.ds(j * BLK, BLK), :], dyb[...]))

    step("out")
    def attend_back(p, carry):
        for i in range(2):
            r, ls = heads_of(p, i)
            q, k, v = (mix[r, l] for l in ls)
            q = q * jnp.asarray(0.125, BF16)
            k8 = k * jnp.asarray(0.125, BF16)
            kt = k8.T
            do = o[r, ls[0]]
            pr = prob[p * 2 + i]
            dv = dot(pr.reshape(TOK, ROWS), do)
            dp = dot_t(split(v), do).reshape(2, ROWS, ROWS)
            prf = pr.astype(F32)
            row = jnp.sum(prf * dp, 1, keepdims=True)
            ds = (prf * (dp - row)).astype(BF16)
            dq = [dot(kt[HEAD_DIM * e : HEAD_DIM * (e + 1)], ds[e]) for e in range(2)]
            dk = dot(ds.reshape(TOK, ROWS), q)
            dmix[r, ls[0]] = jnp.concatenate(dq, axis=0).astype(BF16).T
            dmix[r, ls[1]] = jnp.where(first_half, dk[:ROWS], dk[ROWS:]).astype(BF16)
            dmix[r, ls[2]] = jnp.where(first_half, dv[:ROWS], dv[ROWS:]).astype(BF16)
        return carry

    for part in range(4):
        lax.fori_loop(*parts[part], attend_back, 0)
        step("back%d" % part)

    at[...] = a[...].T
    for j in range(3):
        da[:, pl.ds(j * BLK, BLK)] = dot_t(dmix[...], row_block(T_QKV, 18, j))
    for j in range(3):
        for k in range(3):
            put_rows(T_QKV, 18, j, 6 * k, dot(at[pl.ds(j * BLK, BLK), :], dmix[:, pl.ds(k * D, D)]))
    step("qkv_back")
    d_gain1, d_shift1 = norm_grads(h, 0, gain1)
    d_norms = jnp.concatenate([jnp.sum(d, 0, keepdims=True) for d in (d_gain1, d_shift1, d_gain2, d_shift2)] + [jnp.zeros((12, D), F32)], axis=0).astype(BF16)
    for j in range(6):
        G[T_NORM + j] = d_norms[:, j * 128 : (j + 1) * 128]
    step("norms")
    at[...] = x[...].T
    row_id = lax.broadcasted_iota(jnp.int32, (ROWS, BLK), 0)
    for j in range(3):
        put_cols(T_E, 6, 48, j, dot(at[...], dyb[:, pl.ds(j * BLK, BLK)]))
        c = pl.ds(j * BLK, BLK)
        s = slice(j * BLK, (j + 1) * BLK)
        d_pos = dh[pl.ds(0, ROWS), c] + dh[pl.ds(ROWS, ROWS), c]
        d_pos = jnp.where(row_id < P_SIZE, d_pos, 0.0)
        d_pos = jnp.where(row_id == P_SIZE, jnp.broadcast_to(d_gain_end[:, s], (ROWS, BLK)), d_pos)
        d_pos = jnp.where(row_id == P_SIZE + 1, jnp.broadcast_to(d_shift_end[:, s], (ROWS, BLK)), d_pos)
        put_cols(T_POS, 6, 13, j, d_pos)
    step("embed")


FORWARD = {
    "start": (
        (0, 0), (1, 0), (2, 0), (3, 0), (0, 1), (2, 1), (1, 1), (0, 2), (1, 2), (0, 3), (1, 3), (2, 2),
        (1, 4), (0, 4), (0, 6), (3, 1), (2, 3),
    ),
    "embedded": ((1, 5), (3, 2),),
    "qkv": ((1, 6),),
    "attend0": ((2, 4),),
    "attend2": ((3, 3),),
    "attend3": ((2, 5),),
    "up": ((2, 6), (3, 4),),
    "down": ((3, 5), (3, 6),),
}
BACKWARD = {
    "fc_out1": ((3, 0, 0), (3, 1, 0),),
    "fc_in3": ((3, 1, 1), (2, 0, 0), (2, 1, 0), (3, 0, 1),),
    "back0": ((2, 1, 1), (2, 0, 1),),
    "back3": ((3, 1, 2), (3, 0, 2),),
    "qkv_back": ((1, 0, 0), (2, 1, 2),),
    "norms": ((0, 1, 0), (1, 1, 0), (2, 0, 2),),
    "embed": (
        (3, 0, 3), (1, 0, 1), (0, 1, 1), (1, 1, 1), (0, 0, 0), (0, 0, 1), (1, 0, 2), (3, 1, 3), (0, 1, 2), (2, 0, 3), (1, 1, 2), (0, 0, 2),
        (0, 1, 3), (2, 1, 3), (1, 0, 3), (1, 1, 3), (0, 0, 3), (3, 0, 4), (3, 1, 4), (2, 1, 4), (2, 0, 4), (0, 1, 4), (1, 0, 4), (1, 1, 4),
        (0, 0, 4), (3, 1, 5), (1, 0, 5), (2, 1, 5), (2, 0, 5), (3, 0, 5), (0, 1, 5), (0, 0, 5), (1, 1, 5),
    ),
}


def grads_kernel(w_ref, patch_ref, labels_ref, counts_ref, red_ref, loss_out, T, R, RA, RB, g_send, g_recv, r_send, r_recv, LS, l_send, l_recv, patch_in, meta_in, meta, loss, *rest):
    gather_refs, compute_refs, out_sem = rest[:12], rest[12:-1], rest[-1]
    links = Links(T, R, RA, RB, g_send, g_recv, r_send, r_recv)
    xl, b, z, a, y = links.xl, links.b, links.z, links.a, links.y
    swap = a != b
    mirror = device(xl, b, a, z, y)
    units_here, finish_start = start_gather(links, w_ref, patch_ref, labels_ref, counts_ref, T, patch_in, meta_in, meta, *gather_refs)

    def loss_send(src, dst, target):
        links.go(LS.at[src], LS.at[dst], l_send.at[dst], l_recv.at[dst], target)

    def loss_wait(*slots):
        for k in slots:
            links.landed(LS.at[k], l_send.at[k], l_recv.at[k])

    def loss_step(n):
        if n == 0:
            LS[0] = loss[...]
            loss_send(0, 1, links.sibling)
        elif n == 1:
            loss_wait(1)
            LS[8] = LS[0] + LS[1]
            loss_send(8, 2, links.at_y(1))
            loss_send(8, 3, links.at_y(3))
        elif n == 2:
            loss_wait(2, 3)
            loss_send(2, 4, links.at_y(1))
        elif n == 3:
            loss_wait(4)
            LS[9] = (LS[8] + LS[4]) + (LS[2] + LS[3])
            loss_send(9, 5, links.at_z(1))
            loss_send(9, 6, links.at_z(3))
        elif n == 4:
            loss_wait(5, 6)
            loss_send(5, 7, links.at_z(1))
        elif n == 5:
            loss_wait(7)
            LS[10] = (LS[9] + LS[7]) + (LS[5] + LS[6])

            @pl.when(swap)
            def _():
                loss_swap.start()

        else:

            @pl.when(swap)
            def _():
                loss_swap.wait()
                loss_out[...] = LS[11]

            @pl.when(jnp.logical_not(swap))
            def _():
                loss_out[...] = LS[10]

    loss_swap = pltpu.make_async_remote_copy(src_ref=LS.at[10], dst_ref=LS.at[11], send_sem=l_send.at[11], recv_sem=l_recv.at[11], device_id=mirror, device_id_type=MESH)
    losses = {"fc_out0": 0, "fc_in2": 1, "out": 2, "back1": 3, "back3": 4, "norms": 5}

    def step(name):
        if name == "pool":
            links.sent()
        for item in FORWARD.get(name, ()):
            if item[1] == 0:
                units_here(item[0])
            links.gather_step(*item)
        if name == "start":
            finish_start()
        for item in BACKWARD.get(name, ()):
            links.reduce_step(*item)
        if name in losses:
            loss_step(losses[name])

    compute(step, patch_in, meta_in, loss, T, *compute_refs)
    loss_step(6)
    mine = T.reshape(ROUNDS, 32, UNIT, 16, 128).at[:, z * 8 + b * 4 + y]
    out = pltpu.make_async_copy(mine, red_ref, out_sem)
    out.start()
    links.sent()
    out.wait()


def grads(weights, patches, labels, counts):
    hbm = pl.BlockSpec(memory_space=pl.ANY)
    vmem = pl.BlockSpec(memory_space=pltpu.VMEM)
    V = pltpu.VMEM
    dma = pltpu.SemaphoreType.DMA
    return pl.pallas_call(
        grads_kernel,
        out_shape=(jax.ShapeDtypeStruct((ROUNDS, UNIT, 16, 128), BF16), jax.ShapeDtypeStruct((8, 128), F32)),
        in_specs=[hbm] * 2 + [pl.BlockSpec(memory_space=pltpu.SMEM)] * 2,
        out_specs=(hbm, vmem),
        scratch_shapes=[
            V((NTILES, 16, 128), BF16),
            V((ROUNDS, 4, 4, UNIT, 16, 128), BF16),
            V((6, ROUNDS, 2, UNIT, 16, 128), BF16),
            V((6, ROUNDS, 3, 16, 128), BF16),
            dma((192,)),
            dma((192,)),
            dma((104,)),
            dma((104,)),
            V((12, 8, 128), F32),
            dma((12,)),
            dma((12,)),
            V(patches.shape, BF16),
            V((8, 128), F32),
            V((8, 128), F32),
            V((8, 128), F32),
            V((FROWS, 128), F32),
            V((128, 128), F32),
            V((LO, 128), BF16),
            V((HI, 128), BF16),
            V((HI, 128), BF16),
            V((LO, 128), BF16),
            V((SLOT, 16, 128), BF16),
            dma((4,)),
            dma((4,)),
            dma((4,)),
            dma((ROUNDS,)),
            dma((ROUNDS,)),
            V((TOK, D), BF16),
            V((TOK, D), F32),
            V((TOK, D), BF16),
            V((D, TOK), BF16),
            V((TOK, 3 * D), BF16),
            V((12, 2, ROWS, ROWS), BF16),
            V((TOK, D), BF16),
            V((TOK, D), F32),
            V((TOK, D), BF16),
            V((TOK, FF), BF16),
            V((TOK, FF), BF16),
            V((TOK, D), F32),
            V((TOK, D), F32),
            V((TOK, D), BF16),
            V((TOK, 128), F32),
            dma,
        ],
        compiler_params=pltpu.CompilerParams(collective_id=0, has_side_effects=True, vmem_limit_bytes=60 * 1024 * 1024),
        name="grads",
    )(weights, patches, labels, counts)


EDGE = 24
FRONT = 768
BACK_ROWS = FRONT + SHARD + 640 + 6
PADDED = 2112
STEP = 10
EDGE_UNITS = 4
WINDOW = ROUNDS + 2 * EDGE_UNITS
BETA_ONE = 0.9
BETA_TWO = 0.95
ADAM_EPS = 1e-08
DECAY = 0.05
INNER_RATE = 0.01
OUTER_RATE = 0.7
OUTER_MU = 0.9


def update_kernel(
    red_ref, first_ref, second_ref,
    sum_out, first_out, second_out,
    red, window, flat, headrows, first_row, second_row, first, second, low, low2, pair, pair2, total, total2,
    load_sem, x_send, x_recv, o_send, e_send, w_recv,
):
    xl, b, z, a, y = coords()
    fs = z * 8 + a * 4 + y
    holder = z * 8 + b * 4 + y
    sibling = device(xl, a, 1 - b, z, y)
    across = device(1 - xl, a, b, z, y)
    extra = [pltpu.make_async_copy(src, dst, load_sem.at[i]) for i, (src, dst) in enumerate(((first_ref, first_row), (second_ref, second_row)))]
    load = pltpu.make_async_copy(red_ref, red, load_sem.at[4])
    load.start()
    for copy in extra:
        copy.start()

    barrier = pltpu.get_barrier_semaphore()

    def greet(target):
        pl.semaphore_signal(barrier, inc=1, device_id=target, device_id_type=MESH)

    greet(sibling)
    greet(across)
    first_unit = ROUNDS * fs - EDGE_UNITS

    def window_unit(p):
        k = first_unit + p
        d = lax.rem(k + 32, 32)
        inside = jnp.logical_and(k >= 0, k < 32 * ROUNDS)
        mine = jnp.logical_and(a == b, d == holder)
        return inside, mine, device(xl, b, lax.rem(lax.div(d, 4), 2), lax.div(d, 8), lax.rem(d, 4))

    def greet_holder(p, carry):
        inside, mine, source = window_unit(p)

        @pl.when(jnp.logical_and(inside, jnp.logical_not(mine)))
        def _():
            greet(source)

        return carry

    lax.fori_loop(0, WINDOW, greet_holder, 0)

    def held_unit(j):
        k = 32 * j + holder
        q = lax.div(k, ROUNDS)
        r = lax.rem(k, ROUNDS)
        shift = jnp.where(r < EDGE_UNITS, -1, jnp.where(r >= ROUNDS - EDGE_UNITS, 1, 0))
        near = jnp.logical_and(shift != 0, jnp.logical_and(q + shift >= 0, q + shift < NSLOT))
        return k, q, jnp.where(near, q + shift, q), near

    def to_owner(j, k, s, send):
        p = k - (ROUNDS * s - EDGE_UNITS)
        src = red.at[j]
        dst = window.at[pl.ds(UNIT * p, UNIT)]
        sa = lax.rem(lax.div(s, 4), 2)
        mine = jnp.logical_and(a == b, s == fs)
        target = device(xl, sa, a, lax.div(s, 8), lax.rem(s, 4))
        away = pltpu.make_async_remote_copy(src_ref=src, dst_ref=dst, send_sem=send.at[j], recv_sem=w_recv.at[p], device_id=target, device_id_type=MESH)
        here = pltpu.make_async_copy(src, dst, load_sem.at[10])
        return mine, away, here

    def count(j, n):
        k, q, s, near = held_unit(j)
        first_away = jnp.logical_not(jnp.logical_and(a == b, q == fs))
        second_away = jnp.logical_and(near, jnp.logical_not(jnp.logical_and(a == b, s == fs)))
        return n + jnp.where(first_away, 1, 0) + jnp.where(second_away, 1, 0)

    outgoing = lax.fori_loop(0, ROUNDS, count, 2)
    pl.semaphore_wait(barrier, outgoing)
    load.wait()

    def give(j, carry):
        k, q, s, near = held_unit(j)
        mine, away, here = to_owner(j, k, q, o_send)

        @pl.when(mine)
        def _():
            here.start()

        @pl.when(jnp.logical_not(mine))
        def _():
            away.start()

        mine2, away2, here2 = to_owner(j, k, s, e_send)

        @pl.when(jnp.logical_and(near, mine2))
        def _():
            here2.start()

        @pl.when(jnp.logical_and(near, jnp.logical_not(mine2)))
        def _():
            away2.start()

        return carry

    lax.fori_loop(0, ROUNDS, give, 0)

    def given(j, carry):
        k, q, s, near = held_unit(j)
        mine, away, here = to_owner(j, k, q, o_send)

        @pl.when(jnp.logical_not(mine))
        def _():
            away.wait_send()

        mine2, away2, here2 = to_owner(j, k, s, e_send)

        @pl.when(jnp.logical_and(near, jnp.logical_not(mine2)))
        def _():
            away2.wait_send()

        return carry

    def clear(i, carry):
        flat[pl.ds(pl.multiple_of(i * 32, 32), 32), :] = jnp.zeros((32, 128), F32)
        return carry

    lax.fori_loop(0, BACK_ROWS // 32, clear, 0)

    for copy in extra:
        copy.wait()
    for source, rows_of in ((first_row, first), (second_row, second)):

        def eight(i, carry):
            rows_of[pl.ds(pl.multiple_of(i * 8, 8), 8), :] = source[0, pl.ds(pl.multiple_of(i * 1024, 1024), 1024)].reshape(8, 128)
            return carry

        whole = SHARD // 8
        lax.fori_loop(0, whole, eight, 0, unroll=2)
        rows_of[pl.ds(whole * 8, SHARD - whole * 8), :] = source[0, pl.ds(whole * 1024, (SHARD - whole * 8) * 128)].reshape(SHARD - whole * 8, 128)

    def got(p, carry):
        inside, mine, source = window_unit(p)
        place = window.at[pl.ds(UNIT * p, UNIT)]

        @pl.when(jnp.logical_and(inside, mine))
        def _():
            pltpu.make_async_copy(place, place, load_sem.at[10]).wait()

        @pl.when(jnp.logical_and(inside, jnp.logical_not(mine)))
        def _():
            pltpu.make_async_remote_copy(src_ref=place, dst_ref=place, send_sem=x_send.at[0], recv_sem=w_recv.at[p], device_id=sibling, device_id_type=MESH).wait_recv()

        return carry

    lax.fori_loop(0, WINDOW, got, 0)
    sends = []

    def go(src, dst, send, recv, k, target):
        copy = pltpu.make_async_remote_copy(src_ref=src, dst_ref=dst, send_sem=send.at[k], recv_sem=recv.at[k], device_id=target, device_id_type=MESH)
        copy.start()
        sends.append(copy)

    def arrive(dst, recv, k):
        pltpu.make_async_remote_copy(src_ref=dst, dst_ref=dst, send_sem=x_send.at[k], recv_sem=recv.at[k], device_id=sibling, device_id_type=MESH).wait_recv()

    low_tile = SLOT * fs - EDGE
    high_tile = SLOT * fs + SLOT + EDGE
    origin = SHARD * fs - FRONT
    for index, (base, c, groups, per, start) in enumerate(SECTIONS):
        if index == 1:
            lane = lax.broadcasted_iota(jnp.int32, (8, 128), 1)
            g0 = lax.div(jnp.maximum(SHARD * fs - base, 0), per)
            g1 = lax.div(jnp.maximum(SHARD * (fs + 1) - base, 0) + per - 1, per)

            def head_group(g, carry):
                t = start + g * 8 - low_tile
                for j in range(8):
                    headrows[pl.ds(j, 16, stride=8), :] = window[t + j].astype(F32)
                row = base + per * g - origin
                for i in range(16):
                    q, s = divmod(1000 * i, 128)
                    value = headrows[pl.ds(i * 8, 8), :]
                    if s:
                        value = pltpu.roll(value, s, 1)
                        flat[pl.ds(row + q, 8), :] += jnp.where(lane >= s, value, 0.0)
                        flat[pl.ds(row + q + 1, 8), :] += jnp.where(lane < s, value, 0.0)
                    else:
                        flat[pl.ds(row + q, 8), :] += value
                return carry

            lax.fori_loop(jnp.minimum(g0, groups), jnp.minimum(g1, groups), head_group, 0)
        else:

            def unit(n, carry):
                t = UNIT * n - start
                row = base + 16 * c * lax.div(t, c) + lax.rem(t, c) - origin
                for m in range(UNIT):
                    flat[pl.ds(row + m, 16, stride=c), :] = window[UNIT * n - low_tile + m].astype(F32)
                return carry

            lax.fori_loop(lax.div(jnp.maximum(low_tile, start), UNIT), lax.div(jnp.minimum(high_tile, start + c * groups), UNIT), unit, 0)

    fix_one = 1.0 / (1.0 - BETA_ONE**STEP)
    fix_two = 1.0 / (1.0 - BETA_TWO**STEP)

    half = PADDED // 2
    step = 96
    for rows_of in (first, second):
        rows_of[pl.ds(SHARD, PADDED - SHARD), :] = jnp.zeros((PADDED - SHARD, 128), F32)

    def in_half(fn):
        def rows_step(i, carry):
            fn(pl.multiple_of(i * step, step), step)
            return carry

        lax.fori_loop(0, half // step, rows_step, 0)

    def adam_half(q):
        def adam(r, n):
            at = pl.ds(pl.multiple_of(q * half + r, 16), n)
            grad = flat[pl.ds(pl.multiple_of(FRONT + q * half + r, 16), n), :]
            m = BETA_ONE * first[at, :] + (1.0 - BETA_ONE) * grad
            s = BETA_TWO * second[at, :] + (1.0 - BETA_TWO) * grad * grad
            first[at, :] = m
            second[at, :] = s
            low[at, :] = ((m * fix_one) / (jnp.sqrt(s * fix_two) + ADAM_EPS)).astype(BF16)

        in_half(adam)

    adam_half(1 - b)
    go(low.at[pl.ds(pl.multiple_of((1 - b) * half, 16), half)], low2, x_send, x_recv, 0, sibling)
    adam_half(b)
    outs = [pltpu.make_async_copy(src.at[pl.ds(0, SHARD)], dst, load_sem.at[5 + i]) for i, (src, dst) in enumerate(((first, first_out), (second, second_out)))]
    for copy in outs:
        copy.start()
    arrive(low2, x_recv, 0)

    def pairs(r, n):
        pair[pl.ds(r, n), :] = low[pl.ds(pl.multiple_of(b * half + r, 16), n), :] + low2[pl.ds(r, n), :]

    in_half(pairs)
    go(pair, pair2, x_send, x_recv, 1, across)
    arrive(pair2, x_recv, 1)

    def fours(r, n):
        total[pl.ds(r, n), :] = pair[pl.ds(r, n), :].astype(F32) + pair2[pl.ds(r, n), :].astype(F32)

    in_half(fours)
    go(total, total2, x_send, x_recv, 2, sibling)

    arrive(total2, x_recv, 2)
    other = half - b * half
    final = [(total, sum_out.at[pl.ds(pl.multiple_of(b * half, 16), half)]), (total2, sum_out.at[pl.ds(pl.multiple_of(other, 16), half)])]
    final = [pltpu.make_async_copy(src, dst, load_sem.at[7 + i]) for i, (src, dst) in enumerate(final)]
    for copy in final:
        copy.start()
    for copy in sends:
        copy.wait_send()
    lax.fori_loop(0, ROUNDS, given, 0)
    for copy in outs + final:
        copy.wait()


def update(red, first, second):
    hbm = pl.BlockSpec(memory_space=pl.ANY)
    V = pltpu.VMEM
    flat = jax.ShapeDtypeStruct((SHARD, 128), F32)
    dma = pltpu.SemaphoreType.DMA
    return pl.pallas_call(
        update_kernel,
        out_shape=(jax.ShapeDtypeStruct((PADDED, 128), F32), flat, flat),
        in_specs=[hbm] * 3,
        out_specs=(hbm,) * 3,
        scratch_shapes=[
            V((ROUNDS, UNIT, 16, 128), BF16),
            V((EDGE + SLOT + EDGE, 16, 128), BF16),
            V((BACK_ROWS, 128), F32),
            V((128, 128), F32),
            V((1, SHARD * 128), F32),
            V((1, SHARD * 128), F32),
            V((PADDED, 128), F32),
            V((PADDED, 128), F32),
            V((PADDED, 128), BF16),
            V((PADDED // 2, 128), BF16),
            V((PADDED // 2, 128), BF16),
            V((PADDED // 2, 128), BF16),
            V((PADDED // 2, 128), F32),
            V((PADDED // 2, 128), F32),
            dma((11,)),
            dma((3,)),
            dma((3,)),
            dma((ROUNDS,)),
            dma((ROUNDS,)),
            dma((WINDOW,)),
        ],
        compiler_params=pltpu.CompilerParams(collective_id=1, has_side_effects=True, vmem_limit_bytes=60 * 1024 * 1024),
        name="update",
    )(red, first, second)


def finish_kernel(
    sum_ref, w_ref, mom_ref, first_ref, second_ref, loss_ref,
    avg_out, mom_out, new_out, first_out, second_out, loss_out,
    total, w, mom, first, second, averaged, sem, out_sem,
):
    cut = PADDED // 2
    pieces = [pl.ds(0, cut), pl.ds(cut, SHARD - cut)]
    loads = []
    for i, at in enumerate(pieces):
        loads.append([pltpu.make_async_copy(src.at[at], dst.at[at], sem.at[3 * i + k]) for k, (src, dst) in enumerate(((sum_ref, total), (w_ref, w), (mom_ref, mom)))])
    moments = [pltpu.make_async_copy(src, dst, sem.at[6 + i]) for i, (src, dst) in enumerate(((first_ref, first), (second_ref, second)))]
    for copy in loads[0] + loads[1] + moments:
        copy.start()
    outs = []

    def send(src, dst):
        copy = pltpu.make_async_copy(src, dst, out_sem.at[len(outs)])
        copy.start()
        outs.append(copy)

    loss_out[...] = loss_ref[0:1, 0:1]

    def outer(r, n):
        at = pl.ds(r, n)
        old = w[at, :]
        mean = INNER_RATE * (total[at, :] * 0.25 + DECAY * old)
        momentum = OUTER_MU * mom[at, :] + mean
        averaged[at, :] = mean
        mom[at, :] = momentum
        w[at, :] = old - OUTER_RATE * (mean + OUTER_MU * momentum)

    def block(i, carry):
        outer(pl.multiple_of(i * 96, 96), 96)
        return carry

    for i, at in enumerate(pieces):
        for copy in loads[i]:
            copy.wait()
        if i == 0:
            lax.fori_loop(0, cut // 96, block, 0)
        else:
            lax.fori_loop(cut // 96, SHARD // 96, block, 0)
            outer(SHARD // 96 * 96, SHARD - SHARD // 96 * 96)
        for src, dst in ((averaged, avg_out), (mom, mom_out), (w, new_out)):
            send(src.at[at], dst.at[at])
        if i == 0:
            for copy, src, dst in zip(moments, (first, second), (first_out, second_out)):
                copy.wait()
                send(src, dst.reshape(SHARD, 128))
    for copy in outs:
        copy.wait()


def finish(total, weights, momentum, first, second, loss):
    hbm = pl.BlockSpec(memory_space=pl.ANY)
    vmem = pl.BlockSpec(memory_space=pltpu.VMEM)
    V = pltpu.VMEM
    rows = jax.ShapeDtypeStruct((SHARD, 128), F32)
    row = jax.ShapeDtypeStruct((1, SHARD * 128), F32)
    return pl.pallas_call(
        finish_kernel,
        out_shape=(rows,) * 3 + (row,) * 2 + (jax.ShapeDtypeStruct((1, 1), F32),),
        in_specs=[hbm] * 5 + [vmem],
        out_specs=(hbm,) * 5 + (vmem,),
        scratch_shapes=[V((PADDED, 128), F32)] + [V((SHARD, 128), F32)] * 5 + [pltpu.SemaphoreType.DMA((8,)), pltpu.SemaphoreType.DMA((8,))],
        compiler_params=pltpu.CompilerParams(vmem_limit_bytes=60 * 1024 * 1024),
        name="finish",
    )(total, weights, momentum, first, second, loss)


def body(patches, labels, counts, weights, first_moments, second_moments, outer_momentum):
    flat = weights.reshape(SHARD, 128)
    reduced, loss = grads(flat, patches.reshape(2, P_SIZE, D), labels.reshape(2), counts.reshape(2))
    total, first, second = update(reduced, first_moments, second_moments)
    averaged, momentum, new_weights, first, second, loss = finish(total, flat, outer_momentum.reshape(SHARD, 128), first, second, loss)
    return (
        averaged.reshape(-1),
        momentum.reshape(-1),
        new_weights.reshape(-1),
        first,
        second,
        loss,
    )


def solution(mesh):
    placed = (
        P("rep", None, None, "fsdp", None, None),
        P("rep", None, None, "fsdp"),
        P("rep", None, None),
        P("fsdp"),
        P("rep", "fsdp"),
        P("rep", "fsdp"),
        P("fsdp"),
    )
    return jax.shard_map(
        body,
        mesh=mesh,
        in_specs=placed,
        out_specs=(
            P("fsdp"),
            P("fsdp"),
            P("fsdp"),
            P("rep", "fsdp"),
            P("rep", "fsdp"),
            P("rep", None),
        ),
        check_vma=False,
    )
```

```python
from functools import partial

import jax
import jax.numpy as jnp
from jax import lax
from jax.experimental import pallas as pl
from jax.experimental.pallas import tpu as pltpu
from jax.sharding import PartitionSpec as P

SHARD = 2098
SLOT = 132
HALF = 66
QUART = 33
NSLOT = 32
ROUNDS = 22
UNIT = 6
STAGES = ((0, 4), (4, 10), (10, 16), (16, 22))
SECTIONS = []
_t = 0
for _base, _c, _g, _rpg in ((0, 6, 61, 96), (5796, 8, 48, 125), (11796, 6, 1, 96), (11820, 18, 48, 288), (25644, 6, 48, 96), (30252, 24, 48, 384), (48684, 6, 192, 96)):
    SECTIONS.append((_base, _c, _g, _rpg, _t))
    _t += _c * _g
NTILE = _t
HI = 352
LO = 224
MARGIN = 512
FROWS = 3072
HEAD_ROWS = 16
MESH = pl.DeviceIdType.MESH


def coords():
    rep = lax.axis_index("rep")
    fs = lax.axis_index("fsdp")
    return lax.div(rep, 2), lax.rem(rep, 2), lax.div(fs, 8), lax.rem(lax.div(fs, 4), 2), lax.rem(fs, 4)


def device(xl, xh, core, z, y):
    return {"rep": xl * 2 + core, "fsdp": z * 8 + xh * 4 + y}


def flat_device(xl, core, s):
    return device(xl, lax.rem(lax.div(s, 4), 2), core, lax.div(s, 8), lax.rem(s, 4))


class Links:

    def __init__(self, T, R, RA, RB, g_send, g_recv, r_send, r_recv):
        self.xl, self.b, self.z, self.a, self.y = coords()
        self.T5 = T.reshape(ROUNDS, 4, 2, 4, UNIT, 16, 128)
        self.R, self.RA, self.RB = R, RA, RB
        self.g_send, self.g_recv, self.r_send, self.r_recv = g_send, g_recv, r_send, r_recv
        self.pending = []
        self.sibling = device(self.xl, self.a, 1 - self.b, self.z, self.y)

    def at_y(self, k):
        return device(self.xl, self.a, self.b, self.z, lax.rem(self.y + k, 4))

    def at_z(self, k):
        return device(self.xl, self.a, self.b, lax.rem(self.z + k, 4), self.y)

    def at_x(self, k):
        a = lax.rem(self.a + (self.xl if k == 1 else 1 - self.xl), 2)
        return device(1 - self.xl, a, self.b, self.z, self.y)

    def go(self, src, dst, send, recv, target):
        copy = pltpu.make_async_remote_copy(src_ref=src, dst_ref=dst, send_sem=send, recv_sem=recv, device_id=target, device_id_type=MESH)
        copy.start()
        self.pending.append(copy)

    def landed(self, dst, send, recv):
        pltpu.make_async_remote_copy(src_ref=dst, dst_ref=dst, send_sem=send, recv_sem=recv, device_id=self.sibling, device_id_type=MESH).wait_recv()

    def sent(self):
        for copy in self.pending:
            copy.wait_send()
        self.pending = []

    def span(self, i, h):
        lo, hi = STAGES[i]
        n = (hi - lo) // 2
        return pl.ds(lo + h * n, n)

    def first_axis(self, h, k):
        return (self.at_y if h == 0 else self.at_z)(k)

    def second_axis(self, h, k):
        return (self.at_z if h == 0 else self.at_y)(k)

    def gathered(self, i, h):
        lo, hi = STAGES[i]
        n = (hi - lo) // 2
        if i == 0:
            return pl.ds(lo + h * n, n)
        return pl.ds(lo + h * n + self.xl, 2)

    def single(self, i, h, own):
        lo, hi = STAGES[i]
        parity = self.xl if own else 1 - self.xl
        return pl.ds(lo + h * ((hi - lo) // 2) + 2 * parity, 1)

    def one(self, i, h, k, q=None):
        rd = self.gathered(i, h)
        t = pl.ds(0, UNIT) if q is None else pl.ds(3 * q, 3)
        if h == 0:
            return self.T5.at[rd, self.z, self.b, lax.rem(self.y + k, 4), t]
        return self.T5.at[rd, lax.rem(self.z + k, 4), self.b, self.y, t]

    def row(self, rd, h, k, core=None, p=None):
        core = self.b if core is None else core
        t = pl.ds(0, 4) if p is None else pl.ds(2 * p, 2)
        if h == 0:
            return self.T5.at[rd, lax.rem(self.z + k, 4), core, t]
        return self.T5.at[rd, t, core, lax.rem(self.y + k, 4)]

    def gsem(self, i, h, k):
        n = (i * 2 + h) * 24 + k
        return self.g_send.at[n], self.g_recv.at[n]

    def gather_go(self, i, h, k, view, target):
        self.go(view, view, *self.gsem(i, h, k), target)

    def gather_wait(self, i, h, k, view):
        self.landed(view, *self.gsem(i, h, k))

    def share(self, i, h, m, k):
        self.gather_go(i, h, 8 + m, self.row(self.gathered(i, h), h, k), self.sibling)
        if i > 0:
            rd = self.single(i, h, True)
            self.gather_go(i, h, 12 + m, self.row(rd, h, k, p=0), self.at_x(1))
            self.gather_go(i, h, 16 + m, self.row(rd, h, k, p=1), self.at_x(3))

    def gather_step(self, i, step):
        for h in range(2):
            rd = self.gathered(i, h)
            if step == 0:
                self.gather_go(i, h, 0, self.one(i, h, 0), self.first_axis(h, 1))
                self.gather_go(i, h, 1, self.one(i, h, 0), self.first_axis(h, 3))
            elif step == 1:
                self.gather_wait(i, h, 0, self.one(i, h, 3))
                self.gather_go(i, h, 2, self.one(i, h, 3, 0), self.first_axis(h, 1))
                self.gather_wait(i, h, 1, self.one(i, h, 1))
                self.gather_go(i, h, 3, self.one(i, h, 1, 1), self.first_axis(h, 3))
            elif step == 2:
                self.gather_wait(i, h, 2, self.one(i, h, 2, 0))
                self.gather_wait(i, h, 3, self.one(i, h, 2, 1))
                self.gather_go(i, h, 4, self.row(rd, h, 0), self.second_axis(h, 1))
                self.gather_go(i, h, 5, self.row(rd, h, 0), self.second_axis(h, 3))
                self.share(i, h, 0, 0)
            elif step == 3:
                self.gather_wait(i, h, 4, self.row(rd, h, 3))
                self.gather_go(i, h, 6, self.row(rd, h, 3, p=0), self.second_axis(h, 1))
                self.share(i, h, 1, 3)
                self.gather_wait(i, h, 5, self.row(rd, h, 1))
                self.gather_go(i, h, 7, self.row(rd, h, 1, p=1), self.second_axis(h, 3))
                self.share(i, h, 2, 1)
            elif step == 4:
                self.gather_wait(i, h, 6, self.row(rd, h, 2, p=0))
                self.gather_wait(i, h, 7, self.row(rd, h, 2, p=1))
                self.share(i, h, 3, 2)
            elif step == 5:
                if i > 0:
                    other = self.single(i, h, False)
                    for m, k in enumerate((0, 3, 1, 2)):
                        self.gather_wait(i, h, 12 + m, self.row(other, h, k, p=0))
                        self.gather_wait(i, h, 16 + m, self.row(other, h, k, p=1))
                        self.gather_go(i, h, 20 + m, self.row(other, h, k), self.sibling)
            else:
                for m, k in enumerate((0, 3, 1, 2)):
                    self.gather_wait(i, h, 8 + m, self.row(rd, h, k, core=1 - self.b))
                    if i > 0:
                        self.gather_wait(i, h, 20 + m, self.row(self.single(i, h, False), h, k, core=1 - self.b))

    def rsem(self, i, h, k):
        n = (i * 2 + h) * 13 + k
        return self.r_send.at[n], self.r_recv.at[n]

    def cell(self, i, h, k, q):
        rd = self.span(i, h)
        t = pl.ds(3 * q, 3)
        if h == 0:
            return self.T5.at[rd, self.z, self.b, lax.rem(self.y + k, 4), t]
        return self.T5.at[rd, lax.rem(self.z + k, 4), self.b, self.y, t]

    def add(self, dst, *sources, inner=()):
        n = dst.shape[0]

        def one(r, carry):
            for k in range(inner) if inner else (None,):
                at = (r,) if k is None else (r, k)
                if len(sources) == 1:
                    dst[at] = dst[at] + sources[0][at]
                else:
                    total = dst[at].astype(jnp.float32)
                    for source in sources:
                        total = total + source[at].astype(jnp.float32)
                    dst[at] = total.astype(jnp.bfloat16)
            return carry

        lax.fori_loop(0, n, one, 0)

    def reduce_step(self, i, h, step):
        rd = self.span(i, h)
        T5 = self.T5

        def send_a(k, ka, p, shift):
            self.go(self.row(rd, h, ka, p=p), self.RA.at[k, rd], *self.rsem(i, h, 1 + k), self.second_axis(h, shift))

        def wait_a(k):
            self.landed(self.RA.at[k, rd], *self.rsem(i, h, 1 + k))

        def send_b(k, kb, q, shift):
            self.go(self.cell(i, h, kb, q), self.RB.at[k, rd], *self.rsem(i, h, 7 + k), self.first_axis(h, shift))

        def wait_b(k):
            self.landed(self.RB.at[k, rd], *self.rsem(i, h, 7 + k))

        if step == 0:
            self.go(T5.at[rd, :, 1 - self.b], self.R.at[rd], *self.rsem(i, h, 0), self.sibling)
        elif step == 1:
            self.landed(self.R.at[rd], *self.rsem(i, h, 0))
            mine, theirs = T5.at[rd, :, self.b], self.R.at[rd]
            n = mine.shape[0]

            def both(r, carry):
                q = lax.div(r, 4)
                w = lax.rem(r, 4)
                for k in range(4):
                    mine[q, w, k] = mine[q, w, k] + theirs[q, w, k]
                return carry

            lax.fori_loop(0, 4 * n, both, 0)
            send_a(0, 2, 0, 1)
            send_a(1, 2, 1, 3)
            send_a(2, 1, 1, 1)
            send_a(3, 3, 0, 3)
        elif step == 2:
            wait_a(0)
            self.add(self.row(rd, h, 1, p=0), self.RA.at[0, rd], inner=2)
            send_a(4, 1, 0, 1)
            wait_a(1)
            self.add(self.row(rd, h, 3, p=1), self.RA.at[1, rd], inner=2)
            send_a(5, 3, 1, 3)
        elif step == 3:
            for k in (2, 3, 4, 5):
                wait_a(k)
            self.add(self.row(rd, h, 0, p=0), self.RA.at[3, rd], self.RA.at[4, rd], inner=2)
            self.add(self.row(rd, h, 0, p=1), self.RA.at[2, rd], self.RA.at[5, rd], inner=2)
            send_b(0, 2, 0, 1)
            send_b(1, 2, 1, 3)
            send_b(2, 1, 1, 1)
            send_b(3, 3, 0, 3)
        elif step == 4:
            wait_b(0)
            self.add(self.cell(i, h, 1, 0), self.RB.at[0, rd])
            send_b(4, 1, 0, 1)
            wait_b(1)
            self.add(self.cell(i, h, 3, 1), self.RB.at[1, rd])
            send_b(5, 3, 1, 3)
        else:
            for k in (2, 3, 4, 5):
                wait_b(k)
            self.add(self.cell(i, h, 0, 0), self.RB.at[3, rd], self.RB.at[4, rd])
            self.add(self.cell(i, h, 0, 1), self.RB.at[2, rd], self.RB.at[5, rd])


def start_gather(links, w_ref, patch_ref, labels_ref, counts_ref, T, patch_in, meta_in, meta_ref, flat, headrows, lob, hib, rlo, rhi, slot, local_sem, x_send, x_recv, u_send, u_recv):
    xl, b, z, a, y = links.xl, links.b, links.z, links.a, links.y
    fs = z * 8 + a * 4 + y
    swap = a != b
    xo = lax.rem(xl + a + b, 2)
    holder = z * 8 + b * 4 + y
    up = flat_device(xl, b, lax.rem(fs + 1, NSLOT))
    down = flat_device(xl, b, lax.rem(fs + NSLOT - 1, NSLOT))
    mirror = device(xl, b, a, z, y)
    load = pltpu.make_async_copy(w_ref, flat.at[pl.ds(MARGIN, SHARD)], local_sem.at[0])
    load.start()
    barrier = pltpu.get_barrier_semaphore()
    total = (counts_ref[0] + counts_ref[1]).astype(jnp.float32)
    for m in range(2):
        valid = jnp.full((1, 128), jnp.where(fs < counts_ref[m], 1.0, 0.0), jnp.float32)
        meta_ref[m : m + 1, :] = jnp.full((1, 128), labels_ref[m].astype(jnp.float32), jnp.float32)
        meta_ref[2 + m : 3 + m, :] = valid / jnp.full((1, 128), total, jnp.float32)
        meta_ref[4 + m : 5 + m, :] = valid
    meta_ref[6:8, :] = jnp.zeros((2, 128), jnp.float32)

    def greet(target):
        pl.semaphore_signal(barrier, inc=1, device_id=target, device_id_type=MESH)

    def wanted(j, parity):
        return jnp.logical_or(j < STAGES[0][1], lax.rem(j + 3 - STAGES[0][1] % 3, 3) != 2 * (1 - parity))

    for target in (up, down, links.at_x(1), links.at_x(3), links.at_y(1), links.at_y(3), links.at_z(1), links.at_z(3), links.sibling):
        greet(target)

    @pl.when(swap)
    def _():
        greet(mirror)

    own_index = lax.rem(fs * 11, NSLOT)
    keeps = jnp.logical_and(a == b, own_index < ROUNDS)

    def greet_source(j, carry):
        s = lax.div(32 * j + holder, ROUNDS)
        sa = lax.rem(lax.div(s, 4), 2)

        @pl.when(jnp.logical_and(wanted(j, xl), jnp.logical_not(jnp.logical_and(keeps, s == fs))))
        def _():
            greet(device(lax.rem(xl + sa + a, 2), sa, a, lax.div(s, 8), lax.rem(s, 4)))

        return carry

    lax.fori_loop(0, ROUNDS, greet_source, 0)
    def unit_goes(i):
        there = wanted(lax.div(ROUNDS * fs + i, 32), xo)
        stays = jnp.logical_and(keeps, i == own_index)
        return jnp.logical_and(there, jnp.logical_not(stays)), jnp.logical_and(there, stays)

    outgoing = lax.fori_loop(0, ROUNDS, lambda i, n: n + jnp.where(unit_goes(i)[0], 1, 0), 9)
    pl.semaphore_wait(barrier, outgoing + jnp.where(swap, 1, 0))
    load.wait()

    def remote(src, dst, k, target):
        return pltpu.make_async_remote_copy(src_ref=src, dst_ref=dst, send_sem=x_send.at[k], recv_sem=x_recv.at[k], device_id=target, device_id_type=MESH)

    hib[...] = flat[pl.ds(MARGIN + SHARD - HI, HI), :].astype(jnp.bfloat16)
    to_up = remote(hib, rlo, 0, up)
    to_up.start()
    lob[...] = flat[pl.ds(MARGIN, LO), :].astype(jnp.bfloat16)
    to_down = remote(lob, rhi, 1, down)
    to_down.start()
    patch_swap = remote(patch_ref, patch_in, 2, mirror)
    meta_swap = remote(meta_ref, meta_in, 3, mirror)
    patch_keep = pltpu.make_async_copy(patch_ref, patch_in, local_sem.at[1])
    meta_keep = pltpu.make_async_copy(meta_ref, meta_in, local_sem.at[2])
    first = ROUNDS * fs
    origin = SHARD * fs - MARGIN

    def unit_copy(i):
        k = first + i
        d = lax.rem(k, 32)
        src = slot.at[pl.ds(UNIT * i, UNIT)]
        dst = T.at[pl.ds(UNIT * k, UNIT)]
        target = device(xo, b, lax.rem(lax.div(d, 4), 2), lax.div(d, 8), lax.rem(d, 4))
        away = pltpu.make_async_remote_copy(src_ref=src, dst_ref=dst, send_sem=u_send.at[i], recv_sem=u_recv.at[lax.div(k, 32)], device_id=target, device_id_type=MESH)
        return away, (src, dst)

    def send_unit(i):
        away, (src, dst) = unit_copy(i)
        goes, stays = unit_goes(i)

        @pl.when(stays)
        def _():
            pltpu.make_async_copy(src, dst, local_sem.at[3]).start()

        @pl.when(goes)
        def _():
            away.start()

    lane = lax.broadcasted_iota(jnp.int32, (8, 128), 1)

    def head_group(g, base, per, start):
        row = base + per * g - origin
        for i in range(16):
            q, s = divmod(1000 * i, 128)
            one = flat[pl.ds(row + q, 8), :]
            if s:
                two = flat[pl.ds(row + q + 1, 8), :]
                one = jnp.where(lane < 128 - s, pltpu.roll(one, 128 - s, 1), pltpu.roll(two, 128 - s, 1))
            headrows[pl.ds(i * 8, 8), :] = one
        for j in range(8):
            t = start + g * 8 + j - UNIT * first

            @pl.when(jnp.logical_and(t >= 0, t < SLOT))
            def _():
                slot[t] = headrows[pl.ds(j, 16, stride=8), :].astype(jnp.bfloat16)

    def inside(row, rows):
        return jnp.logical_and(row >= MARGIN, row + rows <= MARGIN + SHARD)

    def convert(near):
        for index, (base, c, groups, per, start) in enumerate(SECTIONS):
            lo = jnp.maximum(UNIT * first, start)
            hi = jnp.minimum(UNIT * first + SLOT, start + c * groups)
            if index == 1:

                def group(g, carry):
                    @pl.when(inside(base + per * g - origin, per + 1) == near)
                    def _():
                        head_group(g, base, per, start)

                    return carry

                lax.fori_loop(lax.div(jnp.maximum(lo, start) - start, 8), lax.div(jnp.maximum(hi, start) - start + 7, 8), group, 0)
                if not near:

                    def deal(u, carry):
                        send_unit(u - first)
                        return carry

                    lax.fori_loop(lax.div(lo, UNIT), lax.div(hi, UNIT), deal, 0)
            else:

                def unit(u, carry):
                    t = UNIT * u - start
                    g = lax.div(t, c)
                    row = base + 16 * c * g + lax.rem(t, c) - origin

                    @pl.when(inside(row, 15 * c + UNIT) == near)
                    def _():
                        for k in range(UNIT):
                            slot[UNIT * (u - first) + k] = flat[pl.ds(row + k, 16, stride=c), :].astype(jnp.bfloat16)
                        send_unit(u - first)

                    return carry

                lax.fori_loop(lax.div(lo, UNIT), lax.div(hi, UNIT), unit, 0)

    convert(True)
    to_up.wait_recv()
    flat[pl.ds(MARGIN - HI, HI), :] = rlo[...].astype(jnp.float32)
    to_down.wait_recv()
    flat[pl.ds(MARGIN + SHARD, LO), :] = rhi[...].astype(jnp.float32)
    convert(False)

    @pl.when(fs == NSLOT - 1)
    def _():
        slot[pl.ds(SLOT - 12, 12)] = jnp.zeros((12, 16, 128), jnp.bfloat16)
        send_unit(ROUNDS - 2)
        send_unit(ROUNDS - 1)

    @pl.when(swap)
    def _():
        patch_swap.start()
        meta_swap.start()

    @pl.when(jnp.logical_not(swap))
    def _():
        patch_keep.start()
        meta_keep.start()

    def units_here(i):
        def wait(j, carry):
            place = T.at[pl.ds(UNIT * (32 * j + holder), UNIT)]
            mine = jnp.logical_and(keeps, lax.div(32 * j + holder, ROUNDS) == fs)

            @pl.when(jnp.logical_and(wanted(j, xl), mine))
            def _():
                pltpu.make_async_copy(place, place, local_sem.at[3]).wait()

            @pl.when(jnp.logical_and(wanted(j, xl), jnp.logical_not(mine)))
            def _():
                pltpu.make_async_remote_copy(src_ref=place, dst_ref=place, send_sem=u_send.at[0], recv_sem=u_recv.at[j], device_id=links.sibling, device_id_type=MESH).wait_recv()

            return carry

        lax.fori_loop(*STAGES[i], wait, 0)

    def finish_start():
        def wait(i, carry):
            away, unused = unit_copy(i)

            @pl.when(unit_goes(i)[0])
            def _():
                away.wait_send()

            return carry

        lax.fori_loop(0, ROUNDS, wait, 0)
        to_up.wait_send()
        to_down.wait_send()

        @pl.when(swap)
        def _():
            patch_swap.wait()
            meta_swap.wait()

        @pl.when(jnp.logical_not(swap))
        def _():
            patch_keep.wait()
            meta_keep.wait()

    return units_here, finish_start


D = 768
HEADS = 12
HEAD_DIM = 64
FF = 3072
CLS = 1000
P_SIZE = 196
ROWS = 208
TOK = 2 * ROWS
NORM_EPS = 1e-06
SMOOTHING = 0.1
NTILES = 4224
T_E, T_HEAD, T_NORM, T_QKV, T_OUT, T_IN, T_FO = 0, 366, 750, 756, 1620, 1908, 3060
T_POS = 288
BLK = 256
BLOCKS = ((0, 96), (96, 112), (208, 96), (304, 112))
F32 = jnp.float32
BF16 = jnp.bfloat16
ROOT_HALF = 0.7071067811865476
INV_ROOT_TWO_PI = 0.3989422804014327


def dot(x, w):
    return lax.dot_general(x, w, (((1,), (0,)), ((), ())), preferred_element_type=F32)


def dot_t(x, w):
    return lax.dot_general(x, w, (((1,), (1,)), ((), ())), preferred_element_type=F32)


def t_dot(x, w):
    return lax.dot_general(x, w, (((0,), (0,)), ((), ())), preferred_element_type=F32)


def stats(x, keep, r, k):
    mean = jnp.sum(x, -1, keepdims=True) * (1.0 / D)
    centred = x - mean
    var = jnp.sum(centred * centred, -1, keepdims=True) * (1.0 / D)
    rstd = lax.rsqrt(var + NORM_EPS)
    keep[r, k : k + 1] = mean
    keep[r, k + 1 : k + 2] = rstd
    return centred * rstd


def kept(x, keep, r, k):
    rstd = keep[r, k + 1 : k + 2]
    return (x - keep[r, k : k + 1]) * rstd, rstd


def norm_back(d_hat, hat, rstd):
    m1 = jnp.sum(d_hat, -1, keepdims=True) * (1.0 / D)
    m2 = jnp.sum(d_hat * hat, -1, keepdims=True) * (1.0 / D)
    return rstd * (d_hat - m1 - hat * m2)


def compute(step, patch_ref, meta_ref, loss_ref, T, x, h, a, at, mix, prob, o, h1, a2, hid, slope, h2, dh, dyb, keep):
    G = T
    dmix = mix

    def section(ref, start, c, groups):
        return ref.at[pl.ds(start, groups * c)].reshape(groups, c, 16, 128)

    def cols(start, c, groups, j):
        part = section(T, start, c, groups)
        return jnp.concatenate([part[:, 2 * j + k].reshape(groups * 16, 128) for k in range(2)], axis=1)

    def put_cols(start, c, groups, j, value):
        low = value.astype(BF16)
        part = section(G, start, c, groups)
        for k in range(2):
            part[:, 2 * j + k] = low[:, k * 128 : (k + 1) * 128].reshape(groups, 16, 128)

    def row_of(start, k):
        return jnp.concatenate([T[start + j][k : k + 1, :] for j in range(6)], axis=1).astype(F32)

    def lanes(j):
        return pl.ds(pl.multiple_of(j * BLK, BLK), BLK)

    step("start")
    for i in range(2):
        x[pl.ds(i * ROWS, 192), :] = patch_ref[i, pl.ds(0, 192), :]
        x[pl.ds(i * ROWS + 192, 16), :] = jnp.concatenate([patch_ref[i, pl.ds(192, 4), :], jnp.zeros((12, D), BF16)], axis=0)

    real = lax.broadcasted_iota(jnp.int32, (ROWS, 128), 0) < P_SIZE
    for j in range(3):
        acc = dot(x[...], cols(T_E, 6, 48, j))
        p = cols(T_POS, 6, 13, j).astype(F32)
        p = jnp.where(lax.broadcasted_iota(jnp.int32, (ROWS, BLK), 0) < P_SIZE, p, 0.0)
        for i in range(2):
            h[pl.ds(i * ROWS, ROWS), pl.ds(j * BLK, BLK)] = acc[i * ROWS : (i + 1) * ROWS] + p

    step("embedded")
    gain1, shift1, gain2, shift2 = (row_of(T_NORM, k) for k in range(4))

    for at_row, n in BLOCKS:
        r = pl.ds(at_row, n)
        a[r, :] = (stats(h[r, :], keep, r, 0) * gain1 + shift1).astype(BF16)

    step("qkv")
    def wide_cols(start, c, groups, j):
        return jnp.concatenate([cols(start, c, groups, 3 * j + k) for k in range(3)], axis=1)

    def wide_lanes(j):
        return pl.ds(pl.multiple_of(j * D, D), D)

    def mix_block(j, carry):
        mix[:, wide_lanes(j)] = dot(a[...], wide_cols(T_QKV, 18, 48, j)).astype(BF16)
        return carry

    lax.fori_loop(0, 3, mix_block, 0)

    first_half = lax.broadcasted_iota(jnp.int32, (ROWS, 128), 1) < HEAD_DIM
    key_ok = lax.broadcasted_iota(jnp.int32, (ROWS, ROWS), 0) < P_SIZE
    first_rows = lax.broadcasted_iota(jnp.int32, (128, ROWS), 0) < HEAD_DIM
    halves = (first_half, jnp.logical_not(first_half))
    zero = jnp.zeros((ROWS, 128), BF16)

    def split(block):
        return jnp.concatenate([jnp.where(first_half, block, zero), jnp.where(first_half, zero, block)], axis=0)

    def heads_of(p, i):
        r = pl.ds(i * ROWS, ROWS)
        return r, [pl.ds(pl.multiple_of(p * 128 + D * k, 128), 128) for k in range(3)]

    def attend(p, carry):
        for i in range(2):
            r, ls = heads_of(p, i)
            q, k, v = (mix[r, l] for l in ls)
            q = q * jnp.asarray(0.125, BF16)
            vt = v.T
            outs = []
            for e in range(2):
                s = dot_t(jnp.where(halves[e], k, zero), q)
                s = jnp.where(key_ok, s, -jnp.inf)
                ex = jnp.exp(s - jnp.max(s, 0, keepdims=True))
                pr = (ex * (1.0 / jnp.sum(ex, 0, keepdims=True))).astype(BF16)
                prob[p * 2 + i, e] = pr
                outs.append(dot(vt, pr))
            o[r, ls[0]] = jnp.where(first_rows, outs[0], outs[1]).astype(BF16).T
        return carry

    parts = ((0, 2), (2, 3), (3, 5), (5, 6))
    for part in range(4):
        step("attend%d" % part)
        lax.fori_loop(*parts[part], attend, 0)
    step("attended")
    for j in range(3):
        h1[:, pl.ds(j * BLK, BLK)] = h[:, pl.ds(j * BLK, BLK)] + dot(o[...], cols(T_OUT, 6, 48, j))

    for at_row, n in BLOCKS:
        r = pl.ds(at_row, n)
        a2[r, :] = (stats(h1[r, :], keep, r, 2) * gain2 + shift2).astype(BF16)

    step("up")
    def up_block(j, carry):
        u = dot(a2[...], wide_cols(T_IN, 24, 48, j))
        phi = 0.5 * (1.0 + lax.erf(u * ROOT_HALF))
        pdf = jnp.exp(-0.5 * u * u) * INV_ROOT_TWO_PI
        hid[:, wide_lanes(j)] = (u * phi).astype(BF16)
        slope[:, wide_lanes(j)] = (phi + u * pdf).astype(BF16)
        return carry

    lax.fori_loop(0, 4, up_block, 0)
    step("down")
    for j in range(3):
        h2[:, pl.ds(j * BLK, BLK)] = h1[:, pl.ds(j * BLK, BLK)] + dot(hid[...], cols(T_FO, 6, 192, j))

    step("pool")
    gain_end, shift_end = (row_of(T_POS + 72, 4 + k) for k in range(2))
    means = []
    last_rows = lax.broadcasted_iota(jnp.int32, (112, D), 0) < P_SIZE - 96
    for i in range(2):
        total = jnp.zeros((8, D), F32)
        for at_row, n in BLOCKS[2 * i : 2 * i + 2]:
            r = pl.ds(at_row, n)
            hat = stats(h2[r, :], keep, r, 4)
            if n == 112:
                hat = jnp.where(last_rows, hat, 0.0)
            total = total + jnp.sum(hat.reshape(n // 8, 8, D), 0)
        means.append(jnp.sum(total, 0, keepdims=True) * (1.0 / P_SIZE))
    mean_hat = jnp.concatenate(means + [jnp.zeros((14, D), F32)], axis=0)
    two = lax.broadcasted_iota(jnp.int32, (16, D), 0) < 2
    pooled = jnp.where(two, mean_hat * gain_end + shift_end, 0.0).astype(BF16)
    logits = jnp.concatenate([dot(pooled, cols(T_HEAD, 8, 48, j)) for j in range(4)], axis=1)
    lane = lax.broadcasted_iota(jnp.int32, (16, 1024), 1)
    lane_f = lane.astype(F32)
    inside = lane < CLS
    logits = jnp.where(inside, logits, -1e30)
    top = jnp.max(logits, -1, keepdims=True)
    total = jnp.sum(jnp.where(inside, jnp.exp(logits - top), 0.0), -1, keepdims=True)
    logp = logits - top - jnp.log(total)
    meta = meta_ref[...]
    pad14 = jnp.zeros((14, 1), F32)
    label = jnp.concatenate([meta[0:2, 0:1], pad14], axis=0)
    scale = jnp.concatenate([meta[2:4, 0:1], pad14], axis=0)
    valid = jnp.concatenate([meta[4:6, 0:1], pad14], axis=0)
    target = jnp.where(lane_f == label, 1.0 - SMOOTHING, 0.0) + SMOOTHING / CLS
    values = -jnp.sum(jnp.where(inside, target * logp, 0.0), -1, keepdims=True)
    loss_ref[...] = jnp.broadcast_to(jnp.sum(values * valid, 0, keepdims=True), (8, 128))
    d_logits = jnp.where(inside, scale * (jnp.exp(logp) - target), 0.0).astype(BF16)
    d_pooled = jnp.zeros((16, D), F32)
    for j in range(4):
        w = cols(T_HEAD, 8, 48, j)
        d_pooled = d_pooled + dot_t(d_logits[:, j * BLK : (j + 1) * BLK], w)
        put_cols(T_HEAD, 8, 48, j, t_dot(pooled, d_logits[:, j * BLK : (j + 1) * BLK]))
    d_gain_end = jnp.sum(d_pooled * mean_hat, 0, keepdims=True)
    d_shift_end = jnp.sum(d_pooled, 0, keepdims=True)
    for i in range(2):
        d_hat = d_pooled[i : i + 1, :] * (1.0 / P_SIZE) * gain_end

        m1 = jnp.sum(d_hat, -1, keepdims=True) * (1.0 / D)
        for at_row, n in BLOCKS[2 * i : 2 * i + 2]:
            r = pl.ds(at_row, n)
            hat, rstd = kept(h2[r, :], keep, r, 4)
            m2 = jnp.sum(d_hat * hat, -1, keepdims=True) * (1.0 / D)
            d = rstd * ((d_hat - m1) - hat * m2)
            if n == 112:
                d = jnp.where(last_rows, d, 0.0)
            dh[r, :] = d
            dyb[r, :] = d.astype(BF16)

    step("backward")
    at[...] = a2[...].T
    da = h2

    wide = D // 16

    def down_block(j, carry):
        part = section(T, T_FO + j * wide * 6, 6, wide)
        w = jnp.concatenate([part[:, k].reshape(D, 128) for k in range(6)], axis=1)
        dy = dyb[...]
        d_w = t_dot(hid[:, wide_lanes(j)], dy).astype(BF16)
        hid[:, wide_lanes(j)] = (dot_t(dy, w) * slope[:, wide_lanes(j)].astype(F32)).astype(BF16)
        for k in range(6):
            part[:, k] = d_w[:, k * 128 : (k + 1) * 128].reshape(wide, 16, 128)
        return carry

    G[pl.ds(4212, 12)] = jnp.zeros((12, 16, 128), BF16)
    lax.fori_loop(0, 3, down_block, 0)
    step("fc_out0")
    lax.fori_loop(3, 4, down_block, 0)
    step("fc_out1")
    def row_block(start, c, j):
        part = section(T, start + j * 16 * c, c, 16)
        return jnp.concatenate([part[:, k].reshape(BLK, 128) for k in range(c)], axis=1)

    def put_rows(start, c, j, first, value):
        part = section(G, start + j * 16 * c, c, 16)
        low = value.astype(BF16)
        for k in range(value.shape[1] // 128):
            part[:, first + k] = low[:, k * 128 : (k + 1) * 128].reshape(16, 16, 128)

    for j in range(3):
        da[:, pl.ds(j * BLK, BLK)] = dot_t(hid[...], row_block(T_IN, 24, j))
    step("fc_in0")
    for j in range(3):
        for k in range(4):
            put_rows(T_IN, 24, j, 6 * k, dot(at[pl.ds(j * BLK, BLK), :], hid[:, pl.ds(k * D, D)]))
        step("fc_in%d" % (j + 1))

    def norm_grads(inputs, column, gain):
        dg, ds = jnp.zeros((8, D), F32), jnp.zeros((8, D), F32)
        for at_row, n in BLOCKS:
            r = pl.ds(at_row, n)
            hat, rstd = kept(inputs[r, :], keep, r, column)
            d = da[r, :]
            new = dh[r, :] + norm_back(d * gain, hat, rstd)
            dh[r, :] = new
            dyb[r, :] = new.astype(BF16)
            dg = dg + jnp.sum((d * hat).reshape(n // 8, 8, D), 0)
            ds = ds + jnp.sum(d.reshape(n // 8, 8, D), 0)
        return dg, ds

    d_gain2, d_shift2 = norm_grads(h1, 2, gain2)

    step("normed2")
    at[...] = o[...].T
    for j in range(3):
        o[:, pl.ds(j * BLK, BLK)] = dot_t(dyb[...], row_block(T_OUT, 6, j)).astype(BF16)
    for j in range(3):
        put_rows(T_OUT, 6, j, 0, dot(at[pl.ds(j * BLK, BLK), :], dyb[...]))

    step("out")
    def attend_back(p, carry):
        for i in range(2):
            r, ls = heads_of(p, i)
            q, k, v = (mix[r, l] for l in ls)
            q = q * jnp.asarray(0.125, BF16)
            k8 = k * jnp.asarray(0.125, BF16)
            kt = k8.T
            do = o[r, ls[0]]
            pr = prob[p * 2 + i]
            dv = dot(pr.reshape(TOK, ROWS), do)
            dp = dot_t(split(v), do).reshape(2, ROWS, ROWS)
            prf = pr.astype(F32)
            row = jnp.sum(prf * dp, 1, keepdims=True)
            ds = (prf * (dp - row)).astype(BF16)
            dq = [dot(kt[HEAD_DIM * e : HEAD_DIM * (e + 1)], ds[e]) for e in range(2)]
            dk = dot(ds.reshape(TOK, ROWS), q)
            dmix[r, ls[0]] = jnp.concatenate(dq, axis=0).astype(BF16).T
            dmix[r, ls[1]] = jnp.where(first_half, dk[:ROWS], dk[ROWS:]).astype(BF16)
            dmix[r, ls[2]] = jnp.where(first_half, dv[:ROWS], dv[ROWS:]).astype(BF16)
        return carry

    for part in range(4):
        lax.fori_loop(*parts[part], attend_back, 0)
        step("back%d" % part)

    at[...] = a[...].T
    for j in range(3):
        da[:, pl.ds(j * BLK, BLK)] = dot_t(dmix[...], row_block(T_QKV, 18, j))
    for j in range(3):
        for k in range(3):
            put_rows(T_QKV, 18, j, 6 * k, dot(at[pl.ds(j * BLK, BLK), :], dmix[:, pl.ds(k * D, D)]))
    step("qkv_back")
    d_gain1, d_shift1 = norm_grads(h, 0, gain1)
    d_norms = jnp.concatenate([jnp.sum(d, 0, keepdims=True) for d in (d_gain1, d_shift1, d_gain2, d_shift2)] + [jnp.zeros((12, D), F32)], axis=0).astype(BF16)
    for j in range(6):
        G[T_NORM + j] = d_norms[:, j * 128 : (j + 1) * 128]
    step("norms")
    at[...] = x[...].T
    row_id = lax.broadcasted_iota(jnp.int32, (ROWS, BLK), 0)
    for j in range(3):
        put_cols(T_E, 6, 48, j, dot(at[...], dyb[:, pl.ds(j * BLK, BLK)]))
        c = pl.ds(j * BLK, BLK)
        s = slice(j * BLK, (j + 1) * BLK)
        d_pos = dh[pl.ds(0, ROWS), c] + dh[pl.ds(ROWS, ROWS), c]
        d_pos = jnp.where(row_id < P_SIZE, d_pos, 0.0)
        d_pos = jnp.where(row_id == P_SIZE, jnp.broadcast_to(d_gain_end[:, s], (ROWS, BLK)), d_pos)
        d_pos = jnp.where(row_id == P_SIZE + 1, jnp.broadcast_to(d_shift_end[:, s], (ROWS, BLK)), d_pos)
        put_cols(T_POS, 6, 13, j, d_pos)
    step("embed")


FORWARD = {
    "start": (
        (1, 0), (3, 0), (1, 1), (0, 0), (2, 0), (1, 2), (0, 1), (0, 2), (2, 1), (1, 3), (2, 2), (1, 4),
        (0, 3), (3, 1), (2, 3), (3, 2), (0, 4), (1, 5), (0, 6),
    ),
    "qkv": ((1, 6), (2, 4),),
    "attend0": ((3, 3),),
    "attend1": ((2, 5),),
    "attend2": ((3, 4),),
    "attend3": ((2, 6),),
    "up": ((3, 5),),
    "down": ((3, 6),),
}
BACKWARD = {
    "fc_out1": ((3, 0, 0), (3, 1, 0),),
    "fc_in3": ((3, 1, 1), (2, 0, 0), (2, 1, 0), (3, 0, 1),),
    "back0": ((2, 1, 1), (2, 0, 1),),
    "back3": ((3, 1, 2), (3, 0, 2),),
    "qkv_back": ((1, 0, 0), (2, 1, 2),),
    "norms": ((0, 1, 0), (1, 1, 0), (2, 0, 2),),
    "embed": (
        (3, 0, 3), (1, 0, 1), (0, 1, 1), (1, 1, 1), (0, 0, 0), (0, 0, 1), (1, 0, 2), (3, 1, 3), (0, 1, 2), (2, 0, 3), (1, 1, 2), (0, 0, 2),
        (0, 1, 3), (2, 1, 3), (1, 0, 3), (1, 1, 3), (0, 0, 3), (3, 0, 4), (3, 1, 4), (2, 1, 4), (2, 0, 4), (0, 1, 4), (1, 0, 4), (1, 1, 4),
        (0, 0, 4), (3, 1, 5), (1, 0, 5), (2, 1, 5), (2, 0, 5), (3, 0, 5), (0, 1, 5), (0, 0, 5), (1, 1, 5),
    ),
}


def grads_kernel(w_ref, patch_ref, labels_ref, counts_ref, red_ref, loss_out, T, R, RA, RB, g_send, g_recv, r_send, r_recv, LS, l_send, l_recv, patch_in, meta_in, meta, loss, *rest):
    gather_refs, compute_refs, out_sem = rest[:12], rest[12:-1], rest[-1]
    links = Links(T, R, RA, RB, g_send, g_recv, r_send, r_recv)
    xl, b, z, a, y = links.xl, links.b, links.z, links.a, links.y
    swap = a != b
    mirror = device(xl, b, a, z, y)
    units_here, finish_start = start_gather(links, w_ref, patch_ref, labels_ref, counts_ref, T, patch_in, meta_in, meta, *gather_refs)

    def loss_send(src, dst, target):
        links.go(LS.at[src], LS.at[dst], l_send.at[dst], l_recv.at[dst], target)

    def loss_wait(*slots):
        for k in slots:
            links.landed(LS.at[k], l_send.at[k], l_recv.at[k])

    def loss_step(n):
        if n == 0:
            LS[0] = loss[...]
            loss_send(0, 1, links.sibling)
        elif n == 1:
            loss_wait(1)
            LS[8] = LS[0] + LS[1]
            loss_send(8, 2, links.at_y(1))
            loss_send(8, 3, links.at_y(3))
        elif n == 2:
            loss_wait(2, 3)
            loss_send(2, 4, links.at_y(1))
        elif n == 3:
            loss_wait(4)
            LS[9] = (LS[8] + LS[4]) + (LS[2] + LS[3])
            loss_send(9, 5, links.at_z(1))
            loss_send(9, 6, links.at_z(3))
        elif n == 4:
            loss_wait(5, 6)
            loss_send(5, 7, links.at_z(1))
        elif n == 5:
            loss_wait(7)
            LS[10] = (LS[9] + LS[7]) + (LS[5] + LS[6])

            @pl.when(swap)
            def _():
                loss_swap.start()

        else:

            @pl.when(swap)
            def _():
                loss_swap.wait()
                loss_out[...] = LS[11]

            @pl.when(jnp.logical_not(swap))
            def _():
                loss_out[...] = LS[10]

    loss_swap = pltpu.make_async_remote_copy(src_ref=LS.at[10], dst_ref=LS.at[11], send_sem=l_send.at[11], recv_sem=l_recv.at[11], device_id=mirror, device_id_type=MESH)
    losses = {"fc_out0": 0, "fc_in2": 1, "out": 2, "back1": 3, "back3": 4, "norms": 5}

    def step(name):
        if name == "pool":
            links.sent()
        for item in FORWARD.get(name, ()):
            if item[1] == 0:
                units_here(item[0])
            links.gather_step(*item)
        if name == "start":
            finish_start()
        for item in BACKWARD.get(name, ()):
            links.reduce_step(*item)
        if name in losses:
            loss_step(losses[name])

    compute(step, patch_in, meta_in, loss, T, *compute_refs)
    loss_step(6)
    mine = T.reshape(ROUNDS, 32, UNIT, 16, 128).at[:, z * 8 + b * 4 + y]
    out = pltpu.make_async_copy(mine, red_ref, out_sem)
    out.start()
    links.sent()
    out.wait()


def grads(weights, patches, labels, counts):
    hbm = pl.BlockSpec(memory_space=pl.ANY)
    vmem = pl.BlockSpec(memory_space=pltpu.VMEM)
    V = pltpu.VMEM
    dma = pltpu.SemaphoreType.DMA
    return pl.pallas_call(
        grads_kernel,
        out_shape=(jax.ShapeDtypeStruct((ROUNDS, UNIT, 16, 128), BF16), jax.ShapeDtypeStruct((8, 128), F32)),
        in_specs=[hbm] * 2 + [pl.BlockSpec(memory_space=pltpu.SMEM)] * 2,
        out_specs=(hbm, vmem),
        scratch_shapes=[
            V((NTILES, 16, 128), BF16),
            V((ROUNDS, 4, 4, UNIT, 16, 128), BF16),
            V((6, ROUNDS, 2, UNIT, 16, 128), BF16),
            V((6, ROUNDS, 3, 16, 128), BF16),
            dma((192,)),
            dma((192,)),
            dma((104,)),
            dma((104,)),
            V((12, 8, 128), F32),
            dma((12,)),
            dma((12,)),
            V(patches.shape, BF16),
            V((8, 128), F32),
            V((8, 128), F32),
            V((8, 128), F32),
            V((FROWS, 128), F32),
            V((128, 128), F32),
            V((LO, 128), BF16),
            V((HI, 128), BF16),
            V((HI, 128), BF16),
            V((LO, 128), BF16),
            V((SLOT, 16, 128), BF16),
            dma((4,)),
            dma((4,)),
            dma((4,)),
            dma((ROUNDS,)),
            dma((ROUNDS,)),
            V((TOK, D), BF16),
            V((TOK, D), F32),
            V((TOK, D), BF16),
            V((D, TOK), BF16),
            V((TOK, 3 * D), BF16),
            V((12, 2, ROWS, ROWS), BF16),
            V((TOK, D), BF16),
            V((TOK, D), F32),
            V((TOK, D), BF16),
            V((TOK, FF), BF16),
            V((TOK, FF), BF16),
            V((TOK, D), F32),
            V((TOK, D), F32),
            V((TOK, D), BF16),
            V((TOK, 128), F32),
            dma,
        ],
        compiler_params=pltpu.CompilerParams(collective_id=0, has_side_effects=True, vmem_limit_bytes=60 * 1024 * 1024),
        name="grads",
    )(weights, patches, labels, counts)


EDGE = 24
FRONT = 768
BACK_ROWS = FRONT + SHARD + 640 + 6
PADDED = 2112
STEP = 10
EDGE_UNITS = 4
WINDOW = ROUNDS + 2 * EDGE_UNITS
BETA_ONE = 0.9
BETA_TWO = 0.95
ADAM_EPS = 1e-08
DECAY = 0.05
INNER_RATE = 0.01
OUTER_RATE = 0.7
OUTER_MU = 0.9


def update_kernel(
    red_ref, first_ref, second_ref,
    sum_out, first_out, second_out,
    red, window, flat, headrows, first_row, second_row, first, second, low, low2, pair, pair2, total, total2,
    load_sem, x_send, x_recv, o_send, e_send, w_recv,
):
    xl, b, z, a, y = coords()
    fs = z * 8 + a * 4 + y
    holder = z * 8 + b * 4 + y
    sibling = device(xl, a, 1 - b, z, y)
    across = device(1 - xl, a, b, z, y)
    extra = [pltpu.make_async_copy(src, dst, load_sem.at[i]) for i, (src, dst) in enumerate(((first_ref, first_row), (second_ref, second_row)))]
    load = pltpu.make_async_copy(red_ref, red, load_sem.at[4])
    load.start()
    for copy in extra:
        copy.start()

    barrier = pltpu.get_barrier_semaphore()

    def greet(target):
        pl.semaphore_signal(barrier, inc=1, device_id=target, device_id_type=MESH)

    greet(sibling)
    greet(across)
    first_unit = ROUNDS * fs - EDGE_UNITS

    def window_unit(p):
        k = first_unit + p
        d = lax.rem(k + 32, 32)
        inside = jnp.logical_and(k >= 0, k < 32 * ROUNDS)
        mine = jnp.logical_and(a == b, d == holder)
        return inside, mine, device(xl, b, lax.rem(lax.div(d, 4), 2), lax.div(d, 8), lax.rem(d, 4))

    def greet_holder(p, carry):
        inside, mine, source = window_unit(p)

        @pl.when(jnp.logical_and(inside, jnp.logical_not(mine)))
        def _():
            greet(source)

        return carry

    lax.fori_loop(0, WINDOW, greet_holder, 0)

    def held_unit(j):
        k = 32 * j + holder
        q = lax.div(k, ROUNDS)
        r = lax.rem(k, ROUNDS)
        shift = jnp.where(r < EDGE_UNITS, -1, jnp.where(r >= ROUNDS - EDGE_UNITS, 1, 0))
        near = jnp.logical_and(shift != 0, jnp.logical_and(q + shift >= 0, q + shift < NSLOT))
        return k, q, jnp.where(near, q + shift, q), near

    def to_owner(j, k, s, send):
        p = k - (ROUNDS * s - EDGE_UNITS)
        src = red.at[j]
        dst = window.at[pl.ds(UNIT * p, UNIT)]
        sa = lax.rem(lax.div(s, 4), 2)
        mine = jnp.logical_and(a == b, s == fs)
        target = device(xl, sa, a, lax.div(s, 8), lax.rem(s, 4))
        away = pltpu.make_async_remote_copy(src_ref=src, dst_ref=dst, send_sem=send.at[j], recv_sem=w_recv.at[p], device_id=target, device_id_type=MESH)
        here = pltpu.make_async_copy(src, dst, load_sem.at[10])
        return mine, away, here

    def count(j, n):
        k, q, s, near = held_unit(j)
        first_away = jnp.logical_not(jnp.logical_and(a == b, q == fs))
        second_away = jnp.logical_and(near, jnp.logical_not(jnp.logical_and(a == b, s == fs)))
        return n + jnp.where(first_away, 1, 0) + jnp.where(second_away, 1, 0)

    outgoing = lax.fori_loop(0, ROUNDS, count, 2)
    pl.semaphore_wait(barrier, outgoing)
    load.wait()

    def give(j, carry):
        k, q, s, near = held_unit(j)
        mine, away, here = to_owner(j, k, q, o_send)

        @pl.when(mine)
        def _():
            here.start()

        @pl.when(jnp.logical_not(mine))
        def _():
            away.start()

        mine2, away2, here2 = to_owner(j, k, s, e_send)

        @pl.when(jnp.logical_and(near, mine2))
        def _():
            here2.start()

        @pl.when(jnp.logical_and(near, jnp.logical_not(mine2)))
        def _():
            away2.start()

        return carry

    lax.fori_loop(0, ROUNDS, give, 0)

    def given(j, carry):
        k, q, s, near = held_unit(j)
        mine, away, here = to_owner(j, k, q, o_send)

        @pl.when(jnp.logical_not(mine))
        def _():
            away.wait_send()

        mine2, away2, here2 = to_owner(j, k, s, e_send)

        @pl.when(jnp.logical_and(near, jnp.logical_not(mine2)))
        def _():
            away2.wait_send()

        return carry

    def clear(i, carry):
        flat[pl.ds(pl.multiple_of(i * 32, 32), 32), :] = jnp.zeros((32, 128), F32)
        return carry

    lax.fori_loop(0, BACK_ROWS // 32, clear, 0)

    for copy in extra:
        copy.wait()
    for source, rows_of in ((first_row, first), (second_row, second)):

        def eight(i, carry):
            rows_of[pl.ds(pl.multiple_of(i * 8, 8), 8), :] = source[0, pl.ds(pl.multiple_of(i * 1024, 1024), 1024)].reshape(8, 128)
            return carry

        whole = SHARD // 8
        lax.fori_loop(0, whole, eight, 0, unroll=2)
        rows_of[pl.ds(whole * 8, SHARD - whole * 8), :] = source[0, pl.ds(whole * 1024, (SHARD - whole * 8) * 128)].reshape(SHARD - whole * 8, 128)

    def got(p, carry):
        inside, mine, source = window_unit(p)
        place = window.at[pl.ds(UNIT * p, UNIT)]

        @pl.when(jnp.logical_and(inside, mine))
        def _():
            pltpu.make_async_copy(place, place, load_sem.at[10]).wait()

        @pl.when(jnp.logical_and(inside, jnp.logical_not(mine)))
        def _():
            pltpu.make_async_remote_copy(src_ref=place, dst_ref=place, send_sem=x_send.at[0], recv_sem=w_recv.at[p], device_id=sibling, device_id_type=MESH).wait_recv()

        return carry

    lax.fori_loop(0, WINDOW, got, 0)
    sends = []

    def go(src, dst, send, recv, k, target):
        copy = pltpu.make_async_remote_copy(src_ref=src, dst_ref=dst, send_sem=send.at[k], recv_sem=recv.at[k], device_id=target, device_id_type=MESH)
        copy.start()
        sends.append(copy)

    def arrive(dst, recv, k):
        pltpu.make_async_remote_copy(src_ref=dst, dst_ref=dst, send_sem=x_send.at[k], recv_sem=recv.at[k], device_id=sibling, device_id_type=MESH).wait_recv()

    low_tile = SLOT * fs - EDGE
    high_tile = SLOT * fs + SLOT + EDGE
    origin = SHARD * fs - FRONT
    for index, (base, c, groups, per, start) in enumerate(SECTIONS):
        if index == 1:
            lane = lax.broadcasted_iota(jnp.int32, (8, 128), 1)
            g0 = lax.div(jnp.maximum(SHARD * fs - base, 0), per)
            g1 = lax.div(jnp.maximum(SHARD * (fs + 1) - base, 0) + per - 1, per)

            def head_group(g, carry):
                t = start + g * 8 - low_tile
                for j in range(8):
                    headrows[pl.ds(j, 16, stride=8), :] = window[t + j].astype(F32)
                row = base + per * g - origin
                for i in range(16):
                    q, s = divmod(1000 * i, 128)
                    value = headrows[pl.ds(i * 8, 8), :]
                    if s:
                        value = pltpu.roll(value, s, 1)
                        flat[pl.ds(row + q, 8), :] += jnp.where(lane >= s, value, 0.0)
                        flat[pl.ds(row + q + 1, 8), :] += jnp.where(lane < s, value, 0.0)
                    else:
                        flat[pl.ds(row + q, 8), :] += value
                return carry

            lax.fori_loop(jnp.minimum(g0, groups), jnp.minimum(g1, groups), head_group, 0)
        else:

            def unit(n, carry):
                t = UNIT * n - start
                row = base + 16 * c * lax.div(t, c) + lax.rem(t, c) - origin
                for m in range(UNIT):
                    flat[pl.ds(row + m, 16, stride=c), :] = window[UNIT * n - low_tile + m].astype(F32)
                return carry

            lax.fori_loop(lax.div(jnp.maximum(low_tile, start), UNIT), lax.div(jnp.minimum(high_tile, start + c * groups), UNIT), unit, 0)

    fix_one = 1.0 / (1.0 - BETA_ONE**STEP)
    fix_two = 1.0 / (1.0 - BETA_TWO**STEP)

    half = PADDED // 2
    step = 96
    for rows_of in (first, second):
        rows_of[pl.ds(SHARD, PADDED - SHARD), :] = jnp.zeros((PADDED - SHARD, 128), F32)

    def in_half(fn):
        def rows_step(i, carry):
            fn(pl.multiple_of(i * step, step), step)
            return carry

        lax.fori_loop(0, half // step, rows_step, 0)

    def adam_half(q):
        def adam(r, n):
            at = pl.ds(pl.multiple_of(q * half + r, 16), n)
            grad = flat[pl.ds(pl.multiple_of(FRONT + q * half + r, 16), n), :]
            m = BETA_ONE * first[at, :] + (1.0 - BETA_ONE) * grad
            s = BETA_TWO * second[at, :] + (1.0 - BETA_TWO) * grad * grad
            first[at, :] = m
            second[at, :] = s
            low[at, :] = ((m * fix_one) / (jnp.sqrt(s * fix_two) + ADAM_EPS)).astype(BF16)

        in_half(adam)

    adam_half(1 - b)
    go(low.at[pl.ds(pl.multiple_of((1 - b) * half, 16), half)], low2, x_send, x_recv, 0, sibling)
    adam_half(b)
    outs = [pltpu.make_async_copy(src.at[pl.ds(0, SHARD)], dst, load_sem.at[5 + i]) for i, (src, dst) in enumerate(((first, first_out), (second, second_out)))]
    for copy in outs:
        copy.start()
    arrive(low2, x_recv, 0)

    def pairs(r, n):
        pair[pl.ds(r, n), :] = low[pl.ds(pl.multiple_of(b * half + r, 16), n), :] + low2[pl.ds(r, n), :]

    in_half(pairs)
    go(pair, pair2, x_send, x_recv, 1, across)
    arrive(pair2, x_recv, 1)

    def fours(r, n):
        total[pl.ds(r, n), :] = pair[pl.ds(r, n), :].astype(F32) + pair2[pl.ds(r, n), :].astype(F32)

    in_half(fours)
    go(total, total2, x_send, x_recv, 2, sibling)

    arrive(total2, x_recv, 2)
    other = half - b * half
    final = [(total, sum_out.at[pl.ds(pl.multiple_of(b * half, 16), half)]), (total2, sum_out.at[pl.ds(pl.multiple_of(other, 16), half)])]
    final = [pltpu.make_async_copy(src, dst, load_sem.at[7 + i]) for i, (src, dst) in enumerate(final)]
    for copy in final:
        copy.start()
    for copy in sends:
        copy.wait_send()
    lax.fori_loop(0, ROUNDS, given, 0)
    for copy in outs + final:
        copy.wait()


def update(red, first, second):
    hbm = pl.BlockSpec(memory_space=pl.ANY)
    V = pltpu.VMEM
    flat = jax.ShapeDtypeStruct((SHARD, 128), F32)
    dma = pltpu.SemaphoreType.DMA
    return pl.pallas_call(
        update_kernel,
        out_shape=(jax.ShapeDtypeStruct((PADDED, 128), F32), flat, flat),
        in_specs=[hbm] * 3,
        out_specs=(hbm,) * 3,
        scratch_shapes=[
            V((ROUNDS, UNIT, 16, 128), BF16),
            V((EDGE + SLOT + EDGE, 16, 128), BF16),
            V((BACK_ROWS, 128), F32),
            V((128, 128), F32),
            V((1, SHARD * 128), F32),
            V((1, SHARD * 128), F32),
            V((PADDED, 128), F32),
            V((PADDED, 128), F32),
            V((PADDED, 128), BF16),
            V((PADDED // 2, 128), BF16),
            V((PADDED // 2, 128), BF16),
            V((PADDED // 2, 128), BF16),
            V((PADDED // 2, 128), F32),
            V((PADDED // 2, 128), F32),
            dma((11,)),
            dma((3,)),
            dma((3,)),
            dma((ROUNDS,)),
            dma((ROUNDS,)),
            dma((WINDOW,)),
        ],
        compiler_params=pltpu.CompilerParams(collective_id=1, has_side_effects=True, vmem_limit_bytes=60 * 1024 * 1024),
        name="update",
    )(red, first, second)


def finish_kernel(
    sum_ref, w_ref, mom_ref, first_ref, second_ref, loss_ref,
    avg_out, mom_out, new_out, first_out, second_out, loss_out,
    total, w, mom, first, second, averaged, sem, out_sem,
):
    cut = PADDED // 2
    pieces = [pl.ds(0, cut), pl.ds(cut, SHARD - cut)]
    loads = []
    for i, at in enumerate(pieces):
        loads.append([pltpu.make_async_copy(src.at[at], dst.at[at], sem.at[3 * i + k]) for k, (src, dst) in enumerate(((sum_ref, total), (w_ref, w), (mom_ref, mom)))])
    moments = [pltpu.make_async_copy(src, dst, sem.at[6 + i]) for i, (src, dst) in enumerate(((first_ref, first), (second_ref, second)))]
    for copy in loads[0] + loads[1] + moments:
        copy.start()
    outs = []

    def send(src, dst):
        copy = pltpu.make_async_copy(src, dst, out_sem.at[len(outs)])
        copy.start()
        outs.append(copy)

    loss_out[...] = loss_ref[0:1, 0:1]

    def outer(r, n):
        at = pl.ds(r, n)
        old = w[at, :]
        mean = INNER_RATE * (total[at, :] * 0.25 + DECAY * old)
        momentum = OUTER_MU * mom[at, :] + mean
        averaged[at, :] = mean
        mom[at, :] = momentum
        w[at, :] = old - OUTER_RATE * (mean + OUTER_MU * momentum)

    def block(i, carry):
        outer(pl.multiple_of(i * 96, 96), 96)
        return carry

    for i, at in enumerate(pieces):
        for copy in loads[i]:
            copy.wait()
        if i == 0:
            lax.fori_loop(0, cut // 96, block, 0)
        else:
            lax.fori_loop(cut // 96, SHARD // 96, block, 0)
            outer(SHARD // 96 * 96, SHARD - SHARD // 96 * 96)
        for src, dst in ((averaged, avg_out), (mom, mom_out), (w, new_out)):
            send(src.at[at], dst.at[at])
        if i == 0:
            for copy, src, dst in zip(moments, (first, second), (first_out, second_out)):
                copy.wait()
                send(src, dst.reshape(SHARD, 128))
    for copy in outs:
        copy.wait()


def finish(total, weights, momentum, first, second, loss):
    hbm = pl.BlockSpec(memory_space=pl.ANY)
    vmem = pl.BlockSpec(memory_space=pltpu.VMEM)
    V = pltpu.VMEM
    rows = jax.ShapeDtypeStruct((SHARD, 128), F32)
    row = jax.ShapeDtypeStruct((1, SHARD * 128), F32)
    return pl.pallas_call(
        finish_kernel,
        out_shape=(rows,) * 3 + (row,) * 2 + (jax.ShapeDtypeStruct((1, 1), F32),),
        in_specs=[hbm] * 5 + [vmem],
        out_specs=(hbm,) * 5 + (vmem,),
        scratch_shapes=[V((PADDED, 128), F32)] + [V((SHARD, 128), F32)] * 5 + [pltpu.SemaphoreType.DMA((8,)), pltpu.SemaphoreType.DMA((8,))],
        compiler_params=pltpu.CompilerParams(vmem_limit_bytes=60 * 1024 * 1024),
        name="finish",
    )(total, weights, momentum, first, second, loss)


def body(patches, labels, counts, weights, first_moments, second_moments, outer_momentum):
    flat = weights.reshape(SHARD, 128)
    reduced, loss = grads(flat, patches.reshape(2, P_SIZE, D), labels.reshape(2), counts.reshape(2))
    total, first, second = update(reduced, first_moments, second_moments)
    averaged, momentum, new_weights, first, second, loss = finish(total, flat, outer_momentum.reshape(SHARD, 128), first, second, loss)
    return (
        averaged.reshape(-1),
        momentum.reshape(-1),
        new_weights.reshape(-1),
        first,
        second,
        loss,
    )


def solution(mesh):
    placed = (
        P("rep", None, None, "fsdp", None, None),
        P("rep", None, None, "fsdp"),
        P("rep", None, None),
        P("fsdp"),
        P("rep", "fsdp"),
        P("rep", "fsdp"),
        P("fsdp"),
    )
    return jax.shard_map(
        body,
        mesh=mesh,
        in_specs=placed,
        out_specs=(
            P("fsdp"),
            P("fsdp"),
            P("fsdp"),
            P("rep", "fsdp"),
            P("rep", "fsdp"),
            P("rep", None),
        ),
        check_vma=False,
    )
```

```python
from functools import partial

import jax
import jax.numpy as jnp
from jax import lax
from jax.experimental import pallas as pl
from jax.experimental.pallas import tpu as pltpu
from jax.sharding import PartitionSpec as P

SHARD = 2098
SLOT = 132
HALF = 66
QUART = 33
NSLOT = 32
ROUNDS = 22
UNIT = 6
STAGES = ((0, 4), (4, 10), (10, 16), (16, 22))
SECTIONS = []
_t = 0
for _base, _c, _g, _rpg in ((0, 6, 61, 96), (5796, 8, 48, 125), (11796, 6, 1, 96), (11820, 18, 48, 288), (25644, 6, 48, 96), (30252, 24, 48, 384), (48684, 6, 192, 96)):
    SECTIONS.append((_base, _c, _g, _rpg, _t))
    _t += _c * _g
NTILE = _t
HI = 352
LO = 224
MARGIN = 512
FROWS = 3072
HEAD_ROWS = 16
MESH = pl.DeviceIdType.MESH


def coords():
    rep = lax.axis_index("rep")
    fs = lax.axis_index("fsdp")
    return lax.div(rep, 2), lax.rem(rep, 2), lax.div(fs, 8), lax.rem(lax.div(fs, 4), 2), lax.rem(fs, 4)


def device(xl, xh, core, z, y):
    return {"rep": xl * 2 + core, "fsdp": z * 8 + xh * 4 + y}


def flat_device(xl, core, s):
    return device(xl, lax.rem(lax.div(s, 4), 2), core, lax.div(s, 8), lax.rem(s, 4))


class Links:

    def __init__(self, T, R, RA, RB, g_send, g_recv, r_send, r_recv):
        self.xl, self.b, self.z, self.a, self.y = coords()
        self.T5 = T.reshape(ROUNDS, 4, 2, 4, UNIT, 16, 128)
        self.R, self.RA, self.RB = R, RA, RB
        self.g_send, self.g_recv, self.r_send, self.r_recv = g_send, g_recv, r_send, r_recv
        self.pending = []
        self.sibling = device(self.xl, self.a, 1 - self.b, self.z, self.y)

    def at_y(self, k):
        return device(self.xl, self.a, self.b, self.z, lax.rem(self.y + k, 4))

    def at_z(self, k):
        return device(self.xl, self.a, self.b, lax.rem(self.z + k, 4), self.y)

    def at_x(self, k):
        a = lax.rem(self.a + (self.xl if k == 1 else 1 - self.xl), 2)
        return device(1 - self.xl, a, self.b, self.z, self.y)

    def go(self, src, dst, send, recv, target):
        copy = pltpu.make_async_remote_copy(src_ref=src, dst_ref=dst, send_sem=send, recv_sem=recv, device_id=target, device_id_type=MESH)
        copy.start()
        self.pending.append(copy)

    def landed(self, dst, send, recv):
        pltpu.make_async_remote_copy(src_ref=dst, dst_ref=dst, send_sem=send, recv_sem=recv, device_id=self.sibling, device_id_type=MESH).wait_recv()

    def sent(self):
        for copy in self.pending:
            copy.wait_send()
        self.pending = []

    def span(self, i, h):
        lo, hi = STAGES[i]
        n = (hi - lo) // 2
        return pl.ds(lo + h * n, n)

    def first_axis(self, h, k):
        return (self.at_y if h == 0 else self.at_z)(k)

    def second_axis(self, h, k):
        return (self.at_z if h == 0 else self.at_y)(k)

    def gathered(self, i, h):
        lo, hi = STAGES[i]
        n = (hi - lo) // 2
        if i == 0:
            return pl.ds(lo + h * n, n)
        return pl.ds(lo + h * n + self.xl, 2)

    def single(self, i, h, own):
        lo, hi = STAGES[i]
        parity = self.xl if own else 1 - self.xl
        return pl.ds(lo + h * ((hi - lo) // 2) + 2 * parity, 1)

    def one(self, i, h, k, q=None):
        rd = self.gathered(i, h)
        t = pl.ds(0, UNIT) if q is None else pl.ds(3 * q, 3)
        if h == 0:
            return self.T5.at[rd, self.z, self.b, lax.rem(self.y + k, 4), t]
        return self.T5.at[rd, lax.rem(self.z + k, 4), self.b, self.y, t]

    def row(self, rd, h, k, core=None, p=None):
        core = self.b if core is None else core
        t = pl.ds(0, 4) if p is None else pl.ds(2 * p, 2)
        if h == 0:
            return self.T5.at[rd, lax.rem(self.z + k, 4), core, t]
        return self.T5.at[rd, t, core, lax.rem(self.y + k, 4)]

    def gsem(self, i, h, k):
        n = (i * 2 + h) * 24 + k
        return self.g_send.at[n], self.g_recv.at[n]

    def gather_go(self, i, h, k, view, target):
        self.go(view, view, *self.gsem(i, h, k), target)

    def gather_wait(self, i, h, k, view):
        self.landed(view, *self.gsem(i, h, k))

    def share(self, i, h, m, k):
        self.gather_go(i, h, 8 + m, self.row(self.gathered(i, h), h, k), self.sibling)
        if i > 0:
            rd = self.single(i, h, True)
            self.gather_go(i, h, 12 + m, self.row(rd, h, k, p=0), self.at_x(1))
            self.gather_go(i, h, 16 + m, self.row(rd, h, k, p=1), self.at_x(3))

    def gather_step(self, i, step):
        for h in range(2):
            rd = self.gathered(i, h)
            if step == 0:
                self.gather_go(i, h, 0, self.one(i, h, 0), self.first_axis(h, 1))
                self.gather_go(i, h, 1, self.one(i, h, 0), self.first_axis(h, 3))
            elif step == 1:
                self.gather_wait(i, h, 0, self.one(i, h, 3))
                self.gather_go(i, h, 2, self.one(i, h, 3, 0), self.first_axis(h, 1))
                self.gather_wait(i, h, 1, self.one(i, h, 1))
                self.gather_go(i, h, 3, self.one(i, h, 1, 1), self.first_axis(h, 3))
            elif step == 2:
                self.gather_wait(i, h, 2, self.one(i, h, 2, 0))
                self.gather_wait(i, h, 3, self.one(i, h, 2, 1))
                self.gather_go(i, h, 4, self.row(rd, h, 0), self.second_axis(h, 1))
                self.gather_go(i, h, 5, self.row(rd, h, 0), self.second_axis(h, 3))
                self.share(i, h, 0, 0)
            elif step == 3:
                self.gather_wait(i, h, 4, self.row(rd, h, 3))
                self.gather_go(i, h, 6, self.row(rd, h, 3, p=0), self.second_axis(h, 1))
                self.share(i, h, 1, 3)
                self.gather_wait(i, h, 5, self.row(rd, h, 1))
                self.gather_go(i, h, 7, self.row(rd, h, 1, p=1), self.second_axis(h, 3))
                self.share(i, h, 2, 1)
            elif step == 4:
                self.gather_wait(i, h, 6, self.row(rd, h, 2, p=0))
                self.gather_wait(i, h, 7, self.row(rd, h, 2, p=1))
                self.share(i, h, 3, 2)
            elif step == 5:
                if i > 0:
                    other = self.single(i, h, False)
                    for m, k in enumerate((0, 3, 1, 2)):
                        self.gather_wait(i, h, 12 + m, self.row(other, h, k, p=0))
                        self.gather_wait(i, h, 16 + m, self.row(other, h, k, p=1))
                        self.gather_go(i, h, 20 + m, self.row(other, h, k), self.sibling)
            else:
                for m, k in enumerate((0, 3, 1, 2)):
                    self.gather_wait(i, h, 8 + m, self.row(rd, h, k, core=1 - self.b))
                    if i > 0:
                        self.gather_wait(i, h, 20 + m, self.row(self.single(i, h, False), h, k, core=1 - self.b))

    def rsem(self, i, h, k):
        n = (i * 2 + h) * 13 + k
        return self.r_send.at[n], self.r_recv.at[n]

    def cell(self, i, h, k, q):
        rd = self.span(i, h)
        t = pl.ds(3 * q, 3)
        if h == 0:
            return self.T5.at[rd, self.z, self.b, lax.rem(self.y + k, 4), t]
        return self.T5.at[rd, lax.rem(self.z + k, 4), self.b, self.y, t]

    def add(self, dst, *sources, inner=()):
        n = dst.shape[0]

        def one(r, carry):
            for k in range(inner) if inner else (None,):
                at = (r,) if k is None else (r, k)
                if len(sources) == 1:
                    dst[at] = dst[at] + sources[0][at]
                else:
                    total = dst[at].astype(jnp.float32)
                    for source in sources:
                        total = total + source[at].astype(jnp.float32)
                    dst[at] = total.astype(jnp.bfloat16)
            return carry

        lax.fori_loop(0, n, one, 0)

    def reduce_step(self, i, h, step):
        rd = self.span(i, h)
        T5 = self.T5

        def send_a(k, ka, p, shift):
            self.go(self.row(rd, h, ka, p=p), self.RA.at[k, rd], *self.rsem(i, h, 1 + k), self.second_axis(h, shift))

        def wait_a(k):
            self.landed(self.RA.at[k, rd], *self.rsem(i, h, 1 + k))

        def send_b(k, kb, q, shift):
            self.go(self.cell(i, h, kb, q), self.RB.at[k, rd], *self.rsem(i, h, 7 + k), self.first_axis(h, shift))

        def wait_b(k):
            self.landed(self.RB.at[k, rd], *self.rsem(i, h, 7 + k))

        if step == 0:
            self.go(T5.at[rd, :, 1 - self.b], self.R.at[rd], *self.rsem(i, h, 0), self.sibling)
        elif step == 1:
            self.landed(self.R.at[rd], *self.rsem(i, h, 0))
            mine, theirs = T5.at[rd, :, self.b], self.R.at[rd]
            n = mine.shape[0]

            def both(r, carry):
                q = lax.div(r, 4)
                w = lax.rem(r, 4)
                for k in range(4):
                    mine[q, w, k] = mine[q, w, k] + theirs[q, w, k]
                return carry

            lax.fori_loop(0, 4 * n, both, 0)
            send_a(0, 2, 0, 1)
            send_a(1, 2, 1, 3)
            send_a(2, 1, 1, 1)
            send_a(3, 3, 0, 3)
        elif step == 2:
            wait_a(0)
            self.add(self.row(rd, h, 1, p=0), self.RA.at[0, rd], inner=2)
            send_a(4, 1, 0, 1)
            wait_a(1)
            self.add(self.row(rd, h, 3, p=1), self.RA.at[1, rd], inner=2)
            send_a(5, 3, 1, 3)
        elif step == 3:
            for k in (2, 3, 4, 5):
                wait_a(k)
            self.add(self.row(rd, h, 0, p=0), self.RA.at[3, rd], self.RA.at[4, rd], inner=2)
            self.add(self.row(rd, h, 0, p=1), self.RA.at[2, rd], self.RA.at[5, rd], inner=2)
            send_b(0, 2, 0, 1)
            send_b(1, 2, 1, 3)
            send_b(2, 1, 1, 1)
            send_b(3, 3, 0, 3)
        elif step == 4:
            wait_b(0)
            self.add(self.cell(i, h, 1, 0), self.RB.at[0, rd])
            send_b(4, 1, 0, 1)
            wait_b(1)
            self.add(self.cell(i, h, 3, 1), self.RB.at[1, rd])
            send_b(5, 3, 1, 3)
        else:
            for k in (2, 3, 4, 5):
                wait_b(k)
            self.add(self.cell(i, h, 0, 0), self.RB.at[3, rd], self.RB.at[4, rd])
            self.add(self.cell(i, h, 0, 1), self.RB.at[2, rd], self.RB.at[5, rd])


def start_gather(links, w_ref, patch_ref, labels_ref, counts_ref, T, patch_in, meta_in, meta_ref, flat, headrows, lob, hib, rlo, rhi, slot, local_sem, x_send, x_recv, u_send, u_recv):
    xl, b, z, a, y = links.xl, links.b, links.z, links.a, links.y
    fs = z * 8 + a * 4 + y
    swap = a != b
    xo = lax.rem(xl + a + b, 2)
    holder = z * 8 + b * 4 + y
    up = flat_device(xl, b, lax.rem(fs + 1, NSLOT))
    down = flat_device(xl, b, lax.rem(fs + NSLOT - 1, NSLOT))
    mirror = device(xl, b, a, z, y)
    load = pltpu.make_async_copy(w_ref, flat.at[pl.ds(MARGIN, SHARD)], local_sem.at[0])
    load.start()
    barrier = pltpu.get_barrier_semaphore()
    total = (counts_ref[0] + counts_ref[1]).astype(jnp.float32)
    for m in range(2):
        valid = jnp.full((1, 128), jnp.where(fs < counts_ref[m], 1.0, 0.0), jnp.float32)
        meta_ref[m : m + 1, :] = jnp.full((1, 128), labels_ref[m].astype(jnp.float32), jnp.float32)
        meta_ref[2 + m : 3 + m, :] = valid / jnp.full((1, 128), total, jnp.float32)
        meta_ref[4 + m : 5 + m, :] = valid
    meta_ref[6:8, :] = jnp.zeros((2, 128), jnp.float32)

    def greet(target):
        pl.semaphore_signal(barrier, inc=1, device_id=target, device_id_type=MESH)

    def wanted(j, parity):
        return jnp.logical_or(j < STAGES[0][1], lax.rem(j + 3 - STAGES[0][1] % 3, 3) != 2 * (1 - parity))

    for target in (up, down, links.at_x(1), links.at_x(3), links.at_y(1), links.at_y(3), links.at_z(1), links.at_z(3), links.sibling):
        greet(target)

    @pl.when(swap)
    def _():
        greet(mirror)

    own_index = lax.rem(fs * 11, NSLOT)
    keeps = jnp.logical_and(a == b, own_index < ROUNDS)

    def greet_source(j, carry):
        s = lax.div(32 * j + holder, ROUNDS)
        sa = lax.rem(lax.div(s, 4), 2)

        @pl.when(jnp.logical_and(wanted(j, xl), jnp.logical_not(jnp.logical_and(keeps, s == fs))))
        def _():
            greet(device(lax.rem(xl + sa + a, 2), sa, a, lax.div(s, 8), lax.rem(s, 4)))

        return carry

    lax.fori_loop(0, ROUNDS, greet_source, 0)
    def unit_goes(i):
        there = wanted(lax.div(ROUNDS * fs + i, 32), xo)
        stays = jnp.logical_and(keeps, i == own_index)
        return jnp.logical_and(there, jnp.logical_not(stays)), jnp.logical_and(there, stays)

    outgoing = lax.fori_loop(0, ROUNDS, lambda i, n: n + jnp.where(unit_goes(i)[0], 1, 0), 9)
    pl.semaphore_wait(barrier, outgoing + jnp.where(swap, 1, 0))
    load.wait()

    def remote(src, dst, k, target):
        return pltpu.make_async_remote_copy(src_ref=src, dst_ref=dst, send_sem=x_send.at[k], recv_sem=x_recv.at[k], device_id=target, device_id_type=MESH)

    hib[...] = flat[pl.ds(MARGIN + SHARD - HI, HI), :].astype(jnp.bfloat16)
    to_up = remote(hib, rlo, 0, up)
    to_up.start()
    lob[...] = flat[pl.ds(MARGIN, LO), :].astype(jnp.bfloat16)
    to_down = remote(lob, rhi, 1, down)
    to_down.start()
    patch_swap = remote(patch_ref, patch_in, 2, mirror)
    meta_swap = remote(meta_ref, meta_in, 3, mirror)
    patch_keep = pltpu.make_async_copy(patch_ref, patch_in, local_sem.at[1])
    meta_keep = pltpu.make_async_copy(meta_ref, meta_in, local_sem.at[2])
    first = ROUNDS * fs
    origin = SHARD * fs - MARGIN

    def unit_copy(i):
        k = first + i
        d = lax.rem(k, 32)
        src = slot.at[pl.ds(UNIT * i, UNIT)]
        dst = T.at[pl.ds(UNIT * k, UNIT)]
        target = device(xo, b, lax.rem(lax.div(d, 4), 2), lax.div(d, 8), lax.rem(d, 4))
        away = pltpu.make_async_remote_copy(src_ref=src, dst_ref=dst, send_sem=u_send.at[i], recv_sem=u_recv.at[lax.div(k, 32)], device_id=target, device_id_type=MESH)
        return away, (src, dst)

    def send_unit(i):
        away, (src, dst) = unit_copy(i)
        goes, stays = unit_goes(i)

        @pl.when(stays)
        def _():
            pltpu.make_async_copy(src, dst, local_sem.at[3]).start()

        @pl.when(goes)
        def _():
            away.start()

    lane = lax.broadcasted_iota(jnp.int32, (8, 128), 1)

    def head_group(g, base, per, start):
        row = base + per * g - origin
        for i in range(16):
            q, s = divmod(1000 * i, 128)
            one = flat[pl.ds(row + q, 8), :]
            if s:
                two = flat[pl.ds(row + q + 1, 8), :]
                one = jnp.where(lane < 128 - s, pltpu.roll(one, 128 - s, 1), pltpu.roll(two, 128 - s, 1))
            headrows[pl.ds(i * 8, 8), :] = one
        for j in range(8):
            t = start + g * 8 + j - UNIT * first

            @pl.when(jnp.logical_and(t >= 0, t < SLOT))
            def _():
                slot[t] = headrows[pl.ds(j, 16, stride=8), :].astype(jnp.bfloat16)

    def inside(row, rows):
        return jnp.logical_and(row >= MARGIN, row + rows <= MARGIN + SHARD)

    def convert(near):
        for index, (base, c, groups, per, start) in enumerate(SECTIONS):
            lo = jnp.maximum(UNIT * first, start)
            hi = jnp.minimum(UNIT * first + SLOT, start + c * groups)
            if index == 1:

                def group(g, carry):
                    @pl.when(inside(base + per * g - origin, per + 1) == near)
                    def _():
                        head_group(g, base, per, start)

                    return carry

                lax.fori_loop(lax.div(jnp.maximum(lo, start) - start, 8), lax.div(jnp.maximum(hi, start) - start + 7, 8), group, 0)
                if not near:

                    def deal(u, carry):
                        send_unit(u - first)
                        return carry

                    lax.fori_loop(lax.div(lo, UNIT), lax.div(hi, UNIT), deal, 0)
            else:

                def unit(u, carry):
                    t = UNIT * u - start
                    g = lax.div(t, c)
                    row = base + 16 * c * g + lax.rem(t, c) - origin

                    @pl.when(inside(row, 15 * c + UNIT) == near)
                    def _():
                        for k in range(UNIT):
                            slot[UNIT * (u - first) + k] = flat[pl.ds(row + k, 16, stride=c), :].astype(jnp.bfloat16)
                        send_unit(u - first)

                    return carry

                lax.fori_loop(lax.div(lo, UNIT), lax.div(hi, UNIT), unit, 0)

    convert(True)
    to_up.wait_recv()
    flat[pl.ds(MARGIN - HI, HI), :] = rlo[...].astype(jnp.float32)
    to_down.wait_recv()
    flat[pl.ds(MARGIN + SHARD, LO), :] = rhi[...].astype(jnp.float32)
    convert(False)

    @pl.when(fs == NSLOT - 1)
    def _():
        slot[pl.ds(SLOT - 12, 12)] = jnp.zeros((12, 16, 128), jnp.bfloat16)
        send_unit(ROUNDS - 2)
        send_unit(ROUNDS - 1)

    @pl.when(swap)
    def _():
        patch_swap.start()
        meta_swap.start()

    @pl.when(jnp.logical_not(swap))
    def _():
        patch_keep.start()
        meta_keep.start()

    def units_here(i):
        def wait(j, carry):
            place = T.at[pl.ds(UNIT * (32 * j + holder), UNIT)]
            mine = jnp.logical_and(keeps, lax.div(32 * j + holder, ROUNDS) == fs)

            @pl.when(jnp.logical_and(wanted(j, xl), mine))
            def _():
                pltpu.make_async_copy(place, place, local_sem.at[3]).wait()

            @pl.when(jnp.logical_and(wanted(j, xl), jnp.logical_not(mine)))
            def _():
                pltpu.make_async_remote_copy(src_ref=place, dst_ref=place, send_sem=u_send.at[0], recv_sem=u_recv.at[j], device_id=links.sibling, device_id_type=MESH).wait_recv()

            return carry

        lax.fori_loop(*STAGES[i], wait, 0)

    def finish_start():
        def wait(i, carry):
            away, unused = unit_copy(i)

            @pl.when(unit_goes(i)[0])
            def _():
                away.wait_send()

            return carry

        lax.fori_loop(0, ROUNDS, wait, 0)
        to_up.wait_send()
        to_down.wait_send()

        @pl.when(swap)
        def _():
            patch_swap.wait()
            meta_swap.wait()

        @pl.when(jnp.logical_not(swap))
        def _():
            patch_keep.wait()
            meta_keep.wait()

    return units_here, finish_start


D = 768
HEADS = 12
HEAD_DIM = 64
FF = 3072
CLS = 1000
P_SIZE = 196
ROWS = 208
TOK = 2 * ROWS
NORM_EPS = 1e-06
SMOOTHING = 0.1
NTILES = 4224
T_E, T_HEAD, T_NORM, T_QKV, T_OUT, T_IN, T_FO = 0, 366, 750, 756, 1620, 1908, 3060
T_POS = 288
BLK = 256
BLOCKS = ((0, 96), (96, 112), (208, 96), (304, 112))
F32 = jnp.float32
BF16 = jnp.bfloat16
ROOT_HALF = 0.7071067811865476
INV_ROOT_TWO_PI = 0.3989422804014327


def dot(x, w):
    return lax.dot_general(x, w, (((1,), (0,)), ((), ())), preferred_element_type=F32)


def dot_t(x, w):
    return lax.dot_general(x, w, (((1,), (1,)), ((), ())), preferred_element_type=F32)


def t_dot(x, w):
    return lax.dot_general(x, w, (((0,), (0,)), ((), ())), preferred_element_type=F32)


def stats(x, keep, r, k):
    mean = jnp.sum(x, -1, keepdims=True) * (1.0 / D)
    centred = x - mean
    var = jnp.sum(centred * centred, -1, keepdims=True) * (1.0 / D)
    rstd = lax.rsqrt(var + NORM_EPS)
    keep[r, k : k + 1] = mean
    keep[r, k + 1 : k + 2] = rstd
    return centred * rstd


def kept(x, keep, r, k):
    rstd = keep[r, k + 1 : k + 2]
    return (x - keep[r, k : k + 1]) * rstd, rstd


def norm_back(d_hat, hat, rstd):
    m1 = jnp.sum(d_hat, -1, keepdims=True) * (1.0 / D)
    m2 = jnp.sum(d_hat * hat, -1, keepdims=True) * (1.0 / D)
    return rstd * (d_hat - m1 - hat * m2)


def compute(step, patch_ref, meta_ref, loss_ref, T, x, h, a, at, mix, prob, o, h1, a2, hid, slope, h2, dh, dyb, keep):
    G = T
    dmix = mix

    def section(ref, start, c, groups):
        return ref.at[pl.ds(start, groups * c)].reshape(groups, c, 16, 128)

    def cols(start, c, groups, j):
        part = section(T, start, c, groups)
        return jnp.concatenate([part[:, 2 * j + k].reshape(groups * 16, 128) for k in range(2)], axis=1)

    def put_cols(start, c, groups, j, value):
        low = value.astype(BF16)
        part = section(G, start, c, groups)
        for k in range(2):
            part[:, 2 * j + k] = low[:, k * 128 : (k + 1) * 128].reshape(groups, 16, 128)

    def row_of(start, k):
        return jnp.concatenate([T[start + j][k : k + 1, :] for j in range(6)], axis=1).astype(F32)

    def lanes(j):
        return pl.ds(pl.multiple_of(j * BLK, BLK), BLK)

    step("start")
    for i in range(2):
        x[pl.ds(i * ROWS, 192), :] = patch_ref[i, pl.ds(0, 192), :]
        x[pl.ds(i * ROWS + 192, 16), :] = jnp.concatenate([patch_ref[i, pl.ds(192, 4), :], jnp.zeros((12, D), BF16)], axis=0)

    real = lax.broadcasted_iota(jnp.int32, (ROWS, 128), 0) < P_SIZE
    for j in range(3):
        acc = dot(x[...], cols(T_E, 6, 48, j))
        p = cols(T_POS, 6, 13, j).astype(F32)
        p = jnp.where(lax.broadcasted_iota(jnp.int32, (ROWS, BLK), 0) < P_SIZE, p, 0.0)
        for i in range(2):
            h[pl.ds(i * ROWS, ROWS), pl.ds(j * BLK, BLK)] = acc[i * ROWS : (i + 1) * ROWS] + p

    step("embedded")
    gain1, shift1, gain2, shift2 = (row_of(T_NORM, k) for k in range(4))

    for at_row, n in BLOCKS:
        r = pl.ds(at_row, n)
        a[r, :] = (stats(h[r, :], keep, r, 0) * gain1 + shift1).astype(BF16)

    step("qkv")
    def wide_cols(start, c, groups, j):
        return jnp.concatenate([cols(start, c, groups, 3 * j + k) for k in range(3)], axis=1)

    def wide_lanes(j):
        return pl.ds(pl.multiple_of(j * D, D), D)

    def mix_block(j, carry):
        mix[:, wide_lanes(j)] = dot(a[...], wide_cols(T_QKV, 18, 48, j)).astype(BF16)
        return carry

    lax.fori_loop(0, 3, mix_block, 0)

    first_half = lax.broadcasted_iota(jnp.int32, (ROWS, 128), 1) < HEAD_DIM
    key_ok = lax.broadcasted_iota(jnp.int32, (ROWS, ROWS), 0) < P_SIZE
    first_rows = lax.broadcasted_iota(jnp.int32, (128, ROWS), 0) < HEAD_DIM
    halves = (first_half, jnp.logical_not(first_half))
    zero = jnp.zeros((ROWS, 128), BF16)

    def split(block):
        return jnp.concatenate([jnp.where(first_half, block, zero), jnp.where(first_half, zero, block)], axis=0)

    def heads_of(p, i):
        r = pl.ds(i * ROWS, ROWS)
        return r, [pl.ds(pl.multiple_of(p * 128 + D * k, 128), 128) for k in range(3)]

    def attend(p, carry):
        for i in range(2):
            r, ls = heads_of(p, i)
            q, k, v = (mix[r, l] for l in ls)
            q = q * jnp.asarray(0.125, BF16)
            vt = v.T
            outs = []
            for e in range(2):
                s = dot_t(jnp.where(halves[e], k, zero), q)
                s = jnp.where(key_ok, s, -jnp.inf)
                ex = jnp.exp(s - jnp.max(s, 0, keepdims=True))
                pr = (ex * (1.0 / jnp.sum(ex, 0, keepdims=True))).astype(BF16)
                prob[p * 2 + i, e] = pr
                outs.append(dot(vt, pr))
            o[r, ls[0]] = jnp.where(first_rows, outs[0], outs[1]).astype(BF16).T
        return carry

    parts = ((0, 2), (2, 3), (3, 5), (5, 6))
    for part in range(4):
        step("attend%d" % part)
        lax.fori_loop(*parts[part], attend, 0)
    step("attended")
    for j in range(3):
        h1[:, pl.ds(j * BLK, BLK)] = h[:, pl.ds(j * BLK, BLK)] + dot(o[...], cols(T_OUT, 6, 48, j))

    for at_row, n in BLOCKS:
        r = pl.ds(at_row, n)
        a2[r, :] = (stats(h1[r, :], keep, r, 2) * gain2 + shift2).astype(BF16)

    step("up")
    def up_block(j, carry):
        u = dot(a2[...], wide_cols(T_IN, 24, 48, j))
        phi = 0.5 * (1.0 + lax.erf(u * ROOT_HALF))
        pdf = jnp.exp(-0.5 * u * u) * INV_ROOT_TWO_PI
        hid[:, wide_lanes(j)] = (u * phi).astype(BF16)
        slope[:, wide_lanes(j)] = (phi + u * pdf).astype(BF16)
        return carry

    lax.fori_loop(0, 4, up_block, 0)
    step("down")
    for j in range(3):
        h2[:, pl.ds(j * BLK, BLK)] = h1[:, pl.ds(j * BLK, BLK)] + dot(hid[...], cols(T_FO, 6, 192, j))

    step("pool")
    gain_end, shift_end = (row_of(T_POS + 72, 4 + k) for k in range(2))
    means = []
    last_rows = lax.broadcasted_iota(jnp.int32, (112, D), 0) < P_SIZE - 96
    for i in range(2):
        total = jnp.zeros((8, D), F32)
        for at_row, n in BLOCKS[2 * i : 2 * i + 2]:
            r = pl.ds(at_row, n)
            hat = stats(h2[r, :], keep, r, 4)
            if n == 112:
                hat = jnp.where(last_rows, hat, 0.0)
            total = total + jnp.sum(hat.reshape(n // 8, 8, D), 0)
        means.append(jnp.sum(total, 0, keepdims=True) * (1.0 / P_SIZE))
    mean_hat = jnp.concatenate(means + [jnp.zeros((14, D), F32)], axis=0)
    two = lax.broadcasted_iota(jnp.int32, (16, D), 0) < 2
    pooled = jnp.where(two, mean_hat * gain_end + shift_end, 0.0).astype(BF16)
    logits = jnp.concatenate([dot(pooled, cols(T_HEAD, 8, 48, j)) for j in range(4)], axis=1)
    lane = lax.broadcasted_iota(jnp.int32, (16, 1024), 1)
    lane_f = lane.astype(F32)
    inside = lane < CLS
    logits = jnp.where(inside, logits, -1e30)
    top = jnp.max(logits, -1, keepdims=True)
    total = jnp.sum(jnp.where(inside, jnp.exp(logits - top), 0.0), -1, keepdims=True)
    logp = logits - top - jnp.log(total)
    meta = meta_ref[...]
    pad14 = jnp.zeros((14, 1), F32)
    label = jnp.concatenate([meta[0:2, 0:1], pad14], axis=0)
    scale = jnp.concatenate([meta[2:4, 0:1], pad14], axis=0)
    valid = jnp.concatenate([meta[4:6, 0:1], pad14], axis=0)
    target = jnp.where(lane_f == label, 1.0 - SMOOTHING, 0.0) + SMOOTHING / CLS
    values = -jnp.sum(jnp.where(inside, target * logp, 0.0), -1, keepdims=True)
    loss_ref[...] = jnp.broadcast_to(jnp.sum(values * valid, 0, keepdims=True), (8, 128))
    d_logits = jnp.where(inside, scale * (jnp.exp(logp) - target), 0.0).astype(BF16)
    d_pooled = jnp.zeros((16, D), F32)
    for j in range(4):
        w = cols(T_HEAD, 8, 48, j)
        d_pooled = d_pooled + dot_t(d_logits[:, j * BLK : (j + 1) * BLK], w)
        put_cols(T_HEAD, 8, 48, j, t_dot(pooled, d_logits[:, j * BLK : (j + 1) * BLK]))
    d_gain_end = jnp.sum(d_pooled * mean_hat, 0, keepdims=True)
    d_shift_end = jnp.sum(d_pooled, 0, keepdims=True)
    for i in range(2):
        d_hat = d_pooled[i : i + 1, :] * (1.0 / P_SIZE) * gain_end

        m1 = jnp.sum(d_hat, -1, keepdims=True) * (1.0 / D)
        for at_row, n in BLOCKS[2 * i : 2 * i + 2]:
            r = pl.ds(at_row, n)
            hat, rstd = kept(h2[r, :], keep, r, 4)
            m2 = jnp.sum(d_hat * hat, -1, keepdims=True) * (1.0 / D)
            d = rstd * ((d_hat - m1) - hat * m2)
            if n == 112:
                d = jnp.where(last_rows, d, 0.0)
            dh[r, :] = d
            dyb[r, :] = d.astype(BF16)

    step("backward")
    at[...] = a2[...].T
    da = h2

    wide = D // 16

    def down_block(j, carry):
        part = section(T, T_FO + j * wide * 6, 6, wide)
        w = jnp.concatenate([part[:, k].reshape(D, 128) for k in range(6)], axis=1)
        dy = dyb[...]
        d_w = t_dot(hid[:, wide_lanes(j)], dy).astype(BF16)
        hid[:, wide_lanes(j)] = (dot_t(dy, w) * slope[:, wide_lanes(j)].astype(F32)).astype(BF16)
        for k in range(6):
            part[:, k] = d_w[:, k * 128 : (k + 1) * 128].reshape(wide, 16, 128)
        return carry

    G[pl.ds(4212, 12)] = jnp.zeros((12, 16, 128), BF16)
    lax.fori_loop(0, 3, down_block, 0)
    step("fc_out0")
    lax.fori_loop(3, 4, down_block, 0)
    step("fc_out1")
    def row_block(start, c, j):
        part = section(T, start + j * 16 * c, c, 16)
        return jnp.concatenate([part[:, k].reshape(BLK, 128) for k in range(c)], axis=1)

    def put_rows(start, c, j, first, value):
        part = section(G, start + j * 16 * c, c, 16)
        low = value.astype(BF16)
        for k in range(value.shape[1] // 128):
            part[:, first + k] = low[:, k * 128 : (k + 1) * 128].reshape(16, 16, 128)

    for j in range(3):
        da[:, pl.ds(j * BLK, BLK)] = dot_t(hid[...], row_block(T_IN, 24, j))
    step("fc_in0")
    for j in range(3):
        for k in range(4):
            put_rows(T_IN, 24, j, 6 * k, dot(at[pl.ds(j * BLK, BLK), :], hid[:, pl.ds(k * D, D)]))
        step("fc_in%d" % (j + 1))

    def norm_grads(inputs, column, gain):
        dg, ds = jnp.zeros((8, D), F32), jnp.zeros((8, D), F32)
        for at_row, n in BLOCKS:
            r = pl.ds(at_row, n)
            hat, rstd = kept(inputs[r, :], keep, r, column)
            d = da[r, :]
            new = dh[r, :] + norm_back(d * gain, hat, rstd)
            dh[r, :] = new
            dyb[r, :] = new.astype(BF16)
            dg = dg + jnp.sum((d * hat).reshape(n // 8, 8, D), 0)
            ds = ds + jnp.sum(d.reshape(n // 8, 8, D), 0)
        return dg, ds

    d_gain2, d_shift2 = norm_grads(h1, 2, gain2)

    step("normed2")
    at[...] = o[...].T
    for j in range(3):
        o[:, pl.ds(j * BLK, BLK)] = dot_t(dyb[...], row_block(T_OUT, 6, j)).astype(BF16)
    for j in range(3):
        put_rows(T_OUT, 6, j, 0, dot(at[pl.ds(j * BLK, BLK), :], dyb[...]))

    step("out")
    def attend_back(p, carry):
        for i in range(2):
            r, ls = heads_of(p, i)
            q, k, v = (mix[r, l] for l in ls)
            q = q * jnp.asarray(0.125, BF16)
            k8 = k * jnp.asarray(0.125, BF16)
            kt = k8.T
            do = o[r, ls[0]]
            pr = prob[p * 2 + i]
            dv = dot(pr.reshape(TOK, ROWS), do)
            dp = dot_t(split(v), do).reshape(2, ROWS, ROWS)
            prf = pr.astype(F32)
            row = jnp.sum(prf * dp, 1, keepdims=True)
            ds = (prf * (dp - row)).astype(BF16)
            dq = [dot(kt[HEAD_DIM * e : HEAD_DIM * (e + 1)], ds[e]) for e in range(2)]
            dk = dot(ds.reshape(TOK, ROWS), q)
            dmix[r, ls[0]] = jnp.concatenate(dq, axis=0).astype(BF16).T
            dmix[r, ls[1]] = jnp.where(first_half, dk[:ROWS], dk[ROWS:]).astype(BF16)
            dmix[r, ls[2]] = jnp.where(first_half, dv[:ROWS], dv[ROWS:]).astype(BF16)
        return carry

    for part in range(4):
        lax.fori_loop(*parts[part], attend_back, 0)
        step("back%d" % part)

    at[...] = a[...].T
    for j in range(3):
        da[:, pl.ds(j * BLK, BLK)] = dot_t(dmix[...], row_block(T_QKV, 18, j))
    for j in range(3):
        for k in range(3):
            put_rows(T_QKV, 18, j, 6 * k, dot(at[pl.ds(j * BLK, BLK), :], dmix[:, pl.ds(k * D, D)]))
    step("qkv_back")
    d_gain1, d_shift1 = norm_grads(h, 0, gain1)
    d_norms = jnp.concatenate([jnp.sum(d, 0, keepdims=True) for d in (d_gain1, d_shift1, d_gain2, d_shift2)] + [jnp.zeros((12, D), F32)], axis=0).astype(BF16)
    for j in range(6):
        G[T_NORM + j] = d_norms[:, j * 128 : (j + 1) * 128]
    step("norms")
    at[...] = x[...].T
    row_id = lax.broadcasted_iota(jnp.int32, (ROWS, BLK), 0)
    for j in range(3):
        put_cols(T_E, 6, 48, j, dot(at[...], dyb[:, pl.ds(j * BLK, BLK)]))
        c = pl.ds(j * BLK, BLK)
        s = slice(j * BLK, (j + 1) * BLK)
        d_pos = dh[pl.ds(0, ROWS), c] + dh[pl.ds(ROWS, ROWS), c]
        d_pos = jnp.where(row_id < P_SIZE, d_pos, 0.0)
        d_pos = jnp.where(row_id == P_SIZE, jnp.broadcast_to(d_gain_end[:, s], (ROWS, BLK)), d_pos)
        d_pos = jnp.where(row_id == P_SIZE + 1, jnp.broadcast_to(d_shift_end[:, s], (ROWS, BLK)), d_pos)
        put_cols(T_POS, 6, 13, j, d_pos)
    step("embed")


FORWARD = {
    "start": (
        (1, 0), (3, 0), (1, 1), (0, 0), (2, 0), (1, 2), (0, 1), (0, 2), (2, 1), (1, 3), (2, 2), (1, 4),
        (0, 3), (3, 1), (2, 3), (3, 2), (0, 4), (1, 5), (0, 6),
    ),
    "qkv": ((1, 6), (2, 4),),
    "attend0": ((3, 3),),
    "attend1": ((2, 5),),
    "attend2": ((3, 4),),
    "attend3": ((2, 6),),
    "up": ((3, 5),),
    "down": ((3, 6),),
}
BACKWARD = {
    "fc_out1": ((3, 0, 0), (3, 1, 0),),
    "fc_in3": ((3, 1, 1), (2, 0, 0), (2, 1, 0), (3, 0, 1),),
    "back0": ((2, 1, 1), (2, 0, 1),),
    "back3": ((3, 1, 2), (3, 0, 2),),
    "qkv_back": ((1, 0, 0), (2, 1, 2),),
    "norms": ((0, 1, 0), (1, 1, 0), (2, 0, 2),),
    "embed": (
        (3, 0, 3), (1, 0, 1), (0, 1, 1), (1, 1, 1), (0, 0, 0), (0, 0, 1), (1, 0, 2), (3, 1, 3), (0, 1, 2), (2, 0, 3), (1, 1, 2), (0, 0, 2),
        (0, 1, 3), (2, 1, 3), (1, 0, 3), (1, 1, 3), (0, 0, 3), (3, 0, 4), (3, 1, 4), (2, 1, 4), (2, 0, 4), (0, 1, 4), (1, 0, 4), (1, 1, 4),
        (0, 0, 4), (3, 1, 5), (1, 0, 5), (2, 1, 5), (2, 0, 5), (3, 0, 5), (0, 1, 5), (0, 0, 5), (1, 1, 5),
    ),
}


def grads_kernel(w_ref, patch_ref, labels_ref, counts_ref, red_ref, loss_out, T, R, RA, RB, g_send, g_recv, r_send, r_recv, LS, l_send, l_recv, patch_in, meta_in, meta, loss, *rest):
    gather_refs, compute_refs, out_sem = rest[:12], rest[12:-1], rest[-1]
    links = Links(T, R, RA, RB, g_send, g_recv, r_send, r_recv)
    xl, b, z, a, y = links.xl, links.b, links.z, links.a, links.y
    swap = a != b
    mirror = device(xl, b, a, z, y)
    units_here, finish_start = start_gather(links, w_ref, patch_ref, labels_ref, counts_ref, T, patch_in, meta_in, meta, *gather_refs)

    def loss_send(src, dst, target):
        links.go(LS.at[src], LS.at[dst], l_send.at[dst], l_recv.at[dst], target)

    def loss_wait(*slots):
        for k in slots:
            links.landed(LS.at[k], l_send.at[k], l_recv.at[k])

    def loss_step(n):
        if n == 0:
            LS[0] = loss[...]
            loss_send(0, 1, links.sibling)
        elif n == 1:
            loss_wait(1)
            LS[8] = LS[0] + LS[1]
            loss_send(8, 2, links.at_y(1))
            loss_send(8, 3, links.at_y(3))
        elif n == 2:
            loss_wait(2, 3)
            loss_send(2, 4, links.at_y(1))
        elif n == 3:
            loss_wait(4)
            LS[9] = (LS[8] + LS[4]) + (LS[2] + LS[3])
            loss_send(9, 5, links.at_z(1))
            loss_send(9, 6, links.at_z(3))
        elif n == 4:
            loss_wait(5, 6)
            loss_send(5, 7, links.at_z(1))
        elif n == 5:
            loss_wait(7)
            LS[10] = (LS[9] + LS[7]) + (LS[5] + LS[6])

            @pl.when(swap)
            def _():
                loss_swap.start()

        else:

            @pl.when(swap)
            def _():
                loss_swap.wait()
                loss_out[...] = LS[11]

            @pl.when(jnp.logical_not(swap))
            def _():
                loss_out[...] = LS[10]

    loss_swap = pltpu.make_async_remote_copy(src_ref=LS.at[10], dst_ref=LS.at[11], send_sem=l_send.at[11], recv_sem=l_recv.at[11], device_id=mirror, device_id_type=MESH)
    losses = {"fc_out0": 0, "fc_in2": 1, "out": 2, "back1": 3, "back3": 4, "norms": 5}

    def step(name):
        if name == "pool":
            links.sent()
        for item in FORWARD.get(name, ()):
            if item[1] == 0:
                units_here(item[0])
            links.gather_step(*item)
        if name == "start":
            finish_start()
        for item in BACKWARD.get(name, ()):
            links.reduce_step(*item)
        if name in losses:
            loss_step(losses[name])

    compute(step, patch_in, meta_in, loss, T, *compute_refs)
    loss_step(6)
    mine = T.reshape(ROUNDS, 32, UNIT, 16, 128).at[:, z * 8 + b * 4 + y]
    out = pltpu.make_async_copy(mine, red_ref, out_sem)
    out.start()
    links.sent()
    out.wait()


def grads(weights, patches, labels, counts):
    hbm = pl.BlockSpec(memory_space=pl.ANY)
    vmem = pl.BlockSpec(memory_space=pltpu.VMEM)
    V = pltpu.VMEM
    dma = pltpu.SemaphoreType.DMA
    return pl.pallas_call(
        grads_kernel,
        out_shape=(jax.ShapeDtypeStruct((ROUNDS, UNIT, 16, 128), BF16), jax.ShapeDtypeStruct((8, 128), F32)),
        in_specs=[hbm] * 2 + [pl.BlockSpec(memory_space=pltpu.SMEM)] * 2,
        out_specs=(hbm, vmem),
        scratch_shapes=[
            V((NTILES, 16, 128), BF16),
            V((ROUNDS, 4, 4, UNIT, 16, 128), BF16),
            V((6, ROUNDS, 2, UNIT, 16, 128), BF16),
            V((6, ROUNDS, 3, 16, 128), BF16),
            dma((192,)),
            dma((192,)),
            dma((104,)),
            dma((104,)),
            V((12, 8, 128), F32),
            dma((12,)),
            dma((12,)),
            V(patches.shape, BF16),
            V((8, 128), F32),
            V((8, 128), F32),
            V((8, 128), F32),
            V((FROWS, 128), F32),
            V((128, 128), F32),
            V((LO, 128), BF16),
            V((HI, 128), BF16),
            V((HI, 128), BF16),
            V((LO, 128), BF16),
            V((SLOT, 16, 128), BF16),
            dma((4,)),
            dma((4,)),
            dma((4,)),
            dma((ROUNDS,)),
            dma((ROUNDS,)),
            V((TOK, D), BF16),
            V((TOK, D), F32),
            V((TOK, D), BF16),
            V((D, TOK), BF16),
            V((TOK, 3 * D), BF16),
            V((12, 2, ROWS, ROWS), BF16),
            V((TOK, D), BF16),
            V((TOK, D), F32),
            V((TOK, D), BF16),
            V((TOK, FF), BF16),
            V((TOK, FF), BF16),
            V((TOK, D), F32),
            V((TOK, D), F32),
            V((TOK, D), BF16),
            V((TOK, 128), F32),
            dma,
        ],
        compiler_params=pltpu.CompilerParams(collective_id=0, has_side_effects=True, vmem_limit_bytes=60 * 1024 * 1024),
        name="grads",
    )(weights, patches, labels, counts)


EDGE = 24
FRONT = 768
BACK_ROWS = FRONT + SHARD + 640 + 6
PADDED = 2112
STEP = 10
EDGE_UNITS = 4
WINDOW = ROUNDS + 2 * EDGE_UNITS
BETA_ONE = 0.9
BETA_TWO = 0.95
ADAM_EPS = 1e-08
DECAY = 0.05
INNER_RATE = 0.01
OUTER_RATE = 0.7
OUTER_MU = 0.9


def update_kernel(
    red_ref, first_ref, second_ref,
    sum_out, first_out, second_out,
    red, window, flat, headrows, first_row, second_row, first, second, low, low2, pair, pair2, total, total2,
    load_sem, x_send, x_recv, o_send, e_send, w_recv,
):
    xl, b, z, a, y = coords()
    fs = z * 8 + a * 4 + y
    holder = z * 8 + b * 4 + y
    sibling = device(xl, a, 1 - b, z, y)
    across = device(1 - xl, a, b, z, y)
    extra = [pltpu.make_async_copy(src, dst, load_sem.at[i]) for i, (src, dst) in enumerate(((first_ref, first_row), (second_ref, second_row)))]
    load = pltpu.make_async_copy(red_ref, red, load_sem.at[4])
    load.start()
    for copy in extra:
        copy.start()

    barrier = pltpu.get_barrier_semaphore()

    def greet(target):
        pl.semaphore_signal(barrier, inc=1, device_id=target, device_id_type=MESH)

    greet(sibling)
    greet(across)
    first_unit = ROUNDS * fs - EDGE_UNITS

    def window_unit(p):
        k = first_unit + p
        d = lax.rem(k + 32, 32)
        inside = jnp.logical_and(k >= 0, k < 32 * ROUNDS)
        mine = jnp.logical_and(a == b, d == holder)
        return inside, mine, device(xl, b, lax.rem(lax.div(d, 4), 2), lax.div(d, 8), lax.rem(d, 4))

    def greet_holder(p, carry):
        inside, mine, source = window_unit(p)

        @pl.when(jnp.logical_and(inside, jnp.logical_not(mine)))
        def _():
            greet(source)

        return carry

    lax.fori_loop(0, WINDOW, greet_holder, 0)

    def held_unit(j):
        k = 32 * j + holder
        q = lax.div(k, ROUNDS)
        r = lax.rem(k, ROUNDS)
        shift = jnp.where(r < EDGE_UNITS, -1, jnp.where(r >= ROUNDS - EDGE_UNITS, 1, 0))
        near = jnp.logical_and(shift != 0, jnp.logical_and(q + shift >= 0, q + shift < NSLOT))
        return k, q, jnp.where(near, q + shift, q), near

    def to_owner(j, k, s, send):
        p = k - (ROUNDS * s - EDGE_UNITS)
        src = red.at[j]
        dst = window.at[pl.ds(UNIT * p, UNIT)]
        sa = lax.rem(lax.div(s, 4), 2)
        mine = jnp.logical_and(a == b, s == fs)
        target = device(xl, sa, a, lax.div(s, 8), lax.rem(s, 4))
        away = pltpu.make_async_remote_copy(src_ref=src, dst_ref=dst, send_sem=send.at[j], recv_sem=w_recv.at[p], device_id=target, device_id_type=MESH)
        here = pltpu.make_async_copy(src, dst, load_sem.at[10])
        return mine, away, here

    def count(j, n):
        k, q, s, near = held_unit(j)
        first_away = jnp.logical_not(jnp.logical_and(a == b, q == fs))
        second_away = jnp.logical_and(near, jnp.logical_not(jnp.logical_and(a == b, s == fs)))
        return n + jnp.where(first_away, 1, 0) + jnp.where(second_away, 1, 0)

    outgoing = lax.fori_loop(0, ROUNDS, count, 2)
    pl.semaphore_wait(barrier, outgoing)
    load.wait()

    def give(j, carry):
        k, q, s, near = held_unit(j)
        mine, away, here = to_owner(j, k, q, o_send)

        @pl.when(mine)
        def _():
            here.start()

        @pl.when(jnp.logical_not(mine))
        def _():
            away.start()

        mine2, away2, here2 = to_owner(j, k, s, e_send)

        @pl.when(jnp.logical_and(near, mine2))
        def _():
            here2.start()

        @pl.when(jnp.logical_and(near, jnp.logical_not(mine2)))
        def _():
            away2.start()

        return carry

    lax.fori_loop(0, ROUNDS, give, 0)

    def given(j, carry):
        k, q, s, near = held_unit(j)
        mine, away, here = to_owner(j, k, q, o_send)

        @pl.when(jnp.logical_not(mine))
        def _():
            away.wait_send()

        mine2, away2, here2 = to_owner(j, k, s, e_send)

        @pl.when(jnp.logical_and(near, jnp.logical_not(mine2)))
        def _():
            away2.wait_send()

        return carry

    def clear(i, carry):
        flat[pl.ds(pl.multiple_of(i * 32, 32), 32), :] = jnp.zeros((32, 128), F32)
        return carry

    lax.fori_loop(0, BACK_ROWS // 32, clear, 0)

    for copy in extra:
        copy.wait()
    for source, rows_of in ((first_row, first), (second_row, second)):

        def eight(i, carry):
            rows_of[pl.ds(pl.multiple_of(i * 8, 8), 8), :] = source[0, pl.ds(pl.multiple_of(i * 1024, 1024), 1024)].reshape(8, 128)
            return carry

        whole = SHARD // 8
        lax.fori_loop(0, whole, eight, 0, unroll=2)
        rows_of[pl.ds(whole * 8, SHARD - whole * 8), :] = source[0, pl.ds(whole * 1024, (SHARD - whole * 8) * 128)].reshape(SHARD - whole * 8, 128)

    def got(p, carry):
        inside, mine, source = window_unit(p)
        place = window.at[pl.ds(UNIT * p, UNIT)]

        @pl.when(jnp.logical_and(inside, mine))
        def _():
            pltpu.make_async_copy(place, place, load_sem.at[10]).wait()

        @pl.when(jnp.logical_and(inside, jnp.logical_not(mine)))
        def _():
            pltpu.make_async_remote_copy(src_ref=place, dst_ref=place, send_sem=x_send.at[0], recv_sem=w_recv.at[p], device_id=sibling, device_id_type=MESH).wait_recv()

        return carry

    lax.fori_loop(0, WINDOW, got, 0)
    sends = []

    def go(src, dst, send, recv, k, target):
        copy = pltpu.make_async_remote_copy(src_ref=src, dst_ref=dst, send_sem=send.at[k], recv_sem=recv.at[k], device_id=target, device_id_type=MESH)
        copy.start()
        sends.append(copy)

    def arrive(dst, recv, k):
        pltpu.make_async_remote_copy(src_ref=dst, dst_ref=dst, send_sem=x_send.at[k], recv_sem=recv.at[k], device_id=sibling, device_id_type=MESH).wait_recv()

    low_tile = SLOT * fs - EDGE
    high_tile = SLOT * fs + SLOT + EDGE
    origin = SHARD * fs - FRONT
    for index, (base, c, groups, per, start) in enumerate(SECTIONS):
        if index == 1:
            lane = lax.broadcasted_iota(jnp.int32, (8, 128), 1)
            g0 = lax.div(jnp.maximum(SHARD * fs - base, 0), per)
            g1 = lax.div(jnp.maximum(SHARD * (fs + 1) - base, 0) + per - 1, per)

            def head_group(g, carry):
                t = start + g * 8 - low_tile
                for j in range(8):
                    headrows[pl.ds(j, 16, stride=8), :] = window[t + j].astype(F32)
                row = base + per * g - origin
                for i in range(16):
                    q, s = divmod(1000 * i, 128)
                    value = headrows[pl.ds(i * 8, 8), :]
                    if s:
                        value = pltpu.roll(value, s, 1)
                        flat[pl.ds(row + q, 8), :] += jnp.where(lane >= s, value, 0.0)
                        flat[pl.ds(row + q + 1, 8), :] += jnp.where(lane < s, value, 0.0)
                    else:
                        flat[pl.ds(row + q, 8), :] += value
                return carry

            lax.fori_loop(jnp.minimum(g0, groups), jnp.minimum(g1, groups), head_group, 0)
        else:

            def unit(n, carry):
                t = UNIT * n - start
                row = base + 16 * c * lax.div(t, c) + lax.rem(t, c) - origin
                for m in range(UNIT):
                    flat[pl.ds(row + m, 16, stride=c), :] = window[UNIT * n - low_tile + m].astype(F32)
                return carry

            lax.fori_loop(lax.div(jnp.maximum(low_tile, start), UNIT), lax.div(jnp.minimum(high_tile, start + c * groups), UNIT), unit, 0)

    fix_one = 1.0 / (1.0 - BETA_ONE**STEP)
    fix_two = 1.0 / (1.0 - BETA_TWO**STEP)

    half = PADDED // 2
    step = 176
    for rows_of in (first, second):
        rows_of[pl.ds(SHARD, PADDED - SHARD), :] = jnp.zeros((PADDED - SHARD, 128), F32)

    def in_half(fn):
        def rows_step(i, carry):
            fn(pl.multiple_of(i * step, step), step)
            return carry

        lax.fori_loop(0, half // step, rows_step, 0)

    def adam_half(q):
        def adam(r, n):
            at = pl.ds(pl.multiple_of(q * half + r, 16), n)
            grad = flat[pl.ds(pl.multiple_of(FRONT + q * half + r, 16), n), :]
            m = BETA_ONE * first[at, :] + (1.0 - BETA_ONE) * grad
            s = BETA_TWO * second[at, :] + (1.0 - BETA_TWO) * grad * grad
            first[at, :] = m
            second[at, :] = s
            low[at, :] = ((m * fix_one) / (jnp.sqrt(s * fix_two) + ADAM_EPS)).astype(BF16)

        in_half(adam)

    adam_half(1 - b)
    go(low.at[pl.ds(pl.multiple_of((1 - b) * half, 16), half)], low2, x_send, x_recv, 0, sibling)
    adam_half(b)
    outs = [pltpu.make_async_copy(src.at[pl.ds(0, SHARD)], dst, load_sem.at[5 + i]) for i, (src, dst) in enumerate(((first, first_out), (second, second_out)))]
    for copy in outs:
        copy.start()
    arrive(low2, x_recv, 0)

    def pairs(r, n):
        pair[pl.ds(r, n), :] = low[pl.ds(pl.multiple_of(b * half + r, 16), n), :] + low2[pl.ds(r, n), :]

    in_half(pairs)
    go(pair, pair2, x_send, x_recv, 1, across)
    arrive(pair2, x_recv, 1)

    def fours(r, n):
        total[pl.ds(r, n), :] = pair[pl.ds(r, n), :].astype(F32) + pair2[pl.ds(r, n), :].astype(F32)

    in_half(fours)
    go(total, total2, x_send, x_recv, 2, sibling)

    arrive(total2, x_recv, 2)
    other = half - b * half
    final = [(total, sum_out.at[pl.ds(pl.multiple_of(b * half, 16), half)]), (total2, sum_out.at[pl.ds(pl.multiple_of(other, 16), half)])]
    final = [pltpu.make_async_copy(src, dst, load_sem.at[7 + i]) for i, (src, dst) in enumerate(final)]
    for copy in final:
        copy.start()
    for copy in sends:
        copy.wait_send()
    lax.fori_loop(0, ROUNDS, given, 0)
    for copy in outs + final:
        copy.wait()


def update(red, first, second):
    hbm = pl.BlockSpec(memory_space=pl.ANY)
    V = pltpu.VMEM
    flat = jax.ShapeDtypeStruct((SHARD, 128), F32)
    dma = pltpu.SemaphoreType.DMA
    return pl.pallas_call(
        update_kernel,
        out_shape=(jax.ShapeDtypeStruct((PADDED, 128), F32), flat, flat),
        in_specs=[hbm] * 3,
        out_specs=(hbm,) * 3,
        scratch_shapes=[
            V((ROUNDS, UNIT, 16, 128), BF16),
            V((EDGE + SLOT + EDGE, 16, 128), BF16),
            V((BACK_ROWS, 128), F32),
            V((128, 128), F32),
            V((1, SHARD * 128), F32),
            V((1, SHARD * 128), F32),
            V((PADDED, 128), F32),
            V((PADDED, 128), F32),
            V((PADDED, 128), BF16),
            V((PADDED // 2, 128), BF16),
            V((PADDED // 2, 128), BF16),
            V((PADDED // 2, 128), BF16),
            V((PADDED // 2, 128), F32),
            V((PADDED // 2, 128), F32),
            dma((11,)),
            dma((3,)),
            dma((3,)),
            dma((ROUNDS,)),
            dma((ROUNDS,)),
            dma((WINDOW,)),
        ],
        compiler_params=pltpu.CompilerParams(collective_id=1, has_side_effects=True, vmem_limit_bytes=60 * 1024 * 1024),
        name="update",
    )(red, first, second)


def finish_kernel(
    sum_ref, w_ref, mom_ref, first_ref, second_ref, loss_ref,
    avg_out, mom_out, new_out, first_out, second_out, loss_out,
    total, w, mom, first, second, averaged, sem, out_sem,
):
    cut = PADDED // 2
    pieces = [pl.ds(0, cut), pl.ds(cut, SHARD - cut)]
    loads = []
    for i, at in enumerate(pieces):
        loads.append([pltpu.make_async_copy(src.at[at], dst.at[at], sem.at[3 * i + k]) for k, (src, dst) in enumerate(((sum_ref, total), (w_ref, w), (mom_ref, mom)))])
    moments = [pltpu.make_async_copy(src, dst, sem.at[6 + i]) for i, (src, dst) in enumerate(((first_ref, first), (second_ref, second)))]
    for copy in loads[0] + loads[1] + moments:
        copy.start()
    outs = []

    def send(src, dst):
        copy = pltpu.make_async_copy(src, dst, out_sem.at[len(outs)])
        copy.start()
        outs.append(copy)

    loss_out[...] = loss_ref[0:1, 0:1]

    def outer(r, n):
        at = pl.ds(r, n)
        old = w[at, :]
        mean = INNER_RATE * (total[at, :] * 0.25 + DECAY * old)
        momentum = OUTER_MU * mom[at, :] + mean
        averaged[at, :] = mean
        mom[at, :] = momentum
        w[at, :] = old - OUTER_RATE * (mean + OUTER_MU * momentum)

    def block(i, carry):
        outer(pl.multiple_of(i * 96, 96), 96)
        return carry

    for i, at in enumerate(pieces):
        for copy in loads[i]:
            copy.wait()
        if i == 0:
            lax.fori_loop(0, cut // 96, block, 0)
        else:
            lax.fori_loop(cut // 96, SHARD // 96, block, 0)
            outer(SHARD // 96 * 96, SHARD - SHARD // 96 * 96)
        for src, dst in ((averaged, avg_out), (mom, mom_out), (w, new_out)):
            send(src.at[at], dst.at[at])
        if i == 0:
            for copy, src, dst in zip(moments, (first, second), (first_out, second_out)):
                copy.wait()
                send(src, dst.reshape(SHARD, 128))
    for copy in outs:
        copy.wait()


def finish(total, weights, momentum, first, second, loss):
    hbm = pl.BlockSpec(memory_space=pl.ANY)
    vmem = pl.BlockSpec(memory_space=pltpu.VMEM)
    V = pltpu.VMEM
    rows = jax.ShapeDtypeStruct((SHARD, 128), F32)
    row = jax.ShapeDtypeStruct((1, SHARD * 128), F32)
    return pl.pallas_call(
        finish_kernel,
        out_shape=(rows,) * 3 + (row,) * 2 + (jax.ShapeDtypeStruct((1, 1), F32),),
        in_specs=[hbm] * 5 + [vmem],
        out_specs=(hbm,) * 5 + (vmem,),
        scratch_shapes=[V((PADDED, 128), F32)] + [V((SHARD, 128), F32)] * 5 + [pltpu.SemaphoreType.DMA((8,)), pltpu.SemaphoreType.DMA((8,))],
        compiler_params=pltpu.CompilerParams(vmem_limit_bytes=60 * 1024 * 1024),
        name="finish",
    )(total, weights, momentum, first, second, loss)


def body(patches, labels, counts, weights, first_moments, second_moments, outer_momentum):
    flat = weights.reshape(SHARD, 128)
    reduced, loss = grads(flat, patches.reshape(2, P_SIZE, D), labels.reshape(2), counts.reshape(2))
    total, first, second = update(reduced, first_moments, second_moments)
    averaged, momentum, new_weights, first, second, loss = finish(total, flat, outer_momentum.reshape(SHARD, 128), first, second, loss)
    return (
        averaged.reshape(-1),
        momentum.reshape(-1),
        new_weights.reshape(-1),
        first,
        second,
        loss,
    )


def solution(mesh):
    placed = (
        P("rep", None, None, "fsdp", None, None),
        P("rep", None, None, "fsdp"),
        P("rep", None, None),
        P("fsdp"),
        P("rep", "fsdp"),
        P("rep", "fsdp"),
        P("fsdp"),
    )
    return jax.shard_map(
        body,
        mesh=mesh,
        in_specs=placed,
        out_specs=(
            P("fsdp"),
            P("fsdp"),
            P("fsdp"),
            P("rep", "fsdp"),
            P("rep", "fsdp"),
            P("rep", None),
        ),
        check_vma=False,
    )
```
